32 devices in a mesh: req: 4 (over x, core), blk: 8 (over z, y).
Axes of the slice: x: 2, y: 2, z: 4, core: 2. Of those that a mesh axis runs over, the one named last changes fastest.
Arguments:
- queries: bfloat16 [4, 8, 512, 512], P('req', 'blk'), may hold values from -6 to 6
- keys: bfloat16 [4, 8, 512, 256], P('req', 'blk'), may hold values from -25 to 25
- values: bfloat16 [4, 8, 512, 256], P('req', 'blk'), may hold values from -6 to 6
- block_map: int32 [4, 2, 2], P('req'), may hold values from 0 to 3, as said below
- lengths: int32 [4], P('req'), may hold values from 256 to 1024
- group_of_prompt: int32 [4], replicated, may hold values from 0 to 3, each once
- decode_rank: int32 [4, 8], P('req'), may hold values from 0 to 7, as said below
Outputs:
- attended: bfloat16 [4, 8, 512, 512], P('req', 'blk')
- cache: bfloat16 [4, 1024, 2048], P('req', 'blk')
The draws below stay inside these ranges and needn't reach their ends.
Inputs may be any that keep to these rules, and one draw needn't show every extreme that they name: In each group, block_map[g] holds each of 0 to 3 once, and the two halves of each slot hold blocks b and 3 - b, in either order. `decode_rank`: each group's row holds each of 0 to 7 once.
All inputs are finite; a program needn't handle non-finite values.
Results may differ from the reference program's by a relative error of at most 0.0098.
Values may be sent and summed in bfloat16 or wider, within the bound.
No kernel may reach another device: no remote copies, remote signals or barrier semaphores. Data moves between devices by JAX's collectives and lax.ppermute only.
A program may use at most 64 MiB of HBM per device.

```python
import math
import jax
import jax.numpy as jnp
from jax import lax

QUERY_HEADS = 16
KEY_VALUE_HEADS = 8
HEAD_SIZE = 128
HEAD_DIVISIONS = 4
TOK_DEV = 512
BLOCK = 256
Q_DEV = 4
KV_DEV = 2
SLOTS = 2
PROMPT_CAPACITY = 1024
DEC_DEV = 128
N_REQ = 4
N_BLK = 8


def draw_keys(key, part):
    scale_key, noise_key = jax.random.split(jax.random.fold_in(key, 7), 2)
    spread = jnp.exp(jax.random.uniform(scale_key, (N_REQ, N_BLK, TOK_DEV, KV_DEV, 1), jnp.float32, math.log(2.7), math.log(3.3)))
    noise_part = jnp.clip(jax.random.normal(noise_key, (N_REQ, N_BLK, TOK_DEV, KV_DEV, HEAD_SIZE), jnp.float32), -5.0, 5.0)
    return (noise_part * spread).reshape(N_REQ, N_BLK, TOK_DEV, KV_DEV * HEAD_SIZE).astype(jnp.bfloat16)


def draw_block_map(key, part):
    order_key, flip_key = jax.random.split(jax.random.fold_in(key, 11), 2)
    key_list = jax.random.split(order_key, N_REQ)
    ordering = jax.vmap(lambda subkey: jax.random.permutation(subkey, SLOTS))(key_list).astype(jnp.int32)
    mirrored = (2 * SLOTS - 1 - ordering).astype(jnp.int32)
    flipped = jax.random.randint(flip_key, (N_REQ, SLOTS), 0, 2, jnp.int32)
    first_half = jnp.where(flipped == 1, mirrored, ordering)
    second_half = jnp.where(flipped == 1, ordering, mirrored)
    return jnp.stack([first_half, second_half], axis=2).astype(jnp.int32)


def draw_decode_rank(key, part):
    key_list = jax.random.split(jax.random.fold_in(key, 13), N_REQ)
    ordering = jax.vmap(lambda subkey: jax.random.permutation(subkey, N_BLK))(key_list)
    return ordering.astype(jnp.int32)


def set_ends(drawn, stream_key, least, top_value):
    longest = drawn.shape.index(max(drawn.shape))
    spots = []
    for shift in (0, 1):
        where = [jax.random.randint(jax.random.fold_in(stream_key, axis), (), 0, length) for axis, length in enumerate(drawn.shape)]
        where[longest] = (where[longest] + shift) % drawn.shape[longest]
        spots.append(tuple(where))
    return drawn.at[spots[0]].set(least).at[spots[1]].set(top_value)


def levels(rng, shape, cuts, low, largest):
    loudness = 1.0
    for dim, shards_of in cuts:
        draws = jax.random.uniform(jax.random.fold_in(jax.random.fold_in(rng, 6), dim), (shards_of,), jnp.float32, low / len(cuts), largest / len(cuts))
        loudness = loudness * jnp.repeat(jnp.exp(draws), shape[dim] // shards_of).reshape((-1,) + (1,) * (len(shape) - 1 - dim))
    return loudness


def centred(own_key, shape, scale, reach, cuts=(), kind=jnp.bfloat16):
    values = jax.random.normal(own_key, shape, jnp.float32) * scale
    if len(cuts) > 0:
        values = levels(own_key, shape, cuts, -0.22, 0.18) * values
    return jnp.clip(values, min=-reach, max=reach).astype(kind)


def setup_inputs(seed: int = 0) -> dict:
    seeds = jax.random.split(jax.random.key(seed), 8)
    queries = centred(seeds[0], (N_REQ, N_BLK, TOK_DEV, Q_DEV * HEAD_SIZE), 1.0, 6.0, ((0, 4), (1, 8)))
    keys = draw_keys(jax.random.fold_in(seeds[7], 71), 0)
    values = centred(seeds[2], (N_REQ, N_BLK, TOK_DEV, KV_DEV * HEAD_SIZE), 1.0, 6.0, ((0, 4), (1, 8)))
    block_map = draw_block_map(jax.random.fold_in(seeds[7], 71), 0)
    lengths = set_ends(jax.random.randint(seeds[4], (N_REQ,), PROMPT_CAPACITY // 4, PROMPT_CAPACITY + 1), jax.random.fold_in(seeds[4], 1), PROMPT_CAPACITY // 4, PROMPT_CAPACITY).astype(jnp.int32)
    group_of_prompt = jax.random.permutation(seeds[5], N_REQ).astype(jnp.int32)
    decode_rank = draw_decode_rank(jax.random.fold_in(seeds[7], 71), 0)
    return dict(queries=queries, keys=keys, values=values, block_map=block_map, lengths=lengths, group_of_prompt=group_of_prompt, decode_rank=decode_rank)


cap_value = 50.0
query_scale = 1.0 / 12.0
rope_base = 10000.0


def apply_rotary(row_block, token_position, head_count):
    row_count = row_block.shape[0]
    head_width = row_block.shape[1] // head_count
    half_width = head_width // 2
    shaped = row_block.astype(jnp.float32).reshape(row_count, head_count, head_width)
    frequency = jnp.exp(-math.log(rope_base) * (2.0 * jnp.arange(half_width, dtype=jnp.float32)) / head_width)
    angles = token_position.astype(jnp.float32)[:, None] * frequency[None, :]
    cosine = jnp.cos(angles)[:, None, :]
    sine_part = jnp.sin(angles)[:, None, :]
    front_half = shaped[:, :, :half_width]
    second = shaped[:, :, half_width:]
    turned = jnp.concatenate([front_half * cosine - second * sine_part, second * cosine + front_half * sine_part], axis=2)
    return turned.reshape(row_count, head_count * head_width)


def whole_rows(array, cache_slot_count):
    width = array.shape[2]
    shaped = array.reshape(cache_slot_count, HEAD_DIVISIONS, TOK_DEV, width)
    return jnp.transpose(shaped, (0, 2, 1, 3)).reshape(PROMPT_CAPACITY, HEAD_DIVISIONS * width)


def reference(queries, keys, values, block_map, lengths, group_of_prompt, decode_rank):
    cache_slot_count = N_BLK // HEAD_DIVISIONS
    key_value_width = KEY_VALUE_HEADS * HEAD_SIZE
    group_portion = QUERY_HEADS // KEY_VALUE_HEADS
    row_ids = jnp.arange(PROMPT_CAPACITY, dtype=jnp.int32)
    query_extent = 512 if PROMPT_CAPACITY % 512 == 0 else PROMPT_CAPACITY
    group_ids = jnp.arange(N_REQ, dtype=jnp.int32)

    def one_group(element):
        query_dev, key_dev, value_dev, block_table, rank_of, group_id = element
        query_rows = whole_rows(query_dev, cache_slot_count)
        key_row_list = whole_rows(key_dev, cache_slot_count)
        value_row_list = whole_rows(value_dev, cache_slot_count)
        length = jnp.sum(jnp.where(group_of_prompt == group_id, lengths, 0))
        flat_map = block_table.reshape(-1)
        token_position = (flat_map[row_ids // BLOCK] * BLOCK + row_ids % BLOCK).astype(jnp.int32)
        query_rot = (apply_rotary(query_rows, token_position, QUERY_HEADS) * query_scale).astype(jnp.bfloat16)
        rotated_key = apply_rotary(key_row_list, token_position, KEY_VALUE_HEADS).astype(jnp.bfloat16)
        widened_keys = rotated_key.astype(jnp.float32).reshape(PROMPT_CAPACITY, KEY_VALUE_HEADS, HEAD_SIZE)
        widened_values = value_row_list.astype(jnp.float32).reshape(PROMPT_CAPACITY, KEY_VALUE_HEADS, HEAD_SIZE)

        def one_block(pair):
            query_piece, query_pos = pair
            query_head_rows = query_piece.astype(jnp.float32).reshape(query_extent, KEY_VALUE_HEADS, group_portion, HEAD_SIZE)
            scores = jnp.einsum("qkgd,nkd->kgqn", query_head_rows, widened_keys, precision=lax.Precision.HIGHEST)
            capped = cap_value * jnp.tanh(scores / cap_value)
            allowed = token_position[None, :] <= query_pos[:, None]
            expo_vals = jnp.where(allowed[None, None], jnp.exp(capped), jnp.float32(0.0))
            weight = lax.optimization_barrier(expo_vals.astype(jnp.bfloat16)).astype(jnp.float32)
            numerator = jnp.einsum("kgqn,nkd->qkgd", weight, widened_values, precision=lax.Precision.HIGHEST)
            denominator = jnp.sum(expo_vals, axis=3)
            output = numerator / jnp.transpose(denominator, (2, 0, 1))[..., None]
            output = output.reshape(query_extent, QUERY_HEADS * HEAD_SIZE)
            return jnp.where((query_pos < length)[:, None], output, jnp.float32(0.0)).astype(jnp.bfloat16)

        attended = lax.map(one_block, (query_rot.reshape(PROMPT_CAPACITY // query_extent, query_extent, QUERY_HEADS * HEAD_SIZE), token_position.reshape(PROMPT_CAPACITY // query_extent, query_extent)))
        attended = attended.reshape(cache_slot_count, TOK_DEV, HEAD_DIVISIONS, Q_DEV * HEAD_SIZE)
        attended = jnp.transpose(attended, (0, 2, 1, 3)).reshape(N_BLK, TOK_DEV, Q_DEV * HEAD_SIZE)
        joined = jnp.concatenate([rotated_key, value_row_list], axis=1)
        joined = jnp.where((token_position < length)[:, None], joined, jnp.zeros_like(joined))
        target = (rank_of[token_position % N_BLK] * DEC_DEV + token_position // N_BLK).astype(jnp.int32)
        cache_rows = jnp.zeros((PROMPT_CAPACITY, 2 * key_value_width), jnp.bfloat16).at[target].set(joined)
        return attended, cache_rows

    attended, cache_rows = lax.map(one_group, (queries, keys, values, block_map, decode_rank, group_ids))
    return attended, cache_rows
```

```python
import math

import jax
import jax.numpy as jnp
import numpy as np
from jax import lax
from jax.experimental import pallas as pl
from jax.experimental.pallas import tpu as pltpu
from jax.sharding import PartitionSpec as P

QUERY_HEADS = 16
KEY_VALUE_HEADS = 8
HEAD_SIZE = 128
HEAD_DIVISIONS = 4
Q_DEV = 4
KV_DEV = 2
KV_WIDTH = KV_DEV * HEAD_SIZE

cap_value = 50.0
query_scale = 1.0 / 12.0
rope_base = 10000.0
VMEM_BYTES = 48 * 1024 * 1024

f32 = jnp.float32
bf16 = jnp.bfloat16
SMEM = pl.BlockSpec(memory_space=pltpu.SMEM)
VMEM = pl.BlockSpec(memory_space=pltpu.VMEM)


def shifted(shard, axis, by):
    peers = lax.axis_size(axis)
    return lax.ppermute(shard, axis, [(i, (i + by) % peers) for i in range(peers)])


def crossed(shard, axis, by):
    peers = lax.axis_size(axis)
    return lax.ppermute(shard, axis, [(i, i ^ by) for i in range(peers)])


def rotary_tables(block_len, block_count):
    half = HEAD_SIZE // 2
    frequency = np.exp(
        np.float32(-math.log(rope_base)) * (2.0 * np.arange(half, dtype=np.float32)) / HEAD_SIZE
    ).astype(np.float64)

    def table(positions):
        angles = positions.astype(np.float64)[:, None] * frequency[None, :]
        cosine, sine = np.cos(angles), np.sin(angles)
        return np.stack(
            [np.concatenate([cosine, cosine], 1), np.concatenate([-sine, sine], 1)]
        ).astype(np.float32)

    return table(np.arange(block_len)), table(np.arange(block_count) * block_len)


def block_angles(row_table, block_table, block):
    row_cos, row_sin = row_table[0], row_table[1]
    blk_cos, blk_sin = block_table[0, pl.ds(block, 1)], block_table[1, pl.ds(block, 1)]
    return row_cos * blk_cos - row_sin * blk_sin, row_sin * blk_cos + row_cos * blk_sin


def turned(head, angles):
    x = head.astype(f32)
    return x * angles[0] + pltpu.roll(x, HEAD_SIZE // 2, 1) * angles[1]


def send_index(rank_ref, slot, head_group, row_ids, residues):
    residue = row_ids % residues
    rank = jnp.zeros_like(row_ids)
    for r in range(residues):
        rank = jnp.where(residue == r, rank_ref[0, r], rank)
    ahead = (rank - HEAD_DIVISIONS * slot + residues) % residues
    return jnp.where(ahead < HEAD_DIVISIONS, ahead ^ head_group, ahead)


def order_matrix(rank_ref, slot, head_group, out_rows, rows, residues):
    row_ids = lax.broadcasted_iota(jnp.int32, (1, rows), 1)
    ahead = send_index(rank_ref, slot, head_group, row_ids, residues)
    index = ahead * (rows // residues) + row_ids // residues
    out_ids = lax.broadcasted_iota(jnp.int32, (out_rows, rows), 0)
    return jnp.where(out_ids == index, 1.0, 0.0).astype(bf16)


def dot(a, b):
    return jnp.dot(a, b, preferred_element_type=f32)


def dot_t(a, b):
    return lax.dot_general(a, b, (((1,), (1,)), ((), ())), preferred_element_type=f32)


def expo_of(scores):
    return jnp.exp(cap_value * jnp.tanh(scores * (1.0 / cap_value)))


def columns(index, width=HEAD_SIZE):
    return slice(index * width, (index + 1) * width)


def call(body, out_shape, in_specs, name, scratch=(), flops=10**8, moved=10**6):
    return pl.pallas_call(
        body,
        out_shape=out_shape,
        in_specs=in_specs,
        out_specs=jax.tree.map(lambda _: VMEM, out_shape),
        scratch_shapes=scratch,
        compiler_params=pltpu.CompilerParams(vmem_limit_bytes=VMEM_BYTES),
        cost_estimate=pl.CostEstimate(flops=flops, bytes_accessed=moved, transcendentals=0),
        name=name,
    )


def order_values(values, decode_rank, slots, member):
    rows, width = values.shape
    block_len = rows // 2
    residues = decode_rank.shape[1]
    first = block_len // slots

    def body(me_ref, rank_ref, v_ref, *outs):
        slot, head_group = me_ref[0] // HEAD_DIVISIONS, me_ref[0] % HEAD_DIVISIONS
        for turn in range(1, slots):
            order = order_matrix(
                rank_ref, (slot + turn) % slots, head_group, block_len, block_len, residues
            )
            head_ref, tail_ref = outs[2 * turn - 2], outs[2 * turn - 1]
            rest = block_len - first
            for half in range(2):
                moved = dot(order, v_ref[half * block_len : (half + 1) * block_len]).astype(bf16)
                head_ref[half * first : (half + 1) * first] = moved[:first]
                tail_ref[half * rest : (half + 1) * rest] = moved[first:]

    shapes = []
    for _ in range(1, slots):
        shapes.append(jax.ShapeDtypeStruct((2 * first, width), bf16))
        shapes.append(jax.ShapeDtypeStruct((2 * (block_len - first), width), bf16))
    return call(body, shapes, [SMEM, SMEM, VMEM], "order_values")(member, decode_rank, values)


def own_part(queries, keys, values, table, member, tables):
    rows = queries.shape[0]
    block_len = rows // 2

    def body(me_ref, map_ref, q_ref, k_ref, v_ref, row_ref, blk_ref, qr_ref, kr_ref, num_ref, den_ref):
        slot = me_ref[0] // HEAD_DIVISIONS
        num_ref[...] = jnp.zeros_like(num_ref)
        den_ref[...] = jnp.zeros_like(den_ref)
        for half in range(2):
            part = columns(half, block_len)
            angles = block_angles(row_ref, blk_ref, map_ref[0, slot, half])
            for head in range(Q_DEV):
                qr_ref[part, columns(head)] = (
                    turned(q_ref[part, columns(head)], angles) * query_scale
                ).astype(bf16)
            for head in range(KV_DEV):
                kr_ref[part, columns(head)] = turned(k_ref[part, columns(head)], angles).astype(bf16)

        def tile(half, other, diagonal):
            q_part, k_part = columns(half, block_len), columns(other, block_len)
            for head in range(Q_DEV):
                key_head = head * KV_DEV // Q_DEV
                expo = expo_of(dot_t(qr_ref[q_part, columns(head)], kr_ref[k_part, columns(key_head)]))
                if diagonal:
                    row = lax.broadcasted_iota(jnp.int32, expo.shape, 0)
                    col = lax.broadcasted_iota(jnp.int32, expo.shape, 1)
                    expo = jnp.where(col <= row, expo, 0.0)
                num_ref[q_part, columns(head)] += dot(
                    expo.astype(bf16), v_ref[k_part, columns(key_head)]
                )
                lanes = expo[:, :HEAD_SIZE]
                for j in range(1, block_len // HEAD_SIZE):
                    lanes = lanes + expo[:, columns(j)]
                den_ref[q_part, columns(head)] += lanes

        for half in range(2):
            tile(half, half, True)
            pl.when(map_ref[0, slot, 1 - half] < map_ref[0, slot, half])(
                lambda half=half: tile(half, 1 - half, False)
            )

    shapes = [
        jax.ShapeDtypeStruct(queries.shape, bf16),
        jax.ShapeDtypeStruct(keys.shape, bf16),
        jax.ShapeDtypeStruct(queries.shape, f32),
        jax.ShapeDtypeStruct(queries.shape, f32),
    ]
    return call(body, shapes, [SMEM, SMEM] + [VMEM] * 5, "own_part", flops=4 * 10**8, moved=4 * 10**6)(
        member, table, queries, keys, values, *tables
    )


def other_keys(arrived, query_rot, key_rot, values, den, table, decode_rank, member, length, tables):
    rows, width = key_rot.shape
    block_len = rows // 2
    slots = table.shape[1]
    residues = decode_rank.shape[1]
    piece = rows // residues

    def body(me_ref, map_ref, rank_ref, len_ref, q_ref, k_ref, v_ref, den_ref, row_ref, blk_ref, *rest):
        in_refs, rest = rest[: slots - 1], rest[slots - 1 :]
        w_refs, rest = rest[: slots - 1], rest[slots - 1 :]
        inv_ref, e_refs, k_scr, d_scr = rest[0], rest[1:5], rest[5], rest[6]
        slot, head_group = me_ref[0] // HEAD_DIVISIONS, me_ref[0] % HEAD_DIVISIONS
        select = order_matrix(rank_ref, slot, head_group, rows // slots, rows, residues)

        def emit(place, rotated):
            chosen = dot(select, rotated).astype(bf16)
            for m in range(HEAD_DIVISIONS):
                e_refs[m][columns(place, piece)] = chosen[columns(m, piece)]

        emit(0, k_ref[...])
        emit(slots, v_ref[...])
        d_scr[...] = den_ref[...]
        order = order_matrix(rank_ref, slot, head_group, block_len, block_len, residues)
        for turn in range(1, slots):
            source = (slot - turn + slots) % slots
            w_ref = w_refs[turn - 1]
            for half in range(2):
                part = columns(half, block_len)
                angles = block_angles(row_ref, blk_ref, map_ref[0, source, half])
                for head in range(KV_DEV):
                    k_scr[part, columns(head)] = turned(
                        in_refs[turn - 1][part, columns(head)], angles
                    ).astype(bf16)
            emit(turn, k_scr[...])
            for half in range(2):
                part = columns(half, block_len)
                k_scr[part] = dot(order, k_scr[part]).astype(bf16)

            def tile(half, other):
                q_part, k_part = columns(half, block_len), columns(other, block_len)
                for head in range(Q_DEV):
                    key_head = head * KV_DEV // Q_DEV
                    expo = expo_of(
                        dot_t(q_ref[q_part, columns(head)], k_scr[k_part, columns(key_head)])
                    )
                    w_ref[head, q_part, k_part] = expo.astype(bf16)
                    lanes = expo[:, :HEAD_SIZE]
                    for j in range(1, block_len // HEAD_SIZE):
                        lanes = lanes + expo[:, columns(j)]
                    d_scr[q_part, columns(head)] += lanes

            for half in range(2):
                for other in range(2):
                    pl.when(map_ref[0, source, other] < map_ref[0, slot, half])(
                        lambda half=half, other=other: tile(half, other)
                    )
        for half in range(2):
            part = columns(half, block_len)
            start = map_ref[0, slot, half] * block_len
            live = start + lax.broadcasted_iota(jnp.int32, (block_len, 1), 0) < len_ref[0]
            for head in range(Q_DEV):
                total = jnp.sum(d_scr[part, columns(head)], axis=1, keepdims=True)
                inv_ref[part, head : head + 1] = jnp.where(live, 1.0 / total, 0.0)

    shapes = [jax.ShapeDtypeStruct((Q_DEV, rows, rows), bf16) for _ in range(1, slots)]
    shapes.append(jax.ShapeDtypeStruct((rows, HEAD_SIZE), f32))
    shapes += [
        jax.ShapeDtypeStruct(((slots + 1) * piece, width), bf16) for _ in range(HEAD_DIVISIONS)
    ]
    scratch = [pltpu.VMEM((rows, width), bf16), pltpu.VMEM((rows, Q_DEV * HEAD_SIZE), f32)]
    outs = call(
        body,
        shapes,
        [SMEM] * 4 + [VMEM] * (5 + slots),
        "other_keys",
        scratch,
        flops=3 * 10**8,
        moved=4 * 10**6,
    )(member, table, decode_rank, length, query_rot, key_rot, values, den, *tables, *arrived)
    return outs[: slots - 1], outs[slots - 1], outs[slots:]


def cache_part(first, second, table, decode_rank, member, length, block_len):
    slots = table.shape[1]
    residues = decode_rank.shape[1]
    run = block_len // residues
    cache_rows = 2 * slots * run
    width = first[0].shape[1]

    def body(me_ref, map_ref, rank_ref, len_ref, *refs):
        f_refs, s_refs, out_ref = refs[:4], refs[4:8], refs[8]
        slot, head_group = me_ref[0] // HEAD_DIVISIONS, me_ref[0] % HEAD_DIVISIONS
        residue = 0
        for r in range(1, residues):
            residue = jnp.where(rank_ref[0, r] == me_ref[0], r, residue)
        col = lax.broadcasted_iota(jnp.int32, (1, cache_rows), 1)
        part, offset = col // run, col % run
        target = jnp.zeros_like(col)
        for turn in range(slots):
            for half in range(2):
                block = map_ref[0, (slot - turn + slots) % slots, half]
                target = jnp.where(part == 2 * turn + half, block * run + offset, target)
        target = jnp.where(target * residues + residue < len_ref[0], target, -1)
        row = lax.broadcasted_iota(jnp.int32, (cache_rows, cache_rows), 0)
        place = jnp.where(row == target, 1.0, 0.0).astype(bf16)
        for m in range(HEAD_DIVISIONS):
            column = (head_group ^ m) * width
            keys = f_refs[m][:cache_rows]
            values = jnp.concatenate([f_refs[m][cache_rows:], s_refs[m][...]], axis=0)
            out_ref[:, pl.ds(pl.multiple_of(column, HEAD_SIZE), width)] = dot(place, keys).astype(bf16)
            column = column + HEAD_DIVISIONS * width
            out_ref[:, pl.ds(pl.multiple_of(column, HEAD_SIZE), width)] = dot(place, values).astype(bf16)

    shape = jax.ShapeDtypeStruct((cache_rows, 2 * HEAD_DIVISIONS * width), bf16)
    return call(body, shape, [SMEM] * 4 + [VMEM] * 8, "cache_part")(
        member, table, decode_rank, length, *first, *second
    )


def finish(weights, heads, tails, num, inverse, table, member):
    rows = num.shape[0]
    block_len = rows // 2
    slots = table.shape[1]

    def body(me_ref, map_ref, num_ref, inv_ref, *refs):
        w_refs, h_refs, t_refs = refs[: slots - 1], refs[slots - 1 : 2 * slots - 2], refs[2 * slots - 2 : 3 * slots - 3]
        out_ref, acc = refs[-2:]
        slot = me_ref[0] // HEAD_DIVISIONS
        acc[...] = num_ref[...]
        for turn in range(1, slots):
            source = (slot - turn + slots) % slots
            h_ref, t_ref, w_ref = h_refs[turn - 1], t_refs[turn - 1], w_refs[turn - 1]
            for other in range(2):
                first, rest = h_ref.shape[0] // 2, t_ref.shape[0] // 2

                def tile(half):
                    q_part, k_part = columns(half, block_len), columns(other, block_len)
                    block = jnp.concatenate(
                        [h_ref[columns(other, first)], t_ref[columns(other, rest)]], axis=0
                    )
                    for head in range(Q_DEV):
                        key_head = head * KV_DEV // Q_DEV
                        acc[q_part, columns(head)] += dot(
                            w_ref[head, q_part, k_part], block[:, columns(key_head)]
                        )

                for half in range(2):
                    pl.when(map_ref[0, source, other] < map_ref[0, slot, half])(
                        lambda half=half: tile(half)
                    )
        for head in range(Q_DEV):
            out_ref[:, columns(head)] = (acc[:, columns(head)] * inv_ref[:, head : head + 1]).astype(bf16)

    shape = jax.ShapeDtypeStruct(num.shape, bf16)
    return call(
        body,
        shape,
        [SMEM] * 2 + [VMEM] * (2 + 3 * (slots - 1)),
        "finish",
        [pltpu.VMEM(num.shape, f32)],
        flops=3 * 10**8,
        moved=4 * 10**6,
    )(member, table, num, inverse, *weights, *heads, *tails)


def on_device(queries, keys, values, block_map, lengths, group_of_prompt, decode_rank):
    rows = queries.shape[2]
    block_len = rows // 2
    slots = block_map.shape[1]
    member = lax.axis_index("blk").reshape(1).astype(jnp.int32)
    group_id = lax.axis_index("req")
    q, k, v = queries[0, 0], keys[0, 0], values[0, 0]
    tables = rotary_tables(block_len, 2 * slots)

    key_in = [shifted(k, "blk", HEAD_DIVISIONS * turn) for turn in range(1, slots)]
    ordered = order_values(v, decode_rank, slots, member)
    heads = [shifted(ordered[2 * t - 2], "blk", HEAD_DIVISIONS * t) for t in range(1, slots)]
    tails = [shifted(ordered[2 * t - 1], "blk", HEAD_DIVISIONS * t) for t in range(1, slots)]

    all_lengths = lax.all_gather(lengths, "req", axis=0, tiled=True)
    length = jnp.sum(jnp.where(group_of_prompt == group_id, all_lengths, 0)).reshape(1)

    query_rot, key_rot, num, den = own_part(q, k, v, block_map, member, tables)
    weights, inverse, pieces = other_keys(
        key_in, query_rot, key_rot, v, den, block_map, decode_rank, member, length, tables
    )
    first = [pieces[0]] + [crossed(pieces[m], "blk", m) for m in range(1, HEAD_DIVISIONS)]

    def value_piece(m):
        parts = []
        for head in heads:
            run = head.shape[0] // 2 // HEAD_DIVISIONS
            shaped = head.reshape(2, HEAD_DIVISIONS, run, KV_WIDTH)
            parts.append(shaped[:, m].reshape(2 * run, KV_WIDTH))
        return jnp.concatenate(parts, axis=0)

    second = [value_piece(0)] + [
        crossed(value_piece(m), "blk", m) for m in range(1, HEAD_DIVISIONS)
    ]
    cache = cache_part(first, second, block_map, decode_rank, member, length, block_len)
    attended = finish(weights, heads, tails, num, inverse, block_map, member)
    return (attended[None, None], cache[None])


def solution(mesh):
    placed = (
        P("req", "blk", None, None),
        P("req", "blk", None, None),
        P("req", "blk", None, None),
        P("req", None, None),
        P("req"),
        P(),
        P("req", None),
    )
    return jax.shard_map(
        on_device,
        mesh=mesh,
        in_specs=placed,
        out_specs=(P("req", "blk", None, None), P("req", "blk", None)),
        check_vma=False,
    )
```

```python
import math

import jax
import jax.numpy as jnp
import numpy as np
from jax import lax
from jax.experimental import pallas as pl
from jax.experimental.pallas import tpu as pltpu
from jax.sharding import PartitionSpec as P

QUERY_HEADS = 16
KEY_VALUE_HEADS = 8
HEAD_SIZE = 128
HEAD_DIVISIONS = 4
Q_DEV = 4
KV_DEV = 2
KV_WIDTH = KV_DEV * HEAD_SIZE

cap_value = 50.0
query_scale = 1.0 / 12.0
rope_base = 10000.0
VMEM_BYTES = 48 * 1024 * 1024

f32 = jnp.float32
bf16 = jnp.bfloat16
SMEM = pl.BlockSpec(memory_space=pltpu.SMEM)
VMEM = pl.BlockSpec(memory_space=pltpu.VMEM)
HBM = pl.BlockSpec(memory_space=pltpu.HBM)


def shifted(shard, axis, by):
    peers = lax.axis_size(axis)
    return lax.ppermute(shard, axis, [(i, (i + by) % peers) for i in range(peers)])


def crossed(shard, axis, by):
    peers = lax.axis_size(axis)
    return lax.ppermute(shard, axis, [(i, i ^ by) for i in range(peers)])


def rotary_tables(block_len, block_count):
    half = HEAD_SIZE // 2
    frequency = np.exp(
        np.float32(-math.log(rope_base)) * (2.0 * np.arange(half, dtype=np.float32)) / HEAD_SIZE
    ).astype(np.float64)

    def table(positions):
        angles = positions.astype(np.float64)[:, None] * frequency[None, :]
        cosine, sine = np.cos(angles), np.sin(angles)
        return np.stack(
            [np.concatenate([cosine, cosine], 1), np.concatenate([-sine, sine], 1)]
        ).astype(np.float32)

    return table(np.arange(block_len)), table(np.arange(block_count) * block_len)


def block_angles(row_table, block_table, block):
    row_cos, row_sin = row_table[0], row_table[1]
    blk_cos, blk_sin = block_table[0, pl.ds(block, 1)], block_table[1, pl.ds(block, 1)]
    return row_cos * blk_cos - row_sin * blk_sin, row_sin * blk_cos + row_cos * blk_sin


def turned(head, angles):
    x = head.astype(f32)
    return x * angles[0] + pltpu.roll(x, HEAD_SIZE // 2, 1) * angles[1]


def send_index(rank_ref, slot, head_group, row_ids, residues):
    residue = row_ids % residues
    rank = jnp.zeros_like(row_ids)
    for r in range(residues):
        rank = jnp.where(residue == r, rank_ref[0, r], rank)
    ahead = (rank - HEAD_DIVISIONS * slot + residues) % residues
    return jnp.where(ahead < HEAD_DIVISIONS, ahead ^ head_group, ahead)


def order_matrix(rank_ref, slot, head_group, out_rows, rows, residues):
    row_ids = lax.broadcasted_iota(jnp.int32, (1, rows), 1)
    ahead = send_index(rank_ref, slot, head_group, row_ids, residues)
    index = ahead * (rows // residues) + row_ids // residues
    out_ids = lax.broadcasted_iota(jnp.int32, (out_rows, rows), 0)
    return jnp.where(out_ids == index, 1.0, 0.0).astype(bf16)


def dot(a, b):
    return jnp.dot(a, b, preferred_element_type=f32)


def dot_t(a, b):
    return lax.dot_general(a, b, (((1,), (1,)), ((), ())), preferred_element_type=f32)


def expo_of(scores):
    return jnp.exp2(cap_value * math.log2(math.e) * jnp.tanh(scores * (1.0 / cap_value)))


def columns(index, width=HEAD_SIZE):
    return slice(index * width, (index + 1) * width)


def call(body, out_shape, in_specs, name, scratch=(), flops=10**8, moved=10**6):
    return pl.pallas_call(
        body,
        out_shape=out_shape,
        in_specs=in_specs,
        out_specs=jax.tree.map(lambda _: VMEM, out_shape),
        scratch_shapes=scratch,
        compiler_params=pltpu.CompilerParams(vmem_limit_bytes=VMEM_BYTES),
        cost_estimate=pl.CostEstimate(flops=flops, bytes_accessed=moved, transcendentals=0),
        name=name,
    )


def fetch(sources, targets, sems):
    copies = [pltpu.make_async_copy(s, t, sems.at[i]) for i, (s, t) in enumerate(zip(sources, targets))]
    for copy in copies:
        copy.start()
    return copies


def lane_sums(expo):
    lanes = expo[:, :HEAD_SIZE]
    for j in range(1, expo.shape[1] // HEAD_SIZE):
        lanes = lanes + expo[:, columns(j)]
    return lanes


def halves_of(map_ref, slot):
    high = jnp.where(map_ref[0, slot, 1] > map_ref[0, slot, 0], 1, 0)
    return 1 - high, high


def active_tiles(map_ref, slot, source):
    low, high = halves_of(map_ref, slot)
    source_low, source_high = halves_of(map_ref, source)
    outer = map_ref[0, slot, low] < map_ref[0, source, source_low]
    return (
        (jnp.where(outer, high, low), source_low),
        (high, jnp.where(outer, source_high, source_low)),
    )


def rows_at(index, block_len):
    return pl.ds(pl.multiple_of(index * block_len, block_len), block_len)


def own_part(queries, keys, values, table, decode_rank, tables):
    rows = queries.shape[0]
    block_len = rows // 2
    slots = table.shape[1]
    residues = decode_rank.shape[1]
    piece = rows // residues
    first = block_len // slots
    rest = block_len - first
    width = keys.shape[1]

    def body(*refs):
        inputs, refs = refs[:7], refs[7:]
        qr_ref, num_ref, den_ref, select_ref, order_ref, angle_ref = refs[:6]
        e_refs, refs = refs[6:10], refs[10:]
        sent_refs, refs = refs[: 2 * (slots - 1)], refs[2 * (slots - 1) :]
        kr_ref, scratch, sems = refs[0], refs[1:8], refs[8]
        q_ref, k_ref, v_ref, row_ref, blk_ref, map_ref, rank_ref = scratch
        copies = fetch(inputs, scratch, sems)
        member = lax.axis_index("blk")
        slot, head_group = member // HEAD_DIVISIONS, member % HEAD_DIVISIONS

        copies[6].wait()
        copies[2].wait()
        for turn in range(1, slots):
            order = order_matrix(
                rank_ref, (slot + turn) % slots, head_group, block_len, block_len, residues
            )
            head_ref, tail_ref = sent_refs[2 * turn - 2], sent_refs[2 * turn - 1]
            for half in range(2):
                moved = dot(order, v_ref[columns(half, block_len)]).astype(bf16)
                head_ref[columns(half, first)] = moved[:first]
                tail_ref[columns(half, rest)] = moved[first:]
        select = order_matrix(rank_ref, slot, head_group, rows // slots, rows, residues)
        select_ref[...] = select
        order_ref[...] = order_matrix(rank_ref, slot, head_group, block_len, block_len, residues)

        copies[0].wait()
        copies[1].wait()
        copies[3].wait()
        copies[4].wait()
        copies[5].wait()
        for half in range(2):
            part = columns(half, block_len)
            angles = block_angles(row_ref, blk_ref, map_ref[0, slot, half])
            for head in range(Q_DEV):
                qr_ref[part, columns(head)] = (
                    turned(q_ref[part, columns(head)], angles) * query_scale
                ).astype(bf16)
            for head in range(KV_DEV):
                kr_ref[part, columns(head)] = turned(k_ref[part, columns(head)], angles).astype(bf16)
            for turn in range(1, slots):
                other = block_angles(row_ref, blk_ref, map_ref[0, (slot - turn + slots) % slots, half])
                angle_ref[turn - 1, half, 0] = other[0]
                angle_ref[turn - 1, half, 1] = other[1]
        for place, source in ((0, kr_ref), (1, v_ref)):
            chosen = dot(select, source[...]).astype(bf16)
            for m in range(HEAD_DIVISIONS):
                e_refs[m][columns(place, piece)] = chosen[columns(m, piece)]

        low, high = halves_of(map_ref, slot)
        low, high = rows_at(low, block_len), rows_at(high, block_len)
        row = lax.broadcasted_iota(jnp.int32, (block_len, block_len), 0)
        col = lax.broadcasted_iota(jnp.int32, (block_len, block_len), 1)
        for head in range(Q_DEV):
            key_head = columns(head * KV_DEV // Q_DEV)

            def tile(q_part, k_part, diagonal):
                expo = expo_of(dot_t(qr_ref[q_part, columns(head)], kr_ref[k_part, key_head]))
                if diagonal:
                    expo = jnp.where(col <= row, expo, 0.0)
                return dot(expo.astype(bf16), v_ref[k_part, key_head]), lane_sums(expo)

            num, den = tile(low, low, True)
            num_ref[low, columns(head)] = num
            den_ref[low, columns(head)] = den
            num, den = tile(high, high, True)
            more, lanes = tile(high, low, False)
            num_ref[high, columns(head)] = num + more
            den_ref[high, columns(head)] = den + lanes

    shapes = [
        jax.ShapeDtypeStruct(queries.shape, bf16),
        jax.ShapeDtypeStruct(queries.shape, f32),
        jax.ShapeDtypeStruct(queries.shape, f32),
        jax.ShapeDtypeStruct((rows // slots, rows), bf16),
        jax.ShapeDtypeStruct((block_len, block_len), bf16),
        jax.ShapeDtypeStruct((slots - 1, 2, 2, block_len, HEAD_SIZE), f32),
    ]
    shapes += [jax.ShapeDtypeStruct((2 * piece, width), bf16) for _ in range(HEAD_DIVISIONS)]
    for _ in range(1, slots):
        shapes.append(jax.ShapeDtypeStruct((2 * first, width), bf16))
        shapes.append(jax.ShapeDtypeStruct((2 * rest, width), bf16))
    arrays = (queries, keys, values, *tables, table, decode_rank)
    scratch = [pltpu.VMEM(keys.shape, bf16)]
    scratch += [pltpu.VMEM(x.shape, x.dtype) for x in arrays[:5]]
    scratch += [pltpu.SMEM(x.shape, x.dtype) for x in arrays[5:]]
    scratch.append(pltpu.SemaphoreType.DMA((7,)))
    outs = call(body, shapes, [HBM] * 7, "own_part", scratch, flops=6 * 10**8, moved=6 * 10**6)(*arrays)
    return outs[:6], outs[6:10], outs[10:]


def other_keys(arrived, query_rot, den, select, order, angles, table, decode_rank, owner, lens):
    rows, width = arrived[0].shape
    block_len = rows // 2
    slots = table.shape[1]
    residues = decode_rank.shape[1]
    piece = rows // residues
    run = block_len // residues
    cache_rows = slots * piece
    groups = len(lens)

    def body(*refs):
        small, refs = refs[: 3 + groups], refs[3 + groups :]
        q_ref, den_ref, select_ref, order_ref, angle_ref = refs[:5]
        refs = refs[5:]
        in_refs, refs = refs[: slots - 1], refs[slots - 1 :]
        w_refs, refs = refs[: slots - 1], refs[slots - 1 :]
        inv_ref, place_ref, e_refs = refs[0], refs[1], refs[2:6]
        k_scr, p_scr, d_scr, refs = refs[6], refs[7], refs[8], refs[9:]
        map_ref, rank_ref, owner_ref = refs[:3]
        len_refs, sems = refs[3 : 3 + groups], refs[3 + groups]
        copies = fetch(small, refs[: 3 + groups], sems)
        member = lax.axis_index("blk")
        group = lax.axis_index("req")
        slot = member // HEAD_DIVISIONS

        for copy in copies:
            copy.wait()
        d_scr[...] = den_ref[...]
        for turn in range(1, slots):
            source = (slot - turn + slots) % slots
            for half in range(2):
                part = columns(half, block_len)
                there = angle_ref[turn - 1, half, 0], angle_ref[turn - 1, half, 1]
                for head in range(KV_DEV):
                    k_scr[part, columns(head)] = turned(
                        in_refs[turn - 1][part, columns(head)], there
                    ).astype(bf16)
                p_scr[part] = dot(order_ref[...], k_scr[part]).astype(bf16)
            chosen = dot(select_ref[...], k_scr[...]).astype(bf16)
            for m in range(HEAD_DIVISIONS):
                e_refs[m][columns(turn - 1, piece)] = chosen[columns(m, piece)]
            for index, (half, other) in enumerate(active_tiles(map_ref, slot, source)):
                q_part, k_part = rows_at(half, block_len), rows_at(other, block_len)
                for head in range(Q_DEV):
                    key_head = columns(head * KV_DEV // Q_DEV)
                    expo = expo_of(dot_t(q_ref[q_part, columns(head)], p_scr[k_part, key_head]))
                    w_refs[turn - 1][index, head] = expo.astype(bf16)
                    d_scr[q_part, columns(head)] += lane_sums(expo)

        length = 0
        for turn in range(groups):
            mine = owner_ref[lax.rem(group - turn + groups, groups)] == group
            length = length + jnp.where(mine, len_refs[turn][0], 0)
        for half in range(2):
            part = columns(half, block_len)
            start = map_ref[0, slot, half] * block_len
            live = start + lax.broadcasted_iota(jnp.int32, (block_len, 1), 0) < length
            for head in range(Q_DEV):
                total = jnp.sum(d_scr[part, columns(head)], axis=1, keepdims=True)
                inv_ref[part, head : head + 1] = jnp.where(live, 1.0 / total, 0.0)

        residue = 0
        for r in range(1, residues):
            residue = jnp.where(rank_ref[0, r] == member, r, residue)
        col = lax.broadcasted_iota(jnp.int32, (1, cache_rows), 1)
        part, offset = col // run, col % run
        target = jnp.zeros_like(col)
        for turn in range(slots):
            for half in range(2):
                block = map_ref[0, (slot - turn + slots) % slots, half]
                target = jnp.where(part == 2 * turn + half, block * run + offset, target)
        target = jnp.where(target * residues + residue < length, target, -1)
        row = lax.broadcasted_iota(jnp.int32, (cache_rows, cache_rows), 0)
        place_ref[...] = jnp.where(row == target, 1.0, 0.0).astype(bf16)

    shapes = [
        jax.ShapeDtypeStruct((2, Q_DEV, block_len, block_len), bf16) for _ in range(1, slots)
    ]
    shapes.append(jax.ShapeDtypeStruct((rows, HEAD_SIZE), f32))
    shapes.append(jax.ShapeDtypeStruct((cache_rows, cache_rows), bf16))
    shapes += [
        jax.ShapeDtypeStruct(((slots - 1) * piece, width), bf16) for _ in range(HEAD_DIVISIONS)
    ]
    small = (table, decode_rank, owner, *lens)
    scratch = [pltpu.VMEM((rows, width), bf16)] * 2 + [pltpu.VMEM(den.shape, f32)]
    scratch += [pltpu.SMEM(x.shape, x.dtype) for x in small]
    scratch.append(pltpu.SemaphoreType.DMA((len(small),)))
    outs = call(
        body,
        shapes,
        [HBM] * len(small) + [VMEM] * (4 + slots),
        "other_keys",
        scratch,
        flops=3 * 10**8,
        moved=4 * 10**6,
    )(*small, query_rot, den, select, order, angles, *arrived)
    return outs[: slots - 1], outs[slots - 1], outs[slots], outs[slots + 1 :]


def cache_part(early, late, place):
    cache_rows = place.shape[0]
    piece = early[0].shape[0] // 2
    width = early[0].shape[1]

    def body(place_ref, *refs):
        f_refs, s_refs, out_ref = refs[:4], refs[4:8], refs[8]
        head_group = lax.axis_index("blk") % HEAD_DIVISIONS
        later = cache_rows - piece
        for m in range(HEAD_DIVISIONS):
            for kind in range(2):
                lines = jnp.concatenate(
                    [f_refs[m][columns(kind, piece)], s_refs[m][columns(kind, later)]], axis=0
                )
                column = ((head_group ^ m) + kind * HEAD_DIVISIONS) * width
                out_ref[:, pl.ds(pl.multiple_of(column, HEAD_SIZE), width)] = dot(
                    place_ref[...], lines
                ).astype(bf16)

    shape = jax.ShapeDtypeStruct((cache_rows, 2 * HEAD_DIVISIONS * width), bf16)
    return call(body, shape, [VMEM] * 9, "cache_part")(place, *early, *late)


def finish(weights, heads, tails, num, inverse, table):
    rows = num.shape[0]
    block_len = rows // 2
    slots = table.shape[1]

    def body(map_ref, num_ref, inv_ref, *refs):
        others = slots - 1
        w_refs, h_refs, t_refs = refs[:others], refs[others : 2 * others], refs[2 * others : 3 * others]
        out_ref, v_scr, acc = refs[-3:]
        slot = lax.axis_index("blk") // HEAD_DIVISIONS
        acc[...] = num_ref[...]
        for turn in range(1, slots):
            source = (slot - turn + slots) % slots
            h_ref, t_ref, w_ref = h_refs[turn - 1], t_refs[turn - 1], w_refs[turn - 1]
            first, rest = h_ref.shape[0] // 2, t_ref.shape[0] // 2
            for other in range(2):
                v_scr[columns(other, block_len)] = jnp.concatenate(
                    [h_ref[columns(other, first)], t_ref[columns(other, rest)]], axis=0
                )
            for index, (half, other) in enumerate(active_tiles(map_ref, slot, source)):
                q_part, k_part = rows_at(half, block_len), rows_at(other, block_len)
                for head in range(Q_DEV):
                    key_head = columns(head * KV_DEV // Q_DEV)
                    acc[q_part, columns(head)] += dot(w_ref[index, head], v_scr[k_part, key_head])
        for head in range(Q_DEV):
            out_ref[:, columns(head)] = (acc[:, columns(head)] * inv_ref[:, head : head + 1]).astype(bf16)

    shape = jax.ShapeDtypeStruct(num.shape, bf16)
    return call(
        body,
        shape,
        [SMEM] + [VMEM] * (2 + 3 * (slots - 1)),
        "finish",
        [pltpu.VMEM((rows, KV_WIDTH), bf16), pltpu.VMEM(num.shape, f32)],
        flops=3 * 10**8,
        moved=4 * 10**6,
    )(table, num, inverse, *weights, *heads, *tails)


def on_device(queries, keys, values, block_map, lengths, group_of_prompt, decode_rank):
    block_len = queries.shape[2] // 2
    slots = block_map.shape[1]
    q, k, v = queries[0, 0], keys[0, 0], values[0, 0]
    tables = rotary_tables(block_len, 2 * slots)

    key_in = [shifted(k, "blk", HEAD_DIVISIONS * turn) for turn in range(1, slots)]
    lens = [lengths] + [shifted(lengths, "req", t) for t in range(1, lax.axis_size("req"))]
    (query_rot, num, den, select, order, angles), early, sent = own_part(
        q, k, v, block_map, decode_rank, tables
    )
    heads = [shifted(sent[2 * t - 2], "blk", HEAD_DIVISIONS * t) for t in range(1, slots)]
    tails = [shifted(sent[2 * t - 1], "blk", HEAD_DIVISIONS * t) for t in range(1, slots)]
    early = [early[0]] + [crossed(early[m], "blk", m) for m in range(1, HEAD_DIVISIONS)]

    weights, inverse, place, pieces = other_keys(
        key_in, query_rot, den, select, order, angles, block_map, decode_rank, group_of_prompt, lens
    )

    def late_piece(m):
        parts = [pieces[m]]
        for head in heads:
            run = head.shape[0] // 2 // HEAD_DIVISIONS
            shaped = head.reshape(2, HEAD_DIVISIONS, run, KV_WIDTH)
            parts.append(shaped[:, m].reshape(2 * run, KV_WIDTH))
        return jnp.concatenate(parts, axis=0)

    late = [late_piece(0)] + [crossed(late_piece(m), "blk", m) for m in range(1, HEAD_DIVISIONS)]
    cache = cache_part(early, late, place)
    attended = finish(weights, heads, tails, num, inverse, block_map)
    return (attended[None, None], cache[None])


def solution(mesh):
    placed = (
        P("req", "blk", None, None),
        P("req", "blk", None, None),
        P("req", "blk", None, None),
        P("req", None, None),
        P("req"),
        P(),
        P("req", None),
    )
    return jax.shard_map(
        on_device,
        mesh=mesh,
        in_specs=placed,
        out_specs=(P("req", "blk", None, None), P("req", "blk", None)),
        check_vma=False,
    )
```

```python
import math

import jax
import jax.numpy as jnp
import numpy as np
from jax import lax
from jax.experimental import pallas as pl
from jax.experimental.pallas import tpu as pltpu
from jax.sharding import PartitionSpec as P

QUERY_HEADS = 16
KEY_VALUE_HEADS = 8
HEAD_SIZE = 128
HEAD_DIVISIONS = 4
Q_DEV = 4
KV_DEV = 2
KV_WIDTH = KV_DEV * HEAD_SIZE

cap_value = 50.0
query_scale = 1.0 / 12.0
rope_base = 10000.0
VMEM_BYTES = 48 * 1024 * 1024

f32 = jnp.float32
bf16 = jnp.bfloat16
SMEM = pl.BlockSpec(memory_space=pltpu.SMEM)
VMEM = pl.BlockSpec(memory_space=pltpu.VMEM)
HBM = pl.BlockSpec(memory_space=pltpu.HBM)


def shifted(shard, axis, by):
    peers = lax.axis_size(axis)
    return lax.ppermute(shard, axis, [(i, (i + by) % peers) for i in range(peers)])


def crossed(shard, axis, by):
    peers = lax.axis_size(axis)
    return lax.ppermute(shard, axis, [(i, i ^ by) for i in range(peers)])


def rotary_tables(block_len, block_count):
    half = HEAD_SIZE // 2
    frequency = np.exp(
        np.float32(-math.log(rope_base)) * (2.0 * np.arange(half, dtype=np.float32)) / HEAD_SIZE
    ).astype(np.float64)

    def table(positions):
        angles = positions.astype(np.float64)[:, None] * frequency[None, :]
        cosine, sine = np.cos(angles), np.sin(angles)
        return np.stack(
            [np.concatenate([cosine, cosine], 1), np.concatenate([-sine, sine], 1)]
        ).astype(np.float32)

    return table(np.arange(block_len)), table(np.arange(block_count) * block_len)


def block_angles(row_table, block_table, block):
    row_cos, row_sin = row_table[0], row_table[1]
    blk_cos, blk_sin = block_table[0, pl.ds(block, 1)], block_table[1, pl.ds(block, 1)]
    return row_cos * blk_cos - row_sin * blk_sin, row_sin * blk_cos + row_cos * blk_sin


def turned(head, angles):
    x = head.astype(f32)
    return x * angles[0] + pltpu.roll(x, HEAD_SIZE // 2, 1) * angles[1]


def send_index(rank_ref, slot, head_group, row_ids, residues):
    residue = row_ids % residues
    rank = jnp.zeros_like(row_ids)
    for r in range(residues):
        rank = jnp.where(residue == r, rank_ref[0, r], rank)
    ahead = (rank - HEAD_DIVISIONS * slot + residues) % residues
    return jnp.where(ahead < HEAD_DIVISIONS, ahead ^ head_group, ahead)


def order_matrix(rank_ref, slot, head_group, out_rows, rows, residues):
    row_ids = lax.broadcasted_iota(jnp.int32, (1, rows), 1)
    ahead = send_index(rank_ref, slot, head_group, row_ids, residues)
    index = ahead * (rows // residues) + row_ids // residues
    out_ids = lax.broadcasted_iota(jnp.int32, (out_rows, rows), 0)
    return jnp.where(out_ids == index, 1.0, 0.0).astype(bf16)


def dot(a, b):
    return jnp.dot(a, b, preferred_element_type=f32)


def dot_t(a, b):
    return lax.dot_general(a, b, (((1,), (1,)), ((), ())), preferred_element_type=f32)


def expo_of(scores):
    return jnp.exp2(cap_value * math.log2(math.e) * jnp.tanh(scores * (1.0 / cap_value)))


def columns(index, width=HEAD_SIZE):
    return slice(index * width, (index + 1) * width)


def call(body, out_shape, in_specs, name, scratch=(), cost=1000):
    return pl.pallas_call(
        body,
        out_shape=out_shape,
        in_specs=in_specs,
        out_specs=jax.tree.map(lambda _: VMEM, out_shape),
        scratch_shapes=scratch,
        compiler_params=pltpu.CompilerParams(vmem_limit_bytes=VMEM_BYTES),
        cost_estimate=pl.CostEstimate(flops=cost, bytes_accessed=1000, transcendentals=0),
        name=name,
    )


def fetch(sources, targets, sems):
    copies = [pltpu.make_async_copy(s, t, sems.at[i]) for i, (s, t) in enumerate(zip(sources, targets))]
    for copy in copies:
        copy.start()
    return copies


def halves_of(map_ref, slot):
    high = jnp.where(map_ref[0, slot, 1] > map_ref[0, slot, 0], 1, 0)
    return 1 - high, high


def active_tiles(map_ref, slot, source):
    low, high = halves_of(map_ref, slot)
    source_low, source_high = halves_of(map_ref, source)
    outer = map_ref[0, slot, low] < map_ref[0, source, source_low]
    return (
        (jnp.where(outer, high, low), source_low),
        (high, jnp.where(outer, source_high, source_low)),
    )


def rows_at(index, block_len):
    return pl.ds(pl.multiple_of(index * block_len, block_len), block_len)


def own_part(queries, keys, values, table, decode_rank, owner, lens, tables):
    rows = queries.shape[0]
    block_len = rows // 2
    slots = table.shape[1]
    residues = decode_rank.shape[1]
    piece = rows // residues
    first = block_len // slots
    rest = block_len - first
    width = keys.shape[1]
    run = block_len // residues
    cache_rows = slots * piece
    groups = len(lens)
    arrays = (queries, keys, values, *tables, table, decode_rank, owner, *lens)
    count = len(arrays)

    def body(*refs):
        inputs, refs = refs[:count], refs[count:]
        qr_ref, num_ref, den_ref, select_ref, order_ref, angle_ref, place_ref, live_ref = refs[:8]
        e_refs, refs = refs[8:12], refs[12:]
        sent_refs, refs = refs[: 2 * (slots - 1)], refs[2 * (slots - 1) :]
        kr_ref, vx_ref, scratch, sems = refs[0], refs[1], refs[2 : 2 + count], refs[2 + count]
        q_ref, k_ref, v_ref, row_ref, blk_ref, map_ref, rank_ref, owner_ref = scratch[:8]
        len_refs = scratch[8:]
        copies = fetch(inputs, scratch, sems)
        member, group = lax.axis_index("blk"), lax.axis_index("req")
        slot, head_group = member // HEAD_DIVISIONS, member % HEAD_DIVISIONS

        for copy in copies[5:]:
            copy.wait()
        copies[2].wait()
        for head in range(KV_DEV):
            vx_ref[:, columns(2 * head)] = v_ref[:, columns(head)]
            vx_ref[:, columns(2 * head + 1)] = jnp.ones((rows, HEAD_SIZE), bf16)
        for turn in range(1, slots):
            order = order_matrix(
                rank_ref, (slot + turn) % slots, head_group, block_len, block_len, residues
            )
            head_ref, tail_ref = sent_refs[2 * turn - 2], sent_refs[2 * turn - 1]
            for half in range(2):
                moved = dot(order, v_ref[columns(half, block_len)]).astype(bf16)
                head_ref[columns(half, first)] = moved[:first]
                tail_ref[columns(half, rest)] = moved[first:]
        select = order_matrix(rank_ref, slot, head_group, rows // slots, rows, residues)
        select_ref[...] = select
        order_ref[...] = order_matrix(rank_ref, slot, head_group, block_len, block_len, residues)

        copies[0].wait()
        copies[1].wait()
        copies[3].wait()
        copies[4].wait()
        for half in range(2):
            part = columns(half, block_len)
            angles = block_angles(row_ref, blk_ref, map_ref[0, slot, half])
            for head in range(Q_DEV):
                qr_ref[part, columns(head)] = (
                    turned(q_ref[part, columns(head)], angles) * query_scale
                ).astype(bf16)
            for head in range(KV_DEV):
                kr_ref[part, columns(head)] = turned(k_ref[part, columns(head)], angles).astype(bf16)
            for turn in range(1, slots):
                other = block_angles(row_ref, blk_ref, map_ref[0, (slot - turn + slots) % slots, half])
                angle_ref[turn - 1, half, 0] = other[0]
                angle_ref[turn - 1, half, 1] = other[1]
        for place, source in ((0, kr_ref), (1, v_ref)):
            chosen = dot(select, source[...]).astype(bf16)
            for m in range(HEAD_DIVISIONS):
                e_refs[m][columns(place, piece)] = chosen[columns(m, piece)]

        length = 0
        for turn in range(groups):
            mine = owner_ref[lax.rem(group - turn + groups, groups)] == group
            length = length + jnp.where(mine, len_refs[turn][0], 0)
        for half in range(2):
            part = columns(half, block_len)
            start = map_ref[0, slot, half] * block_len
            live = start + lax.broadcasted_iota(jnp.int32, (block_len, 1), 0) < length
            live_ref[part] = jnp.where(live, 1.0, 0.0) + jnp.zeros((block_len, Q_DEV * HEAD_SIZE), f32)

        residue = 0
        for r in range(1, residues):
            residue = jnp.where(rank_ref[0, r] == member, r, residue)
        col = lax.broadcasted_iota(jnp.int32, (1, cache_rows), 1)
        place, offset = col // run, col % run
        target = jnp.zeros_like(col)
        for turn in range(slots):
            for half in range(2):
                block = map_ref[0, (slot - turn + slots) % slots, half]
                target = jnp.where(place == 2 * turn + half, block * run + offset, target)
        target = jnp.where(target * residues + residue < length, target, -1)
        row = lax.broadcasted_iota(jnp.int32, (cache_rows, cache_rows), 0)
        place_ref[...] = jnp.where(row == target, 1.0, 0.0).astype(bf16)

        low, high = halves_of(map_ref, slot)
        low, high = rows_at(low, block_len), rows_at(high, block_len)
        row = lax.broadcasted_iota(jnp.int32, (block_len, block_len), 0)
        col = lax.broadcasted_iota(jnp.int32, (block_len, block_len), 1)
        for head in range(Q_DEV):
            key_head = columns(head * KV_DEV // Q_DEV)

            beside = columns(head * KV_DEV // Q_DEV, 2 * HEAD_SIZE)

            def tile(q_part, k_part, diagonal):
                expo = expo_of(dot_t(qr_ref[q_part, columns(head)], kr_ref[k_part, key_head]))
                if diagonal:
                    expo = jnp.where(col <= row, expo, 0.0)
                return dot(expo.astype(bf16), vx_ref[k_part, beside])

            for q_part, sums in (
                (low, tile(low, low, True)),
                (high, tile(high, high, True) + tile(high, low, False)),
            ):
                num_ref[q_part, columns(head)] = sums[:, :HEAD_SIZE]
                den_ref[q_part, columns(head)] = sums[:, HEAD_SIZE:]

    shapes = [
        jax.ShapeDtypeStruct(queries.shape, bf16),
        jax.ShapeDtypeStruct(queries.shape, f32),
        jax.ShapeDtypeStruct(queries.shape, f32),
        jax.ShapeDtypeStruct((rows // slots, rows), bf16),
        jax.ShapeDtypeStruct((block_len, block_len), bf16),
        jax.ShapeDtypeStruct((slots - 1, 2, 2, block_len, HEAD_SIZE), f32),
        jax.ShapeDtypeStruct((cache_rows, cache_rows), bf16),
        jax.ShapeDtypeStruct(queries.shape, f32),
    ]
    shapes += [jax.ShapeDtypeStruct((2 * piece, width), bf16) for _ in range(HEAD_DIVISIONS)]
    for _ in range(1, slots):
        shapes.append(jax.ShapeDtypeStruct((2 * first, width), bf16))
        shapes.append(jax.ShapeDtypeStruct((2 * rest, width), bf16))
    scratch = [pltpu.VMEM(keys.shape, bf16), pltpu.VMEM((rows, 2 * width), bf16)]
    scratch += [pltpu.VMEM(x.shape, x.dtype) for x in arrays[:5]]
    scratch += [pltpu.SMEM(x.shape, x.dtype) for x in arrays[5:]]
    scratch.append(pltpu.SemaphoreType.DMA((count,)))
    outs = call(body, shapes, [HBM] * count, "own_part", scratch)(*arrays)
    return outs[:8], outs[8:12], outs[12:]


def other_keys(arrived, query_rot, den, select, order, angles, live, table):
    rows, width = arrived[0].shape
    block_len = rows // 2
    slots = table.shape[1]

    def body(map_ref, *refs):
        q_ref, den_ref, select_ref, order_ref, angle_ref, live_ref = refs[:6]
        refs = refs[6:]
        in_refs, refs = refs[: slots - 1], refs[slots - 1 :]
        w_refs, refs = refs[: slots - 1], refs[slots - 1 :]
        inv_ref, e_ref, k_scr, p_scr, d_scr = refs
        slot = lax.axis_index("blk") // HEAD_DIVISIONS

        d_scr[...] = den_ref[...]
        ones = jnp.ones((block_len, HEAD_SIZE), bf16)
        for turn in range(1, slots):
            source = (slot - turn + slots) % slots
            for half in range(2):
                part = columns(half, block_len)
                there = angle_ref[turn - 1, half, 0], angle_ref[turn - 1, half, 1]
                for head in range(KV_DEV):
                    k_scr[part, columns(head)] = turned(
                        in_refs[turn - 1][part, columns(head)], there
                    ).astype(bf16)
                p_scr[part] = dot(order_ref[...], k_scr[part]).astype(bf16)
            e_ref[turn - 1] = dot(select_ref[...], k_scr[...]).astype(bf16)
            for index, (half, other) in enumerate(active_tiles(map_ref, slot, source)):
                q_part, k_part = rows_at(half, block_len), rows_at(other, block_len)
                for head in range(Q_DEV):
                    key_head = columns(head * KV_DEV // Q_DEV)
                    expo = expo_of(dot_t(q_ref[q_part, columns(head)], p_scr[k_part, key_head]))
                    weight = expo.astype(bf16)
                    w_refs[turn - 1][index, head] = weight
                    d_scr[q_part, columns(head)] += dot(weight, ones)

        inv_ref[...] = live_ref[...] / d_scr[...]

    shapes = [
        jax.ShapeDtypeStruct((2, Q_DEV, block_len, block_len), bf16) for _ in range(1, slots)
    ]
    shapes.append(jax.ShapeDtypeStruct(den.shape, f32))
    shapes.append(jax.ShapeDtypeStruct((slots - 1, select.shape[0], width), bf16))
    scratch = [pltpu.VMEM((rows, width), bf16)] * 2 + [pltpu.VMEM(den.shape, f32)]
    outs = call(
        body,
        shapes,
        [SMEM] + [VMEM] * (5 + slots),
        "other_keys",
        scratch,
        cost=10**10,
    )(table, query_rot, den, select, order, angles, live, *arrived)
    return outs[: slots - 1], outs[slots - 1], outs[slots]


def late_pieces(chosen, heads):
    others, rows, width = chosen.shape
    piece = rows // HEAD_DIVISIONS
    run = piece // 2

    def body(chosen_ref, *refs):
        v_refs, e_refs = refs[:others], refs[others:]
        for m in range(HEAD_DIVISIONS):
            for index in range(others):
                e_refs[m][columns(index, piece)] = chosen_ref[index, columns(m, piece)]
                lines = [
                    v_refs[index][columns(half, 2 * piece)].astype(f32)[columns(m, run)]
                    for half in range(2)
                ]
                e_refs[m][columns(others + index, piece)] = jnp.concatenate(lines, 0).astype(bf16)

    shapes = [
        jax.ShapeDtypeStruct((2 * others * piece, width), bf16) for _ in range(HEAD_DIVISIONS)
    ]
    return call(body, shapes, [VMEM] * (1 + others), "late_pieces")(chosen, *heads)


def cache_part(early, late, place):
    cache_rows = place.shape[0]
    piece = early[0].shape[0] // 2
    width = early[0].shape[1]

    def body(place_ref, *refs):
        f_refs, s_refs, out_ref, mark_ref = refs[:4], refs[4:8], refs[8], refs[9]
        mark_ref[...] = jnp.zeros_like(mark_ref)
        head_group = lax.axis_index("blk") % HEAD_DIVISIONS
        later = cache_rows - piece
        for m in range(HEAD_DIVISIONS):
            for kind in range(2):
                lines = jnp.concatenate(
                    [f_refs[m][columns(kind, piece)], s_refs[m][columns(kind, later)]], axis=0
                )
                column = ((head_group ^ m) + kind * HEAD_DIVISIONS) * width
                out_ref[:, pl.ds(pl.multiple_of(column, HEAD_SIZE), width)] = dot(
                    place_ref[...], lines
                ).astype(bf16)

    shapes = [
        jax.ShapeDtypeStruct((cache_rows, 2 * HEAD_DIVISIONS * width), bf16),
        jax.ShapeDtypeStruct((8, HEAD_SIZE), f32),
    ]
    return call(body, shapes, [VMEM] * 9, "cache_part")(place, *early, *late)


def finish(weights, heads, tails, num, inverse, table, mark):
    rows = num.shape[0]
    block_len = rows // 2
    slots = table.shape[1]

    def body(map_ref, mark_ref, num_ref, inv_ref, *refs):
        others = slots - 1
        w_refs, h_refs, t_refs = refs[:others], refs[others : 2 * others], refs[2 * others : 3 * others]
        out_ref, v_scr, acc = refs[-3:]
        slot = lax.axis_index("blk") // HEAD_DIVISIONS
        acc[...] = num_ref[...]
        for turn in range(1, slots):
            source = (slot - turn + slots) % slots
            h_ref, t_ref, w_ref = h_refs[turn - 1], t_refs[turn - 1], w_refs[turn - 1]
            first, rest = h_ref.shape[0] // 2, t_ref.shape[0] // 2
            for other in range(2):
                v_scr[columns(other, block_len)] = jnp.concatenate(
                    [h_ref[columns(other, first)], t_ref[columns(other, rest)]], axis=0
                )
            for index, (half, other) in enumerate(active_tiles(map_ref, slot, source)):
                q_part, k_part = rows_at(half, block_len), rows_at(other, block_len)
                for head in range(Q_DEV):
                    key_head = columns(head * KV_DEV // Q_DEV)
                    acc[q_part, columns(head)] += dot(w_ref[index, head], v_scr[k_part, key_head])
        for head in range(Q_DEV):
            out_ref[:, columns(head)] = (acc[:, columns(head)] * inv_ref[:, columns(head)]).astype(bf16)

    shape = jax.ShapeDtypeStruct(num.shape, bf16)
    return call(
        body,
        shape,
        [SMEM] + [VMEM] * (3 + 3 * (slots - 1)),
        "finish",
        [pltpu.VMEM((rows, KV_WIDTH), bf16), pltpu.VMEM(num.shape, f32)],
    )(table, mark, num, inverse, *weights, *heads, *tails)


def on_device(queries, keys, values, block_map, lengths, group_of_prompt, decode_rank):
    block_len = queries.shape[2] // 2
    slots = block_map.shape[1]
    q, k, v = queries[0, 0], keys[0, 0], values[0, 0]
    tables = rotary_tables(block_len, 2 * slots)

    key_in = [shifted(k, "blk", HEAD_DIVISIONS * turn) for turn in range(1, slots)]
    lens = [lengths] + [shifted(lengths, "req", t) for t in range(1, lax.axis_size("req"))]
    (query_rot, num, den, select, order, angles, place, live), early, sent = own_part(
        q, k, v, block_map, decode_rank, group_of_prompt, lens, tables
    )
    heads = [shifted(sent[2 * t - 2], "blk", HEAD_DIVISIONS * t) for t in range(1, slots)]
    tails, key_in = lax.optimization_barrier((sent[1::2], key_in))
    tails = [shifted(tails[t - 1], "blk", HEAD_DIVISIONS * t) for t in range(1, slots)]
    early = [early[0]] + [crossed(early[m], "blk", m) for m in range(1, HEAD_DIVISIONS)]

    weights, inverse, chosen = other_keys(
        key_in, query_rot, den, select, order, angles, live, block_map
    )
    late = late_pieces(chosen, heads)
    late = [late[0]] + [crossed(late[m], "blk", m) for m in range(1, HEAD_DIVISIONS)]
    cache, mark = cache_part(early, late, place)
    attended = finish(weights, heads, tails, num, inverse, block_map, mark)
    return (attended[None, None], cache[None])


def solution(mesh):
    placed = (
        P("req", "blk", None, None),
        P("req", "blk", None, None),
        P("req", "blk", None, None),
        P("req", None, None),
        P("req"),
        P(),
        P("req", None),
    )
    return jax.shard_map(
        on_device,
        mesh=mesh,
        in_specs=placed,
        out_specs=(P("req", "blk", None, None), P("req", "blk", None)),
        check_vma=False,
    )
```

```python
import math

import jax
import jax.numpy as jnp
import numpy as np
from jax import lax
from jax.experimental import pallas as pl
from jax.experimental.pallas import tpu as pltpu
from jax.sharding import PartitionSpec as P

QUERY_HEADS = 16
KEY_VALUE_HEADS = 8
HEAD_SIZE = 128
HEAD_DIVISIONS = 4
Q_DEV = 4
KV_DEV = 2
KV_WIDTH = KV_DEV * HEAD_SIZE

cap_value = 50.0
query_scale = 1.0 / 12.0
rope_base = 10000.0
CARRIED = 16
VMEM_BYTES = 48 * 1024 * 1024

f32 = jnp.float32
bf16 = jnp.bfloat16
SMEM = pl.BlockSpec(memory_space=pltpu.SMEM)
VMEM = pl.BlockSpec(memory_space=pltpu.VMEM)
HBM = pl.BlockSpec(memory_space=pltpu.HBM)


def shifted(shard, axis, by):
    peers = lax.axis_size(axis)
    return lax.ppermute(shard, axis, [(i, (i + by) % peers) for i in range(peers)])


def crossed(shard, axis, by):
    peers = lax.axis_size(axis)
    return lax.ppermute(shard, axis, [(i, i ^ by) for i in range(peers)])


def spread(shard, turn):
    groups, members = lax.axis_size("req"), lax.axis_size("blk")
    pairs = []
    for group in range(groups):
        for member in range(members):
            target = group + member % HEAD_DIVISIONS + HEAD_DIVISIONS * turn
            pairs.append((group * members + member, target % groups * members + member))
    return lax.ppermute(shard, ("req", "blk"), pairs)


def rotary_tables(block_len, block_count):
    half = HEAD_SIZE // 2
    frequency = np.exp(
        np.float32(-math.log(rope_base)) * (2.0 * np.arange(half, dtype=np.float32)) / HEAD_SIZE
    ).astype(np.float64)

    def table(positions):
        angles = positions.astype(np.float64)[:, None] * frequency[None, :]
        cosine, sine = np.cos(angles), np.sin(angles)
        return np.stack(
            [np.concatenate([cosine, cosine], 1), np.concatenate([-sine, sine], 1)]
        ).astype(np.float32)

    return table(np.arange(block_len)), table(np.arange(block_count) * block_len)


def block_angles(row_table, block_table, block):
    row_cos, row_sin = row_table[0], row_table[1]
    blk_cos, blk_sin = block_table[0, pl.ds(block, 1)], block_table[1, pl.ds(block, 1)]
    return row_cos * blk_cos - row_sin * blk_sin, row_sin * blk_cos + row_cos * blk_sin


def turned(head, angles):
    x = head.astype(f32)
    return x * angles[0] + pltpu.roll(x, HEAD_SIZE // 2, 1) * angles[1]


def send_index(rank_ref, slot, head_group, row_ids, residues):
    residue = row_ids % residues
    rank = jnp.zeros_like(row_ids)
    for r in range(residues):
        rank = jnp.where(residue == r, rank_ref[0, r], rank)
    ahead = (rank - HEAD_DIVISIONS * slot + residues) % residues
    return jnp.where(ahead < HEAD_DIVISIONS, ahead ^ head_group, ahead)


def order_matrix(rank_ref, slot, head_group, out_rows, rows, residues):
    row_ids = lax.broadcasted_iota(jnp.int32, (1, rows), 1)
    ahead = send_index(rank_ref, slot, head_group, row_ids, residues)
    index = ahead * (rows // residues) + row_ids // residues
    out_ids = lax.broadcasted_iota(jnp.int32, (out_rows, rows), 0)
    return jnp.where(out_ids == index, 1.0, 0.0).astype(bf16)


def dot(a, b):
    return jnp.dot(a, b, preferred_element_type=f32)


def dot_t(a, b):
    return lax.dot_general(a, b, (((1,), (1,)), ((), ())), preferred_element_type=f32)


def expo_of(scores):
    return jnp.exp2(cap_value * math.log2(math.e) * jnp.tanh(scores * (1.0 / cap_value)))


def columns(index, width=HEAD_SIZE):
    return slice(index * width, (index + 1) * width)


def call(body, out_shape, in_specs, name, scratch=(), cost=1000):
    return pl.pallas_call(
        body,
        out_shape=out_shape,
        in_specs=in_specs,
        out_specs=jax.tree.map(lambda _: VMEM, out_shape),
        scratch_shapes=scratch,
        compiler_params=pltpu.CompilerParams(vmem_limit_bytes=VMEM_BYTES),
        cost_estimate=pl.CostEstimate(flops=cost, bytes_accessed=1000, transcendentals=0),
        name=name,
    )


def in_hbm(arrays):
    return [pltpu.with_memory_space_constraint(x, pltpu.HBM) for x in arrays]


def fetch(sources, targets, sems):
    copies = [pltpu.make_async_copy(s, t, sems.at[i]) for i, (s, t) in enumerate(zip(sources, targets))]
    for copy in copies:
        copy.start()
    return copies


def halves_of(map_ref, slot):
    high = jnp.where(map_ref[0, slot, 1] > map_ref[0, slot, 0], 1, 0)
    return 1 - high, high


def active_tiles(map_ref, slot, source):
    low, high = halves_of(map_ref, slot)
    source_low, source_high = halves_of(map_ref, source)
    outer = map_ref[0, slot, low] < map_ref[0, source, source_low]
    return (
        (jnp.where(outer, high, low), source_low),
        (high, jnp.where(outer, source_high, source_low)),
    )


def rows_at(index, block_len):
    return pl.ds(pl.multiple_of(index * block_len, block_len), block_len)


def own_part(queries, keys, values, table, decode_rank, owner, lens, tables):
    rows = queries.shape[0]
    block_len = rows // 2
    slots = table.shape[1]
    residues = decode_rank.shape[1]
    piece = rows // residues
    first = block_len // slots
    rest = block_len - first
    width = keys.shape[1]
    run = block_len // residues
    cache_rows = slots * piece
    groups = owner.shape[0]
    arrays = (queries, keys, values, *tables, table, decode_rank, owner)
    count = len(arrays)

    rounds = len(lens)

    def body(*refs):
        len_refs, refs = refs[:rounds], refs[rounds:]
        inputs, refs = refs[:count], refs[count:]
        qr_ref, num_ref, den_ref, select_ref, order_ref, angle_ref = refs[:6]
        place_ref, owned_ref, row_at_ref, cache_at_ref, carried_ref = refs[6:11]
        e_refs, refs = refs[11:15], refs[15:]
        sent_refs, refs = refs[: 2 * (slots - 1)], refs[2 * (slots - 1) :]
        kr_ref, vx_ref, scratch, sems = refs[0], refs[1], refs[2 : 2 + count], refs[2 + count]
        q_ref, k_ref, v_ref, row_ref, blk_ref, map_ref, rank_ref, owner_ref = scratch
        copies = fetch(inputs, scratch, sems)
        member, group = lax.axis_index("blk"), lax.axis_index("req")
        slot, head_group = member // HEAD_DIVISIONS, member % HEAD_DIVISIONS

        for copy in copies[5:]:
            copy.wait()
        copies[2].wait()
        for head in range(KV_DEV):
            vx_ref[:, columns(2 * head)] = v_ref[:, columns(head)]
            vx_ref[:, columns(2 * head + 1)] = jnp.ones((rows, HEAD_SIZE), bf16)
        for turn in range(1, slots):
            order = order_matrix(
                rank_ref, (slot + turn) % slots, head_group, block_len, block_len, residues
            )
            head_ref, tail_ref = sent_refs[2 * turn - 2], sent_refs[2 * turn - 1]
            for half in range(2):
                moved = dot(order, v_ref[columns(half, block_len)]).astype(bf16)
                head_ref[columns(half, first)] = moved[:first]
                tail_ref[columns(half, rest)] = moved[first:]
        select = order_matrix(rank_ref, slot, head_group, rows // slots, rows, residues)
        select_ref[...] = select
        order_ref[...] = order_matrix(rank_ref, slot, head_group, block_len, block_len, residues)

        copies[0].wait()
        copies[1].wait()
        copies[3].wait()
        copies[4].wait()
        for half in range(2):
            part = columns(half, block_len)
            angles = block_angles(row_ref, blk_ref, map_ref[0, slot, half])
            for head in range(Q_DEV):
                qr_ref[part, columns(head)] = (
                    turned(q_ref[part, columns(head)], angles) * query_scale
                ).astype(bf16)
            for head in range(KV_DEV):
                kr_ref[part, columns(head)] = turned(k_ref[part, columns(head)], angles).astype(bf16)
            for turn in range(1, slots):
                other = block_angles(row_ref, blk_ref, map_ref[0, (slot - turn + slots) % slots, half])
                angle_ref[turn - 1, half, 0] = other[0]
                angle_ref[turn - 1, half, 1] = other[1]
        for place, source in ((0, kr_ref), (1, v_ref)):
            chosen = dot(select, source[...]).astype(bf16)
            for m in range(HEAD_DIVISIONS):
                e_refs[m][columns(place, piece)] = chosen[columns(m, piece)]

        col = lax.broadcasted_iota(jnp.int32, (1, cache_rows), 1)
        place, offset = col // run, col % run
        target = jnp.zeros_like(col)
        for turn in range(slots):
            for half in range(2):
                block = map_ref[0, (slot - turn + slots) % slots, half]
                target = jnp.where(place == 2 * turn + half, block * run + offset, target)
        row = lax.broadcasted_iota(jnp.int32, (cache_rows, cache_rows), 0)
        place_ref[...] = jnp.where(row == target, 1.0, 0.0).astype(bf16)
        residue = 0
        for r in range(1, residues):
            residue = jnp.where(rank_ref[0, r] == member, r, residue)
        cache_at_ref[...] = (row * residues + residue).astype(f32)
        for half in range(2):
            offset = lax.broadcasted_iota(jnp.int32, (block_len, HEAD_SIZE), 0)
            row_at_ref[columns(half, block_len)] = (map_ref[0, slot, half] * block_len + offset).astype(f32)
        line = lax.broadcasted_iota(jnp.int32, (CARRIED, width), 0)
        carried = jnp.zeros((CARRIED, width), jnp.int32)
        for index in range(rounds):
            length = len_refs[index][0]
            carried = jnp.where(line == 2 * index, lax.shift_right_logical(length, 6), carried)
            carried = jnp.where(line == 2 * index + 1, length & 63, carried)
        carried_ref[...] = carried.astype(f32).astype(bf16)
        for turn in range(groups):
            mine = owner_ref[lax.rem(group - turn + groups, groups)] == group
            owned_ref[turn : turn + 1] = jnp.full((1, HEAD_SIZE), jnp.where(mine, 1.0, 0.0), f32)

        low, high = halves_of(map_ref, slot)
        low, high = rows_at(low, block_len), rows_at(high, block_len)
        row = lax.broadcasted_iota(jnp.int32, (block_len, block_len), 0)
        col = lax.broadcasted_iota(jnp.int32, (block_len, block_len), 1)
        for head in range(Q_DEV):
            key_head = columns(head * KV_DEV // Q_DEV)

            beside = columns(head * KV_DEV // Q_DEV, 2 * HEAD_SIZE)

            def tile(q_part, k_part, diagonal):
                expo = expo_of(dot_t(qr_ref[q_part, columns(head)], kr_ref[k_part, key_head]))
                if diagonal:
                    expo = jnp.where(col <= row, expo, 0.0)
                return dot(expo.astype(bf16), vx_ref[k_part, beside])

            for q_part, sums in (
                (low, tile(low, low, True)),
                (high, tile(high, high, True) + tile(high, low, False)),
            ):
                num_ref[q_part, columns(head)] = sums[:, :HEAD_SIZE]
                den_ref[q_part, columns(head)] = sums[:, HEAD_SIZE:]

    shapes = [
        jax.ShapeDtypeStruct(queries.shape, bf16),
        jax.ShapeDtypeStruct(queries.shape, f32),
        jax.ShapeDtypeStruct(queries.shape, f32),
        jax.ShapeDtypeStruct((rows // slots, rows), bf16),
        jax.ShapeDtypeStruct((block_len, block_len), bf16),
        jax.ShapeDtypeStruct((slots - 1, 2, 2, block_len, HEAD_SIZE), f32),
        jax.ShapeDtypeStruct((cache_rows, cache_rows), bf16),
        jax.ShapeDtypeStruct((groups, HEAD_SIZE), f32),
        jax.ShapeDtypeStruct((rows, HEAD_SIZE), f32),
        jax.ShapeDtypeStruct((cache_rows, cache_rows), f32),
        jax.ShapeDtypeStruct((CARRIED, width), bf16),
    ]
    shapes += [jax.ShapeDtypeStruct((2 * piece, width), bf16) for _ in range(HEAD_DIVISIONS)]
    for _ in range(1, slots):
        shapes.append(jax.ShapeDtypeStruct((2 * first, width), bf16))
        shapes.append(jax.ShapeDtypeStruct((2 * rest, width), bf16))
    scratch = [pltpu.VMEM(keys.shape, bf16), pltpu.VMEM((rows, 2 * width), bf16)]
    scratch += [pltpu.VMEM(x.shape, x.dtype) for x in arrays[:5]]
    scratch += [pltpu.SMEM(x.shape, x.dtype) for x in arrays[5:]]
    scratch.append(pltpu.SemaphoreType.DMA((count,)))
    specs = [SMEM] * rounds + [HBM] * count
    outs = call(body, shapes, specs, "own_part", scratch)(*lens, *in_hbm(arrays))
    return outs[:6], outs[6:10], outs[10], outs[11:15], outs[15:]


def other_keys(arrived, query_rot, den, select, order, angles, table):
    rows, width = arrived[0].shape
    block_len = rows // 2
    slots = table.shape[1]

    def body(map_hbm, q_ref, den_ref, select_ref, order_ref, angle_ref, *refs):
        in_refs, refs = refs[: slots - 1], refs[slots - 1 :]
        w_refs, refs = refs[: slots - 1], refs[slots - 1 :]
        inv_ref, e_ref, k_scr, p_scr, d_scr, map_ref, sems = refs
        (copy,) = fetch([map_hbm], [map_ref], sems)
        slot = lax.axis_index("blk") // HEAD_DIVISIONS
        d_scr[...] = den_ref[...]
        ones = jnp.ones((block_len, HEAD_SIZE), bf16)
        for turn in range(1, slots):
            source = (slot - turn + slots) % slots
            for half in range(2):
                part = columns(half, block_len)
                there = angle_ref[turn - 1, half, 0], angle_ref[turn - 1, half, 1]
                for head in range(KV_DEV):
                    k_scr[part, columns(head)] = turned(
                        in_refs[turn - 1][part, columns(head)], there
                    ).astype(bf16)
                p_scr[part] = dot(order_ref[...], k_scr[part]).astype(bf16)
            e_ref[turn - 1] = dot(select_ref[...], k_scr[...]).astype(bf16)
            w_refs[turn - 1][...] = jnp.zeros((Q_DEV, rows, rows), bf16)
            if turn == 1:
                copy.wait()
            for half, other in active_tiles(map_ref, slot, source):
                q_part, k_part = rows_at(half, block_len), rows_at(other, block_len)
                for head in range(Q_DEV):
                    key_head = columns(head * KV_DEV // Q_DEV)
                    expo = expo_of(dot_t(q_ref[q_part, columns(head)], p_scr[k_part, key_head]))
                    weight = expo.astype(bf16)
                    w_refs[turn - 1][head, q_part, k_part] = weight
                    d_scr[q_part, columns(head)] += dot(weight, ones)
        inv_ref[...] = 1.0 / d_scr[...]

    shapes = [jax.ShapeDtypeStruct((Q_DEV, rows, rows), bf16) for _ in range(1, slots)]
    shapes.append(jax.ShapeDtypeStruct(den.shape, f32))
    shapes.append(jax.ShapeDtypeStruct((slots - 1, select.shape[0], width), bf16))
    scratch = [pltpu.VMEM((rows, width), bf16)] * 2 + [pltpu.VMEM(den.shape, f32)]
    scratch += [pltpu.SMEM(table.shape, table.dtype), pltpu.SemaphoreType.DMA((1,))]
    outs = call(
        body,
        shapes,
        [HBM] + [VMEM] * (4 + slots),
        "other_keys",
        scratch,
        cost=10**10,
    )(*in_hbm([table]), query_rot, den, select, order, angles, *arrived)
    return outs[: slots - 1], outs[slots - 1], outs[slots]


def late_pieces(chosen, heads, carried, early):
    others, rows, width = chosen.shape
    piece = rows // HEAD_DIVISIONS
    run = piece // 2

    def body(carried_ref, chosen_ref, *refs):
        v_refs, e_refs = refs[:others], refs[-HEAD_DIVISIONS:]
        for m in range(HEAD_DIVISIONS):
            for index in range(others):
                e_refs[m][columns(index, piece)] = chosen_ref[index, columns(m, piece)]
                lines = [
                    v_refs[index][columns(half, 2 * piece)].astype(f32)[columns(m, run)]
                    for half in range(2)
                ]
                e_refs[m][columns(others + index, piece)] = jnp.concatenate(lines, 0).astype(bf16)
            e_refs[m][2 * others * piece :] = carried_ref[...]

    shapes = [
        jax.ShapeDtypeStruct((2 * others * piece + CARRIED, width), bf16)
        for _ in range(HEAD_DIVISIONS)
    ]
    specs = [VMEM] * (2 + others + len(early))
    return call(body, shapes, specs, "late_pieces")(carried, chosen, *heads, *early)


def cache_part(early, late, masks):
    place, owned, row_at, cache_at = masks
    cache_rows = place.shape[0]
    piece = early[0].shape[0] // 2
    width = early[0].shape[1]
    groups = owned.shape[0]

    def body(place_ref, owned_ref, row_at_ref, cache_at_ref, *refs):
        f_refs, s_refs, out_ref, live_ref = refs[:4], refs[4:8], refs[8], refs[9]
        head_group = lax.axis_index("blk") % HEAD_DIVISIONS
        later = cache_rows - piece
        length = jnp.zeros((1, HEAD_SIZE), f32)
        for m in range(HEAD_DIVISIONS):
            carried = s_refs[m][2 * later :, :HEAD_SIZE].astype(f32)
            for index in range(groups // HEAD_DIVISIONS):
                turn = (head_group ^ m) + HEAD_DIVISIONS * index
                value = carried[2 * index : 2 * index + 1] * 64.0 + carried[2 * index + 1 : 2 * index + 2]
                length = length + owned_ref[pl.ds(turn, 1)] * value
        live_ref[...] = jnp.where(row_at_ref[...] < length, 1.0, 0.0)
        kept = jnp.where(cache_at_ref[...] < length[:, :1], place_ref[...].astype(f32), 0.0)
        kept = kept.astype(bf16)
        for m in range(HEAD_DIVISIONS):
            for kind in range(2):
                lines = jnp.concatenate(
                    [f_refs[m][columns(kind, piece)], s_refs[m][columns(kind, later)]], axis=0
                )
                column = ((head_group ^ m) + kind * HEAD_DIVISIONS) * width
                out_ref[:, pl.ds(pl.multiple_of(column, HEAD_SIZE), width)] = dot(kept, lines).astype(
                    bf16
                )

    shapes = [
        jax.ShapeDtypeStruct((cache_rows, 2 * HEAD_DIVISIONS * width), bf16),
        jax.ShapeDtypeStruct(row_at.shape, f32),
    ]
    return call(body, shapes, [VMEM] * 12, "cache_part")(*masks, *early, *late)


def finish(weights, heads, tails, num, inverse, live):
    rows = num.shape[0]
    block_len = rows // 2
    others = len(weights)

    def body(num_ref, inv_ref, live_ref, *refs):
        w_refs, h_refs, t_refs = refs[:others], refs[others : 2 * others], refs[2 * others : 3 * others]
        out_ref, v_scr = refs[-2:]
        for turn in range(others):
            first, rest = h_refs[turn].shape[0] // 2, t_refs[turn].shape[0] // 2
            for half in range(2):
                v_scr[turn, columns(half, block_len)] = jnp.concatenate(
                    [h_refs[turn][columns(half, first)], t_refs[turn][columns(half, rest)]], axis=0
                )
        for head in range(Q_DEV):
            key_head = columns(head * KV_DEV // Q_DEV)
            total = num_ref[:, columns(head)]
            for turn in range(others):
                total = total + dot(w_refs[turn][head], v_scr[turn, :, key_head])
            scale = inv_ref[:, columns(head)] * live_ref[...]
            out_ref[:, columns(head)] = (total * scale).astype(bf16)

    shape = jax.ShapeDtypeStruct(num.shape, bf16)
    scratch = [pltpu.VMEM((others, rows, KV_WIDTH), bf16)]
    return call(body, shape, [VMEM] * (3 + 3 * others), "finish", scratch)(
        num, inverse, live, *weights, *heads, *tails
    )


def on_device(queries, keys, values, block_map, lengths, group_of_prompt, decode_rank):
    block_len = queries.shape[2] // 2
    slots = block_map.shape[1]
    q, k, v = queries[0, 0], keys[0, 0], values[0, 0]
    tables = rotary_tables(block_len, 2 * slots)

    key_in = [shifted(k, "blk", HEAD_DIVISIONS * turn) for turn in range(1, slots)]
    lens = [spread(lengths, t) for t in range(lax.axis_size("req") // HEAD_DIVISIONS)]
    (query_rot, num, den, select, order, angles), masks, carried, early, sent = own_part(
        q, k, v, block_map, decode_rank, group_of_prompt, lens, tables
    )
    heads = [shifted(sent[2 * t - 2], "blk", HEAD_DIVISIONS * t) for t in range(1, slots)]
    tails, key_in = lax.optimization_barrier((sent[1::2], key_in))
    tails = [shifted(tails[t - 1], "blk", HEAD_DIVISIONS * t) for t in range(1, slots)]
    early = [early[0]] + [crossed(early[m], "blk", m) for m in range(1, HEAD_DIVISIONS)]

    weights, inverse, chosen = other_keys(
        key_in, query_rot, den, select, order, angles, block_map
    )
    late = late_pieces(chosen, heads, carried, early[1:])
    late = [late[0]] + [crossed(late[m], "blk", m) for m in range(1, HEAD_DIVISIONS)]
    cache, live = cache_part(early, late, masks)
    attended = finish(weights, heads, tails, num, inverse, live)
    return (attended[None, None], cache[None])


def solution(mesh):
    placed = (
        P("req", "blk", None, None),
        P("req", "blk", None, None),
        P("req", "blk", None, None),
        P("req", None, None),
        P("req"),
        P(),
        P("req", None),
    )
    return jax.shard_map(
        on_device,
        mesh=mesh,
        in_specs=placed,
        out_specs=(P("req", "blk", None, None), P("req", "blk", None)),
        check_vma=False,
    )
```

```python
import math

import jax
import jax.numpy as jnp
import numpy as np
from jax import lax
from jax.experimental import pallas as pl
from jax.experimental.pallas import tpu as pltpu
from jax.sharding import PartitionSpec as P

QUERY_HEADS = 16
KEY_VALUE_HEADS = 8
HEAD_SIZE = 128
HEAD_DIVISIONS = 4
Q_DEV = 4
KV_DEV = 2
KV_WIDTH = KV_DEV * HEAD_SIZE

cap_value = 50.0
query_scale = 1.0 / 12.0
rope_base = 10000.0
CARRIED = 16
VMEM_BYTES = 48 * 1024 * 1024

f32 = jnp.float32
bf16 = jnp.bfloat16
SMEM = pl.BlockSpec(memory_space=pltpu.SMEM)
VMEM = pl.BlockSpec(memory_space=pltpu.VMEM)
HBM = pl.BlockSpec(memory_space=pltpu.HBM)


def shifted(shard, axis, by):
    peers = lax.axis_size(axis)
    return lax.ppermute(shard, axis, [(i, (i + by) % peers) for i in range(peers)])


def crossed(shard, axis, by):
    peers = lax.axis_size(axis)
    return lax.ppermute(shard, axis, [(i, i ^ by) for i in range(peers)])


def spread(shard, turn):
    groups, members = lax.axis_size("req"), lax.axis_size("blk")
    pairs = []
    for group in range(groups):
        for member in range(members):
            target = group + member % HEAD_DIVISIONS + HEAD_DIVISIONS * turn
            pairs.append((group * members + member, target % groups * members + member))
    return lax.ppermute(shard, ("req", "blk"), pairs)


def rotary_tables(block_len, block_count):
    half = HEAD_SIZE // 2
    frequency = np.exp(
        np.float32(-math.log(rope_base)) * (2.0 * np.arange(half, dtype=np.float32)) / HEAD_SIZE
    ).astype(np.float64)

    def table(positions):
        angles = positions.astype(np.float64)[:, None] * frequency[None, :]
        cosine, sine = np.cos(angles), np.sin(angles)
        return np.stack(
            [np.concatenate([cosine, cosine], 1), np.concatenate([-sine, sine], 1)]
        ).astype(np.float32)

    return table(np.arange(block_len)), table(np.arange(block_count) * block_len)


def block_angles(row_table, block_table, block):
    row_cos, row_sin = row_table[0], row_table[1]
    blk_cos, blk_sin = block_table[0, pl.ds(block, 1)], block_table[1, pl.ds(block, 1)]
    return row_cos * blk_cos - row_sin * blk_sin, row_sin * blk_cos + row_cos * blk_sin


def turned(head, angles):
    x = head.astype(f32)
    return x * angles[0] + pltpu.roll(x, HEAD_SIZE // 2, 1) * angles[1]


def order_matrix(rank_of, slot, head_group, first_row, out_rows, rows, residues):
    row_ids = lax.broadcasted_iota(jnp.int32, (1, rows), 1)
    residue = row_ids % residues
    rank = jnp.zeros_like(row_ids)
    for r in range(residues):
        rank = jnp.where(residue == r, rank_of(r), rank)
    ahead = (rank - HEAD_DIVISIONS * slot + residues) % residues
    ahead = jnp.where(ahead < HEAD_DIVISIONS, ahead ^ head_group, ahead)
    index = ahead * (rows // residues) + row_ids // residues
    out_ids = first_row + lax.broadcasted_iota(jnp.int32, (out_rows, rows), 0)
    return jnp.where(out_ids == index, 1.0, 0.0).astype(bf16)


def dot(a, b):
    return jnp.dot(a, b, preferred_element_type=f32)


def dot_t(a, b):
    return lax.dot_general(a, b, (((1,), (1,)), ((), ())), preferred_element_type=f32)


def expo_of(scores):
    return jnp.exp2(cap_value * math.log2(math.e) * jnp.tanh(scores * (1.0 / cap_value)))


def columns(index, width=HEAD_SIZE):
    return slice(index * width, (index + 1) * width)


def call(body, out_shape, in_specs, name, scratch=(), out_specs=None, cost=1000):
    return pl.pallas_call(
        body,
        out_shape=out_shape,
        in_specs=in_specs,
        out_specs=jax.tree.map(lambda _: VMEM, out_shape) if out_specs is None else out_specs,
        scratch_shapes=scratch,
        compiler_params=pltpu.CompilerParams(vmem_limit_bytes=VMEM_BYTES),
        cost_estimate=pl.CostEstimate(flops=cost, bytes_accessed=1000, transcendentals=0),
        name=name,
    )


def in_hbm(arrays):
    return [pltpu.with_memory_space_constraint(x, pltpu.HBM) for x in arrays]


def rows_at(index, size):
    return pl.ds(pl.multiple_of(index * size, size), size)


def beside_ones(values):
    return jnp.concatenate([values, jnp.ones(values.shape, bf16)], axis=1)


class Facts:
    def __init__(self, ref, slots, residues, groups):
        self.ref, self.slots, self.residues, self.groups = ref, slots, residues, groups
        self.size = 2 * slots + residues + groups

    def block(self, slot, half):
        return self.ref[0, 2 * slot + half]

    def rank(self, residue):
        return self.ref[0, 2 * self.slots + residue]

    def owner(self, prompt):
        return self.ref[0, 2 * self.slots + self.residues + prompt]

    def store(self, map_ref, rank_ref, owner_ref):
        for slot in range(self.slots):
            for half in range(2):
                self.ref[0, 2 * slot + half] = map_ref[0, slot, half]
        for residue in range(self.residues):
            self.ref[0, 2 * self.slots + residue] = rank_ref[0, residue]
        for prompt in range(self.groups):
            self.ref[0, 2 * self.slots + self.residues + prompt] = owner_ref[prompt]

    def halves(self, slot):
        high = jnp.where(self.block(slot, 1) > self.block(slot, 0), 1, 0)
        return 1 - high, high


def slot_and_head_group():
    member = lax.axis_index("blk")
    return member // HEAD_DIVISIONS, member % HEAD_DIVISIONS


def prepare(queries, keys, values, table, decode_rank, owner, tables):
    rows, width = keys.shape
    block_len = rows // 2
    slots = table.shape[1]
    residues = decode_rank.shape[1]
    first = block_len // slots
    arrays = (queries, keys, values, *tables, table, decode_rank, owner)
    count = len(arrays)
    facts_of = lambda ref: Facts(ref, slots, residues, owner.shape[0])

    def body(*refs):
        inputs, refs = refs[:count], refs[count:]
        facts_ref, q_ref, v_ref, kr_ref, angle_ref = refs[:5]
        sent_refs, refs = refs[5 : 4 + slots], refs[4 + slots :]
        k_ref, row_ref, blk_ref, map_ref, rank_ref, owner_ref, sems = refs
        targets = (q_ref, k_ref, v_ref, row_ref, blk_ref, map_ref, rank_ref, owner_ref)
        copies = []
        for index in (1, 3, 4, 5, 6, 7, 2, 0):
            copies.append(pltpu.make_async_copy(inputs[index], targets[index], sems.at[index]))
            copies[-1].start()
        slot, head_group = slot_and_head_group()
        for copy in copies[:6]:
            copy.wait()
        facts = facts_of(facts_ref)
        facts.store(map_ref, rank_ref, owner_ref)
        for half in range(2):
            part = columns(half, block_len)
            angles = block_angles(row_ref, blk_ref, map_ref[0, slot, half])
            angle_ref[half, 0] = angles[0]
            angle_ref[half, 1] = angles[1]
            for head in range(KV_DEV):
                kr_ref[part, columns(head)] = turned(k_ref[part, columns(head)], angles).astype(bf16)
        copies[6].wait()
        for turn in range(1, slots):
            order = order_matrix(
                lambda r: rank_ref[0, r],
                (slot + turn) % slots,
                head_group,
                0,
                first,
                block_len,
                residues,
            )
            for kind, source in enumerate((kr_ref, v_ref)):
                for half in range(2):
                    sent_refs[turn - 1][columns(2 * kind + half, first)] = dot(
                        order, source[columns(half, block_len)]
                    ).astype(bf16)
        copies[7].wait()

    shapes = [
        jax.ShapeDtypeStruct((1, facts_of(None).size), jnp.int32),
        jax.ShapeDtypeStruct(queries.shape, bf16),
        jax.ShapeDtypeStruct(values.shape, bf16),
        jax.ShapeDtypeStruct(keys.shape, bf16),
        jax.ShapeDtypeStruct((2, 2, block_len, HEAD_SIZE), f32),
    ]
    shapes += [jax.ShapeDtypeStruct((4 * first, width), bf16) for _ in range(1, slots)]
    scratch = [pltpu.VMEM(x.shape, x.dtype) for x in (keys, *tables)]
    scratch += [pltpu.SMEM(x.shape, x.dtype) for x in (table, decode_rank, owner)]
    scratch.append(pltpu.SemaphoreType.DMA((count,)))
    outs = call(
        body,
        shapes,
        [HBM] * count,
        "prepare",
        scratch,
        out_specs=[SMEM] + [VMEM] * (len(shapes) - 1),
    )(*in_hbm(arrays))
    return outs[0], outs[1:5], outs[5:], facts_of


def own_part(facts_row, facts_of, operands):
    queries, values, key_rot, _ = operands
    rows, width = key_rot.shape
    block_len = rows // 2
    sizes = facts_of(None)
    slots, residues, groups = sizes.slots, sizes.residues, sizes.groups
    first = block_len // slots
    rest = block_len - first
    run = block_len // residues
    cache_rows = 2 * slots * run

    def body(facts_ref, q_ref, v_ref, kr_ref, angle_ref, *refs):
        qr_ref, acc_ref, place_ref, owned_ref, row_at_ref, cache_at_ref = refs[:6]
        e_refs, sent_refs = refs[6:10], refs[10:]
        facts = facts_of(facts_ref)
        slot, head_group = slot_and_head_group()
        group = lax.axis_index("req")

        def ordered(target, start, count):
            return order_matrix(
                facts.rank, target, head_group, start, count, block_len, residues
            )

        for turn in range(1, slots):
            order = ordered((slot + turn) % slots, first, rest)
            for kind, source in enumerate((kr_ref, v_ref)):
                for half in range(2):
                    sent_refs[turn - 1][columns(2 * kind + half, rest)] = dot(
                        order, source[columns(half, block_len)]
                    ).astype(bf16)
        order = ordered(slot, 0, first)
        for kind, source in enumerate((kr_ref, v_ref)):
            chosen = [dot(order, source[columns(half, block_len)]) for half in range(2)]
            for m in range(HEAD_DIVISIONS):
                lines = jnp.concatenate([part[columns(m, run)] for part in chosen], axis=0)
                e_refs[m][columns(kind, 2 * run)] = lines.astype(bf16)

        for half in range(2):
            part = columns(half, block_len)
            angles = angle_ref[half, 0], angle_ref[half, 1]
            for head in range(Q_DEV):
                qr_ref[part, columns(head)] = (
                    turned(q_ref[part, columns(head)], angles) * query_scale
                ).astype(bf16)
        low, high = facts.halves(slot)
        low, high = rows_at(low, block_len), rows_at(high, block_len)
        row = lax.broadcasted_iota(jnp.int32, (block_len, block_len), 0)
        col = lax.broadcasted_iota(jnp.int32, (block_len, block_len), 1)
        for head in range(Q_DEV):
            key_head = columns(head * KV_DEV // Q_DEV)
            both = columns(head, 2 * HEAD_SIZE)

            def tile(q_part, k_part, diagonal):
                expo = expo_of(dot_t(qr_ref[q_part, columns(head)], kr_ref[k_part, key_head]))
                if diagonal:
                    expo = jnp.where(col <= row, expo, 0.0)
                return dot(expo.astype(bf16), beside_ones(v_ref[k_part, key_head]))

            acc_ref[low, both] = tile(low, low, True)
            acc_ref[high, both] = tile(high, high, True) + tile(high, low, False)

        col = lax.broadcasted_iota(jnp.int32, (1, cache_rows), 1)
        part, offset = col // run, col % run
        target = jnp.zeros_like(col)
        for turn in range(slots):
            for half in range(2):
                block = facts.block((slot - turn + slots) % slots, half)
                target = jnp.where(part == 2 * turn + half, block * run + offset, target)
        row = lax.broadcasted_iota(jnp.int32, (cache_rows, cache_rows), 0)
        place_ref[...] = jnp.where(row == target, 1.0, 0.0).astype(bf16)
        residue = 0
        for r in range(1, residues):
            residue = jnp.where(facts.rank(r) == lax.axis_index("blk"), r, residue)
        cache_at_ref[...] = (row * residues + residue).astype(f32)
        for half in range(2):
            offset = lax.broadcasted_iota(jnp.int32, (block_len, HEAD_SIZE), 0)
            at = facts.block(slot, half) * block_len + offset
            row_at_ref[columns(half, block_len)] = at.astype(f32)
        for turn in range(groups):
            mine = facts.owner(lax.rem(group - turn + groups, groups)) == group
            owned_ref[turn : turn + 1] = jnp.full((1, HEAD_SIZE), jnp.where(mine, 1.0, 0.0), f32)

    shapes = [
        jax.ShapeDtypeStruct(queries.shape, bf16),
        jax.ShapeDtypeStruct((rows, 2 * Q_DEV * HEAD_SIZE), f32),
        jax.ShapeDtypeStruct((cache_rows, cache_rows), bf16),
        jax.ShapeDtypeStruct((groups, HEAD_SIZE), f32),
        jax.ShapeDtypeStruct((rows, HEAD_SIZE), f32),
        jax.ShapeDtypeStruct((cache_rows, cache_rows), f32),
    ]
    shapes += [jax.ShapeDtypeStruct((4 * run, width), bf16) for _ in range(HEAD_DIVISIONS)]
    shapes += [jax.ShapeDtypeStruct((4 * rest, width), bf16) for _ in range(1, slots)]
    outs = call(body, shapes, [SMEM] + [VMEM] * 4, "own_part")(facts_row, *operands)
    return outs[0], outs[1], outs[2:6], outs[6:10], outs[10:]


def late_pieces(arrived, lens):
    others = len(arrived)
    width = arrived[0].shape[1]
    first = arrived[0].shape[0] // 4
    run = first // HEAD_DIVISIONS
    rounds = len(lens)

    def body(*refs):
        len_refs, in_refs, e_refs = refs[:rounds], refs[rounds : rounds + others], refs[rounds + others :]
        line = lax.broadcasted_iota(jnp.int32, (CARRIED, width), 0)
        carried = jnp.zeros((CARRIED, width), jnp.int32)
        for index in range(rounds):
            length = len_refs[index][0]
            carried = jnp.where(line == 2 * index, lax.shift_right_logical(length, 6), carried)
            carried = jnp.where(line == 2 * index + 1, length & 63, carried)
        carried = carried.astype(f32).astype(bf16)
        for m in range(HEAD_DIVISIONS):
            for kind in range(2):
                for index in range(others):
                    lines = [
                        in_refs[index][columns(2 * kind + half, first)].astype(f32)[columns(m, run)]
                        for half in range(2)
                    ]
                    e_refs[m][columns(kind * others + index, 2 * run)] = jnp.concatenate(
                        lines, axis=0
                    ).astype(bf16)
            e_refs[m][4 * others * run :] = carried

    shapes = [
        jax.ShapeDtypeStruct((4 * others * run + CARRIED, width), bf16)
        for _ in range(HEAD_DIVISIONS)
    ]
    return call(body, shapes, [SMEM] * rounds + [VMEM] * others, "late_pieces")(*lens, *arrived)


def attend(facts_row, facts_of, query_rot, acc, arrived, live=None):
    rows = query_rot.shape[0]
    block_len = rows // 2
    others = len(arrived)
    size = arrived[0].shape[0] // 4
    sizes = facts_of(None)
    slots = sizes.slots
    last = live is not None

    def body(facts_ref, q_ref, acc_ref, *refs):
        in_refs, out_ref = refs[:others], refs[-1]
        facts = facts_of(facts_ref)
        slot = slot_and_head_group()[0]
        low, high = facts.halves(slot)
        low_rows, high_rows = rows_at(low, block_len), rows_at(high, block_len)
        for head in range(Q_DEV):
            key_head = columns(head * KV_DEV // Q_DEV)
            both = columns(head, 2 * HEAD_SIZE)
            low_sum, high_sum = acc_ref[low_rows, both], acc_ref[high_rows, both]
            for turn in range(1, slots):
                in_ref = in_refs[turn - 1]
                source = (slot - turn + slots) % slots
                source_low, source_high = facts.halves(source)
                outer = facts.block(slot, low) < facts.block(source, source_low)

                def tile(half, other):
                    queries = q_ref[rows_at(half, block_len), columns(head)]
                    expo = expo_of(dot_t(queries, in_ref[rows_at(other, size), key_head]))
                    values = in_ref[rows_at(2 + other, size), key_head]
                    return dot(expo.astype(bf16), beside_ones(values))

                either = tile(jnp.where(outer, high, low), source_low)
                upper = tile(high, jnp.where(outer, source_high, source_low))
                low_sum = low_sum + jnp.where(outer, 0.0, either)
                high_sum = high_sum + upper + jnp.where(outer, either, 0.0)
            for part, total in ((low_rows, low_sum), (high_rows, high_sum)):
                if last:
                    scale = refs[others][part] / total[:, HEAD_SIZE:]
                    out_ref[part, columns(head)] = (total[:, :HEAD_SIZE] * scale).astype(bf16)
                else:
                    out_ref[part, both] = total

    if last:
        shape, name = jax.ShapeDtypeStruct(query_rot.shape, bf16), "attend_rest"
        extra = (live,)
    else:
        shape, name = jax.ShapeDtypeStruct(acc.shape, f32), "attend_first"
        extra = ()
    specs = [SMEM] + [VMEM] * (2 + others + len(extra))
    cost = 1000 if last else 10**10
    return call(body, shape, specs, name, cost=cost)(facts_row, query_rot, acc, *arrived, *extra)


def cache_part(early, late, masks):
    place, owned, row_at, cache_at = masks
    cache_rows = place.shape[0]
    piece = early[0].shape[0] // 2
    width = early[0].shape[1]
    groups = owned.shape[0]

    def body(place_ref, owned_ref, row_at_ref, cache_at_ref, *refs):
        f_refs, s_refs, out_ref, live_ref = refs[:4], refs[4:8], refs[8], refs[9]
        head_group = slot_and_head_group()[1]
        later = cache_rows - piece
        length = jnp.zeros((1, HEAD_SIZE), f32)
        for m in range(HEAD_DIVISIONS):
            carried = s_refs[m][2 * later :, :HEAD_SIZE].astype(f32)
            for index in range(groups // HEAD_DIVISIONS):
                turn = (head_group ^ m) + HEAD_DIVISIONS * index
                value = carried[2 * index : 2 * index + 1] * 64.0 + carried[2 * index + 1 : 2 * index + 2]
                length = length + owned_ref[pl.ds(turn, 1)] * value
        live_ref[...] = jnp.where(row_at_ref[...] < length, 1.0, 0.0)
        kept = jnp.where(cache_at_ref[...] < length[:, :1], place_ref[...].astype(f32), 0.0)
        kept = kept.astype(bf16)
        for m in range(HEAD_DIVISIONS):
            for kind in range(2):
                lines = jnp.concatenate(
                    [f_refs[m][columns(kind, piece)], s_refs[m][columns(kind, later)]], axis=0
                )
                column = ((head_group ^ m) + kind * HEAD_DIVISIONS) * width
                out_ref[:, pl.ds(pl.multiple_of(column, HEAD_SIZE), width)] = dot(kept, lines).astype(
                    bf16
                )

    shapes = [
        jax.ShapeDtypeStruct((cache_rows, 2 * HEAD_DIVISIONS * width), bf16),
        jax.ShapeDtypeStruct(row_at.shape, f32),
    ]
    return call(body, shapes, [VMEM] * 12, "cache_part")(*masks, *early, *late)


def on_device(queries, keys, values, block_map, lengths, group_of_prompt, decode_rank):
    block_len = queries.shape[2] // 2
    slots = block_map.shape[1]
    q, k, v = queries[0, 0], keys[0, 0], values[0, 0]
    tables = rotary_tables(block_len, 2 * slots)

    def to_slots(parts):
        return [shifted(parts[t - 1], "blk", HEAD_DIVISIONS * t) for t in range(1, slots)]

    def hand_on(pieces):
        return [pieces[0]] + [crossed(pieces[m], "blk", m) for m in range(1, HEAD_DIVISIONS)]

    lens = [spread(lengths, t) for t in range(lax.axis_size("req") // HEAD_DIVISIONS)]
    facts_row, operands, sent, facts_of = prepare(
        q, k, v, block_map, decode_rank, group_of_prompt, tables
    )
    first = to_slots(sent)
    query_rot, acc, masks, early, sent = own_part(facts_row, facts_of, operands)
    rest = to_slots(sent)
    early = hand_on(early)
    late = hand_on(late_pieces(first, lens))
    acc = attend(facts_row, facts_of, query_rot, acc, first)
    cache, live = cache_part(early, late, masks)
    attended = attend(facts_row, facts_of, query_rot, acc, rest, live)
    return (attended[None, None], cache[None])


def solution(mesh):
    placed = (
        P("req", "blk", None, None),
        P("req", "blk", None, None),
        P("req", "blk", None, None),
        P("req", None, None),
        P("req"),
        P(),
        P("req", None),
    )
    return jax.shard_map(
        on_device,
        mesh=mesh,
        in_specs=placed,
        out_specs=(P("req", "blk", None, None), P("req", "blk", None)),
        check_vma=False,
    )
```

```python
import math

import jax
import jax.numpy as jnp
import numpy as np
from jax import lax
from jax.experimental import pallas as pl
from jax.experimental.pallas import tpu as pltpu
from jax.sharding import PartitionSpec as P

QUERY_HEADS = 16
KEY_VALUE_HEADS = 8
HEAD_SIZE = 128
HEAD_DIVISIONS = 4
Q_DEV = 4
KV_DEV = 2
KV_WIDTH = KV_DEV * HEAD_SIZE

cap_value = 50.0
query_scale = 1.0 / 12.0
rope_base = 10000.0
CARRIED = 16
VMEM_BYTES = 48 * 1024 * 1024

f32 = jnp.float32
bf16 = jnp.bfloat16
SMEM = pl.BlockSpec(memory_space=pltpu.SMEM)
VMEM = pl.BlockSpec(memory_space=pltpu.VMEM)
HBM = pl.BlockSpec(memory_space=pltpu.HBM)


def shifted(shard, axis, by):
    peers = lax.axis_size(axis)
    return lax.ppermute(shard, axis, [(i, (i + by) % peers) for i in range(peers)])


def crossed(shard, axis, by):
    peers = lax.axis_size(axis)
    return lax.ppermute(shard, axis, [(i, i ^ by) for i in range(peers)])


def spread(shard, turn):
    groups, members = lax.axis_size("req"), lax.axis_size("blk")
    pairs = []
    for group in range(groups):
        for member in range(members):
            target = group + member % HEAD_DIVISIONS + HEAD_DIVISIONS * turn
            pairs.append((group * members + member, target % groups * members + member))
    return lax.ppermute(shard, ("req", "blk"), pairs)


def rotary_tables(block_len, block_count):
    half = HEAD_SIZE // 2
    frequency = np.exp(
        np.float32(-math.log(rope_base)) * (2.0 * np.arange(half, dtype=np.float32)) / HEAD_SIZE
    ).astype(np.float64)

    def table(positions):
        angles = positions.astype(np.float64)[:, None] * frequency[None, :]
        cosine, sine = np.cos(angles), np.sin(angles)
        return np.stack(
            [np.concatenate([cosine, cosine], 1), np.concatenate([-sine, sine], 1)]
        ).astype(np.float32)

    return table(np.arange(block_len)), table(np.arange(block_count) * block_len)


def block_angles(row_table, block_table, block):
    row_cos, row_sin = row_table[0], row_table[1]
    blk_cos, blk_sin = block_table[0, pl.ds(block, 1)], block_table[1, pl.ds(block, 1)]
    return row_cos * blk_cos - row_sin * blk_sin, row_sin * blk_cos + row_cos * blk_sin


def turned(head, angles):
    x = head.astype(f32)
    return x * angles[0] + pltpu.roll(x, HEAD_SIZE // 2, 1) * angles[1]


def order_matrix(rank_of, slot, head_group, first_row, out_rows, rows, residues):
    row_ids = lax.broadcasted_iota(jnp.int32, (1, rows), 1)
    residue = row_ids % residues
    rank = jnp.zeros_like(row_ids)
    for r in range(residues):
        rank = jnp.where(residue == r, rank_of(r), rank)
    ahead = (rank - HEAD_DIVISIONS * slot + residues) % residues
    ahead = jnp.where(ahead < HEAD_DIVISIONS, ahead ^ head_group, ahead)
    index = ahead * (rows // residues) + row_ids // residues
    out_ids = first_row + lax.broadcasted_iota(jnp.int32, (out_rows, rows), 0)
    return jnp.where(out_ids == index, 1.0, 0.0).astype(bf16)


def dot(a, b):
    return jnp.dot(a, b, preferred_element_type=f32)


def dot_t(a, b):
    return lax.dot_general(a, b, (((1,), (1,)), ((), ())), preferred_element_type=f32)


def expo_of(scores):
    return jnp.exp2(cap_value * math.log2(math.e) * jnp.tanh(scores * (1.0 / cap_value)))


def columns(index, width=HEAD_SIZE):
    return slice(index * width, (index + 1) * width)


def call(body, out_shape, in_specs, name, scratch=(), out_specs=None, cost=1000):
    return pl.pallas_call(
        body,
        out_shape=out_shape,
        in_specs=in_specs,
        out_specs=jax.tree.map(lambda _: VMEM, out_shape) if out_specs is None else out_specs,
        scratch_shapes=scratch,
        compiler_params=pltpu.CompilerParams(vmem_limit_bytes=VMEM_BYTES),
        cost_estimate=pl.CostEstimate(flops=cost, bytes_accessed=1000, transcendentals=0),
        name=name,
    )


def in_hbm(arrays):
    return [pltpu.with_memory_space_constraint(x, pltpu.HBM) for x in arrays]


def rows_at(index, size):
    return pl.ds(pl.multiple_of(index * size, size), size)


def beside_ones(values):
    return jnp.concatenate([values, jnp.ones(values.shape, bf16)], axis=1)


class Facts:
    def __init__(self, ref, slots, residues, groups):
        self.ref, self.slots, self.residues, self.groups = ref, slots, residues, groups
        self.size = 2 * slots + residues + groups

    def block(self, slot, half):
        return self.ref[0, 2 * slot + half]

    def rank(self, residue):
        return self.ref[0, 2 * self.slots + residue]

    def owner(self, prompt):
        return self.ref[0, 2 * self.slots + self.residues + prompt]

    def store(self, map_ref, rank_ref, owner_ref):
        for slot in range(self.slots):
            for half in range(2):
                self.ref[0, 2 * slot + half] = map_ref[0, slot, half]
        for residue in range(self.residues):
            self.ref[0, 2 * self.slots + residue] = rank_ref[0, residue]
        for prompt in range(self.groups):
            self.ref[0, 2 * self.slots + self.residues + prompt] = owner_ref[prompt]

    def halves(self, slot):
        high = jnp.where(self.block(slot, 1) > self.block(slot, 0), 1, 0)
        return 1 - high, high


def slot_and_head_group():
    member = lax.axis_index("blk")
    return member // HEAD_DIVISIONS, member % HEAD_DIVISIONS


def prepare(queries, keys, values, table, decode_rank, owner, tables):
    rows, width = keys.shape
    block_len = rows // 2
    slots = table.shape[1]
    residues = decode_rank.shape[1]
    first = block_len // slots
    arrays = (queries, keys, values, *tables, table, decode_rank, owner)
    count = len(arrays)
    facts_of = lambda ref: Facts(ref, slots, residues, owner.shape[0])

    def body(*refs):
        inputs, refs = refs[:count], refs[count:]
        facts_ref, q_ref, v_ref, kr_ref, angle_ref = refs[:5]
        sent_refs, refs = refs[5 : 4 + slots], refs[4 + slots :]
        k_ref, row_ref, blk_ref, map_ref, rank_ref, owner_ref, sems = refs
        targets = (q_ref, k_ref, v_ref, row_ref, blk_ref, map_ref, rank_ref, owner_ref)
        copies = []
        for index in (1, 3, 4, 5, 6, 7, 2, 0):
            copies.append(pltpu.make_async_copy(inputs[index], targets[index], sems.at[index]))
            copies[-1].start()
        slot, head_group = slot_and_head_group()
        for copy in copies[:6]:
            copy.wait()
        facts = facts_of(facts_ref)
        facts.store(map_ref, rank_ref, owner_ref)
        for half in range(2):
            part = columns(half, block_len)
            angles = block_angles(row_ref, blk_ref, map_ref[0, slot, half])
            angle_ref[half, 0] = angles[0]
            angle_ref[half, 1] = angles[1]
            for head in range(KV_DEV):
                kr_ref[part, columns(head)] = turned(k_ref[part, columns(head)], angles).astype(bf16)
        copies[6].wait()
        for turn in range(1, slots):
            order = order_matrix(
                lambda r: rank_ref[0, r],
                (slot + turn) % slots,
                head_group,
                0,
                first,
                block_len,
                residues,
            )
            for kind, source in enumerate((kr_ref, v_ref)):
                for half in range(2):
                    sent_refs[turn - 1][columns(2 * kind + half, first)] = dot(
                        order, source[columns(half, block_len)]
                    ).astype(bf16)
        copies[7].wait()

    shapes = [
        jax.ShapeDtypeStruct((1, facts_of(None).size), jnp.int32),
        jax.ShapeDtypeStruct(queries.shape, bf16),
        jax.ShapeDtypeStruct(values.shape, bf16),
        jax.ShapeDtypeStruct(keys.shape, bf16),
        jax.ShapeDtypeStruct((2, 2, block_len, HEAD_SIZE), f32),
    ]
    shapes += [jax.ShapeDtypeStruct((4 * first, width), bf16) for _ in range(1, slots)]
    scratch = [pltpu.VMEM(x.shape, x.dtype) for x in (keys, *tables)]
    scratch += [pltpu.SMEM(x.shape, x.dtype) for x in (table, decode_rank, owner)]
    scratch.append(pltpu.SemaphoreType.DMA((count,)))
    outs = call(
        body,
        shapes,
        [HBM] * count,
        "prepare",
        scratch,
        out_specs=[SMEM] + [VMEM] * (len(shapes) - 1),
    )(*in_hbm(arrays))
    return outs[0], outs[1:5], outs[5:], facts_of


def own_part(facts_row, facts_of, operands):
    queries, values, key_rot, _ = operands
    rows, width = key_rot.shape
    block_len = rows // 2
    sizes = facts_of(None)
    slots, residues, groups = sizes.slots, sizes.residues, sizes.groups
    first = block_len // slots
    run = block_len // residues
    cache_rows = 2 * slots * run

    def body(facts_ref, q_ref, v_ref, kr_ref, angle_ref, *refs):
        qr_ref, acc_ref, place_ref, owned_ref, row_at_ref, cache_at_ref = refs[:6]
        e_refs = refs[6:]
        facts = facts_of(facts_ref)
        slot, head_group = slot_and_head_group()
        group = lax.axis_index("req")
        order = order_matrix(facts.rank, slot, head_group, 0, first, block_len, residues)
        for kind, source in enumerate((kr_ref, v_ref)):
            chosen = [dot(order, source[columns(half, block_len)]) for half in range(2)]
            for m in range(HEAD_DIVISIONS):
                lines = jnp.concatenate([part[columns(m, run)] for part in chosen], axis=0)
                e_refs[m][columns(kind, 2 * run)] = lines.astype(bf16)

        for half in range(2):
            part = columns(half, block_len)
            angles = angle_ref[half, 0], angle_ref[half, 1]
            for head in range(Q_DEV):
                qr_ref[part, columns(head)] = (
                    turned(q_ref[part, columns(head)], angles) * query_scale
                ).astype(bf16)
        low, high = facts.halves(slot)
        low, high = rows_at(low, block_len), rows_at(high, block_len)
        row = lax.broadcasted_iota(jnp.int32, (block_len, block_len), 0)
        col = lax.broadcasted_iota(jnp.int32, (block_len, block_len), 1)
        for head in range(Q_DEV):
            key_head = columns(head * KV_DEV // Q_DEV)
            both = columns(head, 2 * HEAD_SIZE)

            def tile(q_part, k_part, diagonal):
                expo = expo_of(dot_t(qr_ref[q_part, columns(head)], kr_ref[k_part, key_head]))
                if diagonal:
                    expo = jnp.where(col <= row, expo, 0.0)
                return dot(expo.astype(bf16), beside_ones(v_ref[k_part, key_head]))

            acc_ref[low, both] = tile(low, low, True)
            acc_ref[high, both] = tile(high, high, True) + tile(high, low, False)

        col = lax.broadcasted_iota(jnp.int32, (1, cache_rows), 1)
        part, offset = col // run, col % run
        target = jnp.zeros_like(col)
        for turn in range(slots):
            for half in range(2):
                block = facts.block((slot - turn + slots) % slots, half)
                target = jnp.where(part == 2 * turn + half, block * run + offset, target)
        row = lax.broadcasted_iota(jnp.int32, (cache_rows, cache_rows), 0)
        place_ref[...] = jnp.where(row == target, 1.0, 0.0).astype(bf16)
        residue = 0
        for r in range(1, residues):
            residue = jnp.where(facts.rank(r) == lax.axis_index("blk"), r, residue)
        cache_at_ref[...] = (row * residues + residue).astype(f32)
        for half in range(2):
            offset = lax.broadcasted_iota(jnp.int32, (block_len, HEAD_SIZE), 0)
            at = facts.block(slot, half) * block_len + offset
            row_at_ref[columns(half, block_len)] = at.astype(f32)
        for turn in range(groups):
            mine = facts.owner(lax.rem(group - turn + groups, groups)) == group
            owned_ref[turn : turn + 1] = jnp.full((1, HEAD_SIZE), jnp.where(mine, 1.0, 0.0), f32)

    shapes = [
        jax.ShapeDtypeStruct(queries.shape, bf16),
        jax.ShapeDtypeStruct((rows, 2 * Q_DEV * HEAD_SIZE), f32),
        jax.ShapeDtypeStruct((cache_rows, cache_rows), bf16),
        jax.ShapeDtypeStruct((groups, HEAD_SIZE), f32),
        jax.ShapeDtypeStruct((rows, HEAD_SIZE), f32),
        jax.ShapeDtypeStruct((cache_rows, cache_rows), f32),
    ]
    shapes += [jax.ShapeDtypeStruct((4 * run, width), bf16) for _ in range(HEAD_DIVISIONS)]
    outs = call(body, shapes, [SMEM] + [VMEM] * 4, "own_part")(facts_row, *operands)
    return outs[0], outs[1], outs[2:6], outs[6:]


def second_part(facts_row, facts_of, lens, key_rot, values, after):
    rows, width = key_rot.shape
    block_len = rows // 2
    sizes = facts_of(None)
    slots, residues = sizes.slots, sizes.residues
    first = block_len // slots
    rest = block_len - first
    rounds = len(lens)

    def body(facts_ref, *refs):
        len_refs, refs = refs[:rounds], refs[rounds:]
        kr_ref, v_ref, _, carried_ref, sent_refs = refs[0], refs[1], refs[2], refs[3], refs[4:]
        facts = facts_of(facts_ref)
        slot, head_group = slot_and_head_group()
        for turn in range(1, slots):
            order = order_matrix(
                facts.rank, (slot + turn) % slots, head_group, first, rest, block_len, residues
            )
            for kind, source in enumerate((kr_ref, v_ref)):
                for half in range(2):
                    sent_refs[turn - 1][columns(2 * kind + half, rest)] = dot(
                        order, source[columns(half, block_len)]
                    ).astype(bf16)
        line = lax.broadcasted_iota(jnp.int32, (CARRIED, width), 0)
        carried = jnp.zeros((CARRIED, width), jnp.int32)
        for index in range(rounds):
            length = len_refs[index][0]
            carried = jnp.where(line == 2 * index, lax.shift_right_logical(length, 6), carried)
            carried = jnp.where(line == 2 * index + 1, length & 63, carried)
        carried_ref[...] = carried.astype(f32).astype(bf16)

    shapes = [jax.ShapeDtypeStruct((CARRIED, width), bf16)]
    shapes += [jax.ShapeDtypeStruct((4 * rest, width), bf16) for _ in range(1, slots)]
    specs = [SMEM] * (1 + rounds) + [VMEM] * 3
    outs = call(body, shapes, specs, "second_part")(facts_row, *lens, key_rot, values, after)
    return outs[0], outs[1:]


def late_pieces(arrived, carried):
    others = len(arrived)
    width = arrived[0].shape[1]
    first = arrived[0].shape[0] // 4
    run = first // HEAD_DIVISIONS

    def body(carried_ref, *refs):
        in_refs, e_refs = refs[:others], refs[others:]
        for m in range(HEAD_DIVISIONS):
            for kind in range(2):
                for index in range(others):
                    place = (kind * others + index) * 2
                    if run % 16 == 0:
                        for half in range(2):
                            start = (2 * kind + half) * first + m * run
                            e_refs[m][columns(place + half, run)] = in_refs[index][start : start + run]
                        continue
                    lines = [
                        in_refs[index][columns(2 * kind + half, first)].astype(f32)[columns(m, run)]
                        for half in range(2)
                    ]
                    e_refs[m][place * run : (place + 2) * run] = jnp.concatenate(
                        lines, axis=0
                    ).astype(bf16)
            e_refs[m][4 * others * run :] = carried_ref[...]

    shapes = [
        jax.ShapeDtypeStruct((4 * others * run + CARRIED, width), bf16)
        for _ in range(HEAD_DIVISIONS)
    ]
    return call(body, shapes, [VMEM] * (1 + others), "late_pieces")(carried, *arrived)


def attend(facts_row, facts_of, query_rot, acc, arrived, live=None):
    rows = query_rot.shape[0]
    block_len = rows // 2
    others = len(arrived)
    size = arrived[0].shape[0] // 4
    sizes = facts_of(None)
    slots = sizes.slots
    last = live is not None

    def body(facts_ref, q_ref, acc_ref, *refs):
        in_refs, out_ref = refs[:others], refs[-1]
        facts = facts_of(facts_ref)
        slot = slot_and_head_group()[0]
        low, high = facts.halves(slot)
        low_rows, high_rows = rows_at(low, block_len), rows_at(high, block_len)
        for head in range(Q_DEV):
            key_head = columns(head * KV_DEV // Q_DEV)
            both = columns(head, 2 * HEAD_SIZE)
            low_sum, high_sum = acc_ref[low_rows, both], acc_ref[high_rows, both]
            for turn in range(1, slots):
                in_ref = in_refs[turn - 1]
                source = (slot - turn + slots) % slots
                source_low, source_high = facts.halves(source)
                outer = facts.block(slot, low) < facts.block(source, source_low)

                def tile(half, other):
                    queries = q_ref[rows_at(half, block_len), columns(head)]
                    expo = expo_of(dot_t(queries, in_ref[rows_at(other, size), key_head]))
                    values = in_ref[rows_at(2 + other, size), key_head]
                    return dot(expo.astype(bf16), beside_ones(values))

                either = tile(jnp.where(outer, high, low), source_low)
                upper = tile(high, jnp.where(outer, source_high, source_low))
                low_sum = low_sum + jnp.where(outer, 0.0, either)
                high_sum = high_sum + upper + jnp.where(outer, either, 0.0)
            for part, total in ((low_rows, low_sum), (high_rows, high_sum)):
                if last:
                    scale = refs[others][part] / total[:, HEAD_SIZE:]
                    out_ref[part, columns(head)] = (total[:, :HEAD_SIZE] * scale).astype(bf16)
                else:
                    out_ref[part, both] = total

    if last:
        shape, name = jax.ShapeDtypeStruct(query_rot.shape, bf16), "attend_rest"
        extra = (live,)
    else:
        shape, name = jax.ShapeDtypeStruct(acc.shape, f32), "attend_first"
        extra = ()
    specs = [SMEM] + [VMEM] * (2 + others + len(extra))
    cost = 1000 if last else 10**10
    return call(body, shape, specs, name, cost=cost)(facts_row, query_rot, acc, *arrived, *extra)


def cache_part(early, late, masks):
    place, owned, row_at, cache_at = masks
    cache_rows = place.shape[0]
    piece = early[0].shape[0] // 2
    width = early[0].shape[1]
    groups = owned.shape[0]

    def body(place_ref, owned_ref, row_at_ref, cache_at_ref, *refs):
        f_refs, s_refs, out_ref, live_ref = refs[:4], refs[4:8], refs[8], refs[9]
        head_group = slot_and_head_group()[1]
        later = cache_rows - piece
        length = jnp.zeros((1, HEAD_SIZE), f32)
        for m in range(HEAD_DIVISIONS):
            carried = s_refs[m][2 * later :, :HEAD_SIZE].astype(f32)
            for index in range(groups // HEAD_DIVISIONS):
                turn = (head_group ^ m) + HEAD_DIVISIONS * index
                value = carried[2 * index : 2 * index + 1] * 64.0 + carried[2 * index + 1 : 2 * index + 2]
                length = length + owned_ref[pl.ds(turn, 1)] * value
        live_ref[...] = jnp.where(row_at_ref[...] < length, 1.0, 0.0)
        kept = jnp.where(cache_at_ref[...] < length[:, :1], place_ref[...].astype(f32), 0.0)
        kept = kept.astype(bf16)
        for m in range(HEAD_DIVISIONS):
            for kind in range(2):
                lines = jnp.concatenate(
                    [f_refs[m][columns(kind, piece)], s_refs[m][columns(kind, later)]], axis=0
                )
                column = ((head_group ^ m) + kind * HEAD_DIVISIONS) * width
                out_ref[:, pl.ds(pl.multiple_of(column, HEAD_SIZE), width)] = dot(kept, lines).astype(
                    bf16
                )

    shapes = [
        jax.ShapeDtypeStruct((cache_rows, 2 * HEAD_DIVISIONS * width), bf16),
        jax.ShapeDtypeStruct(row_at.shape, f32),
    ]
    return call(body, shapes, [VMEM] * 12, "cache_part")(*masks, *early, *late)


def on_device(queries, keys, values, block_map, lengths, group_of_prompt, decode_rank):
    block_len = queries.shape[2] // 2
    slots = block_map.shape[1]
    q, k, v = queries[0, 0], keys[0, 0], values[0, 0]
    tables = rotary_tables(block_len, 2 * slots)

    def to_slots(parts):
        return [shifted(parts[t - 1], "blk", HEAD_DIVISIONS * t) for t in range(1, slots)]

    def hand_on(pieces):
        return [pieces[0]] + [crossed(pieces[m], "blk", m) for m in range(1, HEAD_DIVISIONS)]

    lens = [spread(lengths, t) for t in range(lax.axis_size("req") // HEAD_DIVISIONS)]
    facts_row, operands, sent, facts_of = prepare(
        q, k, v, block_map, decode_rank, group_of_prompt, tables
    )
    first = to_slots(sent)
    query_rot, acc, masks, early = own_part(facts_row, facts_of, operands)
    early = hand_on(early)
    carried, sent = second_part(facts_row, facts_of, lens, operands[2], operands[1], masks[1])
    rest = to_slots(sent)
    late = hand_on(late_pieces(first, carried))
    acc = attend(facts_row, facts_of, query_rot, acc, first)
    cache, live = cache_part(early, late, masks)
    attended = attend(facts_row, facts_of, query_rot, acc, rest, live)
    return (attended[None, None], cache[None])


def solution(mesh):
    placed = (
        P("req", "blk", None, None),
        P("req", "blk", None, None),
        P("req", "blk", None, None),
        P("req", None, None),
        P("req"),
        P(),
        P("req", None),
    )
    return jax.shard_map(
        on_device,
        mesh=mesh,
        in_specs=placed,
        out_specs=(P("req", "blk", None, None), P("req", "blk", None)),
        check_vma=False,
    )
```

```python
import math

import jax
import jax.numpy as jnp
import numpy as np
from jax import lax
from jax.experimental import pallas as pl
from jax.experimental.pallas import tpu as pltpu
from jax.sharding import PartitionSpec as P

QUERY_HEADS = 16
KEY_VALUE_HEADS = 8
HEAD_SIZE = 128
HEAD_DIVISIONS = 4
Q_DEV = 4
KV_DEV = 2
KV_WIDTH = KV_DEV * HEAD_SIZE

cap_value = 50.0
query_scale = 1.0 / 12.0
rope_base = 10000.0
CARRIED = 16
VMEM_BYTES = 48 * 1024 * 1024

f32 = jnp.float32
bf16 = jnp.bfloat16
SMEM = pl.BlockSpec(memory_space=pltpu.SMEM)
VMEM = pl.BlockSpec(memory_space=pltpu.VMEM)
HBM = pl.BlockSpec(memory_space=pltpu.HBM)


def shifted(shard, axis, by):
    peers = lax.axis_size(axis)
    return lax.ppermute(shard, axis, [(i, (i + by) % peers) for i in range(peers)])


def crossed(shard, axis, by):
    peers = lax.axis_size(axis)
    return lax.ppermute(shard, axis, [(i, i ^ by) for i in range(peers)])


def spread(shard, turn):
    groups, members = lax.axis_size("req"), lax.axis_size("blk")
    pairs = []
    for group in range(groups):
        for member in range(members):
            target = group + member % HEAD_DIVISIONS + HEAD_DIVISIONS * turn
            pairs.append((group * members + member, target % groups * members + member))
    return lax.ppermute(shard, ("req", "blk"), pairs)


def rotary_tables(block_len, block_count):
    half = HEAD_SIZE // 2
    frequency = np.exp(
        np.float32(-math.log(rope_base)) * (2.0 * np.arange(half, dtype=np.float32)) / HEAD_SIZE
    ).astype(np.float64)

    def table(positions):
        angles = positions.astype(np.float64)[:, None] * frequency[None, :]
        cosine, sine = np.cos(angles), np.sin(angles)
        return np.stack(
            [np.concatenate([cosine, cosine], 1), np.concatenate([-sine, sine], 1)]
        ).astype(np.float32)

    return table(np.arange(block_len)), table(np.arange(block_count) * block_len)


def block_angles(row_table, block_table, block):
    row_cos, row_sin = row_table[0], row_table[1]
    blk_cos, blk_sin = block_table[0, pl.ds(block, 1)], block_table[1, pl.ds(block, 1)]
    return row_cos * blk_cos - row_sin * blk_sin, row_sin * blk_cos + row_cos * blk_sin


def turned(head, angles):
    x = head.astype(f32)
    return x * angles[0] + pltpu.roll(x, HEAD_SIZE // 2, 1) * angles[1]


def order_matrix(rank_of, slot, head_group, first_row, out_rows, rows, residues):
    row_ids = lax.broadcasted_iota(jnp.int32, (1, rows), 1)
    residue = row_ids % residues
    rank = jnp.zeros_like(row_ids)
    for r in range(residues):
        rank = jnp.where(residue == r, rank_of(r), rank)
    ahead = (rank - HEAD_DIVISIONS * slot + residues) % residues
    ahead = jnp.where(ahead < HEAD_DIVISIONS, ahead ^ head_group, ahead)
    index = ahead * (rows // residues) + row_ids // residues
    out_ids = first_row + lax.broadcasted_iota(jnp.int32, (out_rows, rows), 0)
    return jnp.where(out_ids == index, 1.0, 0.0).astype(bf16)


def dot(a, b):
    return jnp.dot(a, b, preferred_element_type=f32)


def dot_t(a, b):
    return lax.dot_general(a, b, (((1,), (1,)), ((), ())), preferred_element_type=f32)


def expo_of(scores):
    return jnp.exp2(cap_value * math.log2(math.e) * jnp.tanh(scores * (1.0 / cap_value)))


def columns(index, width=HEAD_SIZE):
    return slice(index * width, (index + 1) * width)


def call(body, out_shape, in_specs, name, scratch=(), out_specs=None, cost=1000):
    return pl.pallas_call(
        body,
        out_shape=out_shape,
        in_specs=in_specs,
        out_specs=jax.tree.map(lambda _: VMEM, out_shape) if out_specs is None else out_specs,
        scratch_shapes=scratch,
        compiler_params=pltpu.CompilerParams(vmem_limit_bytes=VMEM_BYTES),
        cost_estimate=pl.CostEstimate(flops=cost, bytes_accessed=1000, transcendentals=0),
        name=name,
    )


def in_hbm(arrays):
    return [pltpu.with_memory_space_constraint(x, pltpu.HBM) for x in arrays]


def rows_at(index, size):
    return pl.ds(pl.multiple_of(index * size, size), size)


def beside_ones(values):
    return jnp.concatenate([values, jnp.ones(values.shape, bf16)], axis=1)


class Facts:
    def __init__(self, ref, slots, residues, groups):
        self.ref, self.slots, self.residues, self.groups = ref, slots, residues, groups
        self.size = 2 * slots + residues + groups

    def block(self, slot, half):
        return self.ref[0, 2 * slot + half]

    def rank(self, residue):
        return self.ref[0, 2 * self.slots + residue]

    def owner(self, prompt):
        return self.ref[0, 2 * self.slots + self.residues + prompt]

    def store(self, map_ref, rank_ref, owner_ref):
        for slot in range(self.slots):
            for half in range(2):
                self.ref[0, 2 * slot + half] = map_ref[0, slot, half]
        for residue in range(self.residues):
            self.ref[0, 2 * self.slots + residue] = rank_ref[0, residue]
        for prompt in range(self.groups):
            self.ref[0, 2 * self.slots + self.residues + prompt] = owner_ref[prompt]

    def halves(self, slot):
        high = jnp.where(self.block(slot, 1) > self.block(slot, 0), 1, 0)
        return 1 - high, high


def slot_and_head_group():
    member = lax.axis_index("blk")
    return member // HEAD_DIVISIONS, member % HEAD_DIVISIONS


def prepare(queries, keys, values, table, decode_rank, owner, tables):
    rows, width = keys.shape
    block_len = rows // 2
    slots = table.shape[1]
    residues = decode_rank.shape[1]
    first = block_len // slots
    arrays = (queries, keys, values, *tables, table, decode_rank, owner)
    count = len(arrays)
    facts_of = lambda ref: Facts(ref, slots, residues, owner.shape[0])

    def body(*refs):
        inputs, refs = refs[:count], refs[count:]
        facts_ref, q_ref, v_ref, kr_ref, angle_ref = refs[:5]
        sent_refs, refs = refs[5 : 4 + slots], refs[4 + slots :]
        k_ref, row_ref, blk_ref, map_ref, rank_ref, owner_ref, sems = refs
        targets = (q_ref, k_ref, v_ref, row_ref, blk_ref, map_ref, rank_ref, owner_ref)
        copies = []
        for index in (1, 3, 4, 5, 6, 7, 2, 0):
            copies.append(pltpu.make_async_copy(inputs[index], targets[index], sems.at[index]))
            copies[-1].start()
        slot, head_group = slot_and_head_group()
        for copy in copies[:6]:
            copy.wait()
        facts = facts_of(facts_ref)
        facts.store(map_ref, rank_ref, owner_ref)
        for half in range(2):
            part = columns(half, block_len)
            angles = block_angles(row_ref, blk_ref, map_ref[0, slot, half])
            angle_ref[half, 0] = angles[0]
            angle_ref[half, 1] = angles[1]
            for head in range(KV_DEV):
                kr_ref[part, columns(head)] = turned(k_ref[part, columns(head)], angles).astype(bf16)
        copies[6].wait()
        for turn in range(1, slots):
            order = order_matrix(
                lambda r: rank_ref[0, r],
                (slot + turn) % slots,
                head_group,
                0,
                first,
                block_len,
                residues,
            )
            for kind, source in enumerate((kr_ref, v_ref)):
                for half in range(2):
                    sent_refs[turn - 1][columns(2 * kind + half, first)] = dot(
                        order, source[columns(half, block_len)]
                    ).astype(bf16)
        copies[7].wait()

    shapes = [
        jax.ShapeDtypeStruct((1, facts_of(None).size), jnp.int32),
        jax.ShapeDtypeStruct(queries.shape, bf16),
        jax.ShapeDtypeStruct(values.shape, bf16),
        jax.ShapeDtypeStruct(keys.shape, bf16),
        jax.ShapeDtypeStruct((2, 2, block_len, HEAD_SIZE), f32),
    ]
    shapes += [jax.ShapeDtypeStruct((4 * first, width), bf16) for _ in range(1, slots)]
    scratch = [pltpu.VMEM(x.shape, x.dtype) for x in (keys, *tables)]
    scratch += [pltpu.SMEM(x.shape, x.dtype) for x in (table, decode_rank, owner)]
    scratch.append(pltpu.SemaphoreType.DMA((count,)))
    outs = call(
        body,
        shapes,
        [HBM] * count,
        "prepare",
        scratch,
        out_specs=[SMEM] + [VMEM] * (len(shapes) - 1),
    )(*in_hbm(arrays))
    return outs[0], outs[1:5], outs[5:], facts_of


def own_part(facts_row, facts_of, operands):
    queries, values, key_rot, _ = operands
    rows, width = key_rot.shape
    block_len = rows // 2
    sizes = facts_of(None)
    slots, residues, groups = sizes.slots, sizes.residues, sizes.groups
    first = block_len // slots
    run = block_len // residues
    cache_rows = 2 * slots * run

    def body(facts_ref, q_ref, v_ref, kr_ref, angle_ref, *refs):
        qr_ref, acc_ref, place_ref, owned_ref, row_at_ref, cache_at_ref = refs[:6]
        e_refs = refs[6:]
        facts = facts_of(facts_ref)
        slot, head_group = slot_and_head_group()
        group = lax.axis_index("req")
        order = order_matrix(facts.rank, slot, head_group, 0, first, block_len, residues)
        for kind, source in enumerate((kr_ref, v_ref)):
            chosen = [dot(order, source[columns(half, block_len)]) for half in range(2)]
            for m in range(HEAD_DIVISIONS):
                lines = jnp.concatenate([part[columns(m, run)] for part in chosen], axis=0)
                e_refs[m][columns(kind, 2 * run)] = lines.astype(bf16)

        for half in range(2):
            part = columns(half, block_len)
            angles = angle_ref[half, 0], angle_ref[half, 1]
            for head in range(Q_DEV):
                qr_ref[part, columns(head)] = (
                    turned(q_ref[part, columns(head)], angles) * query_scale
                ).astype(bf16)
        low, high = facts.halves(slot)
        low, high = rows_at(low, block_len), rows_at(high, block_len)
        row = lax.broadcasted_iota(jnp.int32, (block_len, block_len), 0)
        col = lax.broadcasted_iota(jnp.int32, (block_len, block_len), 1)
        for head in range(Q_DEV):
            key_head = columns(head * KV_DEV // Q_DEV)
            both = columns(head, 2 * HEAD_SIZE)

            def tile(q_part, k_part, diagonal):
                expo = expo_of(dot_t(qr_ref[q_part, columns(head)], kr_ref[k_part, key_head]))
                if diagonal:
                    expo = jnp.where(col <= row, expo, 0.0)
                return dot(expo.astype(bf16), beside_ones(v_ref[k_part, key_head]))

            acc_ref[low, both] = tile(low, low, True)
            acc_ref[high, both] = tile(high, high, True) + tile(high, low, False)

        col = lax.broadcasted_iota(jnp.int32, (1, cache_rows), 1)
        part, offset = col // run, col % run
        target = jnp.zeros_like(col)
        for turn in range(slots):
            for half in range(2):
                block = facts.block((slot - turn + slots) % slots, half)
                target = jnp.where(part == 2 * turn + half, block * run + offset, target)
        row = lax.broadcasted_iota(jnp.int32, (cache_rows, cache_rows), 0)
        place_ref[...] = jnp.where(row == target, 1.0, 0.0).astype(bf16)
        residue = 0
        for r in range(1, residues):
            residue = jnp.where(facts.rank(r) == lax.axis_index("blk"), r, residue)
        cache_at_ref[...] = (row * residues + residue).astype(f32)
        for half in range(2):
            offset = lax.broadcasted_iota(jnp.int32, (block_len, HEAD_SIZE), 0)
            at = facts.block(slot, half) * block_len + offset
            row_at_ref[columns(half, block_len)] = at.astype(f32)
        for turn in range(groups):
            mine = facts.owner(lax.rem(group - turn + groups, groups)) == group
            owned_ref[turn : turn + 1] = jnp.full((1, HEAD_SIZE), jnp.where(mine, 1.0, 0.0), f32)

    shapes = [
        jax.ShapeDtypeStruct(queries.shape, bf16),
        jax.ShapeDtypeStruct((rows, 2 * Q_DEV * HEAD_SIZE), f32),
        jax.ShapeDtypeStruct((cache_rows, cache_rows), bf16),
        jax.ShapeDtypeStruct((groups, HEAD_SIZE), f32),
        jax.ShapeDtypeStruct((rows, HEAD_SIZE), f32),
        jax.ShapeDtypeStruct((cache_rows, cache_rows), f32),
    ]
    shapes += [jax.ShapeDtypeStruct((4 * run, width), bf16) for _ in range(HEAD_DIVISIONS)]
    outs = call(body, shapes, [SMEM] + [VMEM] * 4, "own_part")(facts_row, *operands)
    return outs[0], outs[1], outs[2:6], outs[6:]


def second_part(facts_row, facts_of, lens, key_rot, values, after):
    rows, width = key_rot.shape
    block_len = rows // 2
    sizes = facts_of(None)
    slots, residues = sizes.slots, sizes.residues
    first = block_len // slots
    rest = block_len - first
    rounds = len(lens)

    def body(facts_ref, *refs):
        len_refs, refs = refs[:rounds], refs[rounds:]
        kr_ref, v_ref, refs = refs[0], refs[1], refs[2 + len(after) :]
        carried_ref, sent_refs = refs[0], refs[1:]
        facts = facts_of(facts_ref)
        slot, head_group = slot_and_head_group()
        for turn in range(1, slots):
            order = order_matrix(
                facts.rank, (slot + turn) % slots, head_group, first, rest, block_len, residues
            )
            for kind, source in enumerate((kr_ref, v_ref)):
                for half in range(2):
                    sent_refs[turn - 1][columns(2 * kind + half, rest)] = dot(
                        order, source[columns(half, block_len)]
                    ).astype(bf16)
        line = lax.broadcasted_iota(jnp.int32, (CARRIED, width), 0)
        carried = jnp.zeros((CARRIED, width), jnp.int32)
        for index in range(rounds):
            length = len_refs[index][0]
            carried = jnp.where(line == 2 * index, lax.shift_right_logical(length, 6), carried)
            carried = jnp.where(line == 2 * index + 1, length & 63, carried)
        carried_ref[...] = carried.astype(f32).astype(bf16)

    shapes = [jax.ShapeDtypeStruct((CARRIED, width), bf16)]
    shapes += [jax.ShapeDtypeStruct((4 * rest, width), bf16) for _ in range(1, slots)]
    specs = [SMEM] * (1 + rounds) + [VMEM] * (2 + len(after))
    outs = call(body, shapes, specs, "second_part")(facts_row, *lens, key_rot, values, *after)
    return outs[0], outs[1:]


def late_pieces(arrived, carried):
    others = len(arrived)
    width = arrived[0].shape[1]
    first = arrived[0].shape[0] // 4
    run = first // HEAD_DIVISIONS

    def body(carried_ref, *refs):
        in_refs, e_refs = refs[:others], refs[others:]
        for m in range(HEAD_DIVISIONS):
            for kind in range(2):
                for index in range(others):
                    place = (kind * others + index) * 2
                    if run % 16 == 0:
                        for half in range(2):
                            start = (2 * kind + half) * first + m * run
                            e_refs[m][columns(place + half, run)] = in_refs[index][start : start + run]
                        continue
                    lines = [
                        in_refs[index][columns(2 * kind + half, first)].astype(f32)[columns(m, run)]
                        for half in range(2)
                    ]
                    e_refs[m][place * run : (place + 2) * run] = jnp.concatenate(
                        lines, axis=0
                    ).astype(bf16)
            e_refs[m][4 * others * run :] = carried_ref[...]

    shapes = [
        jax.ShapeDtypeStruct((4 * others * run + CARRIED, width), bf16)
        for _ in range(HEAD_DIVISIONS)
    ]
    return call(body, shapes, [VMEM] * (1 + others), "late_pieces")(carried, *arrived)


def attend(facts_row, facts_of, query_rot, acc, arrived, live=None):
    rows = query_rot.shape[0]
    block_len = rows // 2
    others = len(arrived)
    size = arrived[0].shape[0] // 4
    sizes = facts_of(None)
    slots = sizes.slots
    last = live is not None

    def body(facts_ref, q_ref, acc_ref, *refs):
        in_refs, out_ref = refs[:others], refs[-1]
        facts = facts_of(facts_ref)
        slot = slot_and_head_group()[0]
        low, high = facts.halves(slot)
        low_rows, high_rows = rows_at(low, block_len), rows_at(high, block_len)
        for head in range(Q_DEV):
            key_head = columns(head * KV_DEV // Q_DEV)
            both = columns(head, 2 * HEAD_SIZE)
            low_sum, high_sum = acc_ref[low_rows, both], acc_ref[high_rows, both]
            for turn in range(1, slots):
                in_ref = in_refs[turn - 1]
                source = (slot - turn + slots) % slots
                source_low, source_high = facts.halves(source)
                outer = facts.block(slot, low) < facts.block(source, source_low)

                def tile(half, other):
                    queries = q_ref[rows_at(half, block_len), columns(head)]
                    expo = expo_of(dot_t(queries, in_ref[rows_at(other, size), key_head]))
                    values = in_ref[rows_at(2 + other, size), key_head]
                    return dot(expo.astype(bf16), beside_ones(values))

                either = tile(jnp.where(outer, high, low), source_low)
                upper = tile(high, jnp.where(outer, source_high, source_low))
                low_sum = low_sum + jnp.where(outer, 0.0, either)
                high_sum = high_sum + upper + jnp.where(outer, either, 0.0)
            for part, total in ((low_rows, low_sum), (high_rows, high_sum)):
                if last:
                    scale = refs[others][part] / total[:, HEAD_SIZE:]
                    out_ref[part, columns(head)] = (total[:, :HEAD_SIZE] * scale).astype(bf16)
                else:
                    out_ref[part, both] = total

    if last:
        shape, name = jax.ShapeDtypeStruct(query_rot.shape, bf16), "attend_rest"
        extra = (live,)
    else:
        shape, name = jax.ShapeDtypeStruct(acc.shape, f32), "attend_first"
        extra = ()
    specs = [SMEM] + [VMEM] * (2 + others + len(extra))
    cost = 1000 if last else 10**10
    return call(body, shape, specs, name, cost=cost)(facts_row, query_rot, acc, *arrived, *extra)


def cache_part(early, late, masks):
    place, owned, row_at, cache_at = masks
    cache_rows = place.shape[0]
    piece = early[0].shape[0] // 2
    width = early[0].shape[1]
    groups = owned.shape[0]

    def body(place_ref, owned_ref, row_at_ref, cache_at_ref, *refs):
        f_refs, s_refs, out_ref, live_ref = refs[:4], refs[4:8], refs[8], refs[9]
        head_group = slot_and_head_group()[1]
        later = cache_rows - piece
        length = jnp.zeros((1, HEAD_SIZE), f32)
        for m in range(HEAD_DIVISIONS):
            carried = s_refs[m][2 * later :, :HEAD_SIZE].astype(f32)
            for index in range(groups // HEAD_DIVISIONS):
                turn = (head_group ^ m) + HEAD_DIVISIONS * index
                value = carried[2 * index : 2 * index + 1] * 64.0 + carried[2 * index + 1 : 2 * index + 2]
                length = length + owned_ref[pl.ds(turn, 1)] * value
        live_ref[...] = jnp.where(row_at_ref[...] < length, 1.0, 0.0)
        kept = jnp.where(cache_at_ref[...] < length[:, :1], place_ref[...].astype(f32), 0.0)
        kept = kept.astype(bf16)
        for m in range(HEAD_DIVISIONS):
            for kind in range(2):
                lines = jnp.concatenate(
                    [f_refs[m][columns(kind, piece)], s_refs[m][columns(kind, later)]], axis=0
                )
                column = ((head_group ^ m) + kind * HEAD_DIVISIONS) * width
                out_ref[:, pl.ds(pl.multiple_of(column, HEAD_SIZE), width)] = dot(kept, lines).astype(
                    bf16
                )

    shapes = [
        jax.ShapeDtypeStruct((cache_rows, 2 * HEAD_DIVISIONS * width), bf16),
        jax.ShapeDtypeStruct(row_at.shape, f32),
    ]
    return call(body, shapes, [VMEM] * 12, "cache_part")(*masks, *early, *late)


def on_device(queries, keys, values, block_map, lengths, group_of_prompt, decode_rank):
    block_len = queries.shape[2] // 2
    slots = block_map.shape[1]
    q, k, v = queries[0, 0], keys[0, 0], values[0, 0]
    tables = rotary_tables(block_len, 2 * slots)

    def to_slots(parts):
        return [shifted(parts[t - 1], "blk", HEAD_DIVISIONS * t) for t in range(1, slots)]

    def hand_on(pieces):
        return [pieces[0]] + [crossed(pieces[m], "blk", m) for m in range(1, HEAD_DIVISIONS)]

    lens = [spread(lengths, t) for t in range(lax.axis_size("req") // HEAD_DIVISIONS)]
    facts_row, operands, sent, facts_of = prepare(
        q, k, v, block_map, decode_rank, group_of_prompt, tables
    )
    first = to_slots(sent)
    query_rot, acc, masks, early = own_part(facts_row, facts_of, operands)
    early = hand_on(early)
    carried, sent = second_part(facts_row, facts_of, lens, operands[2], operands[1], early[1:])
    rest = to_slots(sent)
    late = hand_on(late_pieces(first, carried))
    acc = attend(facts_row, facts_of, query_rot, acc, first)
    cache, live = cache_part(early, late, masks)
    attended = attend(facts_row, facts_of, query_rot, acc, rest, live)
    return (attended[None, None], cache[None])


def solution(mesh):
    placed = (
        P("req", "blk", None, None),
        P("req", "blk", None, None),
        P("req", "blk", None, None),
        P("req", None, None),
        P("req"),
        P(),
        P("req", None),
    )
    return jax.shard_map(
        on_device,
        mesh=mesh,
        in_specs=placed,
        out_specs=(P("req", "blk", None, None), P("req", "blk", None)),
        check_vma=False,
    )
```

```python
import math

import jax
import jax.numpy as jnp
import numpy as np
from jax import lax
from jax.experimental import pallas as pl
from jax.experimental.pallas import tpu as pltpu
from jax.sharding import PartitionSpec as P

QUERY_HEADS = 16
KEY_VALUE_HEADS = 8
HEAD_SIZE = 128
HEAD_DIVISIONS = 4
Q_DEV = 4
KV_DEV = 2
KV_WIDTH = KV_DEV * HEAD_SIZE

cap_value = 50.0
query_scale = 1.0 / 12.0
rope_base = 10000.0
CARRIED = 16
VMEM_BYTES = 48 * 1024 * 1024

f32 = jnp.float32
bf16 = jnp.bfloat16
SMEM = pl.BlockSpec(memory_space=pltpu.SMEM)
VMEM = pl.BlockSpec(memory_space=pltpu.VMEM)
HBM = pl.BlockSpec(memory_space=pltpu.HBM)


def shifted(shard, axis, by):
    peers = lax.axis_size(axis)
    return lax.ppermute(shard, axis, [(i, (i + by) % peers) for i in range(peers)])


def crossed(shard, axis, by):
    peers = lax.axis_size(axis)
    return lax.ppermute(shard, axis, [(i, i ^ by) for i in range(peers)])


def spread(shard, turn):
    groups, members = lax.axis_size("req"), lax.axis_size("blk")
    pairs = []
    for group in range(groups):
        for member in range(members):
            target = group + member % HEAD_DIVISIONS + HEAD_DIVISIONS * turn
            pairs.append((group * members + member, target % groups * members + member))
    return lax.ppermute(shard, ("req", "blk"), pairs)


def rotary_tables(block_len, block_count):
    half = HEAD_SIZE // 2
    frequency = np.exp(
        np.float32(-math.log(rope_base)) * (2.0 * np.arange(half, dtype=np.float32)) / HEAD_SIZE
    ).astype(np.float64)

    def table(positions):
        angles = positions.astype(np.float64)[:, None] * frequency[None, :]
        cosine, sine = np.cos(angles), np.sin(angles)
        return np.stack(
            [np.concatenate([cosine, cosine], 1), np.concatenate([-sine, sine], 1)]
        ).astype(np.float32)

    return table(np.arange(block_len)), table(np.arange(block_count) * block_len)


def block_angles(row_table, block_table, block):
    row_cos, row_sin = row_table[0], row_table[1]
    blk_cos, blk_sin = block_table[0, pl.ds(block, 1)], block_table[1, pl.ds(block, 1)]
    return row_cos * blk_cos - row_sin * blk_sin, row_sin * blk_cos + row_cos * blk_sin


def turned(head, angles):
    x = head.astype(f32)
    return x * angles[0] + pltpu.roll(x, HEAD_SIZE // 2, 1) * angles[1]


def order_matrix(rank_of, slot, head_group, first_row, out_rows, rows, residues):
    row_ids = lax.broadcasted_iota(jnp.int32, (1, rows), 1)
    residue = row_ids % residues
    rank = jnp.zeros_like(row_ids)
    for r in range(residues):
        rank = jnp.where(residue == r, rank_of(r), rank)
    ahead = (rank - HEAD_DIVISIONS * slot + residues) % residues
    ahead = jnp.where(ahead < HEAD_DIVISIONS, ahead ^ head_group, ahead)
    index = ahead * (rows // residues) + row_ids // residues
    out_ids = first_row + lax.broadcasted_iota(jnp.int32, (out_rows, rows), 0)
    return jnp.where(out_ids == index, 1.0, 0.0).astype(bf16)


def dot(a, b):
    return jnp.dot(a, b, preferred_element_type=f32)


def dot_t(a, b):
    return lax.dot_general(a, b, (((1,), (1,)), ((), ())), preferred_element_type=f32)


def expo_of(scores):
    return jnp.exp2(cap_value * math.log2(math.e) * jnp.tanh(scores * (1.0 / cap_value)))


def columns(index, width=HEAD_SIZE):
    return slice(index * width, (index + 1) * width)


def call(body, out_shape, in_specs, name, scratch=(), out_specs=None, cost=1000):
    return pl.pallas_call(
        body,
        out_shape=out_shape,
        in_specs=in_specs,
        out_specs=jax.tree.map(lambda _: VMEM, out_shape) if out_specs is None else out_specs,
        scratch_shapes=scratch,
        compiler_params=pltpu.CompilerParams(vmem_limit_bytes=VMEM_BYTES),
        cost_estimate=pl.CostEstimate(flops=cost, bytes_accessed=1000, transcendentals=0),
        name=name,
    )


def in_hbm(arrays):
    return [pltpu.with_memory_space_constraint(x, pltpu.HBM) for x in arrays]


def rows_at(index, size):
    return pl.ds(pl.multiple_of(index * size, size), size)


def beside_ones(values):
    return jnp.concatenate([values, jnp.ones(values.shape, bf16)], axis=1)


class Facts:
    def __init__(self, ref, slots, residues, groups):
        self.ref, self.slots, self.residues, self.groups = ref, slots, residues, groups
        self.size = 2 * slots + residues + groups

    def block(self, slot, half):
        return self.ref[0, 2 * slot + half]

    def rank(self, residue):
        return self.ref[0, 2 * self.slots + residue]

    def owner(self, prompt):
        return self.ref[0, 2 * self.slots + self.residues + prompt]

    def store(self, map_ref, rank_ref, owner_ref):
        for slot in range(self.slots):
            for half in range(2):
                self.ref[0, 2 * slot + half] = map_ref[0, slot, half]
        for residue in range(self.residues):
            self.ref[0, 2 * self.slots + residue] = rank_ref[0, residue]
        for prompt in range(self.groups):
            self.ref[0, 2 * self.slots + self.residues + prompt] = owner_ref[prompt]

    def halves(self, slot):
        high = jnp.where(self.block(slot, 1) > self.block(slot, 0), 1, 0)
        return 1 - high, high


def slot_and_head_group():
    member = lax.axis_index("blk")
    return member // HEAD_DIVISIONS, member % HEAD_DIVISIONS


def prepare(queries, keys, values, table, decode_rank, owner, tables):
    rows, width = keys.shape
    block_len = rows // 2
    slots = table.shape[1]
    residues = decode_rank.shape[1]
    first = block_len // slots
    arrays = (queries, keys, values, *tables, table, decode_rank, owner)
    count = len(arrays)
    facts_of = lambda ref: Facts(ref, slots, residues, owner.shape[0])

    def body(*refs):
        inputs, refs = refs[:count], refs[count:]
        facts_ref, q_ref, v_ref, kr_ref, angle_ref = refs[:5]
        sent_refs, refs = refs[5 : 4 + slots], refs[4 + slots :]
        k_ref, row_ref, blk_ref, map_ref, rank_ref, owner_ref, sems = refs
        targets = (q_ref, k_ref, v_ref, row_ref, blk_ref, map_ref, rank_ref, owner_ref)
        copies = []
        for index in (1, 3, 4, 5, 6, 7, 2, 0):
            copies.append(pltpu.make_async_copy(inputs[index], targets[index], sems.at[index]))
            copies[-1].start()
        slot, head_group = slot_and_head_group()
        for copy in copies[:6]:
            copy.wait()
        facts = facts_of(facts_ref)
        facts.store(map_ref, rank_ref, owner_ref)
        for half in range(2):
            part = columns(half, block_len)
            angles = block_angles(row_ref, blk_ref, map_ref[0, slot, half])
            angle_ref[half, 0] = angles[0]
            angle_ref[half, 1] = angles[1]
            for head in range(KV_DEV):
                kr_ref[part, columns(head)] = turned(k_ref[part, columns(head)], angles).astype(bf16)
        copies[6].wait()
        for turn in range(1, slots):
            order = order_matrix(
                lambda r: rank_ref[0, r],
                (slot + turn) % slots,
                head_group,
                0,
                first,
                block_len,
                residues,
            )
            for kind, source in enumerate((kr_ref, v_ref)):
                for half in range(2):
                    sent_refs[turn - 1][columns(2 * kind + half, first)] = dot(
                        order, source[columns(half, block_len)]
                    ).astype(bf16)
        copies[7].wait()

    shapes = [
        jax.ShapeDtypeStruct((1, facts_of(None).size), jnp.int32),
        jax.ShapeDtypeStruct(queries.shape, bf16),
        jax.ShapeDtypeStruct(values.shape, bf16),
        jax.ShapeDtypeStruct(keys.shape, bf16),
        jax.ShapeDtypeStruct((2, 2, block_len, HEAD_SIZE), f32),
    ]
    shapes += [jax.ShapeDtypeStruct((4 * first, width), bf16) for _ in range(1, slots)]
    scratch = [pltpu.VMEM(x.shape, x.dtype) for x in (keys, *tables)]
    scratch += [pltpu.SMEM(x.shape, x.dtype) for x in (table, decode_rank, owner)]
    scratch.append(pltpu.SemaphoreType.DMA((count,)))
    outs = call(
        body,
        shapes,
        [HBM] * count,
        "prepare",
        scratch,
        out_specs=[SMEM] + [VMEM] * (len(shapes) - 1),
    )(*in_hbm(arrays))
    return outs[0], outs[1:5], outs[5:], facts_of


def own_part(facts_row, facts_of, operands):
    queries, values, key_rot, _ = operands
    rows, width = key_rot.shape
    block_len = rows // 2
    sizes = facts_of(None)
    slots, residues, groups = sizes.slots, sizes.residues, sizes.groups
    first = block_len // slots
    run = block_len // residues
    cache_rows = 2 * slots * run

    def body(facts_ref, q_ref, v_ref, kr_ref, angle_ref, *refs):
        qr_ref, acc_ref, place_ref, owned_ref, row_at_ref, cache_at_ref = refs[:6]
        e_refs = refs[6:]
        facts = facts_of(facts_ref)
        slot, head_group = slot_and_head_group()
        group = lax.axis_index("req")
        order = order_matrix(facts.rank, slot, head_group, 0, first, block_len, residues)
        for kind, source in enumerate((kr_ref, v_ref)):
            chosen = [dot(order, source[columns(half, block_len)]) for half in range(2)]
            for m in range(HEAD_DIVISIONS):
                lines = jnp.concatenate([part[columns(m, run)] for part in chosen], axis=0)
                e_refs[m][columns(kind, 2 * run)] = lines.astype(bf16)

        for half in range(2):
            part = columns(half, block_len)
            angles = angle_ref[half, 0], angle_ref[half, 1]
            for head in range(Q_DEV):
                qr_ref[part, columns(head)] = (
                    turned(q_ref[part, columns(head)], angles) * query_scale
                ).astype(bf16)
        low, high = facts.halves(slot)
        low, high = rows_at(low, block_len), rows_at(high, block_len)
        row = lax.broadcasted_iota(jnp.int32, (block_len, block_len), 0)
        col = lax.broadcasted_iota(jnp.int32, (block_len, block_len), 1)
        for head in range(Q_DEV):
            key_head = columns(head * KV_DEV // Q_DEV)
            both = columns(head, 2 * HEAD_SIZE)

            def tile(q_part, k_part, diagonal):
                expo = expo_of(dot_t(qr_ref[q_part, columns(head)], kr_ref[k_part, key_head]))
                if diagonal:
                    expo = jnp.where(col <= row, expo, 0.0)
                return dot(expo.astype(bf16), beside_ones(v_ref[k_part, key_head]))

            acc_ref[low, both] = tile(low, low, True)
            acc_ref[high, both] = tile(high, high, True) + tile(high, low, False)

        col = lax.broadcasted_iota(jnp.int32, (1, cache_rows), 1)
        part, offset = col // run, col % run
        target = jnp.zeros_like(col)
        for turn in range(slots):
            for half in range(2):
                block = facts.block((slot - turn + slots) % slots, half)
                target = jnp.where(part == 2 * turn + half, block * run + offset, target)
        row = lax.broadcasted_iota(jnp.int32, (cache_rows, cache_rows), 0)
        place_ref[...] = jnp.where(row == target, 1.0, 0.0).astype(bf16)
        residue = 0
        for r in range(1, residues):
            residue = jnp.where(facts.rank(r) == lax.axis_index("blk"), r, residue)
        cache_at_ref[...] = (row * residues + residue).astype(f32)
        for half in range(2):
            offset = lax.broadcasted_iota(jnp.int32, (block_len, HEAD_SIZE), 0)
            at = facts.block(slot, half) * block_len + offset
            row_at_ref[columns(half, block_len)] = at.astype(f32)
        for turn in range(groups):
            mine = facts.owner(lax.rem(group - turn + groups, groups)) == group
            owned_ref[turn : turn + 1] = jnp.full((1, HEAD_SIZE), jnp.where(mine, 1.0, 0.0), f32)

    shapes = [
        jax.ShapeDtypeStruct(queries.shape, bf16),
        jax.ShapeDtypeStruct((rows, 2 * Q_DEV * HEAD_SIZE), f32),
        jax.ShapeDtypeStruct((cache_rows, cache_rows), bf16),
        jax.ShapeDtypeStruct((groups, HEAD_SIZE), f32),
        jax.ShapeDtypeStruct((rows, HEAD_SIZE), f32),
        jax.ShapeDtypeStruct((cache_rows, cache_rows), f32),
    ]
    shapes += [jax.ShapeDtypeStruct((4 * run, width), bf16) for _ in range(HEAD_DIVISIONS)]
    outs = call(body, shapes, [SMEM] + [VMEM] * 4, "own_part")(facts_row, *operands)
    return outs[0], outs[1], outs[2:6], outs[6:]


def second_part(facts_row, facts_of, lens, key_rot, values):
    rows, width = key_rot.shape
    block_len = rows // 2
    sizes = facts_of(None)
    slots, residues = sizes.slots, sizes.residues
    first = block_len // slots
    rest = block_len - first
    rounds = len(lens)

    def body(facts_ref, *refs):
        len_refs, refs = refs[:rounds], refs[rounds:]
        kr_ref, v_ref, carried_ref, sent_refs = refs[0], refs[1], refs[2], refs[3:]
        facts = facts_of(facts_ref)
        slot, head_group = slot_and_head_group()
        for turn in range(1, slots):
            order = order_matrix(
                facts.rank, (slot + turn) % slots, head_group, first, rest, block_len, residues
            )
            for kind, source in enumerate((kr_ref, v_ref)):
                for half in range(2):
                    sent_refs[turn - 1][columns(2 * kind + half, rest)] = dot(
                        order, source[columns(half, block_len)]
                    ).astype(bf16)
        line = lax.broadcasted_iota(jnp.int32, (CARRIED, width), 0)
        carried = jnp.zeros((CARRIED, width), jnp.int32)
        for index in range(rounds):
            length = len_refs[index][0]
            carried = jnp.where(line == 2 * index, lax.shift_right_logical(length, 6), carried)
            carried = jnp.where(line == 2 * index + 1, length & 63, carried)
        carried_ref[...] = carried.astype(f32).astype(bf16)

    shapes = [jax.ShapeDtypeStruct((CARRIED, width), bf16)]
    shapes += [jax.ShapeDtypeStruct((4 * rest, width), bf16) for _ in range(1, slots)]
    specs = [SMEM] * (1 + rounds) + [VMEM] * 2
    outs = call(body, shapes, specs, "second_part")(facts_row, *lens, key_rot, values)
    return outs[0], outs[1:]


def late_pieces(arrived, carried, payload):
    others = len(arrived)
    width = arrived[0].shape[1]
    first = arrived[0].shape[0] // 4
    run = first // HEAD_DIVISIONS

    def body(carried_ref, *refs):
        in_refs, pay_refs, refs = refs[:others], refs[others : 2 * others], refs[2 * others :]
        e_refs, out_refs = refs[:HEAD_DIVISIONS], refs[HEAD_DIVISIONS:]
        for pay_ref, out_ref in zip(pay_refs, out_refs):
            out_ref[...] = pay_ref[...]
        for m in range(HEAD_DIVISIONS):
            for kind in range(2):
                for index in range(others):
                    place = (kind * others + index) * 2
                    if run % 16 == 0:
                        for half in range(2):
                            start = (2 * kind + half) * first + m * run
                            e_refs[m][columns(place + half, run)] = in_refs[index][start : start + run]
                        continue
                    lines = [
                        in_refs[index][columns(2 * kind + half, first)].astype(f32)[columns(m, run)]
                        for half in range(2)
                    ]
                    e_refs[m][place * run : (place + 2) * run] = jnp.concatenate(
                        lines, axis=0
                    ).astype(bf16)
            e_refs[m][4 * others * run :] = carried_ref[...]

    shapes = [
        jax.ShapeDtypeStruct((4 * others * run + CARRIED, width), bf16)
        for _ in range(HEAD_DIVISIONS)
    ]
    shapes += [jax.ShapeDtypeStruct(x.shape, bf16) for x in payload]
    outs = call(body, shapes, [VMEM] * (1 + 2 * others), "late_pieces")(carried, *arrived, *payload)
    return outs[:HEAD_DIVISIONS], outs[HEAD_DIVISIONS:]


def attend(facts_row, facts_of, query_rot, acc, arrived, live=None):
    rows = query_rot.shape[0]
    block_len = rows // 2
    others = len(arrived)
    size = arrived[0].shape[0] // 4
    sizes = facts_of(None)
    slots = sizes.slots
    last = live is not None

    def body(facts_ref, q_ref, acc_ref, *refs):
        in_refs, out_ref = refs[:others], refs[-1]
        facts = facts_of(facts_ref)
        slot = slot_and_head_group()[0]
        low, high = facts.halves(slot)
        low_rows, high_rows = rows_at(low, block_len), rows_at(high, block_len)
        for head in range(Q_DEV):
            key_head = columns(head * KV_DEV // Q_DEV)
            both = columns(head, 2 * HEAD_SIZE)
            low_sum, high_sum = acc_ref[low_rows, both], acc_ref[high_rows, both]
            for turn in range(1, slots):
                in_ref = in_refs[turn - 1]
                source = (slot - turn + slots) % slots
                source_low, source_high = facts.halves(source)
                outer = facts.block(slot, low) < facts.block(source, source_low)

                def tile(half, other):
                    queries = q_ref[rows_at(half, block_len), columns(head)]
                    expo = expo_of(dot_t(queries, in_ref[rows_at(other, size), key_head]))
                    values = in_ref[rows_at(2 + other, size), key_head]
                    return dot(expo.astype(bf16), beside_ones(values))

                either = tile(jnp.where(outer, high, low), source_low)
                upper = tile(high, jnp.where(outer, source_high, source_low))
                low_sum = low_sum + jnp.where(outer, 0.0, either)
                high_sum = high_sum + upper + jnp.where(outer, either, 0.0)
            for part, total in ((low_rows, low_sum), (high_rows, high_sum)):
                if last:
                    scale = refs[others][part] / total[:, HEAD_SIZE:]
                    out_ref[part, columns(head)] = (total[:, :HEAD_SIZE] * scale).astype(bf16)
                else:
                    out_ref[part, both] = total

    if last:
        shape, name = jax.ShapeDtypeStruct(query_rot.shape, bf16), "attend_rest"
        extra = (live,)
    else:
        shape, name = jax.ShapeDtypeStruct(acc.shape, f32), "attend_first"
        extra = ()
    specs = [SMEM] + [VMEM] * (2 + others + len(extra))
    cost = 1000 if last else 10**10
    return call(body, shape, specs, name, cost=cost)(facts_row, query_rot, acc, *arrived, *extra)


def cache_part(early, late, masks):
    place, owned, row_at, cache_at = masks
    cache_rows = place.shape[0]
    piece = early[0].shape[0] // 2
    width = early[0].shape[1]
    groups = owned.shape[0]

    def body(place_ref, owned_ref, row_at_ref, cache_at_ref, *refs):
        f_refs, s_refs, out_ref, live_ref = refs[:4], refs[4:8], refs[8], refs[9]
        head_group = slot_and_head_group()[1]
        later = cache_rows - piece
        length = jnp.zeros((1, HEAD_SIZE), f32)
        for m in range(HEAD_DIVISIONS):
            carried = s_refs[m][2 * later :, :HEAD_SIZE].astype(f32)
            for index in range(groups // HEAD_DIVISIONS):
                turn = (head_group ^ m) + HEAD_DIVISIONS * index
                value = carried[2 * index : 2 * index + 1] * 64.0 + carried[2 * index + 1 : 2 * index + 2]
                length = length + owned_ref[pl.ds(turn, 1)] * value
        live_ref[...] = jnp.where(row_at_ref[...] < length, 1.0, 0.0)
        kept = jnp.where(cache_at_ref[...] < length[:, :1], place_ref[...].astype(f32), 0.0)
        kept = kept.astype(bf16)
        for m in range(HEAD_DIVISIONS):
            for kind in range(2):
                lines = jnp.concatenate(
                    [f_refs[m][columns(kind, piece)], s_refs[m][columns(kind, later)]], axis=0
                )
                column = ((head_group ^ m) + kind * HEAD_DIVISIONS) * width
                out_ref[:, pl.ds(pl.multiple_of(column, HEAD_SIZE), width)] = dot(kept, lines).astype(
                    bf16
                )

    shapes = [
        jax.ShapeDtypeStruct((cache_rows, 2 * HEAD_DIVISIONS * width), bf16),
        jax.ShapeDtypeStruct(row_at.shape, f32),
    ]
    return call(body, shapes, [VMEM] * 12, "cache_part")(*masks, *early, *late)


def on_device(queries, keys, values, block_map, lengths, group_of_prompt, decode_rank):
    block_len = queries.shape[2] // 2
    slots = block_map.shape[1]
    q, k, v = queries[0, 0], keys[0, 0], values[0, 0]
    tables = rotary_tables(block_len, 2 * slots)

    def to_slots(parts):
        return [shifted(parts[t - 1], "blk", HEAD_DIVISIONS * t) for t in range(1, slots)]

    def hand_on(pieces):
        return [pieces[0]] + [crossed(pieces[m], "blk", m) for m in range(1, HEAD_DIVISIONS)]

    lens = [spread(lengths, t) for t in range(lax.axis_size("req") // HEAD_DIVISIONS)]
    facts_row, operands, sent, facts_of = prepare(
        q, k, v, block_map, decode_rank, group_of_prompt, tables
    )
    first = to_slots(sent)
    query_rot, acc, masks, early = own_part(facts_row, facts_of, operands)
    early = hand_on(early)
    carried, sent = second_part(facts_row, facts_of, lens, operands[2], operands[1])
    late, sent = late_pieces(first, carried, sent)
    late, rest = hand_on(late), to_slots(sent)
    acc = attend(facts_row, facts_of, query_rot, acc, first)
    cache, live = cache_part(early, late, masks)
    attended = attend(facts_row, facts_of, query_rot, acc, rest, live)
    return (attended[None, None], cache[None])


def solution(mesh):
    placed = (
        P("req", "blk", None, None),
        P("req", "blk", None, None),
        P("req", "blk", None, None),
        P("req", None, None),
        P("req"),
        P(),
        P("req", None),
    )
    return jax.shard_map(
        on_device,
        mesh=mesh,
        in_specs=placed,
        out_specs=(P("req", "blk", None, None), P("req", "blk", None)),
        check_vma=False,
    )
```

```python
import math

import jax
import jax.numpy as jnp
import numpy as np
from jax import lax
from jax.experimental import pallas as pl
from jax.experimental.pallas import tpu as pltpu
from jax.sharding import PartitionSpec as P

QUERY_HEADS = 16
KEY_VALUE_HEADS = 8
HEAD_SIZE = 128
HEAD_DIVISIONS = 4
Q_DEV = 4
KV_DEV = 2
KV_WIDTH = KV_DEV * HEAD_SIZE

cap_value = 50.0
query_scale = 1.0 / 12.0
rope_base = 10000.0
CARRIED = 16
VMEM_BYTES = 48 * 1024 * 1024

f32 = jnp.float32
bf16 = jnp.bfloat16
SMEM = pl.BlockSpec(memory_space=pltpu.SMEM)
VMEM = pl.BlockSpec(memory_space=pltpu.VMEM)
HBM = pl.BlockSpec(memory_space=pltpu.HBM)


def shifted(shard, axis, by):
    peers = lax.axis_size(axis)
    return lax.ppermute(shard, axis, [(i, (i + by) % peers) for i in range(peers)])


def crossed(shard, axis, by):
    peers = lax.axis_size(axis)
    return lax.ppermute(shard, axis, [(i, i ^ by) for i in range(peers)])


def spread(shard, turn):
    groups, members = lax.axis_size("req"), lax.axis_size("blk")
    pairs = []
    for group in range(groups):
        for member in range(members):
            target = group + member % HEAD_DIVISIONS + HEAD_DIVISIONS * turn
            pairs.append((group * members + member, target % groups * members + member))
    return lax.ppermute(shard, ("req", "blk"), pairs)


def rotary_tables(block_len, block_count):
    half = HEAD_SIZE // 2
    frequency = np.exp(
        np.float32(-math.log(rope_base)) * (2.0 * np.arange(half, dtype=np.float32)) / HEAD_SIZE
    ).astype(np.float64)

    def table(positions):
        angles = positions.astype(np.float64)[:, None] * frequency[None, :]
        cosine, sine = np.cos(angles), np.sin(angles)
        return np.stack(
            [np.concatenate([cosine, cosine], 1), np.concatenate([-sine, sine], 1)]
        ).astype(np.float32)

    return table(np.arange(block_len)), table(np.arange(block_count) * block_len)


def block_angles(row_table, block_table, block):
    row_cos, row_sin = row_table[0], row_table[1]
    blk_cos, blk_sin = block_table[0, pl.ds(block, 1)], block_table[1, pl.ds(block, 1)]
    return row_cos * blk_cos - row_sin * blk_sin, row_sin * blk_cos + row_cos * blk_sin


def turned(head, angles):
    x = head.astype(f32)
    return x * angles[0] + pltpu.roll(x, HEAD_SIZE // 2, 1) * angles[1]


def order_matrix(rank_of, slot, head_group, first_row, out_rows, rows, residues):
    row_ids = lax.broadcasted_iota(jnp.int32, (1, rows), 1)
    residue = row_ids % residues
    rank = jnp.zeros_like(row_ids)
    for r in range(residues):
        rank = jnp.where(residue == r, rank_of(r), rank)
    ahead = (rank - HEAD_DIVISIONS * slot + residues) % residues
    ahead = jnp.where(ahead < HEAD_DIVISIONS, ahead ^ head_group, ahead)
    index = ahead * (rows // residues) + row_ids // residues
    out_ids = first_row + lax.broadcasted_iota(jnp.int32, (out_rows, rows), 0)
    return jnp.where(out_ids == index, 1.0, 0.0).astype(bf16)


def dot(a, b):
    return jnp.dot(a, b, preferred_element_type=f32)


def dot_t(a, b):
    return lax.dot_general(a, b, (((1,), (1,)), ((), ())), preferred_element_type=f32)


def expo_of(scores):
    return jnp.exp2(cap_value * math.log2(math.e) * jnp.tanh(scores * (1.0 / cap_value)))


def columns(index, width=HEAD_SIZE):
    return slice(index * width, (index + 1) * width)


def call(body, out_shape, in_specs, name, scratch=(), out_specs=None, cost=1000):
    return pl.pallas_call(
        body,
        out_shape=out_shape,
        in_specs=in_specs,
        out_specs=jax.tree.map(lambda _: VMEM, out_shape) if out_specs is None else out_specs,
        scratch_shapes=scratch,
        compiler_params=pltpu.CompilerParams(vmem_limit_bytes=VMEM_BYTES),
        cost_estimate=pl.CostEstimate(flops=cost, bytes_accessed=1000, transcendentals=0),
        name=name,
    )


def in_hbm(arrays):
    return [pltpu.with_memory_space_constraint(x, pltpu.HBM) for x in arrays]


def rows_at(index, size):
    return pl.ds(pl.multiple_of(index * size, size), size)


def beside_ones(values):
    return jnp.concatenate([values, jnp.ones(values.shape, bf16)], axis=1)


class Facts:
    def __init__(self, ref, slots, residues, groups):
        self.ref, self.slots, self.residues, self.groups = ref, slots, residues, groups
        self.size = 2 * slots + residues + groups

    def block(self, slot, half):
        return self.ref[0, 2 * slot + half]

    def rank(self, residue):
        return self.ref[0, 2 * self.slots + residue]

    def owner(self, prompt):
        return self.ref[0, 2 * self.slots + self.residues + prompt]

    def store(self, map_ref, rank_ref, owner_ref):
        for slot in range(self.slots):
            for half in range(2):
                self.ref[0, 2 * slot + half] = map_ref[0, slot, half]
        for residue in range(self.residues):
            self.ref[0, 2 * self.slots + residue] = rank_ref[0, residue]
        for prompt in range(self.groups):
            self.ref[0, 2 * self.slots + self.residues + prompt] = owner_ref[prompt]

    def halves(self, slot):
        high = jnp.where(self.block(slot, 1) > self.block(slot, 0), 1, 0)
        return 1 - high, high


def slot_and_head_group():
    member = lax.axis_index("blk")
    return member // HEAD_DIVISIONS, member % HEAD_DIVISIONS


def own_part(queries, keys, values, table, decode_rank, owner, lens, tables):
    rows, width = keys.shape
    block_len = rows // 2
    slots = table.shape[1]
    residues = decode_rank.shape[1]
    groups = owner.shape[0]
    rounds = len(lens)
    piece = rows // residues
    run = piece // 2
    cache_rows = slots * piece
    arrays = (queries, keys, values, *tables, table, decode_rank, owner)
    count = len(arrays)
    facts_of = lambda ref: Facts(ref, slots, residues, groups)

    def body(*refs):
        len_refs, refs = refs[:rounds], refs[rounds:]
        inputs, refs = refs[:count], refs[count:]
        facts_ref, qr_ref, acc_ref, select_ref, angle_ref = refs[:5]
        place_ref, owned_ref, row_at_ref, cache_at_ref = refs[5:9]
        e_refs, kr_ref = refs[9:13], refs[13]
        scratch, sems = refs[14 : 14 + count], refs[14 + count]
        q_ref, k_ref, v_ref, row_ref, blk_ref, map_ref, rank_ref, owner_ref = scratch
        copies = []
        for index in range(count):
            copies.append(pltpu.make_async_copy(inputs[index], scratch[index], sems.at[index]))
            copies[-1].start()
        slot, head_group = slot_and_head_group()
        group = lax.axis_index("req")
        line = lax.broadcasted_iota(jnp.int32, (CARRIED, width), 0)
        carried = jnp.zeros((CARRIED, width), jnp.int32)
        for index in range(rounds):
            length = len_refs[index][0]
            carried = jnp.where(line == 2 * index, lax.shift_right_logical(length, 6), carried)
            carried = jnp.where(line == 2 * index + 1, length & 63, carried)
        carried = carried.astype(f32).astype(bf16)
        for copy in copies:
            copy.wait()
        facts = facts_of(facts_ref)
        facts.store(map_ref, rank_ref, owner_ref)

        for half in range(2):
            part = columns(half, block_len)
            angles = block_angles(row_ref, blk_ref, map_ref[0, slot, half])
            for head in range(KV_DEV):
                kr_ref[part, columns(head)] = turned(k_ref[part, columns(head)], angles).astype(bf16)
            for head in range(Q_DEV):
                qr_ref[part, columns(head)] = (
                    turned(q_ref[part, columns(head)], angles) * query_scale
                ).astype(bf16)
            for turn in range(1, slots):
                other = block_angles(row_ref, blk_ref, map_ref[0, (slot - turn + slots) % slots, half])
                angle_ref[turn - 1, half, 0] = other[0]
                angle_ref[turn - 1, half, 1] = other[1]
        select = order_matrix(
            lambda r: rank_ref[0, r], slot, head_group, 0, rows // slots, rows, residues
        )
        select_ref[...] = select
        for kind, source in enumerate((kr_ref, v_ref)):
            chosen = dot(select, source[...]).astype(bf16)
            for m in range(HEAD_DIVISIONS):
                e_refs[m][columns(kind, piece)] = chosen[columns(m, piece)]
        for m in range(HEAD_DIVISIONS):
            e_refs[m][2 * piece :] = carried

        low, high = facts.halves(slot)
        low, high = rows_at(low, block_len), rows_at(high, block_len)
        row = lax.broadcasted_iota(jnp.int32, (block_len, block_len), 0)
        col = lax.broadcasted_iota(jnp.int32, (block_len, block_len), 1)
        for head in range(Q_DEV):
            key_head = columns(head * KV_DEV // Q_DEV)
            both = columns(head, 2 * HEAD_SIZE)

            def tile(q_part, k_part, diagonal):
                expo = expo_of(dot_t(qr_ref[q_part, columns(head)], kr_ref[k_part, key_head]))
                if diagonal:
                    expo = jnp.where(col <= row, expo, 0.0)
                return dot(expo.astype(bf16), beside_ones(v_ref[k_part, key_head]))

            acc_ref[low, both] = tile(low, low, True)
            acc_ref[high, both] = tile(high, high, True) + tile(high, low, False)

        col = lax.broadcasted_iota(jnp.int32, (1, cache_rows), 1)
        part, offset = col // run, col % run
        target = jnp.zeros_like(col)
        for turn in range(slots):
            for half in range(2):
                block = map_ref[0, (slot - turn + slots) % slots, half]
                target = jnp.where(part == 2 * turn + half, block * run + offset, target)
        row = lax.broadcasted_iota(jnp.int32, (cache_rows, cache_rows), 0)
        place_ref[...] = jnp.where(row == target, 1.0, 0.0).astype(bf16)
        residue = 0
        for r in range(1, residues):
            residue = jnp.where(rank_ref[0, r] == lax.axis_index("blk"), r, residue)
        cache_at_ref[...] = (row * residues + residue).astype(f32)
        for half in range(2):
            offset = lax.broadcasted_iota(jnp.int32, (block_len, HEAD_SIZE), 0)
            at = map_ref[0, slot, half] * block_len + offset
            row_at_ref[columns(half, block_len)] = at.astype(f32)
        for turn in range(groups):
            mine = owner_ref[lax.rem(group - turn + groups, groups)] == group
            owned_ref[turn : turn + 1] = jnp.full((1, HEAD_SIZE), jnp.where(mine, 1.0, 0.0), f32)

    shapes = [
        jax.ShapeDtypeStruct((1, facts_of(None).size), jnp.int32),
        jax.ShapeDtypeStruct(queries.shape, bf16),
        jax.ShapeDtypeStruct((rows, 2 * Q_DEV * HEAD_SIZE), f32),
        jax.ShapeDtypeStruct((rows // slots, rows), bf16),
        jax.ShapeDtypeStruct((slots - 1, 2, 2, block_len, HEAD_SIZE), f32),
        jax.ShapeDtypeStruct((cache_rows, cache_rows), bf16),
        jax.ShapeDtypeStruct((groups, HEAD_SIZE), f32),
        jax.ShapeDtypeStruct((rows, HEAD_SIZE), f32),
        jax.ShapeDtypeStruct((cache_rows, cache_rows), f32),
    ]
    shapes += [
        jax.ShapeDtypeStruct((2 * piece + CARRIED, width), bf16) for _ in range(HEAD_DIVISIONS)
    ]
    scratch = [pltpu.VMEM(keys.shape, bf16)]
    scratch += [pltpu.VMEM(x.shape, x.dtype) for x in arrays[:5]]
    scratch += [pltpu.SMEM(x.shape, x.dtype) for x in arrays[5:]]
    scratch.append(pltpu.SemaphoreType.DMA((count,)))
    outs = call(
        body,
        shapes,
        [SMEM] * rounds + [HBM] * count,
        "own_part",
        scratch,
        out_specs=[SMEM] + [VMEM] * (len(shapes) - 1),
    )(*lens, *in_hbm(arrays))
    return outs[0], facts_of, outs[1:3], outs[3:5], outs[5:9], outs[9:]


def receive(key_in, value_in, select, angles):
    others = len(key_in)
    rows, width = key_in[0].shape
    block_len = rows // 2
    piece = select.shape[0] // HEAD_DIVISIONS

    def body(select_ref, angle_ref, *refs):
        k_refs, v_refs, refs = refs[:others], refs[others : 2 * others], refs[2 * others :]
        kr_refs, e_refs = refs[:others], refs[others:]
        for turn in range(others):
            for half in range(2):
                part = columns(half, block_len)
                there = angle_ref[turn, half, 0], angle_ref[turn, half, 1]
                for head in range(KV_DEV):
                    kr_refs[turn][part, columns(head)] = turned(
                        k_refs[turn][part, columns(head)], there
                    ).astype(bf16)
            for kind, source in enumerate((kr_refs[turn], v_refs[turn])):
                chosen = dot(select_ref[...], source[...]).astype(bf16)
                for m in range(HEAD_DIVISIONS):
                    e_refs[m][columns(kind * others + turn, piece)] = chosen[columns(m, piece)]

    shapes = [jax.ShapeDtypeStruct((rows, width), bf16) for _ in range(others)]
    shapes += [
        jax.ShapeDtypeStruct((2 * others * piece, width), bf16) for _ in range(HEAD_DIVISIONS)
    ]
    outs = call(body, shapes, [VMEM] * (2 + 2 * others), "receive")(
        select, angles, *key_in, *value_in
    )
    return outs[:others], outs[others:]


def length_row(owned_ref, early_refs):
    head_group = slot_and_head_group()[1]
    groups = owned_ref.shape[0]
    length = jnp.zeros((1, HEAD_SIZE), f32)
    for m in range(HEAD_DIVISIONS):
        carried = early_refs[m][-CARRIED:, :HEAD_SIZE].astype(f32)
        for index in range(groups // HEAD_DIVISIONS):
            turn = (head_group ^ m) + HEAD_DIVISIONS * index
            value = carried[2 * index : 2 * index + 1] * 64.0 + carried[2 * index + 1 : 2 * index + 2]
            length = length + owned_ref[pl.ds(turn, 1)] * value
    return length


def attend(facts_row, facts_of, query_rot, acc, key_rot, value_in, owned, row_at, early):
    rows = query_rot.shape[0]
    block_len = rows // 2
    others = len(key_rot)
    slots = facts_of(None).slots

    def body(facts_ref, q_ref, acc_ref, owned_ref, row_at_ref, *refs):
        early_refs, refs = refs[:HEAD_DIVISIONS], refs[HEAD_DIVISIONS:]
        k_refs, v_refs, out_ref = refs[:others], refs[others : 2 * others], refs[2 * others]
        facts = facts_of(facts_ref)
        slot = slot_and_head_group()[0]
        length = length_row(owned_ref, early_refs)
        low, high = facts.halves(slot)
        low_rows, high_rows = rows_at(low, block_len), rows_at(high, block_len)
        for head in range(Q_DEV):
            key_head = columns(head * KV_DEV // Q_DEV)
            both = columns(head, 2 * HEAD_SIZE)
            low_sum, high_sum = acc_ref[low_rows, both], acc_ref[high_rows, both]
            for turn in range(1, slots):
                source = (slot - turn + slots) % slots
                source_low, source_high = facts.halves(source)
                outer = facts.block(slot, low) < facts.block(source, source_low)

                def tile(half, other):
                    queries = q_ref[rows_at(half, block_len), columns(head)]
                    there = rows_at(other, block_len)
                    expo = expo_of(dot_t(queries, k_refs[turn - 1][there, key_head]))
                    return dot(expo.astype(bf16), beside_ones(v_refs[turn - 1][there, key_head]))

                either = tile(jnp.where(outer, high, low), source_low)
                upper = tile(high, jnp.where(outer, source_high, source_low))
                low_sum = low_sum + jnp.where(outer, 0.0, either)
                high_sum = high_sum + upper + jnp.where(outer, either, 0.0)
            for part, total in ((low_rows, low_sum), (high_rows, high_sum)):
                scale = jnp.where(row_at_ref[part] < length, 1.0, 0.0) / total[:, HEAD_SIZE:]
                out_ref[part, columns(head)] = (total[:, :HEAD_SIZE] * scale).astype(bf16)

    shape = jax.ShapeDtypeStruct(query_rot.shape, bf16)
    specs = [SMEM] + [VMEM] * (4 + HEAD_DIVISIONS + 2 * others)
    return call(body, shape, specs, "attend", cost=10**10)(
        facts_row, query_rot, acc, owned, row_at, *early, *key_rot, *value_in
    )


def cache_part(early, late, place, owned, cache_at):
    cache_rows = place.shape[0]
    piece = (early[0].shape[0] - CARRIED) // 2
    width = early[0].shape[1]

    def body(place_ref, owned_ref, cache_at_ref, *refs):
        f_refs, s_refs, out_ref = refs[:4], refs[4:8], refs[8]
        head_group = slot_and_head_group()[1]
        later = cache_rows - piece
        length = length_row(owned_ref, f_refs)
        kept = jnp.where(cache_at_ref[...] < length[:, :1], place_ref[...].astype(f32), 0.0)
        kept = kept.astype(bf16)
        for m in range(HEAD_DIVISIONS):
            for kind in range(2):
                lines = jnp.concatenate(
                    [f_refs[m][columns(kind, piece)], s_refs[m][columns(kind, later)]], axis=0
                )
                column = ((head_group ^ m) + kind * HEAD_DIVISIONS) * width
                out_ref[:, pl.ds(pl.multiple_of(column, HEAD_SIZE), width)] = dot(kept, lines).astype(
                    bf16
                )

    shape = jax.ShapeDtypeStruct((cache_rows, 2 * HEAD_DIVISIONS * width), bf16)
    return call(body, shape, [VMEM] * 11, "cache_part")(place, owned, cache_at, *early, *late)


def on_device(queries, keys, values, block_map, lengths, group_of_prompt, decode_rank):
    block_len = queries.shape[2] // 2
    slots = block_map.shape[1]
    q, k, v = queries[0, 0], keys[0, 0], values[0, 0]
    tables = rotary_tables(block_len, 2 * slots)

    def to_slots(part):
        return [shifted(part, "blk", HEAD_DIVISIONS * t) for t in range(1, slots)]

    def hand_on(pieces):
        return [pieces[0]] + [crossed(pieces[m], "blk", m) for m in range(1, HEAD_DIVISIONS)]

    key_in, value_in = to_slots(k), to_slots(v)
    lens = [spread(lengths, t) for t in range(lax.axis_size("req") // HEAD_DIVISIONS)]
    facts_row, facts_of, (query_rot, acc), (select, angles), masks, early = own_part(
        q, k, v, block_map, decode_rank, group_of_prompt, lens, tables
    )
    place, owned, row_at, cache_at = masks
    early = hand_on(early)
    key_rot, late = receive(key_in, value_in, select, angles)
    late = hand_on(late)
    attended = attend(
        facts_row, facts_of, query_rot, acc, key_rot, value_in, owned, row_at, early
    )
    cache = cache_part(early, late, place, owned, cache_at)
    return (attended[None, None], cache[None])


def solution(mesh):
    placed = (
        P("req", "blk", None, None),
        P("req", "blk", None, None),
        P("req", "blk", None, None),
        P("req", None, None),
        P("req"),
        P(),
        P("req", None),
    )
    return jax.shard_map(
        on_device,
        mesh=mesh,
        in_specs=placed,
        out_specs=(P("req", "blk", None, None), P("req", "blk", None)),
        check_vma=False,
    )
```

```python
import math

import jax
import jax.numpy as jnp
import numpy as np
from jax import lax
from jax.experimental import pallas as pl
from jax.experimental.pallas import tpu as pltpu
from jax.sharding import PartitionSpec as P

QUERY_HEADS = 16
KEY_VALUE_HEADS = 8
HEAD_SIZE = 128
HEAD_DIVISIONS = 4
Q_DEV = 4
KV_DEV = 2
KV_WIDTH = KV_DEV * HEAD_SIZE

cap_value = 50.0
query_scale = 1.0 / 12.0
rope_base = 10000.0
CARRIED = 16
VMEM_BYTES = 48 * 1024 * 1024

f32 = jnp.float32
bf16 = jnp.bfloat16
SMEM = pl.BlockSpec(memory_space=pltpu.SMEM)
VMEM = pl.BlockSpec(memory_space=pltpu.VMEM)
HBM = pl.BlockSpec(memory_space=pltpu.HBM)


def shifted(shard, axis, by):
    peers = lax.axis_size(axis)
    return lax.ppermute(shard, axis, [(i, (i + by) % peers) for i in range(peers)])


def spread(shard, turn):
    groups, members = lax.axis_size("req"), lax.axis_size("blk")
    pairs = []
    for group in range(groups):
        for member in range(members):
            target = group + member % HEAD_DIVISIONS + HEAD_DIVISIONS * turn
            pairs.append((group * members + member, target % groups * members + member))
    return lax.ppermute(shard, ("req", "blk"), pairs)


def rotary_tables(block_len, block_count):
    half = HEAD_SIZE // 2
    frequency = np.exp(
        np.float32(-math.log(rope_base)) * (2.0 * np.arange(half, dtype=np.float32)) / HEAD_SIZE
    ).astype(np.float64)

    def table(positions):
        angles = positions.astype(np.float64)[:, None] * frequency[None, :]
        cosine, sine = np.cos(angles), np.sin(angles)
        return np.stack(
            [np.concatenate([cosine, cosine], 1), np.concatenate([-sine, sine], 1)]
        ).astype(np.float32)

    return table(np.arange(block_len)), table(np.arange(block_count) * block_len)


def block_angles(row_table, block_table, block):
    row_cos, row_sin = row_table[0], row_table[1]
    blk_cos, blk_sin = block_table[0, pl.ds(block, 1)], block_table[1, pl.ds(block, 1)]
    return row_cos * blk_cos - row_sin * blk_sin, row_sin * blk_cos + row_cos * blk_sin


def turned(head, angles):
    x = head.astype(f32)
    return x * angles[0] + pltpu.roll(x, HEAD_SIZE // 2, 1) * angles[1]


def order_matrix(rank_of, slot, out_rows, rows, residues):
    row_ids = lax.broadcasted_iota(jnp.int32, (1, rows), 1)
    residue = row_ids % residues
    rank = jnp.zeros_like(row_ids)
    for r in range(residues):
        rank = jnp.where(residue == r, rank_of(r), rank)
    ahead = (rank - HEAD_DIVISIONS * slot + residues) % residues
    index = ahead * (rows // residues) + row_ids // residues
    out_ids = lax.broadcasted_iota(jnp.int32, (out_rows, rows), 0)
    return jnp.where(out_ids == index, 1.0, 0.0).astype(bf16)


def dot(a, b):
    return jnp.dot(a, b, preferred_element_type=f32)


def dot_t(a, b):
    return lax.dot_general(a, b, (((1,), (1,)), ((), ())), preferred_element_type=f32)


def expo_of(scores):
    return jnp.exp2(cap_value * math.log2(math.e) * jnp.tanh(scores * (1.0 / cap_value)))


def columns(index, width=HEAD_SIZE):
    return slice(index * width, (index + 1) * width)


def call(body, out_shape, in_specs, name, scratch=(), out_specs=None, cost=1000):
    return pl.pallas_call(
        body,
        out_shape=out_shape,
        in_specs=in_specs,
        out_specs=jax.tree.map(lambda _: VMEM, out_shape) if out_specs is None else out_specs,
        scratch_shapes=scratch,
        compiler_params=pltpu.CompilerParams(vmem_limit_bytes=VMEM_BYTES),
        cost_estimate=pl.CostEstimate(flops=cost, bytes_accessed=1000, transcendentals=0),
        name=name,
    )


def in_hbm(arrays):
    return [pltpu.with_memory_space_constraint(x, pltpu.HBM) for x in arrays]


def rows_at(index, size):
    return pl.ds(pl.multiple_of(index * size, size), size)


def beside_ones(values):
    return jnp.concatenate([values, jnp.ones(values.shape, bf16)], axis=1)


class Facts:
    def __init__(self, ref, slots, residues, groups):
        self.ref, self.slots, self.residues, self.groups = ref, slots, residues, groups
        self.size = 2 * slots + residues + groups

    def block(self, slot, half):
        return self.ref[0, 2 * slot + half]

    def rank(self, residue):
        return self.ref[0, 2 * self.slots + residue]

    def owner(self, prompt):
        return self.ref[0, 2 * self.slots + self.residues + prompt]

    def store(self, map_ref, rank_ref, owner_ref):
        for slot in range(self.slots):
            for half in range(2):
                self.ref[0, 2 * slot + half] = map_ref[0, slot, half]
        for residue in range(self.residues):
            self.ref[0, 2 * self.slots + residue] = rank_ref[0, residue]
        for prompt in range(self.groups):
            self.ref[0, 2 * self.slots + self.residues + prompt] = owner_ref[prompt]

    def halves(self, slot):
        high = jnp.where(self.block(slot, 1) > self.block(slot, 0), 1, 0)
        return 1 - high, high


def slot_and_head_group():
    member = lax.axis_index("blk")
    return member // HEAD_DIVISIONS, member % HEAD_DIVISIONS


def prepare(queries, keys, values, table, decode_rank, owner, tables):
    rows, width = keys.shape
    block_len = rows // 2
    slots = table.shape[1]
    residues = decode_rank.shape[1]
    piece = rows // residues
    arrays = (keys, values, queries, *tables, table, decode_rank, owner)
    count = len(arrays)
    facts_of = lambda ref: Facts(ref, slots, residues, owner.shape[0])

    def body(*refs):
        inputs, refs = refs[:count], refs[count:]
        facts_ref, qr_ref, kr_ref, v_ref, select_ref, angle_ref, chosen_ref = refs[:7]
        k_ref, q_ref, row_ref, blk_ref, map_ref, rank_ref, owner_ref, sems = refs[7:]
        targets = (k_ref, v_ref, q_ref, row_ref, blk_ref, map_ref, rank_ref, owner_ref)
        copies = []
        for index in range(count):
            copies.append(pltpu.make_async_copy(inputs[index], targets[index], sems.at[index]))
            copies[-1].start()
        slot, head_group = slot_and_head_group()
        for copy in copies:
            copy.wait()
        facts_of(facts_ref).store(map_ref, rank_ref, owner_ref)
        for half in range(2):
            part = columns(half, block_len)
            angles = block_angles(row_ref, blk_ref, map_ref[0, slot, half])
            for head in range(KV_DEV):
                kr_ref[part, columns(head)] = turned(k_ref[part, columns(head)], angles).astype(bf16)
            for head in range(Q_DEV):
                qr_ref[part, columns(head)] = (
                    turned(q_ref[part, columns(head)], angles) * query_scale
                ).astype(bf16)
            for turn in range(1, slots):
                other = block_angles(row_ref, blk_ref, map_ref[0, (slot - turn + slots) % slots, half])
                angle_ref[turn - 1, half, 0] = other[0]
                angle_ref[turn - 1, half, 1] = other[1]
        select = order_matrix(lambda r: rank_ref[0, r], slot, rows // slots, rows, residues)
        select_ref[...] = select
        for kind, source in enumerate((kr_ref, v_ref)):
            chosen = dot(select, source[...]).astype(bf16)
            for m in range(HEAD_DIVISIONS):
                chosen_ref[m, columns(kind, piece)] = chosen[columns(m, piece)]

    shapes = [
        jax.ShapeDtypeStruct((1, facts_of(None).size), jnp.int32),
        jax.ShapeDtypeStruct(queries.shape, bf16),
        jax.ShapeDtypeStruct(keys.shape, bf16),
        jax.ShapeDtypeStruct(values.shape, bf16),
        jax.ShapeDtypeStruct((rows // slots, rows), bf16),
        jax.ShapeDtypeStruct((slots - 1, 2, 2, block_len, HEAD_SIZE), f32),
        jax.ShapeDtypeStruct((HEAD_DIVISIONS, 2 * piece, width), bf16),
    ]
    scratch = [pltpu.VMEM(x.shape, x.dtype) for x in (keys, queries, *tables)]
    scratch += [pltpu.SMEM(x.shape, x.dtype) for x in (table, decode_rank, owner)]
    scratch.append(pltpu.SemaphoreType.DMA((count,)))
    outs = call(
        body,
        shapes,
        [HBM] * count,
        "prepare",
        scratch,
        out_specs=[SMEM] + [VMEM] * (len(shapes) - 1),
    )(*in_hbm(arrays))
    return outs[0], facts_of, outs[1:4], outs[4:6], outs[6]


def with_lengths(lens, chosen):
    rounds = len(lens)
    _, rows, width = chosen.shape

    def body(*refs):
        len_refs, chosen_ref, out_ref = refs[:rounds], refs[rounds], refs[rounds + 1]
        line = lax.broadcasted_iota(jnp.int32, (CARRIED, width), 0)
        carried = jnp.zeros((CARRIED, width), jnp.int32)
        for index in range(rounds):
            length = len_refs[index][0]
            carried = jnp.where(line == 2 * index, lax.shift_right_logical(length, 6), carried)
            carried = jnp.where(line == 2 * index + 1, length & 63, carried)
        carried = carried.astype(f32).astype(bf16)
        for m in range(HEAD_DIVISIONS):
            out_ref[m, :rows] = chosen_ref[m]
            out_ref[m, rows:] = carried

    shape = jax.ShapeDtypeStruct((HEAD_DIVISIONS, rows + CARRIED, width), bf16)
    return call(body, shape, [SMEM] * rounds + [VMEM], "with_lengths")(*lens, chosen)


def own_part(facts_row, facts_of, operands):
    query_rot, key_rot, values = operands
    rows = query_rot.shape[0]
    block_len = rows // 2
    sizes = facts_of(None)
    slots, residues, groups = sizes.slots, sizes.residues, sizes.groups
    run = block_len // residues
    cache_rows = 2 * slots * run

    def body(facts_ref, qr_ref, kr_ref, v_ref, acc_ref, place_ref, owned_ref, row_at_ref, cache_at_ref):
        facts = facts_of(facts_ref)
        slot = slot_and_head_group()[0]
        group = lax.axis_index("req")
        low, high = facts.halves(slot)
        low, high = rows_at(low, block_len), rows_at(high, block_len)
        row = lax.broadcasted_iota(jnp.int32, (block_len, block_len), 0)
        col = lax.broadcasted_iota(jnp.int32, (block_len, block_len), 1)
        for head in range(Q_DEV):
            key_head = columns(head * KV_DEV // Q_DEV)
            both = columns(head, 2 * HEAD_SIZE)

            def tile(q_part, k_part, diagonal):
                expo = expo_of(dot_t(qr_ref[q_part, columns(head)], kr_ref[k_part, key_head]))
                if diagonal:
                    expo = jnp.where(col <= row, expo, 0.0)
                return dot(expo.astype(bf16), beside_ones(v_ref[k_part, key_head]))

            acc_ref[low, both] = tile(low, low, True)
            acc_ref[high, both] = tile(high, high, True) + tile(high, low, False)

        col = lax.broadcasted_iota(jnp.int32, (1, cache_rows), 1)
        part, offset = col // run, col % run
        target = jnp.zeros_like(col)
        for turn in range(slots):
            for half in range(2):
                block = facts.block((slot - turn + slots) % slots, half)
                target = jnp.where(part == 2 * turn + half, block * run + offset, target)
        row = lax.broadcasted_iota(jnp.int32, (cache_rows, cache_rows), 0)
        place_ref[...] = jnp.where(row == target, 1.0, 0.0).astype(bf16)
        residue = 0
        for r in range(1, residues):
            residue = jnp.where(facts.rank(r) == lax.axis_index("blk"), r, residue)
        cache_at_ref[...] = (row * residues + residue).astype(f32)
        for half in range(2):
            offset = lax.broadcasted_iota(jnp.int32, (block_len, HEAD_SIZE), 0)
            at = facts.block(slot, half) * block_len + offset
            row_at_ref[columns(half, block_len)] = at.astype(f32)
        for turn in range(groups):
            mine = facts.owner(lax.rem(group - turn + groups, groups)) == group
            owned_ref[turn : turn + 1] = jnp.full((1, HEAD_SIZE), jnp.where(mine, 1.0, 0.0), f32)

    shapes = [
        jax.ShapeDtypeStruct((rows, 2 * Q_DEV * HEAD_SIZE), f32),
        jax.ShapeDtypeStruct((cache_rows, cache_rows), bf16),
        jax.ShapeDtypeStruct((groups, HEAD_SIZE), f32),
        jax.ShapeDtypeStruct((rows, HEAD_SIZE), f32),
        jax.ShapeDtypeStruct((cache_rows, cache_rows), f32),
    ]
    return call(body, shapes, [SMEM] + [VMEM] * 3, "own_part")(facts_row, *operands)


def receive(key_in, value_in, select, angles):
    others = len(key_in)
    rows, width = key_in[0].shape
    block_len = rows // 2
    piece = select.shape[0] // HEAD_DIVISIONS

    def body(select_ref, angle_ref, *refs):
        k_refs, v_refs, refs = refs[:others], refs[others : 2 * others], refs[2 * others :]
        kr_refs, e_ref = refs[:others], refs[others]
        for turn in range(others):
            for half in range(2):
                part = columns(half, block_len)
                there = angle_ref[turn, half, 0], angle_ref[turn, half, 1]
                for head in range(KV_DEV):
                    kr_refs[turn][part, columns(head)] = turned(
                        k_refs[turn][part, columns(head)], there
                    ).astype(bf16)
            for kind, source in enumerate((kr_refs[turn], v_refs[turn])):
                chosen = dot(select_ref[...], source[...]).astype(bf16)
                for m in range(HEAD_DIVISIONS):
                    e_ref[m, columns(kind * others + turn, piece)] = chosen[columns(m, piece)]

    shapes = [jax.ShapeDtypeStruct((rows, width), bf16) for _ in range(others)]
    shapes.append(jax.ShapeDtypeStruct((HEAD_DIVISIONS, 2 * others * piece, width), bf16))
    outs = call(body, shapes, [VMEM] * (2 + 2 * others), "receive")(
        select, angles, *key_in, *value_in
    )
    return outs[:others], outs[others]


def length_row(owned_ref, early_ref):
    groups = owned_ref.shape[0]
    length = jnp.zeros((1, HEAD_SIZE), f32)
    for m in range(HEAD_DIVISIONS):
        carried = early_ref[m, -CARRIED:, :HEAD_SIZE].astype(f32)
        for index in range(groups // HEAD_DIVISIONS):
            turn = m + HEAD_DIVISIONS * index
            value = carried[2 * index : 2 * index + 1] * 64.0 + carried[2 * index + 1 : 2 * index + 2]
            length = length + owned_ref[turn : turn + 1] * value
    return length


def attend(facts_row, facts_of, query_rot, acc, key_rot, value_in, owned, row_at, early):
    rows = query_rot.shape[0]
    block_len = rows // 2
    others = len(key_rot)
    slots = facts_of(None).slots

    def body(facts_ref, q_ref, acc_ref, owned_ref, row_at_ref, *refs):
        early_ref, refs = refs[0], refs[1:]
        k_refs, v_refs, out_ref = refs[:others], refs[others : 2 * others], refs[2 * others]
        facts = facts_of(facts_ref)
        slot = slot_and_head_group()[0]
        length = length_row(owned_ref, early_ref)
        low, high = facts.halves(slot)
        low_rows, high_rows = rows_at(low, block_len), rows_at(high, block_len)
        for head in range(Q_DEV):
            key_head = columns(head * KV_DEV // Q_DEV)
            both = columns(head, 2 * HEAD_SIZE)
            low_sum, high_sum = acc_ref[low_rows, both], acc_ref[high_rows, both]
            for turn in range(1, slots):
                source = (slot - turn + slots) % slots
                source_low, source_high = facts.halves(source)
                outer = facts.block(slot, low) < facts.block(source, source_low)

                def tile(half, other):
                    queries = q_ref[rows_at(half, block_len), columns(head)]
                    there = rows_at(other, block_len)
                    expo = expo_of(dot_t(queries, k_refs[turn - 1][there, key_head]))
                    return dot(expo.astype(bf16), beside_ones(v_refs[turn - 1][there, key_head]))

                either = tile(jnp.where(outer, high, low), source_low)
                upper = tile(high, jnp.where(outer, source_high, source_low))
                low_sum = low_sum + jnp.where(outer, 0.0, either)
                high_sum = high_sum + upper + jnp.where(outer, either, 0.0)
            for part, total in ((low_rows, low_sum), (high_rows, high_sum)):
                scale = jnp.where(row_at_ref[part] < length, 1.0, 0.0) / total[:, HEAD_SIZE:]
                out_ref[part, columns(head)] = (total[:, :HEAD_SIZE] * scale).astype(bf16)

    shape = jax.ShapeDtypeStruct(query_rot.shape, bf16)
    specs = [SMEM] + [VMEM] * (5 + 2 * others)
    return call(body, shape, specs, "attend", cost=10**10)(
        facts_row, query_rot, acc, owned, row_at, early, *key_rot, *value_in
    )


def cache_part(early, late, place, owned, cache_at):
    cache_rows = place.shape[0]
    piece = (early.shape[1] - CARRIED) // 2
    width = early.shape[2]

    def body(place_ref, owned_ref, cache_at_ref, f_ref, s_ref, out_ref):
        later = cache_rows - piece
        length = length_row(owned_ref, f_ref)
        kept = jnp.where(cache_at_ref[...] < length[:, :1], place_ref[...].astype(f32), 0.0)
        kept = kept.astype(bf16)
        for m in range(HEAD_DIVISIONS):
            for kind in range(2):
                lines = jnp.concatenate(
                    [f_ref[m, columns(kind, piece)], s_ref[m, columns(kind, later)]], axis=0
                )
                out_ref[:, columns(kind * HEAD_DIVISIONS + m, width)] = dot(kept, lines).astype(bf16)

    shape = jax.ShapeDtypeStruct((cache_rows, 2 * HEAD_DIVISIONS * width), bf16)
    return call(body, shape, [VMEM] * 5, "cache_part")(place, owned, cache_at, early, late)


def on_device(queries, keys, values, block_map, lengths, group_of_prompt, decode_rank):
    block_len = queries.shape[2] // 2
    slots = block_map.shape[1]
    q, k, v = queries[0, 0], keys[0, 0], values[0, 0]
    tables = rotary_tables(block_len, 2 * slots)

    def to_slots(part):
        return [shifted(part, "blk", HEAD_DIVISIONS * t) for t in range(1, slots)]

    def hand_on(pieces):
        members = [
            [slot * HEAD_DIVISIONS + m for m in range(HEAD_DIVISIONS)] for slot in range(slots)
        ]
        return lax.all_to_all(
            pieces, "blk", split_axis=0, concat_axis=0, axis_index_groups=members, tiled=True
        )

    key_in, value_in = to_slots(k), to_slots(v)
    lens = [spread(lengths, t) for t in range(lax.axis_size("req") // HEAD_DIVISIONS)]
    facts_row, facts_of, operands, (select, angles), chosen = prepare(
        q, k, v, block_map, decode_rank, group_of_prompt, tables
    )
    early = hand_on(with_lengths(lens, chosen))
    acc, place, owned, row_at, cache_at = own_part(facts_row, facts_of, operands)
    key_rot, late = receive(key_in, value_in, select, angles)
    late = hand_on(late)
    attended = attend(
        facts_row, facts_of, operands[0], acc, key_rot, value_in, owned, row_at, early
    )
    cache = cache_part(early, late, place, owned, cache_at)
    return (attended[None, None], cache[None])


def solution(mesh):
    placed = (
        P("req", "blk", None, None),
        P("req", "blk", None, None),
        P("req", "blk", None, None),
        P("req", None, None),
        P("req"),
        P(),
        P("req", None),
    )
    return jax.shard_map(
        on_device,
        mesh=mesh,
        in_specs=placed,
        out_specs=(P("req", "blk", None, None), P("req", "blk", None)),
        check_vma=False,
    )
```

```python
import math

import jax
import jax.numpy as jnp
import numpy as np
from jax import lax
from jax.experimental import pallas as pl
from jax.experimental.pallas import tpu as pltpu
from jax.sharding import PartitionSpec as P

QUERY_HEADS = 16
KEY_VALUE_HEADS = 8
HEAD_SIZE = 128
HEAD_DIVISIONS = 4
Q_DEV = 4
KV_DEV = 2
KV_WIDTH = KV_DEV * HEAD_SIZE

cap_value = 50.0
query_scale = 1.0 / 12.0
rope_base = 10000.0
VMEM_BYTES = 48 * 1024 * 1024

f32 = jnp.float32
bf16 = jnp.bfloat16
SMEM = pl.BlockSpec(memory_space=pltpu.SMEM)
VMEM = pl.BlockSpec(memory_space=pltpu.VMEM)
HBM = pl.BlockSpec(memory_space=pltpu.HBM)


def shifted(shard, axis, by):
    peers = lax.axis_size(axis)
    return lax.ppermute(shard, axis, [(i, (i + by) % peers) for i in range(peers)])


def crossed(shard, axis, by):
    peers = lax.axis_size(axis)
    return lax.ppermute(shard, axis, [(i, i ^ by) for i in range(peers)])


def rotary_tables(block_len, block_count):
    half = HEAD_SIZE // 2
    frequency = np.exp(
        np.float32(-math.log(rope_base)) * (2.0 * np.arange(half, dtype=np.float32)) / HEAD_SIZE
    ).astype(np.float64)

    def table(positions):
        angles = positions.astype(np.float64)[:, None] * frequency[None, :]
        cosine, sine = np.cos(angles), np.sin(angles)
        return np.stack(
            [np.concatenate([cosine, cosine], 1), np.concatenate([-sine, sine], 1)]
        ).astype(np.float32)

    return table(np.arange(block_len)), table(np.arange(block_count) * block_len)


def block_angles(row_table, block_table, block):
    row_cos, row_sin = row_table[0], row_table[1]
    blk_cos, blk_sin = block_table[0, pl.ds(block, 1)], block_table[1, pl.ds(block, 1)]
    return row_cos * blk_cos - row_sin * blk_sin, row_sin * blk_cos + row_cos * blk_sin


def turned(head, angles):
    x = head.astype(f32)
    return x * angles[0] + pltpu.roll(x, HEAD_SIZE // 2, 1) * angles[1]


def order_matrix(rank_of, slot, head_group, out_rows, rows, residues):
    row_ids = lax.broadcasted_iota(jnp.int32, (1, rows), 1)
    residue = row_ids % residues
    rank = jnp.zeros_like(row_ids)
    for r in range(residues):
        rank = jnp.where(residue == r, rank_of(r), rank)
    ahead = (rank - HEAD_DIVISIONS * slot + residues) % residues
    ahead = jnp.where(ahead < HEAD_DIVISIONS, ahead ^ head_group, ahead)
    index = ahead * (rows // residues) + row_ids // residues
    out_ids = lax.broadcasted_iota(jnp.int32, (out_rows, rows), 0)
    return jnp.where(out_ids == index, 1.0, 0.0).astype(bf16)


def dot(a, b):
    return jnp.dot(a, b, preferred_element_type=f32)


def dot_t(a, b):
    return lax.dot_general(a, b, (((1,), (1,)), ((), ())), preferred_element_type=f32)


def expo_of(scores):
    return jnp.exp2(cap_value * math.log2(math.e) * jnp.tanh(scores * (1.0 / cap_value)))


def columns(index, width=HEAD_SIZE):
    return slice(index * width, (index + 1) * width)


def call(body, out_shape, in_specs, name, scratch=(), out_specs=None, cost=1000):
    return pl.pallas_call(
        body,
        out_shape=out_shape,
        in_specs=in_specs,
        out_specs=jax.tree.map(lambda _: VMEM, out_shape) if out_specs is None else out_specs,
        scratch_shapes=scratch,
        compiler_params=pltpu.CompilerParams(vmem_limit_bytes=VMEM_BYTES),
        cost_estimate=pl.CostEstimate(flops=cost, bytes_accessed=1000, transcendentals=0),
        name=name,
    )


def in_hbm(arrays):
    return [pltpu.with_memory_space_constraint(x, pltpu.HBM) for x in arrays]


def rows_at(index, size):
    return pl.ds(pl.multiple_of(index * size, size), size)


def beside_ones(values):
    return jnp.concatenate([values, jnp.ones(values.shape, bf16)], axis=1)


class Facts:
    def __init__(self, ref, slots, residues, groups):
        self.ref, self.slots, self.residues, self.groups = ref, slots, residues, groups
        self.size = 2 * slots + residues + groups

    def block(self, slot, half):
        return self.ref[0, 2 * slot + half]

    def rank(self, residue):
        return self.ref[0, 2 * self.slots + residue]

    def owner(self, prompt):
        return self.ref[0, 2 * self.slots + self.residues + prompt]

    def store(self, map_ref, rank_ref, owner_ref):
        for slot in range(self.slots):
            for half in range(2):
                self.ref[0, 2 * slot + half] = map_ref[0, slot, half]
        for residue in range(self.residues):
            self.ref[0, 2 * self.slots + residue] = rank_ref[0, residue]
        for prompt in range(self.groups):
            self.ref[0, 2 * self.slots + self.residues + prompt] = owner_ref[prompt]

    def halves(self, slot):
        high = jnp.where(self.block(slot, 1) > self.block(slot, 0), 1, 0)
        return 1 - high, high


def slot_and_head_group():
    member = lax.axis_index("blk")
    return member // HEAD_DIVISIONS, member % HEAD_DIVISIONS


def prepare(queries, keys, values, table, decode_rank, owner, tables, own_length, near_length):
    rows, width = keys.shape
    block_len = rows // 2
    slots = table.shape[1]
    residues = decode_rank.shape[1]
    piece = rows // residues
    arrays = (keys, values, queries, *tables, table, decode_rank, owner)
    count = len(arrays)
    facts_of = lambda ref: Facts(ref, slots, residues, owner.shape[0])

    def body(own_ref, near_ref, *refs):
        inputs, refs = refs[:count], refs[count:]
        facts_ref, pair_ref, qr_ref, kr_ref, v_ref, select_ref, angle_ref = refs[:7]
        e_refs, refs = refs[7:11], refs[11:]
        k_ref, q_ref, row_ref, blk_ref, map_ref, rank_ref, owner_ref, sems = refs
        targets = (k_ref, v_ref, q_ref, row_ref, blk_ref, map_ref, rank_ref, owner_ref)
        copies = []
        for index in range(count):
            copies.append(pltpu.make_async_copy(inputs[index], targets[index], sems.at[index]))
            copies[-1].start()
        slot, head_group = slot_and_head_group()
        odd = lax.axis_index("req") % 2 == 1
        pair_ref[0] = jnp.where(odd, near_ref[0], own_ref[0])
        pair_ref[1] = jnp.where(odd, own_ref[0], near_ref[0])
        for copy in copies:
            copy.wait()
        facts_of(facts_ref).store(map_ref, rank_ref, owner_ref)
        for half in range(2):
            part = columns(half, block_len)
            angles = block_angles(row_ref, blk_ref, map_ref[0, slot, half])
            for head in range(KV_DEV):
                kr_ref[part, columns(head)] = turned(k_ref[part, columns(head)], angles).astype(bf16)
            for head in range(Q_DEV):
                qr_ref[part, columns(head)] = (
                    turned(q_ref[part, columns(head)], angles) * query_scale
                ).astype(bf16)
            for turn in range(1, slots):
                other = block_angles(row_ref, blk_ref, map_ref[0, (slot - turn + slots) % slots, half])
                angle_ref[turn - 1, half, 0] = other[0]
                angle_ref[turn - 1, half, 1] = other[1]
        select = order_matrix(
            lambda r: rank_ref[0, r], slot, head_group, rows // slots, rows, residues
        )
        select_ref[...] = select
        for kind, source in enumerate((kr_ref, v_ref)):
            chosen = dot(select, source[...]).astype(bf16)
            for m in range(HEAD_DIVISIONS):
                e_refs[m][columns(kind, piece)] = chosen[columns(m, piece)]

    shapes = [
        jax.ShapeDtypeStruct((1, facts_of(None).size), jnp.int32),
        jax.ShapeDtypeStruct((2,), jnp.int32),
        jax.ShapeDtypeStruct(queries.shape, bf16),
        jax.ShapeDtypeStruct(keys.shape, bf16),
        jax.ShapeDtypeStruct(values.shape, bf16),
        jax.ShapeDtypeStruct((rows // slots, rows), bf16),
        jax.ShapeDtypeStruct((slots - 1, 2, 2, block_len, HEAD_SIZE), f32),
    ]
    shapes += [jax.ShapeDtypeStruct((2 * piece, width), bf16) for _ in range(HEAD_DIVISIONS)]
    scratch = [pltpu.VMEM(x.shape, x.dtype) for x in (keys, queries, *tables)]
    scratch += [pltpu.SMEM(x.shape, x.dtype) for x in (table, decode_rank, owner)]
    scratch.append(pltpu.SemaphoreType.DMA((count,)))
    outs = call(
        body,
        shapes,
        [SMEM] * 2 + [HBM] * count,
        "prepare",
        scratch,
        out_specs=[SMEM] * 2 + [VMEM] * (len(shapes) - 2),
    )(own_length, near_length, *in_hbm(arrays))
    return outs[0], facts_of, outs[1], outs[2:5], outs[5:7], outs[7:]


def own_part(facts_row, facts_of, operands, lens):
    query_rot, key_rot, values = operands
    rows = query_rot.shape[0]
    block_len = rows // 2
    sizes = facts_of(None)
    slots, residues, groups = sizes.slots, sizes.residues, sizes.groups
    run = block_len // residues
    cache_rows = 2 * slots * run

    def body(facts_ref, here_ref, there_ref, qr_ref, kr_ref, v_ref, acc_ref, kept_ref, live_ref):
        facts = facts_of(facts_ref)
        slot = slot_and_head_group()[0]
        group = lax.axis_index("req")
        low, high = facts.halves(slot)
        low, high = rows_at(low, block_len), rows_at(high, block_len)
        row = lax.broadcasted_iota(jnp.int32, (block_len, block_len), 0)
        col = lax.broadcasted_iota(jnp.int32, (block_len, block_len), 1)
        for head in range(Q_DEV):
            key_head = columns(head * KV_DEV // Q_DEV)
            both = columns(head, 2 * HEAD_SIZE)

            def tile(q_part, k_part, diagonal):
                expo = expo_of(dot_t(qr_ref[q_part, columns(head)], kr_ref[k_part, key_head]))
                if diagonal:
                    expo = jnp.where(col <= row, expo, 0.0)
                return dot(expo.astype(bf16), beside_ones(v_ref[k_part, key_head]))

            acc_ref[low, both] = tile(low, low, True)
            acc_ref[high, both] = tile(high, high, True) + tile(high, low, False)

        col = lax.broadcasted_iota(jnp.int32, (1, cache_rows), 1)
        part, offset = col // run, col % run
        target = jnp.zeros_like(col)
        for turn in range(slots):
            for half in range(2):
                block = facts.block((slot - turn + slots) % slots, half)
                target = jnp.where(part == 2 * turn + half, block * run + offset, target)
        length = 0
        half_count = groups // 2
        for index in range(half_count):
            same = (group & half_count) | index
            length = length + jnp.where(facts.owner(same) == group, here_ref[index], 0)
            other = same ^ half_count
            length = length + jnp.where(facts.owner(other) == group, there_ref[index], 0)
        residue = 0
        for r in range(1, residues):
            residue = jnp.where(facts.rank(r) == lax.axis_index("blk"), r, residue)
        target = jnp.where(target * residues + residue < length, target, -1)
        row = lax.broadcasted_iota(jnp.int32, (cache_rows, cache_rows), 0)
        kept_ref[...] = jnp.where(row == target, 1.0, 0.0).astype(bf16)
        for half in range(2):
            offset = lax.broadcasted_iota(jnp.int32, (block_len, HEAD_SIZE), 0)
            at = facts.block(slot, half) * block_len + offset
            live_ref[columns(half, block_len)] = jnp.where(at < length, 1.0, 0.0)

    shapes = [
        jax.ShapeDtypeStruct((rows, 2 * Q_DEV * HEAD_SIZE), f32),
        jax.ShapeDtypeStruct((cache_rows, cache_rows), bf16),
        jax.ShapeDtypeStruct((rows, HEAD_SIZE), f32),
    ]
    return call(body, shapes, [SMEM] * 3 + [VMEM] * 3, "own_part")(facts_row, *lens, *operands)


def receive(key_in, value_in, select, angles):
    others = len(key_in)
    rows, width = key_in[0].shape
    block_len = rows // 2
    piece = select.shape[0] // HEAD_DIVISIONS

    def body(select_ref, angle_ref, *refs):
        k_refs, v_refs, refs = refs[:others], refs[others : 2 * others], refs[2 * others :]
        kr_refs, e_refs = refs[:others], refs[others:]
        for turn in range(others):
            for half in range(2):
                part = columns(half, block_len)
                there = angle_ref[turn, half, 0], angle_ref[turn, half, 1]
                for head in range(KV_DEV):
                    kr_refs[turn][part, columns(head)] = turned(
                        k_refs[turn][part, columns(head)], there
                    ).astype(bf16)
            for kind, source in enumerate((kr_refs[turn], v_refs[turn])):
                chosen = dot(select_ref[...], source[...]).astype(bf16)
                for m in range(HEAD_DIVISIONS):
                    e_refs[m][columns(kind * others + turn, piece)] = chosen[columns(m, piece)]

    shapes = [jax.ShapeDtypeStruct((rows, width), bf16) for _ in range(others)]
    shapes += [
        jax.ShapeDtypeStruct((2 * others * piece, width), bf16) for _ in range(HEAD_DIVISIONS)
    ]
    outs = call(body, shapes, [VMEM] * (2 + 2 * others), "receive")(
        select, angles, *key_in, *value_in
    )
    return outs[:others], outs[others:]


def attend(facts_row, facts_of, query_rot, acc, key_rot, value_in, live):
    rows = query_rot.shape[0]
    block_len = rows // 2
    others = len(key_rot)
    slots = facts_of(None).slots

    def body(facts_ref, q_ref, acc_ref, live_ref, *refs):
        k_refs, v_refs, out_ref = refs[:others], refs[others : 2 * others], refs[2 * others]
        facts = facts_of(facts_ref)
        slot = slot_and_head_group()[0]
        low, high = facts.halves(slot)
        low_rows, high_rows = rows_at(low, block_len), rows_at(high, block_len)
        for head in range(Q_DEV):
            key_head = columns(head * KV_DEV // Q_DEV)
            both = columns(head, 2 * HEAD_SIZE)
            low_sum, high_sum = acc_ref[low_rows, both], acc_ref[high_rows, both]
            for turn in range(1, slots):
                source = (slot - turn + slots) % slots
                source_low, source_high = facts.halves(source)
                outer = facts.block(slot, low) < facts.block(source, source_low)

                def tile(half, other):
                    queries = q_ref[rows_at(half, block_len), columns(head)]
                    there = rows_at(other, block_len)
                    expo = expo_of(dot_t(queries, k_refs[turn - 1][there, key_head]))
                    return dot(expo.astype(bf16), beside_ones(v_refs[turn - 1][there, key_head]))

                either = tile(jnp.where(outer, high, low), source_low)
                upper = tile(high, jnp.where(outer, source_high, source_low))
                low_sum = low_sum + jnp.where(outer, 0.0, either)
                high_sum = high_sum + upper + jnp.where(outer, either, 0.0)
            for part, total in ((low_rows, low_sum), (high_rows, high_sum)):
                scale = live_ref[part] / total[:, HEAD_SIZE:]
                out_ref[part, columns(head)] = (total[:, :HEAD_SIZE] * scale).astype(bf16)

    shape = jax.ShapeDtypeStruct(query_rot.shape, bf16)
    specs = [SMEM] + [VMEM] * (3 + 2 * others)
    return call(body, shape, specs, "attend", cost=10**10)(
        facts_row, query_rot, acc, live, *key_rot, *value_in
    )


def cache_part(early, late, kept):
    cache_rows = kept.shape[0]
    piece = early[0].shape[0] // 2
    width = early[0].shape[1]

    def body(kept_ref, *refs):
        f_refs, s_refs, out_ref = refs[:4], refs[4:8], refs[8]
        head_group = slot_and_head_group()[1]
        later = cache_rows - piece
        for m in range(HEAD_DIVISIONS):
            for kind in range(2):
                lines = jnp.concatenate(
                    [f_refs[m][columns(kind, piece)], s_refs[m][columns(kind, later)]], axis=0
                )
                column = ((head_group ^ m) + kind * HEAD_DIVISIONS) * width
                out_ref[:, pl.ds(pl.multiple_of(column, HEAD_SIZE), width)] = dot(
                    kept_ref[...], lines
                ).astype(bf16)

    shape = jax.ShapeDtypeStruct((cache_rows, 2 * HEAD_DIVISIONS * width), bf16)
    return call(body, shape, [VMEM] * 9, "cache_part")(kept, *early, *late)


def on_device(queries, keys, values, block_map, lengths, group_of_prompt, decode_rank):
    block_len = queries.shape[2] // 2
    slots = block_map.shape[1]
    q, k, v = queries[0, 0], keys[0, 0], values[0, 0]
    tables = rotary_tables(block_len, 2 * slots)

    def to_slots(part):
        return [shifted(part, "blk", HEAD_DIVISIONS * t) for t in range(1, slots)]

    def hand_on(pieces):
        return [pieces[0]] + [crossed(pieces[m], "blk", m) for m in range(1, HEAD_DIVISIONS)]

    key_in, value_in = to_slots(k), to_slots(v)
    facts_row, facts_of, block, operands, (select, angles), early = prepare(
        q,
        k,
        v,
        block_map,
        decode_rank,
        group_of_prompt,
        tables,
        lengths,
        crossed(lengths, "req", 1),
    )
    early = hand_on(early)
    span, groups = 2, lax.axis_size("req")
    while 2 * span < groups:
        other = crossed(block, "req", span)
        upper = (lax.axis_index("req") & span) > 0
        block = jnp.where(
            upper, jnp.concatenate([other, block]), jnp.concatenate([block, other])
        )
        span = 2 * span
    lens = (block, crossed(block, "req", span))
    acc, kept, live = own_part(facts_row, facts_of, operands, lens)
    key_rot, late = receive(key_in, value_in, select, angles)
    late = hand_on(late)
    attended = attend(facts_row, facts_of, operands[0], acc, key_rot, value_in, live)
    cache = cache_part(early, late, kept)
    return (attended[None, None], cache[None])


def solution(mesh):
    placed = (
        P("req", "blk", None, None),
        P("req", "blk", None, None),
        P("req", "blk", None, None),
        P("req", None, None),
        P("req"),
        P(),
        P("req", None),
    )
    return jax.shard_map(
        on_device,
        mesh=mesh,
        in_specs=placed,
        out_specs=(P("req", "blk", None, None), P("req", "blk", None)),
        check_vma=False,
    )
```

```python
import math

import jax
import jax.numpy as jnp
import numpy as np
from jax import lax
from jax.experimental import pallas as pl
from jax.experimental.pallas import tpu as pltpu
from jax.sharding import PartitionSpec as P

QUERY_HEADS = 16
KEY_VALUE_HEADS = 8
HEAD_SIZE = 128
HEAD_DIVISIONS = 4
Q_DEV = 4
KV_DEV = 2
KV_WIDTH = KV_DEV * HEAD_SIZE

cap_value = 50.0
query_scale = 1.0 / 12.0
HAND_ORDER = (0, 2, 3, 1)
rope_base = 10000.0
VMEM_BYTES = 48 * 1024 * 1024

f32 = jnp.float32
bf16 = jnp.bfloat16
SMEM = pl.BlockSpec(memory_space=pltpu.SMEM)
VMEM = pl.BlockSpec(memory_space=pltpu.VMEM)
HBM = pl.BlockSpec(memory_space=pltpu.HBM)


def shifted(shard, axis, by):
    peers = lax.axis_size(axis)
    return lax.ppermute(shard, axis, [(i, (i + by) % peers) for i in range(peers)])


def crossed(shard, axis, by):
    peers = lax.axis_size(axis)
    return lax.ppermute(shard, axis, [(i, i ^ by) for i in range(peers)])


def rotary_tables(block_len, block_count):
    half = HEAD_SIZE // 2
    frequency = np.exp(
        np.float32(-math.log(rope_base)) * (2.0 * np.arange(half, dtype=np.float32)) / HEAD_SIZE
    ).astype(np.float64)

    def table(positions):
        angles = positions.astype(np.float64)[:, None] * frequency[None, :]
        cosine, sine = np.cos(angles), np.sin(angles)
        return np.stack(
            [np.concatenate([cosine, cosine], 1), np.concatenate([-sine, sine], 1)]
        ).astype(np.float32)

    return table(np.arange(block_len)), table(np.arange(block_count) * block_len)


def block_angles(row_table, block_table, block):
    row_cos, row_sin = row_table[0], row_table[1]
    blk_cos, blk_sin = block_table[0, pl.ds(block, 1)], block_table[1, pl.ds(block, 1)]
    return row_cos * blk_cos - row_sin * blk_sin, row_sin * blk_cos + row_cos * blk_sin


def turned(head, angles):
    x = head.astype(f32)
    return x * angles[0] + pltpu.roll(x, HEAD_SIZE // 2, 1) * angles[1]


def order_matrix(rank_of, slot, head_group, out_rows, rows, residues):
    row_ids = lax.broadcasted_iota(jnp.int32, (1, rows), 1)
    residue = row_ids % residues
    rank = jnp.zeros_like(row_ids)
    for r in range(residues):
        rank = jnp.where(residue == r, rank_of(r), rank)
    ahead = (rank - HEAD_DIVISIONS * slot + residues) % residues
    ahead = jnp.where(ahead < HEAD_DIVISIONS, ahead ^ head_group, ahead)
    index = ahead * (rows // residues) + row_ids // residues
    out_ids = lax.broadcasted_iota(jnp.int32, (out_rows, rows), 0)
    return jnp.where(out_ids == index, 1.0, 0.0).astype(bf16)


def dot(a, b):
    return jnp.dot(a, b, preferred_element_type=f32)


def dot_t(a, b):
    return lax.dot_general(a, b, (((1,), (1,)), ((), ())), preferred_element_type=f32)


def expo_of(scores):
    return jnp.exp2(cap_value * math.log2(math.e) * jnp.tanh(scores * (1.0 / cap_value)))


def columns(index, width=HEAD_SIZE):
    return slice(index * width, (index + 1) * width)


def call(body, out_shape, in_specs, name, scratch=(), out_specs=None, cost=1000):
    return pl.pallas_call(
        body,
        out_shape=out_shape,
        in_specs=in_specs,
        out_specs=jax.tree.map(lambda _: VMEM, out_shape) if out_specs is None else out_specs,
        scratch_shapes=scratch,
        compiler_params=pltpu.CompilerParams(vmem_limit_bytes=VMEM_BYTES),
        cost_estimate=pl.CostEstimate(flops=cost, bytes_accessed=1000, transcendentals=0),
        name=name,
    )


def in_hbm(arrays):
    return [pltpu.with_memory_space_constraint(x, pltpu.HBM) for x in arrays]


def rows_at(index, size):
    return pl.ds(pl.multiple_of(index * size, size), size)


def beside_ones(values):
    return jnp.concatenate([values, jnp.ones(values.shape, bf16)], axis=1)


class Facts:
    def __init__(self, ref, slots, residues, groups):
        self.ref, self.slots, self.residues, self.groups = ref, slots, residues, groups
        self.size = 2 * slots + residues + groups

    def block(self, slot, half):
        return self.ref[0, 2 * slot + half]

    def rank(self, residue):
        return self.ref[0, 2 * self.slots + residue]

    def owner(self, prompt):
        return self.ref[0, 2 * self.slots + self.residues + prompt]

    def store(self, map_ref, rank_ref, owner_ref):
        for slot in range(self.slots):
            for half in range(2):
                self.ref[0, 2 * slot + half] = map_ref[0, slot, half]
        for residue in range(self.residues):
            self.ref[0, 2 * self.slots + residue] = rank_ref[0, residue]
        for prompt in range(self.groups):
            self.ref[0, 2 * self.slots + self.residues + prompt] = owner_ref[prompt]

    def halves(self, slot):
        high = jnp.where(self.block(slot, 1) > self.block(slot, 0), 1, 0)
        return 1 - high, high


def slot_and_head_group():
    member = lax.axis_index("blk")
    return member // HEAD_DIVISIONS, member % HEAD_DIVISIONS


def prepare(queries, keys, values, table, decode_rank, owner, tables, own_length, near_length):
    rows, width = keys.shape
    block_len = rows // 2
    slots = table.shape[1]
    residues = decode_rank.shape[1]
    piece = rows // residues
    arrays = (keys, values, queries, *tables, table, decode_rank, owner)
    count = len(arrays)
    facts_of = lambda ref: Facts(ref, slots, residues, owner.shape[0])

    def body(own_ref, near_ref, *refs):
        inputs, refs = refs[:count], refs[count:]
        facts_ref, pair_ref, q_ref, kr_ref, v_ref, row_ref, blk_ref, select_ref = refs[:8]
        e_refs, refs = refs[8:12], refs[12:]
        k_ref, map_ref, rank_ref, owner_ref, sems = refs
        targets = (k_ref, v_ref, q_ref, row_ref, blk_ref, map_ref, rank_ref, owner_ref)
        copies = []
        for index in range(count):
            copies.append(pltpu.make_async_copy(inputs[index], targets[index], sems.at[index]))
            copies[-1].start()
        slot, head_group = slot_and_head_group()
        odd = lax.axis_index("req") % 2 == 1
        pair_ref[0] = jnp.where(odd, near_ref[0], own_ref[0])
        pair_ref[1] = jnp.where(odd, own_ref[0], near_ref[0])
        for index in (0, 3, 4, 5, 6, 7):
            copies[index].wait()
        facts_of(facts_ref).store(map_ref, rank_ref, owner_ref)
        for half in range(2):
            part = columns(half, block_len)
            angles = block_angles(row_ref, blk_ref, map_ref[0, slot, half])
            for head in range(KV_DEV):
                kr_ref[part, columns(head)] = turned(k_ref[part, columns(head)], angles).astype(bf16)
        select = order_matrix(
            lambda r: rank_ref[0, r], slot, head_group, rows // slots, rows, residues
        )
        select_ref[...] = select
        copies[1].wait()
        for kind, source in enumerate((kr_ref, v_ref)):
            chosen = dot(select, source[...]).astype(bf16)
            for m in range(HEAD_DIVISIONS):
                e_refs[m][columns(kind, piece)] = chosen[columns(m, piece)]
        copies[2].wait()

    shapes = [
        jax.ShapeDtypeStruct((1, facts_of(None).size), jnp.int32),
        jax.ShapeDtypeStruct((2,), jnp.int32),
        jax.ShapeDtypeStruct(queries.shape, bf16),
        jax.ShapeDtypeStruct(keys.shape, bf16),
        jax.ShapeDtypeStruct(values.shape, bf16),
        jax.ShapeDtypeStruct(tables[0].shape, f32),
        jax.ShapeDtypeStruct(tables[1].shape, f32),
        jax.ShapeDtypeStruct((rows // slots, rows), bf16),
    ]
    shapes += [jax.ShapeDtypeStruct((2 * piece, width), bf16) for _ in range(HEAD_DIVISIONS)]
    scratch = [pltpu.VMEM(keys.shape, keys.dtype)]
    scratch += [pltpu.SMEM(x.shape, x.dtype) for x in (table, decode_rank, owner)]
    scratch.append(pltpu.SemaphoreType.DMA((count,)))
    outs = call(
        body,
        shapes,
        [SMEM] * 2 + [HBM] * count,
        "prepare",
        scratch,
        out_specs=[SMEM] * 2 + [VMEM] * (len(shapes) - 2),
    )(own_length, near_length, *in_hbm(arrays))
    return outs[0], facts_of, outs[1], outs[2:5], outs[5:7], outs[7], outs[8:]


def own_part(facts_row, facts_of, operands, tables, lens):
    queries = operands[0]
    rows = queries.shape[0]
    block_len = rows // 2
    sizes = facts_of(None)
    slots, residues, groups = sizes.slots, sizes.residues, sizes.groups
    run = block_len // residues
    cache_rows = 2 * slots * run

    def body(facts_ref, here_ref, there_ref, q_ref, kr_ref, v_ref, row_ref, blk_ref, *refs):
        qr_ref, acc_ref, kept_ref, live_ref, angle_ref = refs
        facts = facts_of(facts_ref)
        slot = slot_and_head_group()[0]
        group = lax.axis_index("req")
        for half in range(2):
            part = columns(half, block_len)
            angles = block_angles(row_ref, blk_ref, facts.block(slot, half))
            for head in range(Q_DEV):
                qr_ref[part, columns(head)] = (
                    turned(q_ref[part, columns(head)], angles) * query_scale
                ).astype(bf16)
            for turn in range(1, slots):
                block = facts.block((slot - turn + slots) % slots, half)
                other = block_angles(row_ref, blk_ref, block)
                angle_ref[turn - 1, half, 0] = other[0]
                angle_ref[turn - 1, half, 1] = other[1]
        low, high = facts.halves(slot)
        low, high = rows_at(low, block_len), rows_at(high, block_len)
        row = lax.broadcasted_iota(jnp.int32, (block_len, block_len), 0)
        col = lax.broadcasted_iota(jnp.int32, (block_len, block_len), 1)
        for head in range(Q_DEV):
            key_head = columns(head * KV_DEV // Q_DEV)
            both = columns(head, 2 * HEAD_SIZE)

            def tile(q_part, k_part, diagonal):
                expo = expo_of(dot_t(qr_ref[q_part, columns(head)], kr_ref[k_part, key_head]))
                if diagonal:
                    expo = jnp.where(col <= row, expo, 0.0)
                return dot(expo.astype(bf16), beside_ones(v_ref[k_part, key_head]))

            acc_ref[low, both] = tile(low, low, True)
            acc_ref[high, both] = tile(high, high, True) + tile(high, low, False)

        col = lax.broadcasted_iota(jnp.int32, (1, cache_rows), 1)
        part, offset = col // run, col % run
        target = jnp.zeros_like(col)
        for turn in range(slots):
            for half in range(2):
                block = facts.block((slot - turn + slots) % slots, half)
                target = jnp.where(part == 2 * turn + half, block * run + offset, target)
        length = 0
        half_count = groups // 2
        for index in range(half_count):
            same = (group & half_count) | index
            length = length + jnp.where(facts.owner(same) == group, here_ref[index], 0)
            other = same ^ half_count
            length = length + jnp.where(facts.owner(other) == group, there_ref[index], 0)
        residue = 0
        for r in range(1, residues):
            residue = jnp.where(facts.rank(r) == lax.axis_index("blk"), r, residue)
        target = jnp.where(target * residues + residue < length, target, -1)
        row = lax.broadcasted_iota(jnp.int32, (cache_rows, cache_rows), 0)
        kept_ref[...] = jnp.where(row == target, 1.0, 0.0).astype(bf16)
        for half in range(2):
            offset = lax.broadcasted_iota(jnp.int32, (block_len, HEAD_SIZE), 0)
            at = facts.block(slot, half) * block_len + offset
            live_ref[columns(half, block_len)] = jnp.where(at < length, 1.0, 0.0)

    shapes = [
        jax.ShapeDtypeStruct(queries.shape, bf16),
        jax.ShapeDtypeStruct((rows, 2 * Q_DEV * HEAD_SIZE), f32),
        jax.ShapeDtypeStruct((cache_rows, cache_rows), bf16),
        jax.ShapeDtypeStruct((rows, HEAD_SIZE), f32),
        jax.ShapeDtypeStruct((slots - 1, 2, 2, block_len, HEAD_SIZE), f32),
    ]
    return call(body, shapes, [SMEM] * 3 + [VMEM] * 5, "own_part")(
        facts_row, *lens, *operands, *tables
    )


def tiles_of(facts, slot, source):
    low, high = facts.halves(slot)
    source_low, source_high = facts.halves(source)
    outer = facts.block(slot, low) < facts.block(source, source_low)
    first = (jnp.where(outer, high, low), source_low)
    second = (high, jnp.where(outer, source_high, source_low))
    return outer, first, second


def receive_keys(facts_row, facts_of, key_in, query_rot, select, angles):
    others = len(key_in)
    rows, width = key_in[0].shape
    block_len = rows // 2
    slots = facts_of(None).slots

    def body(facts_ref, q_ref, select_ref, angle_ref, *refs):
        k_refs, refs = refs[:others], refs[others:]
        w_refs, chosen_ref, kr_ref = refs[:others], refs[others], refs[others + 1]
        facts = facts_of(facts_ref)
        slot = slot_and_head_group()[0]
        for turn in range(1, slots):
            for half in range(2):
                part = columns(half, block_len)
                there = angle_ref[turn - 1, half, 0], angle_ref[turn - 1, half, 1]
                for head in range(KV_DEV):
                    kr_ref[part, columns(head)] = turned(
                        k_refs[turn - 1][part, columns(head)], there
                    ).astype(bf16)
            chosen_ref[turn - 1] = dot(select_ref[...], kr_ref[...]).astype(bf16)
            _, *tiles = tiles_of(facts, slot, (slot - turn + slots) % slots)
            for index, (half, other) in enumerate(tiles):
                for head in range(Q_DEV):
                    key_head = columns(head * KV_DEV // Q_DEV)
                    queries = q_ref[rows_at(half, block_len), columns(head)]
                    expo = expo_of(dot_t(queries, kr_ref[rows_at(other, block_len), key_head]))
                    w_refs[turn - 1][index, head] = expo.astype(bf16)

    shapes = [
        jax.ShapeDtypeStruct((2, Q_DEV, block_len, block_len), bf16) for _ in range(others)
    ]
    shapes.append(jax.ShapeDtypeStruct((others, select.shape[0], width), bf16))
    scratch = [pltpu.VMEM((rows, width), bf16)]
    outs = call(body, shapes, [SMEM] + [VMEM] * (3 + others), "receive_keys", scratch)(
        facts_row, query_rot, select, angles, *key_in
    )
    return outs[:others], outs[others]


def receive_values(value_in, select, key_chosen):
    others = len(value_in)
    rows, width = value_in[0].shape
    piece = select.shape[0] // HEAD_DIVISIONS

    def body(select_ref, key_ref, *refs):
        v_refs, e_refs = refs[:others], refs[others:]
        for turn in range(others):
            chosen = dot(select_ref[...], v_refs[turn][...]).astype(bf16)
            for m in range(HEAD_DIVISIONS):
                e_refs[m][columns(turn, piece)] = key_ref[turn, columns(m, piece)]
                e_refs[m][columns(others + turn, piece)] = chosen[columns(m, piece)]

    shapes = [
        jax.ShapeDtypeStruct((2 * others * piece, width), bf16) for _ in range(HEAD_DIVISIONS)
    ]
    return call(body, shapes, [VMEM] * (2 + others), "receive_values")(select, key_chosen, *value_in)


def attend(facts_row, facts_of, weights, acc, value_in, live):
    rows = live.shape[0]
    block_len = rows // 2
    others = len(weights)
    slots = facts_of(None).slots

    def body(facts_ref, acc_ref, live_ref, *refs):
        w_refs, v_refs, out_ref = refs[:others], refs[others : 2 * others], refs[2 * others]
        facts = facts_of(facts_ref)
        slot = slot_and_head_group()[0]
        low, high = facts.halves(slot)
        low_rows, high_rows = rows_at(low, block_len), rows_at(high, block_len)
        for head in range(Q_DEV):
            key_head = columns(head * KV_DEV // Q_DEV)
            both = columns(head, 2 * HEAD_SIZE)
            low_sum, high_sum = acc_ref[low_rows, both], acc_ref[high_rows, both]
            for turn in range(1, slots):
                outer, *tiles = tiles_of(facts, slot, (slot - turn + slots) % slots)
                either, upper = [
                    dot(
                        w_refs[turn - 1][index, head],
                        beside_ones(v_refs[turn - 1][rows_at(other, block_len), key_head]),
                    )
                    for index, (_, other) in enumerate(tiles)
                ]
                low_sum = low_sum + jnp.where(outer, 0.0, either)
                high_sum = high_sum + upper + jnp.where(outer, either, 0.0)
            for part, total in ((low_rows, low_sum), (high_rows, high_sum)):
                scale = live_ref[part] / total[:, HEAD_SIZE:]
                out_ref[part, columns(head)] = (total[:, :HEAD_SIZE] * scale).astype(bf16)

    shape = jax.ShapeDtypeStruct((rows, Q_DEV * HEAD_SIZE), bf16)
    specs = [SMEM] + [VMEM] * (2 + 2 * others)
    return call(body, shape, specs, "attend", cost=10**10)(
        facts_row, acc, live, *weights, *value_in
    )


def cache_part(early, late, kept):
    cache_rows = kept.shape[0]
    piece = early[0].shape[0] // 2
    width = early[0].shape[1]

    def body(kept_ref, *refs):
        f_refs, s_refs, out_ref = refs[:4], refs[4:8], refs[8]
        head_group = slot_and_head_group()[1]
        later = cache_rows - piece
        for index, m in enumerate(HAND_ORDER):
            for kind in range(2):
                lines = jnp.concatenate(
                    [f_refs[index][columns(kind, piece)], s_refs[index][columns(kind, later)]], axis=0
                )
                column = ((head_group ^ m) + kind * HEAD_DIVISIONS) * width
                out_ref[:, pl.ds(pl.multiple_of(column, HEAD_SIZE), width)] = dot(
                    kept_ref[...], lines
                ).astype(bf16)

    shape = jax.ShapeDtypeStruct((cache_rows, 2 * HEAD_DIVISIONS * width), bf16)
    return call(body, shape, [VMEM] * 9, "cache_part")(kept, *early, *late)


def on_device(queries, keys, values, block_map, lengths, group_of_prompt, decode_rank):
    block_len = queries.shape[2] // 2
    slots = block_map.shape[1]
    q, k, v = queries[0, 0], keys[0, 0], values[0, 0]
    tables = rotary_tables(block_len, 2 * slots)

    def to_slots(part):
        return [shifted(part, "blk", HEAD_DIVISIONS * t) for t in range(1, slots)]

    def hand_on(pieces):
        return [pieces[0]] + [crossed(pieces[m], "blk", m) for m in HAND_ORDER[1:]]

    key_in = to_slots(k)
    facts_row, facts_of, block, operands, tables, select, early = prepare(
        q,
        k,
        v,
        block_map,
        decode_rank,
        group_of_prompt,
        tables,
        lengths,
        crossed(lengths, "req", 1),
    )
    value_in = to_slots(operands[2])
    early = hand_on(early)
    span, groups = 2, lax.axis_size("req")
    while 2 * span < groups:
        other = crossed(block, "req", span)
        upper = (lax.axis_index("req") & span) > 0
        block = jnp.where(
            upper, jnp.concatenate([other, block]), jnp.concatenate([block, other])
        )
        span = 2 * span
    lens = (block, crossed(block, "req", span))
    query_rot, acc, kept, live, angles = own_part(facts_row, facts_of, operands, tables, lens)
    weights, chosen = receive_keys(facts_row, facts_of, key_in, query_rot, select, angles)
    late = hand_on(receive_values(value_in, select, chosen))
    attended = attend(facts_row, facts_of, weights, acc, value_in, live)
    cache = cache_part(early, late, kept)
    return (attended[None, None], cache[None])


def solution(mesh):
    placed = (
        P("req", "blk", None, None),
        P("req", "blk", None, None),
        P("req", "blk", None, None),
        P("req", None, None),
        P("req"),
        P(),
        P("req", None),
    )
    return jax.shard_map(
        on_device,
        mesh=mesh,
        in_specs=placed,
        out_specs=(P("req", "blk", None, None), P("req", "blk", None)),
        check_vma=False,
    )
```

```python
import math

import jax
import jax.numpy as jnp
import numpy as np
from jax import lax
from jax.experimental import pallas as pl
from jax.experimental.pallas import tpu as pltpu
from jax.sharding import PartitionSpec as P

QUERY_HEADS = 16
KEY_VALUE_HEADS = 8
HEAD_SIZE = 128
HEAD_DIVISIONS = 4
Q_DEV = 4
KV_DEV = 2
KV_WIDTH = KV_DEV * HEAD_SIZE

cap_value = 50.0
query_scale = 1.0 / 12.0
HAND_ORDER = (0, 2, 3, 1)
rope_base = 10000.0
VMEM_BYTES = 48 * 1024 * 1024

f32 = jnp.float32
bf16 = jnp.bfloat16
SMEM = pl.BlockSpec(memory_space=pltpu.SMEM)
VMEM = pl.BlockSpec(memory_space=pltpu.VMEM)
HBM = pl.BlockSpec(memory_space=pltpu.HBM)


def shifted(shard, axis, by):
    peers = lax.axis_size(axis)
    return lax.ppermute(shard, axis, [(i, (i + by) % peers) for i in range(peers)])


def crossed(shard, axis, by):
    peers = lax.axis_size(axis)
    return lax.ppermute(shard, axis, [(i, i ^ by) for i in range(peers)])


def rotary_tables(block_len, block_count):
    half = HEAD_SIZE // 2
    frequency = np.exp(
        np.float32(-math.log(rope_base)) * (2.0 * np.arange(half, dtype=np.float32)) / HEAD_SIZE
    ).astype(np.float64)

    def table(positions):
        angles = positions.astype(np.float64)[:, None] * frequency[None, :]
        cosine, sine = np.cos(angles), np.sin(angles)
        return np.stack(
            [np.concatenate([cosine, cosine], 1), np.concatenate([-sine, sine], 1)]
        ).astype(np.float32)

    return table(np.arange(block_len)), table(np.arange(block_count) * block_len)


def block_angles(row_table, block_table, block):
    row_cos, row_sin = row_table[0], row_table[1]
    blk_cos, blk_sin = block_table[0, pl.ds(block, 1)], block_table[1, pl.ds(block, 1)]
    return row_cos * blk_cos - row_sin * blk_sin, row_sin * blk_cos + row_cos * blk_sin


def turned(head, angles):
    x = head.astype(f32)
    return x * angles[0] + pltpu.roll(x, HEAD_SIZE // 2, 1) * angles[1]


def order_matrix(rank_of, slot, head_group, out_rows, rows, residues):
    row_ids = lax.broadcasted_iota(jnp.int32, (1, rows), 1)
    residue = row_ids % residues
    rank = jnp.zeros_like(row_ids)
    for r in range(residues):
        rank = jnp.where(residue == r, rank_of(r), rank)
    ahead = (rank - HEAD_DIVISIONS * slot + residues) % residues
    ahead = jnp.where(ahead < HEAD_DIVISIONS, ahead ^ head_group, ahead)
    index = ahead * (rows // residues) + row_ids // residues
    out_ids = lax.broadcasted_iota(jnp.int32, (out_rows, rows), 0)
    return jnp.where(out_ids == index, 1.0, 0.0).astype(bf16)


def dot(a, b):
    return jnp.dot(a, b, preferred_element_type=f32)


def dot_t(a, b):
    return lax.dot_general(a, b, (((1,), (1,)), ((), ())), preferred_element_type=f32)


def expo_of(scores):
    return jnp.exp2(cap_value * math.log2(math.e) * jnp.tanh(scores * (1.0 / cap_value)))


def columns(index, width=HEAD_SIZE):
    return slice(index * width, (index + 1) * width)


def call(body, out_shape, in_specs, name, scratch=(), out_specs=None, cost=1000):
    return pl.pallas_call(
        body,
        out_shape=out_shape,
        in_specs=in_specs,
        out_specs=jax.tree.map(lambda _: VMEM, out_shape) if out_specs is None else out_specs,
        scratch_shapes=scratch,
        compiler_params=pltpu.CompilerParams(vmem_limit_bytes=VMEM_BYTES),
        cost_estimate=pl.CostEstimate(flops=cost, bytes_accessed=1000, transcendentals=0),
        name=name,
    )


def in_hbm(arrays):
    return [pltpu.with_memory_space_constraint(x, pltpu.HBM) for x in arrays]


def rows_at(index, size):
    return pl.ds(pl.multiple_of(index * size, size), size)


def beside_ones(values):
    return jnp.concatenate([values, jnp.ones(values.shape, bf16)], axis=1)


class Facts:
    def __init__(self, ref, slots, residues, groups):
        self.ref, self.slots, self.residues, self.groups = ref, slots, residues, groups
        self.size = 2 * slots + residues + groups

    def block(self, slot, half):
        return self.ref[0, 2 * slot + half]

    def rank(self, residue):
        return self.ref[0, 2 * self.slots + residue]

    def owner(self, prompt):
        return self.ref[0, 2 * self.slots + self.residues + prompt]

    def store(self, map_ref, rank_ref, owner_ref):
        for slot in range(self.slots):
            for half in range(2):
                self.ref[0, 2 * slot + half] = map_ref[0, slot, half]
        for residue in range(self.residues):
            self.ref[0, 2 * self.slots + residue] = rank_ref[0, residue]
        for prompt in range(self.groups):
            self.ref[0, 2 * self.slots + self.residues + prompt] = owner_ref[prompt]

    def halves(self, slot):
        high = jnp.where(self.block(slot, 1) > self.block(slot, 0), 1, 0)
        return 1 - high, high


def slot_and_head_group():
    member = lax.axis_index("blk")
    return member // HEAD_DIVISIONS, member % HEAD_DIVISIONS


def prepare(queries, keys, values, table, decode_rank, owner, tables, own_length, near_length):
    rows, width = keys.shape
    block_len = rows // 2
    slots = table.shape[1]
    residues = decode_rank.shape[1]
    piece = rows // residues
    first = block_len // slots
    arrays = (keys, values, queries, *tables, table, decode_rank, owner)
    count = len(arrays)
    facts_of = lambda ref: Facts(ref, slots, residues, owner.shape[0])

    def body(own_ref, near_ref, *refs):
        inputs, refs = refs[:count], refs[count:]
        facts_ref, pair_ref, q_ref, kr_ref, v_ref, row_ref, blk_ref, select_ref, order_ref = refs[:9]
        e_refs, refs = refs[9:13], refs[13:]
        sent_refs, refs = refs[: 2 * slots - 2], refs[2 * slots - 2 :]
        k_ref, map_ref, rank_ref, owner_ref, sems = refs
        targets = (k_ref, v_ref, q_ref, row_ref, blk_ref, map_ref, rank_ref, owner_ref)
        copies = []
        for index in range(count):
            copies.append(pltpu.make_async_copy(inputs[index], targets[index], sems.at[index]))
            copies[-1].start()
        slot, head_group = slot_and_head_group()
        odd = lax.axis_index("req") % 2 == 1
        pair_ref[0] = jnp.where(odd, near_ref[0], own_ref[0])
        pair_ref[1] = jnp.where(odd, own_ref[0], near_ref[0])
        for index in (0, 3, 4, 5, 6, 7):
            copies[index].wait()
        facts_of(facts_ref).store(map_ref, rank_ref, owner_ref)
        for half in range(2):
            part = columns(half, block_len)
            angles = block_angles(row_ref, blk_ref, map_ref[0, slot, half])
            for head in range(KV_DEV):
                kr_ref[part, columns(head)] = turned(k_ref[part, columns(head)], angles).astype(bf16)
        select = order_matrix(
            lambda r: rank_ref[0, r], slot, head_group, rows // slots, rows, residues
        )
        select_ref[...] = select
        copies[1].wait()
        for turn in range(1, slots):
            order = order_matrix(
                lambda r: rank_ref[0, r],
                (slot + turn) % slots,
                head_group,
                block_len,
                block_len,
                residues,
            )
            for half in range(2):
                moved = dot(order, v_ref[columns(half, block_len)]).astype(bf16)
                sent_refs[2 * turn - 2][columns(half, first)] = moved[:first]
                sent_refs[2 * turn - 1][columns(half, block_len - first)] = moved[first:]
        order_ref[...] = order_matrix(
            lambda r: rank_ref[0, r], slot, head_group, block_len, block_len, residues
        )
        for kind, source in enumerate((kr_ref, v_ref)):
            chosen = dot(select, source[...]).astype(bf16)
            for m in range(HEAD_DIVISIONS):
                e_refs[m][columns(kind, piece)] = chosen[columns(m, piece)]
        copies[2].wait()

    shapes = [
        jax.ShapeDtypeStruct((1, facts_of(None).size), jnp.int32),
        jax.ShapeDtypeStruct((2,), jnp.int32),
        jax.ShapeDtypeStruct(queries.shape, bf16),
        jax.ShapeDtypeStruct(keys.shape, bf16),
        jax.ShapeDtypeStruct(values.shape, bf16),
        jax.ShapeDtypeStruct(tables[0].shape, f32),
        jax.ShapeDtypeStruct(tables[1].shape, f32),
        jax.ShapeDtypeStruct((rows // slots, rows), bf16),
        jax.ShapeDtypeStruct((block_len, block_len), bf16),
    ]
    shapes += [jax.ShapeDtypeStruct((2 * piece, width), bf16) for _ in range(HEAD_DIVISIONS)]
    for _ in range(1, slots):
        shapes.append(jax.ShapeDtypeStruct((2 * first, width), bf16))
        shapes.append(jax.ShapeDtypeStruct((2 * (block_len - first), width), bf16))
    scratch = [pltpu.VMEM(keys.shape, keys.dtype)]
    scratch += [pltpu.SMEM(x.shape, x.dtype) for x in (table, decode_rank, owner)]
    scratch.append(pltpu.SemaphoreType.DMA((count,)))
    outs = call(
        body,
        shapes,
        [SMEM] * 2 + [HBM] * count,
        "prepare",
        scratch,
        out_specs=[SMEM] * 2 + [VMEM] * (len(shapes) - 2),
    )(own_length, near_length, *in_hbm(arrays))
    return outs[0], facts_of, outs[1], outs[2:5], outs[5:7], outs[7:9], outs[9:13], outs[13:]


def own_part(facts_row, facts_of, operands, tables, lens):
    queries = operands[0]
    rows = queries.shape[0]
    block_len = rows // 2
    sizes = facts_of(None)
    slots, residues, groups = sizes.slots, sizes.residues, sizes.groups
    run = block_len // residues
    cache_rows = 2 * slots * run

    def body(facts_ref, here_ref, there_ref, q_ref, kr_ref, v_ref, row_ref, blk_ref, *refs):
        qr_ref, acc_ref, kept_ref, live_ref, angle_ref = refs
        facts = facts_of(facts_ref)
        slot = slot_and_head_group()[0]
        group = lax.axis_index("req")
        for half in range(2):
            part = columns(half, block_len)
            angles = block_angles(row_ref, blk_ref, facts.block(slot, half))
            for head in range(Q_DEV):
                qr_ref[part, columns(head)] = (
                    turned(q_ref[part, columns(head)], angles) * query_scale
                ).astype(bf16)
            for turn in range(1, slots):
                block = facts.block((slot - turn + slots) % slots, half)
                other = block_angles(row_ref, blk_ref, block)
                angle_ref[turn - 1, half, 0] = other[0]
                angle_ref[turn - 1, half, 1] = other[1]
        low, high = facts.halves(slot)
        low, high = rows_at(low, block_len), rows_at(high, block_len)
        row = lax.broadcasted_iota(jnp.int32, (block_len, block_len), 0)
        col = lax.broadcasted_iota(jnp.int32, (block_len, block_len), 1)
        for head in range(Q_DEV):
            key_head = columns(head * KV_DEV // Q_DEV)
            both = columns(head, 2 * HEAD_SIZE)

            def tile(q_part, k_part, diagonal):
                expo = expo_of(dot_t(qr_ref[q_part, columns(head)], kr_ref[k_part, key_head]))
                if diagonal:
                    expo = jnp.where(col <= row, expo, 0.0)
                return dot(expo.astype(bf16), beside_ones(v_ref[k_part, key_head]))

            acc_ref[low, both] = tile(low, low, True)
            acc_ref[high, both] = tile(high, high, True) + tile(high, low, False)

        col = lax.broadcasted_iota(jnp.int32, (1, cache_rows), 1)
        part, offset = col // run, col % run
        target = jnp.zeros_like(col)
        for turn in range(slots):
            for half in range(2):
                block = facts.block((slot - turn + slots) % slots, half)
                target = jnp.where(part == 2 * turn + half, block * run + offset, target)
        length = 0
        half_count = groups // 2
        for index in range(half_count):
            same = (group & half_count) | index
            length = length + jnp.where(facts.owner(same) == group, here_ref[index], 0)
            other = same ^ half_count
            length = length + jnp.where(facts.owner(other) == group, there_ref[index], 0)
        residue = 0
        for r in range(1, residues):
            residue = jnp.where(facts.rank(r) == lax.axis_index("blk"), r, residue)
        target = jnp.where(target * residues + residue < length, target, -1)
        row = lax.broadcasted_iota(jnp.int32, (cache_rows, cache_rows), 0)
        kept_ref[...] = jnp.where(row == target, 1.0, 0.0).astype(bf16)
        for half in range(2):
            offset = lax.broadcasted_iota(jnp.int32, (block_len, HEAD_SIZE), 0)
            at = facts.block(slot, half) * block_len + offset
            live_ref[columns(half, block_len)] = jnp.where(at < length, 1.0, 0.0)

    shapes = [
        jax.ShapeDtypeStruct(queries.shape, bf16),
        jax.ShapeDtypeStruct((rows, 2 * Q_DEV * HEAD_SIZE), f32),
        jax.ShapeDtypeStruct((cache_rows, cache_rows), bf16),
        jax.ShapeDtypeStruct((rows, HEAD_SIZE), f32),
        jax.ShapeDtypeStruct((slots - 1, 2, 2, block_len, HEAD_SIZE), f32),
    ]
    return call(body, shapes, [SMEM] * 3 + [VMEM] * 5, "own_part")(
        facts_row, *lens, *operands, *tables
    )


def tiles_of(facts, slot, source):
    low, high = facts.halves(slot)
    source_low, source_high = facts.halves(source)
    outer = facts.block(slot, low) < facts.block(source, source_low)
    first = (jnp.where(outer, high, low), source_low)
    second = (high, jnp.where(outer, source_high, source_low))
    return outer, first, second


def receive_keys(key_in, select, order, angles):
    others = len(key_in)
    rows, width = key_in[0].shape
    block_len = rows // 2

    def body(select_ref, order_ref, angle_ref, *refs):
        k_refs, refs = refs[:others], refs[others:]
        p_refs, chosen_ref, kr_ref = refs[:others], refs[others], refs[others + 1]
        for turn in range(others):
            for half in range(2):
                part = columns(half, block_len)
                there = angle_ref[turn, half, 0], angle_ref[turn, half, 1]
                for head in range(KV_DEV):
                    kr_ref[part, columns(head)] = turned(
                        k_refs[turn][part, columns(head)], there
                    ).astype(bf16)
                p_refs[turn][part] = dot(order_ref[...], kr_ref[part]).astype(bf16)
            chosen_ref[turn] = dot(select_ref[...], kr_ref[...]).astype(bf16)

    shapes = [jax.ShapeDtypeStruct((rows, width), bf16) for _ in range(others)]
    shapes.append(jax.ShapeDtypeStruct((others, select.shape[0], width), bf16))
    scratch = [pltpu.VMEM((rows, width), bf16)]
    outs = call(body, shapes, [VMEM] * (3 + others), "receive_keys", scratch, cost=10**10)(
        select, order, angles, *key_in
    )
    return outs[:others], outs[others]


def weigh(facts_row, facts_of, query_rot, key_rot):
    others = len(key_rot)
    rows = query_rot.shape[0]
    block_len = rows // 2
    slots = facts_of(None).slots

    def body(facts_ref, q_ref, *refs):
        k_refs, w_refs = refs[:others], refs[others:]
        facts = facts_of(facts_ref)
        slot = slot_and_head_group()[0]
        for turn in range(1, slots):
            _, *tiles = tiles_of(facts, slot, (slot - turn + slots) % slots)
            for index, (half, other) in enumerate(tiles):
                for head in range(Q_DEV):
                    key_head = columns(head * KV_DEV // Q_DEV)
                    queries = q_ref[rows_at(half, block_len), columns(head)]
                    keys = k_refs[turn - 1][rows_at(other, block_len), key_head]
                    w_refs[turn - 1][index, head] = expo_of(dot_t(queries, keys)).astype(bf16)

    shapes = [
        jax.ShapeDtypeStruct((2, Q_DEV, block_len, block_len), bf16) for _ in range(others)
    ]
    return call(body, shapes, [SMEM] + [VMEM] * (1 + others), "weigh")(
        facts_row, query_rot, *key_rot
    )


def late_pieces(heads, key_chosen):
    others, rows, width = key_chosen.shape
    piece = rows // HEAD_DIVISIONS
    run = piece // 2
    first = heads[0].shape[0] // 2

    def body(key_ref, *refs):
        v_refs, e_refs = refs[:others], refs[others:]
        for m in range(HEAD_DIVISIONS):
            for turn in range(others):
                e_refs[m][columns(turn, piece)] = key_ref[turn, columns(m, piece)]
                place = 2 * (others + turn)
                if run % 16 == 0:
                    for half in range(2):
                        start = half * first + m * run
                        e_refs[m][columns(place + half, run)] = v_refs[turn][start : start + run]
                    continue
                lines = [
                    v_refs[turn][columns(half, first)].astype(f32)[columns(m, run)]
                    for half in range(2)
                ]
                e_refs[m][place * run : (place + 2) * run] = jnp.concatenate(lines, 0).astype(bf16)

    shapes = [
        jax.ShapeDtypeStruct((2 * others * piece, width), bf16) for _ in range(HEAD_DIVISIONS)
    ]
    return call(body, shapes, [VMEM] * (1 + others), "late_pieces")(key_chosen, *heads)


def attend(facts_row, facts_of, weights, acc, heads, tails, live, mark):
    rows = live.shape[0]
    block_len = rows // 2
    others = len(weights)
    slots = facts_of(None).slots

    def body(facts_ref, mark_ref, acc_ref, live_ref, *refs):
        w_refs, h_refs, t_refs = refs[:others], refs[others : 2 * others], refs[2 * others : 3 * others]
        out_ref, v_scr = refs[3 * others :]
        for turn in range(others):
            first, rest = h_refs[turn].shape[0] // 2, t_refs[turn].shape[0] // 2
            for half in range(2):
                v_scr[turn, columns(half, block_len)] = jnp.concatenate(
                    [h_refs[turn][columns(half, first)], t_refs[turn][columns(half, rest)]], axis=0
                )
        facts = facts_of(facts_ref)
        slot = slot_and_head_group()[0]
        low, high = facts.halves(slot)
        low_rows, high_rows = rows_at(low, block_len), rows_at(high, block_len)
        for head in range(Q_DEV):
            key_head = columns(head * KV_DEV // Q_DEV)
            both = columns(head, 2 * HEAD_SIZE)
            low_sum, high_sum = acc_ref[low_rows, both], acc_ref[high_rows, both]
            for turn in range(1, slots):
                outer, *tiles = tiles_of(facts, slot, (slot - turn + slots) % slots)
                either, upper = [
                    dot(
                        w_refs[turn - 1][index, head],
                        beside_ones(v_scr[turn - 1, rows_at(other, block_len), key_head]),
                    )
                    for index, (_, other) in enumerate(tiles)
                ]
                low_sum = low_sum + jnp.where(outer, 0.0, either)
                high_sum = high_sum + upper + jnp.where(outer, either, 0.0)
            for part, total in ((low_rows, low_sum), (high_rows, high_sum)):
                scale = live_ref[part] / total[:, HEAD_SIZE:]
                out_ref[part, columns(head)] = (total[:, :HEAD_SIZE] * scale).astype(bf16)

    shape = jax.ShapeDtypeStruct((rows, Q_DEV * HEAD_SIZE), bf16)
    specs = [SMEM] + [VMEM] * (3 + 3 * others)
    scratch = [pltpu.VMEM((others, rows, KV_WIDTH), bf16)]
    return call(body, shape, specs, "attend", scratch)(
        facts_row, mark, acc, live, *weights, *heads, *tails
    )


def cache_part(early, late, kept):
    cache_rows = kept.shape[0]
    piece = early[0].shape[0] // 2
    width = early[0].shape[1]

    def body(kept_ref, *refs):
        f_refs, s_refs, out_ref, mark_ref = refs[:4], refs[4:8], refs[8], refs[9]
        mark_ref[...] = jnp.zeros_like(mark_ref)
        head_group = slot_and_head_group()[1]
        later = cache_rows - piece
        for index, m in enumerate(HAND_ORDER):
            for kind in range(2):
                lines = jnp.concatenate(
                    [f_refs[index][columns(kind, piece)], s_refs[index][columns(kind, later)]], axis=0
                )
                column = ((head_group ^ m) + kind * HEAD_DIVISIONS) * width
                out_ref[:, pl.ds(pl.multiple_of(column, HEAD_SIZE), width)] = dot(
                    kept_ref[...], lines
                ).astype(bf16)

    shape = [
        jax.ShapeDtypeStruct((cache_rows, 2 * HEAD_DIVISIONS * width), bf16),
        jax.ShapeDtypeStruct((8, HEAD_SIZE), f32),
    ]
    return call(body, shape, [VMEM] * 9, "cache_part")(kept, *early, *late)


def on_device(queries, keys, values, block_map, lengths, group_of_prompt, decode_rank):
    block_len = queries.shape[2] // 2
    slots = block_map.shape[1]
    q, k, v = queries[0, 0], keys[0, 0], values[0, 0]
    tables = rotary_tables(block_len, 2 * slots)

    def to_slots(parts):
        return [shifted(parts[t - 1], "blk", HEAD_DIVISIONS * t) for t in range(1, slots)]

    def hand_on(pieces):
        return [pieces[0]] + [crossed(pieces[m], "blk", m) for m in HAND_ORDER[1:]]

    key_in = to_slots([k] * (slots - 1))
    facts_row, facts_of, block, operands, tables, (select, order), early, sent = prepare(
        q,
        k,
        v,
        block_map,
        decode_rank,
        group_of_prompt,
        tables,
        lengths,
        crossed(lengths, "req", 1),
    )
    heads = to_slots(sent[0::2])
    tails, key_in = lax.optimization_barrier((sent[1::2], key_in))
    tails = to_slots(tails)
    early = hand_on(early)
    span, groups = 2, lax.axis_size("req")
    while 2 * span < groups:
        other = crossed(block, "req", span)
        upper = (lax.axis_index("req") & span) > 0
        block = jnp.where(
            upper, jnp.concatenate([other, block]), jnp.concatenate([block, other])
        )
        span = 2 * span
    lens = (block, crossed(block, "req", span))
    query_rot, acc, kept, live, angles = own_part(facts_row, facts_of, operands, tables, lens)
    key_rot, chosen = receive_keys(key_in, select, order, angles)
    late = hand_on(late_pieces(heads, chosen))
    weights = weigh(facts_row, facts_of, query_rot, key_rot)
    cache, mark = cache_part(early, late, kept)
    attended = attend(facts_row, facts_of, weights, acc, heads, tails, live, mark)
    return (attended[None, None], cache[None])


def solution(mesh):
    placed = (
        P("req", "blk", None, None),
        P("req", "blk", None, None),
        P("req", "blk", None, None),
        P("req", None, None),
        P("req"),
        P(),
        P("req", None),
    )
    return jax.shard_map(
        on_device,
        mesh=mesh,
        in_specs=placed,
        out_specs=(P("req", "blk", None, None), P("req", "blk", None)),
        check_vma=False,
    )
```

```python
import math

import jax
import jax.numpy as jnp
import numpy as np
from jax import lax
from jax.experimental import pallas as pl
from jax.experimental.pallas import tpu as pltpu
from jax.sharding import PartitionSpec as P

QUERY_HEADS = 16
KEY_VALUE_HEADS = 8
HEAD_SIZE = 128
HEAD_DIVISIONS = 4
Q_DEV = 4
KV_DEV = 2
KV_WIDTH = KV_DEV * HEAD_SIZE

cap_value = 50.0
query_scale = 1.0 / 12.0
HAND_ORDER = (0, 2, 3, 1)
rope_base = 10000.0
VMEM_BYTES = 48 * 1024 * 1024

f32 = jnp.float32
bf16 = jnp.bfloat16
SMEM = pl.BlockSpec(memory_space=pltpu.SMEM)
VMEM = pl.BlockSpec(memory_space=pltpu.VMEM)
HBM = pl.BlockSpec(memory_space=pltpu.HBM)


def shifted(shard, axis, by):
    peers = lax.axis_size(axis)
    return lax.ppermute(shard, axis, [(i, (i + by) % peers) for i in range(peers)])


def crossed(shard, axis, by):
    peers = lax.axis_size(axis)
    return lax.ppermute(shard, axis, [(i, i ^ by) for i in range(peers)])


def rotary_tables(block_len, block_count):
    half = HEAD_SIZE // 2
    frequency = np.exp(
        np.float32(-math.log(rope_base)) * (2.0 * np.arange(half, dtype=np.float32)) / HEAD_SIZE
    ).astype(np.float64)

    def table(positions):
        angles = positions.astype(np.float64)[:, None] * frequency[None, :]
        cosine, sine = np.cos(angles), np.sin(angles)
        return np.stack(
            [np.concatenate([cosine, cosine], 1), np.concatenate([-sine, sine], 1)]
        ).astype(np.float32)

    return table(np.arange(block_len)), table(np.arange(block_count) * block_len)


def block_angles(row_table, block_table, block):
    row_cos, row_sin = row_table[0], row_table[1]
    blk_cos, blk_sin = block_table[0, pl.ds(block, 1)], block_table[1, pl.ds(block, 1)]
    return row_cos * blk_cos - row_sin * blk_sin, row_sin * blk_cos + row_cos * blk_sin


def turned(head, angles):
    x = head.astype(f32)
    return x * angles[0] + pltpu.roll(x, HEAD_SIZE // 2, 1) * angles[1]


def order_matrix(rank_of, slot, head_group, out_rows, rows, residues):
    row_ids = lax.broadcasted_iota(jnp.int32, (1, rows), 1)
    residue = row_ids % residues
    rank = jnp.zeros_like(row_ids)
    for r in range(residues):
        rank = jnp.where(residue == r, rank_of(r), rank)
    ahead = (rank - HEAD_DIVISIONS * slot + residues) % residues
    ahead = jnp.where(ahead < HEAD_DIVISIONS, ahead ^ head_group, ahead)
    index = ahead * (rows // residues) + row_ids // residues
    out_ids = lax.broadcasted_iota(jnp.int32, (out_rows, rows), 0)
    return jnp.where(out_ids == index, 1.0, 0.0).astype(bf16)


def dot(a, b):
    return jnp.dot(a, b, preferred_element_type=f32)


def dot_t(a, b):
    return lax.dot_general(a, b, (((1,), (1,)), ((), ())), preferred_element_type=f32)


def expo_of(scores):
    return jnp.exp2(cap_value * math.log2(math.e) * jnp.tanh(scores * (1.0 / cap_value)))


def columns(index, width=HEAD_SIZE):
    return slice(index * width, (index + 1) * width)


def call(body, out_shape, in_specs, name, scratch=(), out_specs=None, cost=1000):
    return pl.pallas_call(
        body,
        out_shape=out_shape,
        in_specs=in_specs,
        out_specs=jax.tree.map(lambda _: VMEM, out_shape) if out_specs is None else out_specs,
        scratch_shapes=scratch,
        compiler_params=pltpu.CompilerParams(vmem_limit_bytes=VMEM_BYTES),
        cost_estimate=pl.CostEstimate(flops=cost, bytes_accessed=1000, transcendentals=0),
        name=name,
    )


def in_hbm(arrays):
    return [pltpu.with_memory_space_constraint(x, pltpu.HBM) for x in arrays]


def rows_at(index, size):
    return pl.ds(pl.multiple_of(index * size, size), size)


def beside_ones(values):
    return jnp.concatenate([values, jnp.ones(values.shape, bf16)], axis=1)


class Facts:
    def __init__(self, ref, slots, residues, groups):
        self.ref, self.slots, self.residues, self.groups = ref, slots, residues, groups
        self.size = 2 * slots + residues + groups

    def block(self, slot, half):
        return self.ref[0, 2 * slot + half]

    def rank(self, residue):
        return self.ref[0, 2 * self.slots + residue]

    def owner(self, prompt):
        return self.ref[0, 2 * self.slots + self.residues + prompt]

    def store(self, map_ref, rank_ref, owner_ref):
        for slot in range(self.slots):
            for half in range(2):
                self.ref[0, 2 * slot + half] = map_ref[0, slot, half]
        for residue in range(self.residues):
            self.ref[0, 2 * self.slots + residue] = rank_ref[0, residue]
        for prompt in range(self.groups):
            self.ref[0, 2 * self.slots + self.residues + prompt] = owner_ref[prompt]

    def halves(self, slot):
        high = jnp.where(self.block(slot, 1) > self.block(slot, 0), 1, 0)
        return 1 - high, high


def slot_and_head_group():
    member = lax.axis_index("blk")
    return member // HEAD_DIVISIONS, member % HEAD_DIVISIONS


def prepare(queries, keys, values, table, decode_rank, owner, tables, own_length, near_length):
    rows, width = keys.shape
    block_len = rows // 2
    slots = table.shape[1]
    residues = decode_rank.shape[1]
    piece = rows // residues
    first = block_len // slots
    arrays = (keys, values, queries, *tables, table, decode_rank, owner)
    count = len(arrays)
    facts_of = lambda ref: Facts(ref, slots, residues, owner.shape[0])

    def body(own_ref, near_ref, *refs):
        inputs, refs = refs[:count], refs[count:]
        facts_ref, pair_ref, q_ref, kr_ref, v_ref, row_ref, blk_ref, select_ref, order_ref = refs[:9]
        e_refs, refs = refs[9:13], refs[13:]
        sent_refs, refs = refs[: 2 * slots - 2], refs[2 * slots - 2 :]
        k_ref, map_ref, rank_ref, owner_ref, sems = refs
        targets = (k_ref, v_ref, q_ref, row_ref, blk_ref, map_ref, rank_ref, owner_ref)
        copies = []
        for index in range(count):
            copies.append(pltpu.make_async_copy(inputs[index], targets[index], sems.at[index]))
            copies[-1].start()
        slot, head_group = slot_and_head_group()
        odd = lax.axis_index("req") % 2 == 1
        pair_ref[0] = jnp.where(odd, near_ref[0], own_ref[0])
        pair_ref[1] = jnp.where(odd, own_ref[0], near_ref[0])
        for index in (0, 3, 4, 5, 6, 7):
            copies[index].wait()
        facts_of(facts_ref).store(map_ref, rank_ref, owner_ref)
        for half in range(2):
            part = columns(half, block_len)
            angles = block_angles(row_ref, blk_ref, map_ref[0, slot, half])
            for head in range(KV_DEV):
                kr_ref[part, columns(head)] = turned(k_ref[part, columns(head)], angles).astype(bf16)
        select = order_matrix(
            lambda r: rank_ref[0, r], slot, head_group, rows // slots, rows, residues
        )
        select_ref[...] = select
        copies[1].wait()
        for turn in range(1, slots):
            order = order_matrix(
                lambda r: rank_ref[0, r],
                (slot + turn) % slots,
                head_group,
                block_len,
                block_len,
                residues,
            )
            for half in range(2):
                moved = dot(order, v_ref[columns(half, block_len)]).astype(bf16)
                sent_refs[2 * turn - 2][columns(half, first)] = moved[:first]
                sent_refs[2 * turn - 1][columns(half, block_len - first)] = moved[first:]
        order_ref[...] = order_matrix(
            lambda r: rank_ref[0, r], slot, head_group, block_len, block_len, residues
        )
        for kind, source in enumerate((kr_ref, v_ref)):
            chosen = dot(select, source[...]).astype(bf16)
            for m in range(HEAD_DIVISIONS):
                e_refs[m][columns(kind, piece)] = chosen[columns(m, piece)]
        copies[2].wait()

    shapes = [
        jax.ShapeDtypeStruct((1, facts_of(None).size), jnp.int32),
        jax.ShapeDtypeStruct((2,), jnp.int32),
        jax.ShapeDtypeStruct(queries.shape, bf16),
        jax.ShapeDtypeStruct(keys.shape, bf16),
        jax.ShapeDtypeStruct(values.shape, bf16),
        jax.ShapeDtypeStruct(tables[0].shape, f32),
        jax.ShapeDtypeStruct(tables[1].shape, f32),
        jax.ShapeDtypeStruct((rows // slots, rows), bf16),
        jax.ShapeDtypeStruct((block_len, block_len), bf16),
    ]
    shapes += [jax.ShapeDtypeStruct((2 * piece, width), bf16) for _ in range(HEAD_DIVISIONS)]
    for _ in range(1, slots):
        shapes.append(jax.ShapeDtypeStruct((2 * first, width), bf16))
        shapes.append(jax.ShapeDtypeStruct((2 * (block_len - first), width), bf16))
    scratch = [pltpu.VMEM(keys.shape, keys.dtype)]
    scratch += [pltpu.SMEM(x.shape, x.dtype) for x in (table, decode_rank, owner)]
    scratch.append(pltpu.SemaphoreType.DMA((count,)))
    outs = call(
        body,
        shapes,
        [SMEM] * 2 + [HBM] * count,
        "prepare",
        scratch,
        out_specs=[SMEM] * 2 + [VMEM] * (len(shapes) - 2),
    )(own_length, near_length, *in_hbm(arrays))
    return outs[0], facts_of, outs[1], outs[2:5], outs[5:7], outs[7:9], outs[9:13], outs[13:]


def own_part(facts_row, facts_of, operands, tables, lens):
    queries = operands[0]
    rows = queries.shape[0]
    block_len = rows // 2
    sizes = facts_of(None)
    slots, residues, groups = sizes.slots, sizes.residues, sizes.groups
    run = block_len // residues
    cache_rows = 2 * slots * run

    def body(facts_ref, here_ref, there_ref, q_ref, kr_ref, v_ref, row_ref, blk_ref, *refs):
        qr_ref, acc_ref, kept_ref, live_ref, angle_ref = refs
        facts = facts_of(facts_ref)
        slot = slot_and_head_group()[0]
        group = lax.axis_index("req")
        for half in range(2):
            part = columns(half, block_len)
            angles = block_angles(row_ref, blk_ref, facts.block(slot, half))
            for head in range(Q_DEV):
                qr_ref[part, columns(head)] = (
                    turned(q_ref[part, columns(head)], angles) * query_scale
                ).astype(bf16)
            for turn in range(1, slots):
                block = facts.block((slot - turn + slots) % slots, half)
                other = block_angles(row_ref, blk_ref, block)
                angle_ref[turn - 1, half, 0] = other[0]
                angle_ref[turn - 1, half, 1] = other[1]
        low, high = facts.halves(slot)
        low, high = rows_at(low, block_len), rows_at(high, block_len)
        row = lax.broadcasted_iota(jnp.int32, (block_len, block_len), 0)
        col = lax.broadcasted_iota(jnp.int32, (block_len, block_len), 1)
        for head in range(Q_DEV):
            key_head = columns(head * KV_DEV // Q_DEV)
            both = columns(head, 2 * HEAD_SIZE)

            def tile(q_part, k_part, diagonal):
                expo = expo_of(dot_t(qr_ref[q_part, columns(head)], kr_ref[k_part, key_head]))
                if diagonal:
                    expo = jnp.where(col <= row, expo, 0.0)
                return dot(expo.astype(bf16), beside_ones(v_ref[k_part, key_head]))

            acc_ref[low, both] = tile(low, low, True)
            acc_ref[high, both] = tile(high, high, True) + tile(high, low, False)

        col = lax.broadcasted_iota(jnp.int32, (1, cache_rows), 1)
        part, offset = col // run, col % run
        target = jnp.zeros_like(col)
        for turn in range(slots):
            for half in range(2):
                block = facts.block((slot - turn + slots) % slots, half)
                target = jnp.where(part == 2 * turn + half, block * run + offset, target)
        length = 0
        half_count = groups // 2
        for index in range(half_count):
            same = (group & half_count) | index
            length = length + jnp.where(facts.owner(same) == group, here_ref[index], 0)
            other = same ^ half_count
            length = length + jnp.where(facts.owner(other) == group, there_ref[index], 0)
        residue = 0
        for r in range(1, residues):
            residue = jnp.where(facts.rank(r) == lax.axis_index("blk"), r, residue)
        target = jnp.where(target * residues + residue < length, target, -1)
        row = lax.broadcasted_iota(jnp.int32, (cache_rows, cache_rows), 0)
        kept_ref[...] = jnp.where(row == target, 1.0, 0.0).astype(bf16)
        for half in range(2):
            offset = lax.broadcasted_iota(jnp.int32, (block_len, HEAD_SIZE), 0)
            at = facts.block(slot, half) * block_len + offset
            live_ref[columns(half, block_len)] = jnp.where(at < length, 1.0, 0.0)

    shapes = [
        jax.ShapeDtypeStruct(queries.shape, bf16),
        jax.ShapeDtypeStruct((rows, 2 * Q_DEV * HEAD_SIZE), f32),
        jax.ShapeDtypeStruct((cache_rows, cache_rows), bf16),
        jax.ShapeDtypeStruct((rows, HEAD_SIZE), f32),
        jax.ShapeDtypeStruct((slots - 1, 2, 2, block_len, HEAD_SIZE), f32),
    ]
    return call(body, shapes, [SMEM] * 3 + [VMEM] * 5, "own_part")(
        facts_row, *lens, *operands, *tables
    )


def tiles_of(facts, slot, source):
    low, high = facts.halves(slot)
    source_low, source_high = facts.halves(source)
    outer = facts.block(slot, low) < facts.block(source, source_low)
    first = (jnp.where(outer, high, low), source_low)
    second = (high, jnp.where(outer, source_high, source_low))
    return outer, first, second


def receive_keys(key_in, select, order, angles):
    others = len(key_in)
    rows, width = key_in[0].shape
    block_len = rows // 2

    def body(select_ref, order_ref, angle_ref, *refs):
        k_refs, refs = refs[:others], refs[others:]
        p_refs, chosen_ref, kr_ref = refs[:others], refs[others], refs[others + 1]
        for turn in range(others):
            for half in range(2):
                part = columns(half, block_len)
                there = angle_ref[turn, half, 0], angle_ref[turn, half, 1]
                for head in range(KV_DEV):
                    kr_ref[part, columns(head)] = turned(
                        k_refs[turn][part, columns(head)], there
                    ).astype(bf16)
                p_refs[turn][part] = dot(order_ref[...], kr_ref[part]).astype(bf16)
            chosen_ref[turn] = dot(select_ref[...], kr_ref[...]).astype(bf16)

    shapes = [jax.ShapeDtypeStruct((rows, width), bf16) for _ in range(others)]
    shapes.append(jax.ShapeDtypeStruct((others, select.shape[0], width), bf16))
    scratch = [pltpu.VMEM((rows, width), bf16)]
    outs = call(body, shapes, [VMEM] * (3 + others), "receive_keys", scratch, cost=10**10)(
        select, order, angles, *key_in
    )
    return outs[:others], outs[others]


def weigh(facts_row, facts_of, query_rot, key_rot, payload):
    others = len(key_rot)
    rows = query_rot.shape[0]
    block_len = rows // 2
    slots = facts_of(None).slots

    def body(facts_ref, q_ref, *refs):
        k_refs, pay_refs, refs = refs[:others], refs[others : 2 * others], refs[2 * others :]
        w_refs, out_refs = refs[:others], refs[others:]
        for pay_ref, out_ref in zip(pay_refs, out_refs):
            out_ref[...] = pay_ref[...]
        facts = facts_of(facts_ref)
        slot = slot_and_head_group()[0]
        for turn in range(1, slots):
            _, *tiles = tiles_of(facts, slot, (slot - turn + slots) % slots)
            for index, (half, other) in enumerate(tiles):
                for head in range(Q_DEV):
                    key_head = columns(head * KV_DEV // Q_DEV)
                    queries = q_ref[rows_at(half, block_len), columns(head)]
                    keys = k_refs[turn - 1][rows_at(other, block_len), key_head]
                    w_refs[turn - 1][index, head] = expo_of(dot_t(queries, keys)).astype(bf16)

    shapes = [
        jax.ShapeDtypeStruct((2, Q_DEV, block_len, block_len), bf16) for _ in range(others)
    ]
    shapes += [jax.ShapeDtypeStruct(x.shape, bf16) for x in payload]
    outs = call(body, shapes, [SMEM] + [VMEM] * (1 + 2 * others), "weigh")(
        facts_row, query_rot, *key_rot, *payload
    )
    return outs[:others], outs[others:]


def late_pieces(heads, key_chosen):
    others, rows, width = key_chosen.shape
    piece = rows // HEAD_DIVISIONS
    run = piece // 2
    first = heads[0].shape[0] // 2

    def body(key_ref, *refs):
        v_refs, e_refs = refs[:others], refs[others:]
        for m in range(HEAD_DIVISIONS):
            for turn in range(others):
                e_refs[m][columns(turn, piece)] = key_ref[turn, columns(m, piece)]
                place = 2 * (others + turn)
                if run % 16 == 0:
                    for half in range(2):
                        start = half * first + m * run
                        e_refs[m][columns(place + half, run)] = v_refs[turn][start : start + run]
                    continue
                lines = [
                    v_refs[turn][columns(half, first)].astype(f32)[columns(m, run)]
                    for half in range(2)
                ]
                e_refs[m][place * run : (place + 2) * run] = jnp.concatenate(lines, 0).astype(bf16)

    shapes = [
        jax.ShapeDtypeStruct((2 * others * piece, width), bf16) for _ in range(HEAD_DIVISIONS)
    ]
    return call(body, shapes, [VMEM] * (1 + others), "late_pieces")(key_chosen, *heads)


def attend(facts_row, facts_of, weights, acc, heads, tails, live, mark):
    rows = live.shape[0]
    block_len = rows // 2
    others = len(weights)
    slots = facts_of(None).slots

    def body(facts_ref, mark_ref, acc_ref, live_ref, *refs):
        w_refs, h_refs, t_refs = refs[:others], refs[others : 2 * others], refs[2 * others : 3 * others]
        out_ref, v_scr = refs[3 * others :]
        for turn in range(others):
            first, rest = h_refs[turn].shape[0] // 2, t_refs[turn].shape[0] // 2
            for half in range(2):
                v_scr[turn, columns(half, block_len)] = jnp.concatenate(
                    [h_refs[turn][columns(half, first)], t_refs[turn][columns(half, rest)]], axis=0
                )
        facts = facts_of(facts_ref)
        slot = slot_and_head_group()[0]
        low, high = facts.halves(slot)
        low_rows, high_rows = rows_at(low, block_len), rows_at(high, block_len)
        for head in range(Q_DEV):
            key_head = columns(head * KV_DEV // Q_DEV)
            both = columns(head, 2 * HEAD_SIZE)
            low_sum, high_sum = acc_ref[low_rows, both], acc_ref[high_rows, both]
            for turn in range(1, slots):
                outer, *tiles = tiles_of(facts, slot, (slot - turn + slots) % slots)
                either, upper = [
                    dot(
                        w_refs[turn - 1][index, head],
                        beside_ones(v_scr[turn - 1, rows_at(other, block_len), key_head]),
                    )
                    for index, (_, other) in enumerate(tiles)
                ]
                low_sum = low_sum + jnp.where(outer, 0.0, either)
                high_sum = high_sum + upper + jnp.where(outer, either, 0.0)
            for part, total in ((low_rows, low_sum), (high_rows, high_sum)):
                scale = live_ref[part] / total[:, HEAD_SIZE:]
                out_ref[part, columns(head)] = (total[:, :HEAD_SIZE] * scale).astype(bf16)

    shape = jax.ShapeDtypeStruct((rows, Q_DEV * HEAD_SIZE), bf16)
    specs = [SMEM] + [VMEM] * (3 + 3 * others)
    scratch = [pltpu.VMEM((others, rows, KV_WIDTH), bf16)]
    return call(body, shape, specs, "attend", scratch)(
        facts_row, mark, acc, live, *weights, *heads, *tails
    )


def cache_part(early, late, kept):
    cache_rows = kept.shape[0]
    piece = early[0].shape[0] // 2
    width = early[0].shape[1]

    def body(kept_ref, *refs):
        f_refs, s_refs, out_ref, mark_ref = refs[:4], refs[4:8], refs[8], refs[9]
        mark_ref[...] = jnp.zeros_like(mark_ref)
        head_group = slot_and_head_group()[1]
        later = cache_rows - piece
        for index, m in enumerate(HAND_ORDER):
            for kind in range(2):
                lines = jnp.concatenate(
                    [f_refs[index][columns(kind, piece)], s_refs[index][columns(kind, later)]], axis=0
                )
                column = ((head_group ^ m) + kind * HEAD_DIVISIONS) * width
                out_ref[:, pl.ds(pl.multiple_of(column, HEAD_SIZE), width)] = dot(
                    kept_ref[...], lines
                ).astype(bf16)

    shape = [
        jax.ShapeDtypeStruct((cache_rows, 2 * HEAD_DIVISIONS * width), bf16),
        jax.ShapeDtypeStruct((8, HEAD_SIZE), f32),
    ]
    return call(body, shape, [VMEM] * 9, "cache_part")(kept, *early, *late)


def on_device(queries, keys, values, block_map, lengths, group_of_prompt, decode_rank):
    block_len = queries.shape[2] // 2
    slots = block_map.shape[1]
    q, k, v = queries[0, 0], keys[0, 0], values[0, 0]
    tables = rotary_tables(block_len, 2 * slots)

    def to_slots(parts):
        return [shifted(parts[t - 1], "blk", HEAD_DIVISIONS * t) for t in range(1, slots)]

    def hand_on(pieces):
        return [pieces[0]] + [crossed(pieces[m], "blk", m) for m in HAND_ORDER[1:]]

    key_in = to_slots([k] * (slots - 1))
    facts_row, facts_of, block, operands, tables, (select, order), early, sent = prepare(
        q,
        k,
        v,
        block_map,
        decode_rank,
        group_of_prompt,
        tables,
        lengths,
        crossed(lengths, "req", 1),
    )
    heads = to_slots(sent[0::2])
    early = hand_on(early)
    span, groups = 2, lax.axis_size("req")
    while 2 * span < groups:
        other = crossed(block, "req", span)
        upper = (lax.axis_index("req") & span) > 0
        block = jnp.where(
            upper, jnp.concatenate([other, block]), jnp.concatenate([block, other])
        )
        span = 2 * span
    lens = (block, crossed(block, "req", span))
    query_rot, acc, kept, live, angles = own_part(facts_row, facts_of, operands, tables, lens)
    key_rot, chosen = receive_keys(key_in, select, order, angles)
    weights, tails = weigh(facts_row, facts_of, query_rot, key_rot, sent[1::2])
    tails = to_slots(tails)
    late = hand_on(late_pieces(heads, chosen))
    cache, mark = cache_part(early, late, kept)
    attended = attend(facts_row, facts_of, weights, acc, heads, tails, live, mark)
    return (attended[None, None], cache[None])


def solution(mesh):
    placed = (
        P("req", "blk", None, None),
        P("req", "blk", None, None),
        P("req", "blk", None, None),
        P("req", None, None),
        P("req"),
        P(),
        P("req", None),
    )
    return jax.shard_map(
        on_device,
        mesh=mesh,
        in_specs=placed,
        out_specs=(P("req", "blk", None, None), P("req", "blk", None)),
        check_vma=False,
    )
```

```python
import math

import jax
import jax.numpy as jnp
import numpy as np
from jax import lax
from jax.experimental import pallas as pl
from jax.experimental.pallas import tpu as pltpu
from jax.sharding import PartitionSpec as P

QUERY_HEADS = 16
KEY_VALUE_HEADS = 8
HEAD_SIZE = 128
HEAD_DIVISIONS = 4
Q_DEV = 4
KV_DEV = 2
KV_WIDTH = KV_DEV * HEAD_SIZE

cap_value = 50.0
query_scale = 1.0 / 12.0
HAND_ORDER = (0, 2, 3, 1)
rope_base = 10000.0
VMEM_BYTES = 48 * 1024 * 1024

f32 = jnp.float32
bf16 = jnp.bfloat16
SMEM = pl.BlockSpec(memory_space=pltpu.SMEM)
VMEM = pl.BlockSpec(memory_space=pltpu.VMEM)
HBM = pl.BlockSpec(memory_space=pltpu.HBM)


def shifted(shard, axis, by):
    peers = lax.axis_size(axis)
    return lax.ppermute(shard, axis, [(i, (i + by) % peers) for i in range(peers)])


def crossed(shard, axis, by):
    peers = lax.axis_size(axis)
    return lax.ppermute(shard, axis, [(i, i ^ by) for i in range(peers)])


def rotary_tables(block_len, block_count):
    half = HEAD_SIZE // 2
    frequency = np.exp(
        np.float32(-math.log(rope_base)) * (2.0 * np.arange(half, dtype=np.float32)) / HEAD_SIZE
    ).astype(np.float64)

    def table(positions):
        angles = positions.astype(np.float64)[:, None] * frequency[None, :]
        cosine, sine = np.cos(angles), np.sin(angles)
        return np.stack(
            [np.concatenate([cosine, cosine], 1), np.concatenate([-sine, sine], 1)]
        ).astype(np.float32)

    return table(np.arange(block_len)), table(np.arange(block_count) * block_len)


def block_angles(row_table, block_table, block):
    row_cos, row_sin = row_table[0], row_table[1]
    blk_cos, blk_sin = block_table[0, pl.ds(block, 1)], block_table[1, pl.ds(block, 1)]
    return row_cos * blk_cos - row_sin * blk_sin, row_sin * blk_cos + row_cos * blk_sin


def turned(head, angles):
    x = head.astype(f32)
    return x * angles[0] + pltpu.roll(x, HEAD_SIZE // 2, 1) * angles[1]


def order_matrix(rank_of, slot, head_group, out_rows, rows, residues):
    row_ids = lax.broadcasted_iota(jnp.int32, (1, rows), 1)
    residue = row_ids % residues
    rank = jnp.zeros_like(row_ids)
    for r in range(residues):
        rank = jnp.where(residue == r, rank_of(r), rank)
    ahead = (rank - HEAD_DIVISIONS * slot + residues) % residues
    ahead = jnp.where(ahead < HEAD_DIVISIONS, ahead ^ head_group, ahead)
    index = ahead * (rows // residues) + row_ids // residues
    out_ids = lax.broadcasted_iota(jnp.int32, (out_rows, rows), 0)
    return jnp.where(out_ids == index, 1.0, 0.0).astype(bf16)


def dot(a, b):
    return jnp.dot(a, b, preferred_element_type=f32)


def dot_t(a, b):
    return lax.dot_general(a, b, (((1,), (1,)), ((), ())), preferred_element_type=f32)


def expo_of(scores):
    return jnp.exp2(cap_value * math.log2(math.e) * jnp.tanh(scores * (1.0 / cap_value)))


def columns(index, width=HEAD_SIZE):
    return slice(index * width, (index + 1) * width)


def call(body, out_shape, in_specs, name, scratch=(), out_specs=None, cost=1000):
    return pl.pallas_call(
        body,
        out_shape=out_shape,
        in_specs=in_specs,
        out_specs=jax.tree.map(lambda _: VMEM, out_shape) if out_specs is None else out_specs,
        scratch_shapes=scratch,
        compiler_params=pltpu.CompilerParams(vmem_limit_bytes=VMEM_BYTES),
        cost_estimate=pl.CostEstimate(flops=cost, bytes_accessed=1000, transcendentals=0),
        name=name,
    )


def in_hbm(arrays):
    return [pltpu.with_memory_space_constraint(x, pltpu.HBM) for x in arrays]


def rows_at(index, size):
    return pl.ds(pl.multiple_of(index * size, size), size)


def beside_ones(values):
    return jnp.concatenate([values, jnp.ones(values.shape, bf16)], axis=1)


class Facts:
    def __init__(self, ref, slots, residues, groups):
        self.ref, self.slots, self.residues, self.groups = ref, slots, residues, groups
        self.size = 2 * slots + residues + groups

    def block(self, slot, half):
        return self.ref[0, 2 * slot + half]

    def rank(self, residue):
        return self.ref[0, 2 * self.slots + residue]

    def owner(self, prompt):
        return self.ref[0, 2 * self.slots + self.residues + prompt]

    def store(self, map_ref, rank_ref, owner_ref):
        for slot in range(self.slots):
            for half in range(2):
                self.ref[0, 2 * slot + half] = map_ref[0, slot, half]
        for residue in range(self.residues):
            self.ref[0, 2 * self.slots + residue] = rank_ref[0, residue]
        for prompt in range(self.groups):
            self.ref[0, 2 * self.slots + self.residues + prompt] = owner_ref[prompt]

    def halves(self, slot):
        high = jnp.where(self.block(slot, 1) > self.block(slot, 0), 1, 0)
        return 1 - high, high


def slot_and_head_group():
    member = lax.axis_index("blk")
    return member // HEAD_DIVISIONS, member % HEAD_DIVISIONS


def prepare(queries, keys, values, table, decode_rank, owner, tables, own_length, near_length):
    rows, width = keys.shape
    block_len = rows // 2
    slots = table.shape[1]
    residues = decode_rank.shape[1]
    piece = rows // residues
    first = block_len // slots
    arrays = (keys, values, queries, *tables, table, decode_rank, owner)
    count = len(arrays)
    facts_of = lambda ref: Facts(ref, slots, residues, owner.shape[0])

    def body(own_ref, near_ref, *refs):
        inputs, refs = refs[:count], refs[count:]
        facts_ref, pair_ref, q_ref, kr_ref, v_ref, row_ref, blk_ref, select_ref, order_ref = refs[:9]
        e_refs, refs = refs[9:13], refs[13:]
        sent_refs, refs = refs[: 2 * slots - 2], refs[2 * slots - 2 :]
        k_ref, map_ref, rank_ref, owner_ref, sems = refs
        targets = (k_ref, v_ref, q_ref, row_ref, blk_ref, map_ref, rank_ref, owner_ref)
        copies = []
        for index in range(count):
            copies.append(pltpu.make_async_copy(inputs[index], targets[index], sems.at[index]))
            copies[-1].start()
        slot, head_group = slot_and_head_group()
        odd = lax.axis_index("req") % 2 == 1
        pair_ref[0] = jnp.where(odd, near_ref[0], own_ref[0])
        pair_ref[1] = jnp.where(odd, own_ref[0], near_ref[0])
        for index in (0, 3, 4, 5, 6, 7):
            copies[index].wait()
        facts_of(facts_ref).store(map_ref, rank_ref, owner_ref)
        for half in range(2):
            part = columns(half, block_len)
            angles = block_angles(row_ref, blk_ref, map_ref[0, slot, half])
            for head in range(KV_DEV):
                kr_ref[part, columns(head)] = turned(k_ref[part, columns(head)], angles).astype(bf16)
        select = order_matrix(
            lambda r: rank_ref[0, r], slot, head_group, rows // slots, rows, residues
        )
        select_ref[...] = select
        copies[1].wait()
        for turn in range(1, slots):
            order = order_matrix(
                lambda r: rank_ref[0, r],
                (slot + turn) % slots,
                head_group,
                block_len,
                block_len,
                residues,
            )
            for half in range(2):
                moved = dot(order, v_ref[columns(half, block_len)]).astype(bf16)
                sent_refs[2 * turn - 2][columns(half, first)] = moved[:first]
                sent_refs[2 * turn - 1][columns(half, block_len - first)] = moved[first:]
        order_ref[...] = order_matrix(
            lambda r: rank_ref[0, r], slot, head_group, block_len, block_len, residues
        )
        for kind, source in enumerate((kr_ref, v_ref)):
            chosen = dot(select, source[...]).astype(bf16)
            for m in range(HEAD_DIVISIONS):
                e_refs[m][columns(kind, piece)] = chosen[columns(m, piece)]
        copies[2].wait()

    shapes = [
        jax.ShapeDtypeStruct((1, facts_of(None).size), jnp.int32),
        jax.ShapeDtypeStruct((2,), jnp.int32),
        jax.ShapeDtypeStruct(queries.shape, bf16),
        jax.ShapeDtypeStruct(keys.shape, bf16),
        jax.ShapeDtypeStruct(values.shape, bf16),
        jax.ShapeDtypeStruct(tables[0].shape, f32),
        jax.ShapeDtypeStruct(tables[1].shape, f32),
        jax.ShapeDtypeStruct((rows // slots, rows), bf16),
        jax.ShapeDtypeStruct((block_len, block_len), bf16),
    ]
    shapes += [jax.ShapeDtypeStruct((2 * piece, width), bf16) for _ in range(HEAD_DIVISIONS)]
    for _ in range(1, slots):
        shapes.append(jax.ShapeDtypeStruct((2 * first, width), bf16))
        shapes.append(jax.ShapeDtypeStruct((2 * (block_len - first), width), bf16))
    scratch = [pltpu.VMEM(keys.shape, keys.dtype)]
    scratch += [pltpu.SMEM(x.shape, x.dtype) for x in (table, decode_rank, owner)]
    scratch.append(pltpu.SemaphoreType.DMA((count,)))
    outs = call(
        body,
        shapes,
        [SMEM] * 2 + [HBM] * count,
        "prepare",
        scratch,
        out_specs=[SMEM] * 2 + [VMEM] * (len(shapes) - 2),
    )(own_length, near_length, *in_hbm(arrays))
    return outs[0], facts_of, outs[1], outs[2:5], outs[5:7], outs[7:9], outs[9:13], outs[13:]


def own_part(facts_row, facts_of, operands, tables, lens):
    queries = operands[0]
    rows = queries.shape[0]
    block_len = rows // 2
    sizes = facts_of(None)
    slots, residues, groups = sizes.slots, sizes.residues, sizes.groups
    run = block_len // residues
    cache_rows = 2 * slots * run

    def body(facts_ref, here_ref, there_ref, q_ref, kr_ref, v_ref, row_ref, blk_ref, *refs):
        qr_ref, acc_ref, kept_ref, live_ref, angle_ref = refs
        facts = facts_of(facts_ref)
        slot = slot_and_head_group()[0]
        group = lax.axis_index("req")
        for half in range(2):
            part = columns(half, block_len)
            angles = block_angles(row_ref, blk_ref, facts.block(slot, half))
            for head in range(Q_DEV):
                qr_ref[part, columns(head)] = (
                    turned(q_ref[part, columns(head)], angles) * query_scale
                ).astype(bf16)
            for turn in range(1, slots):
                block = facts.block((slot - turn + slots) % slots, half)
                other = block_angles(row_ref, blk_ref, block)
                angle_ref[turn - 1, half, 0] = other[0]
                angle_ref[turn - 1, half, 1] = other[1]
        low, high = facts.halves(slot)
        low, high = rows_at(low, block_len), rows_at(high, block_len)
        row = lax.broadcasted_iota(jnp.int32, (block_len, block_len), 0)
        col = lax.broadcasted_iota(jnp.int32, (block_len, block_len), 1)
        for head in range(Q_DEV):
            key_head = columns(head * KV_DEV // Q_DEV)
            both = columns(head, 2 * HEAD_SIZE)

            def tile(q_part, k_part, diagonal):
                expo = expo_of(dot_t(qr_ref[q_part, columns(head)], kr_ref[k_part, key_head]))
                if diagonal:
                    expo = jnp.where(col <= row, expo, 0.0)
                return dot(expo.astype(bf16), beside_ones(v_ref[k_part, key_head]))

            acc_ref[low, both] = tile(low, low, True)
            acc_ref[high, both] = tile(high, high, True) + tile(high, low, False)

        col = lax.broadcasted_iota(jnp.int32, (1, cache_rows), 1)
        part, offset = col // run, col % run
        target = jnp.zeros_like(col)
        for turn in range(slots):
            for half in range(2):
                block = facts.block((slot - turn + slots) % slots, half)
                target = jnp.where(part == 2 * turn + half, block * run + offset, target)
        length = 0
        half_count = groups // 2
        for index in range(half_count):
            same = (group & half_count) | index
            length = length + jnp.where(facts.owner(same) == group, here_ref[index], 0)
            other = same ^ half_count
            length = length + jnp.where(facts.owner(other) == group, there_ref[index], 0)
        residue = 0
        for r in range(1, residues):
            residue = jnp.where(facts.rank(r) == lax.axis_index("blk"), r, residue)
        target = jnp.where(target * residues + residue < length, target, -1)
        row = lax.broadcasted_iota(jnp.int32, (cache_rows, cache_rows), 0)
        kept_ref[...] = jnp.where(row == target, 1.0, 0.0).astype(bf16)
        for half in range(2):
            offset = lax.broadcasted_iota(jnp.int32, (block_len, HEAD_SIZE), 0)
            at = facts.block(slot, half) * block_len + offset
            live_ref[columns(half, block_len)] = jnp.where(at < length, 1.0, 0.0)

    shapes = [
        jax.ShapeDtypeStruct(queries.shape, bf16),
        jax.ShapeDtypeStruct((rows, 2 * Q_DEV * HEAD_SIZE), f32),
        jax.ShapeDtypeStruct((cache_rows, cache_rows), bf16),
        jax.ShapeDtypeStruct((rows, HEAD_SIZE), f32),
        jax.ShapeDtypeStruct((slots - 1, 2, 2, block_len, HEAD_SIZE), f32),
    ]
    return call(body, shapes, [SMEM] * 3 + [VMEM] * 5, "own_part")(
        facts_row, *lens, *operands, *tables
    )


def tiles_of(facts, slot, source):
    low, high = facts.halves(slot)
    source_low, source_high = facts.halves(source)
    outer = facts.block(slot, low) < facts.block(source, source_low)
    first = (jnp.where(outer, high, low), source_low)
    second = (high, jnp.where(outer, source_high, source_low))
    return outer, first, second


def receive_keys(key_in, select, order, angles):
    others = len(key_in)
    rows, width = key_in[0].shape
    block_len = rows // 2

    def body(select_ref, order_ref, angle_ref, *refs):
        k_refs, refs = refs[:others], refs[others:]
        p_refs, chosen_ref, kr_ref = refs[:others], refs[others], refs[others + 1]
        for turn in range(others):
            for half in range(2):
                part = columns(half, block_len)
                there = angle_ref[turn, half, 0], angle_ref[turn, half, 1]
                for head in range(KV_DEV):
                    kr_ref[part, columns(head)] = turned(
                        k_refs[turn][part, columns(head)], there
                    ).astype(bf16)
                p_refs[turn][part] = dot(order_ref[...], kr_ref[part]).astype(bf16)
            chosen_ref[turn] = dot(select_ref[...], kr_ref[...]).astype(bf16)

    shapes = [jax.ShapeDtypeStruct((rows, width), bf16) for _ in range(others)]
    shapes.append(jax.ShapeDtypeStruct((others, select.shape[0], width), bf16))
    scratch = [pltpu.VMEM((rows, width), bf16)]
    outs = call(body, shapes, [VMEM] * (3 + others), "receive_keys", scratch, cost=10**10)(
        select, order, angles, *key_in
    )
    return outs[:others], outs[others]


def weigh(facts_row, facts_of, query_rot, key_rot, payload, after):
    others = len(key_rot)
    rows = query_rot.shape[0]
    block_len = rows // 2
    slots = facts_of(None).slots

    def body(facts_ref, _, q_ref, *refs):
        k_refs, pay_refs, refs = refs[:others], refs[others : 2 * others], refs[2 * others :]
        w_refs, out_refs = refs[:others], refs[others:]
        for pay_ref, out_ref in zip(pay_refs, out_refs):
            out_ref[...] = pay_ref[...]
        facts = facts_of(facts_ref)
        slot = slot_and_head_group()[0]
        for turn in range(1, slots):
            _, *tiles = tiles_of(facts, slot, (slot - turn + slots) % slots)
            for index, (half, other) in enumerate(tiles):
                for head in range(Q_DEV):
                    key_head = columns(head * KV_DEV // Q_DEV)
                    queries = q_ref[rows_at(half, block_len), columns(head)]
                    keys = k_refs[turn - 1][rows_at(other, block_len), key_head]
                    w_refs[turn - 1][index, head] = expo_of(dot_t(queries, keys)).astype(bf16)

    shapes = [
        jax.ShapeDtypeStruct((2, Q_DEV, block_len, block_len), bf16) for _ in range(others)
    ]
    shapes += [jax.ShapeDtypeStruct(x.shape, bf16) for x in payload]
    outs = call(body, shapes, [SMEM] + [VMEM] * (2 + 2 * others), "weigh")(
        facts_row, after, query_rot, *key_rot, *payload
    )
    return outs[:others], outs[others:]


def late_pieces(heads, key_chosen):
    others, rows, width = key_chosen.shape
    piece = rows // HEAD_DIVISIONS
    run = piece // 2
    first = heads[0].shape[0] // 2

    def body(key_ref, *refs):
        v_refs, e_refs = refs[:others], refs[others:]
        for m in range(HEAD_DIVISIONS):
            for turn in range(others):
                e_refs[m][columns(turn, piece)] = key_ref[turn, columns(m, piece)]
                place = 2 * (others + turn)
                if run % 16 == 0:
                    for half in range(2):
                        start = half * first + m * run
                        e_refs[m][columns(place + half, run)] = v_refs[turn][start : start + run]
                    continue
                lines = [
                    v_refs[turn][columns(half, first)].astype(f32)[columns(m, run)]
                    for half in range(2)
                ]
                e_refs[m][place * run : (place + 2) * run] = jnp.concatenate(lines, 0).astype(bf16)

    shapes = [
        jax.ShapeDtypeStruct((2 * others * piece, width), bf16) for _ in range(HEAD_DIVISIONS)
    ]
    return call(body, shapes, [VMEM] * (1 + others), "late_pieces")(key_chosen, *heads)


def attend(facts_row, facts_of, weights, acc, heads, tails, live, mark):
    rows = live.shape[0]
    block_len = rows // 2
    others = len(weights)
    slots = facts_of(None).slots

    def body(facts_ref, mark_ref, acc_ref, live_ref, *refs):
        w_refs, h_refs, t_refs = refs[:others], refs[others : 2 * others], refs[2 * others : 3 * others]
        out_ref, v_scr = refs[3 * others :]
        for turn in range(others):
            first, rest = h_refs[turn].shape[0] // 2, t_refs[turn].shape[0] // 2
            for half in range(2):
                v_scr[turn, columns(half, block_len)] = jnp.concatenate(
                    [h_refs[turn][columns(half, first)], t_refs[turn][columns(half, rest)]], axis=0
                )
        facts = facts_of(facts_ref)
        slot = slot_and_head_group()[0]
        low, high = facts.halves(slot)
        low_rows, high_rows = rows_at(low, block_len), rows_at(high, block_len)
        for head in range(Q_DEV):
            key_head = columns(head * KV_DEV // Q_DEV)
            both = columns(head, 2 * HEAD_SIZE)
            low_sum, high_sum = acc_ref[low_rows, both], acc_ref[high_rows, both]
            for turn in range(1, slots):
                outer, *tiles = tiles_of(facts, slot, (slot - turn + slots) % slots)
                either, upper = [
                    dot(
                        w_refs[turn - 1][index, head],
                        beside_ones(v_scr[turn - 1, rows_at(other, block_len), key_head]),
                    )
                    for index, (_, other) in enumerate(tiles)
                ]
                low_sum = low_sum + jnp.where(outer, 0.0, either)
                high_sum = high_sum + upper + jnp.where(outer, either, 0.0)
            for part, total in ((low_rows, low_sum), (high_rows, high_sum)):
                scale = live_ref[part] / total[:, HEAD_SIZE:]
                out_ref[part, columns(head)] = (total[:, :HEAD_SIZE] * scale).astype(bf16)

    shape = jax.ShapeDtypeStruct((rows, Q_DEV * HEAD_SIZE), bf16)
    specs = [SMEM] + [VMEM] * (3 + 3 * others)
    scratch = [pltpu.VMEM((others, rows, KV_WIDTH), bf16)]
    return call(body, shape, specs, "attend", scratch)(
        facts_row, mark, acc, live, *weights, *heads, *tails
    )


def cache_part(early, late, kept):
    cache_rows = kept.shape[0]
    piece = early[0].shape[0] // 2
    width = early[0].shape[1]

    def body(kept_ref, *refs):
        f_refs, s_refs, out_ref, mark_ref = refs[:4], refs[4:8], refs[8], refs[9]
        mark_ref[...] = jnp.zeros_like(mark_ref)
        head_group = slot_and_head_group()[1]
        later = cache_rows - piece
        for index, m in enumerate(HAND_ORDER):
            for kind in range(2):
                lines = jnp.concatenate(
                    [f_refs[index][columns(kind, piece)], s_refs[index][columns(kind, later)]], axis=0
                )
                column = ((head_group ^ m) + kind * HEAD_DIVISIONS) * width
                out_ref[:, pl.ds(pl.multiple_of(column, HEAD_SIZE), width)] = dot(
                    kept_ref[...], lines
                ).astype(bf16)

    shape = [
        jax.ShapeDtypeStruct((cache_rows, 2 * HEAD_DIVISIONS * width), bf16),
        jax.ShapeDtypeStruct((8, HEAD_SIZE), f32),
    ]
    return call(body, shape, [VMEM] * 9, "cache_part")(kept, *early, *late)


def on_device(queries, keys, values, block_map, lengths, group_of_prompt, decode_rank):
    block_len = queries.shape[2] // 2
    slots = block_map.shape[1]
    q, k, v = queries[0, 0], keys[0, 0], values[0, 0]
    tables = rotary_tables(block_len, 2 * slots)

    def to_slots(parts):
        return [shifted(parts[t - 1], "blk", HEAD_DIVISIONS * t) for t in range(1, slots)]

    def hand_on(pieces):
        return [pieces[0]] + [crossed(pieces[m], "blk", m) for m in HAND_ORDER[1:]]

    key_in = to_slots([k] * (slots - 1))
    facts_row, facts_of, block, operands, tables, (select, order), early, sent = prepare(
        q,
        k,
        v,
        block_map,
        decode_rank,
        group_of_prompt,
        tables,
        lengths,
        crossed(lengths, "req", 1),
    )
    heads = to_slots(sent[0::2])
    early = hand_on(early)
    span, groups = 2, lax.axis_size("req")
    while 2 * span < groups:
        other = crossed(block, "req", span)
        upper = (lax.axis_index("req") & span) > 0
        block = jnp.where(
            upper, jnp.concatenate([other, block]), jnp.concatenate([block, other])
        )
        span = 2 * span
    lens = (block, crossed(block, "req", span))
    query_rot, acc, kept, live, angles = own_part(facts_row, facts_of, operands, tables, lens)
    key_rot, chosen = receive_keys(key_in, select, order, angles)
    weights, tails = weigh(
        facts_row, facts_of, query_rot, key_rot, sent[1::2], early[-1]
    )
    tails = to_slots(tails)
    late = hand_on(late_pieces(heads, chosen))
    cache, mark = cache_part(early, late, kept)
    attended = attend(facts_row, facts_of, weights, acc, heads, tails, live, mark)
    return (attended[None, None], cache[None])


def solution(mesh):
    placed = (
        P("req", "blk", None, None),
        P("req", "blk", None, None),
        P("req", "blk", None, None),
        P("req", None, None),
        P("req"),
        P(),
        P("req", None),
    )
    return jax.shard_map(
        on_device,
        mesh=mesh,
        in_specs=placed,
        out_specs=(P("req", "blk", None, None), P("req", "blk", None)),
        check_vma=False,
    )
```

```python
import math

import jax
import jax.numpy as jnp
import numpy as np
from jax import lax
from jax.experimental import pallas as pl
from jax.experimental.pallas import tpu as pltpu
from jax.sharding import PartitionSpec as P

QUERY_HEADS = 16
KEY_VALUE_HEADS = 8
HEAD_SIZE = 128
HEAD_DIVISIONS = 4
Q_DEV = 4
KV_DEV = 2
KV_WIDTH = KV_DEV * HEAD_SIZE

cap_value = 50.0
query_scale = 1.0 / 12.0
HAND_ORDER = (0, 2, 3, 1)
rope_base = 10000.0
VMEM_BYTES = 48 * 1024 * 1024

f32 = jnp.float32
bf16 = jnp.bfloat16
SMEM = pl.BlockSpec(memory_space=pltpu.SMEM)
VMEM = pl.BlockSpec(memory_space=pltpu.VMEM)
HBM = pl.BlockSpec(memory_space=pltpu.HBM)


def shifted(shard, axis, by):
    peers = lax.axis_size(axis)
    return lax.ppermute(shard, axis, [(i, (i + by) % peers) for i in range(peers)])


def crossed(shard, axis, by):
    peers = lax.axis_size(axis)
    return lax.ppermute(shard, axis, [(i, i ^ by) for i in range(peers)])


def rotary_tables(block_len, block_count):
    half = HEAD_SIZE // 2
    frequency = np.exp(
        np.float32(-math.log(rope_base)) * (2.0 * np.arange(half, dtype=np.float32)) / HEAD_SIZE
    ).astype(np.float64)

    def table(positions):
        angles = positions.astype(np.float64)[:, None] * frequency[None, :]
        cosine, sine = np.cos(angles), np.sin(angles)
        return np.stack(
            [np.concatenate([cosine, cosine], 1), np.concatenate([-sine, sine], 1)]
        ).astype(np.float32)

    return table(np.arange(block_len)), table(np.arange(block_count) * block_len)


def block_angles(row_table, block_table, block):
    row_cos, row_sin = row_table[0], row_table[1]
    blk_cos, blk_sin = block_table[0, pl.ds(block, 1)], block_table[1, pl.ds(block, 1)]
    return row_cos * blk_cos - row_sin * blk_sin, row_sin * blk_cos + row_cos * blk_sin


def turned(head, angles):
    x = head.astype(f32)
    return x * angles[0] + pltpu.roll(x, HEAD_SIZE // 2, 1) * angles[1]


def order_matrix(rank_of, slot, head_group, out_rows, rows, residues):
    row_ids = lax.broadcasted_iota(jnp.int32, (1, rows), 1)
    residue = row_ids % residues
    rank = jnp.zeros_like(row_ids)
    for r in range(residues):
        rank = jnp.where(residue == r, rank_of(r), rank)
    ahead = (rank - HEAD_DIVISIONS * slot + residues) % residues
    ahead = jnp.where(ahead < HEAD_DIVISIONS, ahead ^ head_group, ahead)
    index = ahead * (rows // residues) + row_ids // residues
    out_ids = lax.broadcasted_iota(jnp.int32, (out_rows, rows), 0)
    return jnp.where(out_ids == index, 1.0, 0.0).astype(bf16)


def dot(a, b):
    return jnp.dot(a, b, preferred_element_type=f32)


def dot_t(a, b):
    return lax.dot_general(a, b, (((1,), (1,)), ((), ())), preferred_element_type=f32)


def expo_of(scores):
    return jnp.exp2(cap_value * math.log2(math.e) * jnp.tanh(scores * (1.0 / cap_value)))


def columns(index, width=HEAD_SIZE):
    return slice(index * width, (index + 1) * width)


def call(body, out_shape, in_specs, name, scratch=(), out_specs=None, cost=1000):
    return pl.pallas_call(
        body,
        out_shape=out_shape,
        in_specs=in_specs,
        out_specs=jax.tree.map(lambda _: VMEM, out_shape) if out_specs is None else out_specs,
        scratch_shapes=scratch,
        compiler_params=pltpu.CompilerParams(vmem_limit_bytes=VMEM_BYTES),
        cost_estimate=pl.CostEstimate(flops=cost, bytes_accessed=1000, transcendentals=0),
        name=name,
    )


def in_hbm(arrays):
    return [pltpu.with_memory_space_constraint(x, pltpu.HBM) for x in arrays]


def rows_at(index, size):
    return pl.ds(pl.multiple_of(index * size, size), size)


def beside_ones(values):
    return jnp.concatenate([values, jnp.ones(values.shape, bf16)], axis=1)


class Facts:
    def __init__(self, ref, slots, residues, groups):
        self.ref, self.slots, self.residues, self.groups = ref, slots, residues, groups
        self.size = 2 * slots + residues + groups

    def block(self, slot, half):
        return self.ref[0, 2 * slot + half]

    def rank(self, residue):
        return self.ref[0, 2 * self.slots + residue]

    def owner(self, prompt):
        return self.ref[0, 2 * self.slots + self.residues + prompt]

    def store(self, map_ref, rank_ref, owner_ref):
        for slot in range(self.slots):
            for half in range(2):
                self.ref[0, 2 * slot + half] = map_ref[0, slot, half]
        for residue in range(self.residues):
            self.ref[0, 2 * self.slots + residue] = rank_ref[0, residue]
        for prompt in range(self.groups):
            self.ref[0, 2 * self.slots + self.residues + prompt] = owner_ref[prompt]

    def halves(self, slot):
        high = jnp.where(self.block(slot, 1) > self.block(slot, 0), 1, 0)
        return 1 - high, high


def slot_and_head_group():
    member = lax.axis_index("blk")
    return member // HEAD_DIVISIONS, member % HEAD_DIVISIONS


def prepare(queries, keys, values, table, decode_rank, owner, tables, own_length, near_length):
    rows, width = keys.shape
    block_len = rows // 2
    slots = table.shape[1]
    residues = decode_rank.shape[1]
    piece = rows // residues
    first = block_len // slots
    arrays = (keys, values, queries, *tables, table, decode_rank, owner)
    count = len(arrays)
    facts_of = lambda ref: Facts(ref, slots, residues, owner.shape[0])

    def body(own_ref, near_ref, *refs):
        inputs, refs = refs[:count], refs[count:]
        facts_ref, pair_ref, q_ref, kr_ref, v_ref, row_ref, blk_ref, select_ref, order_ref = refs[:9]
        e_refs, refs = refs[9:13], refs[13:]
        sent_refs, refs = refs[: 2 * slots - 2], refs[2 * slots - 2 :]
        k_ref, map_ref, rank_ref, owner_ref, sems = refs
        targets = (k_ref, v_ref, q_ref, row_ref, blk_ref, map_ref, rank_ref, owner_ref)
        copies = []
        for index in range(count):
            copies.append(pltpu.make_async_copy(inputs[index], targets[index], sems.at[index]))
            copies[-1].start()
        slot, head_group = slot_and_head_group()
        odd = lax.axis_index("req") % 2 == 1
        pair_ref[0] = jnp.where(odd, near_ref[0], own_ref[0])
        pair_ref[1] = jnp.where(odd, own_ref[0], near_ref[0])
        for index in (0, 3, 4, 5, 6, 7):
            copies[index].wait()
        facts_of(facts_ref).store(map_ref, rank_ref, owner_ref)
        for half in range(2):
            part = columns(half, block_len)
            angles = block_angles(row_ref, blk_ref, map_ref[0, slot, half])
            for head in range(KV_DEV):
                kr_ref[part, columns(head)] = turned(k_ref[part, columns(head)], angles).astype(bf16)
        select = order_matrix(
            lambda r: rank_ref[0, r], slot, head_group, rows // slots, rows, residues
        )
        select_ref[...] = select
        copies[1].wait()
        for turn in range(1, slots):
            order = order_matrix(
                lambda r: rank_ref[0, r],
                (slot + turn) % slots,
                head_group,
                block_len,
                block_len,
                residues,
            )
            for half in range(2):
                moved = dot(order, v_ref[columns(half, block_len)]).astype(bf16)
                sent_refs[2 * turn - 2][columns(half, first)] = moved[:first]
                sent_refs[2 * turn - 1][columns(half, block_len - first)] = moved[first:]
        order_ref[...] = order_matrix(
            lambda r: rank_ref[0, r], slot, head_group, block_len, block_len, residues
        )
        for kind, source in enumerate((kr_ref, v_ref)):
            chosen = dot(select, source[...]).astype(bf16)
            for m in range(HEAD_DIVISIONS):
                e_refs[m][columns(kind, piece)] = chosen[columns(m, piece)]
        copies[2].wait()

    shapes = [
        jax.ShapeDtypeStruct((1, facts_of(None).size), jnp.int32),
        jax.ShapeDtypeStruct((2,), jnp.int32),
        jax.ShapeDtypeStruct(queries.shape, bf16),
        jax.ShapeDtypeStruct(keys.shape, bf16),
        jax.ShapeDtypeStruct(values.shape, bf16),
        jax.ShapeDtypeStruct(tables[0].shape, f32),
        jax.ShapeDtypeStruct(tables[1].shape, f32),
        jax.ShapeDtypeStruct((rows // slots, rows), bf16),
        jax.ShapeDtypeStruct((block_len, block_len), bf16),
    ]
    shapes += [jax.ShapeDtypeStruct((2 * piece, width), bf16) for _ in range(HEAD_DIVISIONS)]
    for _ in range(1, slots):
        shapes.append(jax.ShapeDtypeStruct((2 * first, width), bf16))
        shapes.append(jax.ShapeDtypeStruct((2 * (block_len - first), width), bf16))
    scratch = [pltpu.VMEM(keys.shape, keys.dtype)]
    scratch += [pltpu.SMEM(x.shape, x.dtype) for x in (table, decode_rank, owner)]
    scratch.append(pltpu.SemaphoreType.DMA((count,)))
    outs = call(
        body,
        shapes,
        [SMEM] * 2 + [HBM] * count,
        "prepare",
        scratch,
        out_specs=[SMEM] * 2 + [VMEM] * (len(shapes) - 2),
    )(own_length, near_length, *in_hbm(arrays))
    return outs[0], facts_of, outs[1], outs[2:5], outs[5:7], outs[7:9], outs[9:13], outs[13:]


def own_part(facts_row, facts_of, operands, tables, lens):
    queries = operands[0]
    rows = queries.shape[0]
    block_len = rows // 2
    sizes = facts_of(None)
    slots, residues, groups = sizes.slots, sizes.residues, sizes.groups
    run = block_len // residues
    cache_rows = 2 * slots * run

    def body(facts_ref, here_ref, there_ref, q_ref, kr_ref, v_ref, row_ref, blk_ref, *refs):
        qr_ref, acc_ref, kept_ref, live_ref, angle_ref = refs
        facts = facts_of(facts_ref)
        slot = slot_and_head_group()[0]
        group = lax.axis_index("req")
        for half in range(2):
            part = columns(half, block_len)
            angles = block_angles(row_ref, blk_ref, facts.block(slot, half))
            for head in range(Q_DEV):
                qr_ref[part, columns(head)] = (
                    turned(q_ref[part, columns(head)], angles) * query_scale
                ).astype(bf16)
            for turn in range(1, slots):
                block = facts.block((slot - turn + slots) % slots, half)
                other = block_angles(row_ref, blk_ref, block)
                angle_ref[turn - 1, half, 0] = other[0]
                angle_ref[turn - 1, half, 1] = other[1]
        low, high = facts.halves(slot)
        low, high = rows_at(low, block_len), rows_at(high, block_len)
        row = lax.broadcasted_iota(jnp.int32, (block_len, block_len), 0)
        col = lax.broadcasted_iota(jnp.int32, (block_len, block_len), 1)
        for head in range(Q_DEV):
            key_head = columns(head * KV_DEV // Q_DEV)
            both = columns(head, 2 * HEAD_SIZE)

            def tile(q_part, k_part, diagonal):
                expo = expo_of(dot_t(qr_ref[q_part, columns(head)], kr_ref[k_part, key_head]))
                if diagonal:
                    expo = jnp.where(col <= row, expo, 0.0)
                return dot(expo.astype(bf16), beside_ones(v_ref[k_part, key_head]))

            acc_ref[low, both] = tile(low, low, True)
            acc_ref[high, both] = tile(high, high, True) + tile(high, low, False)

        col = lax.broadcasted_iota(jnp.int32, (1, cache_rows), 1)
        part, offset = col // run, col % run
        target = jnp.zeros_like(col)
        for turn in range(slots):
            for half in range(2):
                block = facts.block((slot - turn + slots) % slots, half)
                target = jnp.where(part == 2 * turn + half, block * run + offset, target)
        length = 0
        half_count = groups // 2
        for index in range(half_count):
            same = (group & half_count) | index
            length = length + jnp.where(facts.owner(same) == group, here_ref[index], 0)
            other = same ^ half_count
            length = length + jnp.where(facts.owner(other) == group, there_ref[index], 0)
        residue = 0
        for r in range(1, residues):
            residue = jnp.where(facts.rank(r) == lax.axis_index("blk"), r, residue)
        target = jnp.where(target * residues + residue < length, target, -1)
        row = lax.broadcasted_iota(jnp.int32, (cache_rows, cache_rows), 0)
        kept_ref[...] = jnp.where(row == target, 1.0, 0.0).astype(bf16)
        for half in range(2):
            offset = lax.broadcasted_iota(jnp.int32, (block_len, HEAD_SIZE), 0)
            at = facts.block(slot, half) * block_len + offset
            live_ref[columns(half, block_len)] = jnp.where(at < length, 1.0, 0.0)

    shapes = [
        jax.ShapeDtypeStruct(queries.shape, bf16),
        jax.ShapeDtypeStruct((rows, 2 * Q_DEV * HEAD_SIZE), f32),
        jax.ShapeDtypeStruct((cache_rows, cache_rows), bf16),
        jax.ShapeDtypeStruct((rows, HEAD_SIZE), f32),
        jax.ShapeDtypeStruct((slots - 1, 2, 2, block_len, HEAD_SIZE), f32),
    ]
    return call(body, shapes, [SMEM] * 3 + [VMEM] * 5, "own_part")(
        facts_row, *lens, *operands, *tables
    )


def tiles_of(facts, slot, source):
    low, high = facts.halves(slot)
    source_low, source_high = facts.halves(source)
    outer = facts.block(slot, low) < facts.block(source, source_low)
    first = (jnp.where(outer, high, low), source_low)
    second = (high, jnp.where(outer, source_high, source_low))
    return outer, first, second


def receive_keys(key_in, select, order, angles):
    others = len(key_in)
    rows, width = key_in[0].shape
    block_len = rows // 2

    def body(select_ref, order_ref, angle_ref, *refs):
        k_refs, refs = refs[:others], refs[others:]
        p_refs, chosen_ref, kr_ref = refs[:others], refs[others], refs[others + 1]
        for turn in range(others):
            for half in range(2):
                part = columns(half, block_len)
                there = angle_ref[turn, half, 0], angle_ref[turn, half, 1]
                for head in range(KV_DEV):
                    kr_ref[part, columns(head)] = turned(
                        k_refs[turn][part, columns(head)], there
                    ).astype(bf16)
                p_refs[turn][part] = dot(order_ref[...], kr_ref[part]).astype(bf16)
            chosen_ref[turn] = dot(select_ref[...], kr_ref[...]).astype(bf16)

    shapes = [jax.ShapeDtypeStruct((rows, width), bf16) for _ in range(others)]
    shapes.append(jax.ShapeDtypeStruct((others, select.shape[0], width), bf16))
    scratch = [pltpu.VMEM((rows, width), bf16)]
    outs = call(body, shapes, [VMEM] * (3 + others), "receive_keys", scratch, cost=10**10)(
        select, order, angles, *key_in
    )
    return outs[:others], outs[others]


def weigh(facts_row, facts_of, query_rot, key_rot):
    others = len(key_rot)
    rows = query_rot.shape[0]
    block_len = rows // 2
    slots = facts_of(None).slots

    def body(facts_ref, q_ref, *refs):
        k_refs, w_refs = refs[:others], refs[others:]
        facts = facts_of(facts_ref)
        slot = slot_and_head_group()[0]
        for turn in range(1, slots):
            _, *tiles = tiles_of(facts, slot, (slot - turn + slots) % slots)
            for index, (half, other) in enumerate(tiles):
                for head in range(Q_DEV):
                    key_head = columns(head * KV_DEV // Q_DEV)
                    queries = q_ref[rows_at(half, block_len), columns(head)]
                    keys = k_refs[turn - 1][rows_at(other, block_len), key_head]
                    w_refs[turn - 1][index, head] = expo_of(dot_t(queries, keys)).astype(bf16)

    shapes = [
        jax.ShapeDtypeStruct((2, Q_DEV, block_len, block_len), bf16) for _ in range(others)
    ]
    return call(body, shapes, [SMEM] + [VMEM] * (1 + others), "weigh")(
        facts_row, query_rot, *key_rot
    )


def late_pieces(heads, key_chosen, after):
    others, rows, width = key_chosen.shape
    piece = rows // HEAD_DIVISIONS
    run = piece // 2
    first = heads[0].shape[0] // 2

    def body(key_ref, *refs):
        v_refs, e_refs = refs[:others], refs[others + len(after) :]
        for m in range(HEAD_DIVISIONS):
            for turn in range(others):
                e_refs[m][columns(turn, piece)] = key_ref[turn, columns(m, piece)]
                place = 2 * (others + turn)
                if run % 16 == 0:
                    for half in range(2):
                        start = half * first + m * run
                        e_refs[m][columns(place + half, run)] = v_refs[turn][start : start + run]
                    continue
                lines = [
                    v_refs[turn][columns(half, first)].astype(f32)[columns(m, run)]
                    for half in range(2)
                ]
                e_refs[m][place * run : (place + 2) * run] = jnp.concatenate(lines, 0).astype(bf16)

    shapes = [
        jax.ShapeDtypeStruct((2 * others * piece, width), bf16) for _ in range(HEAD_DIVISIONS)
    ]
    return call(body, shapes, [VMEM] * (1 + others + len(after)), "late_pieces")(
        key_chosen, *heads, *after
    )


def attend(facts_row, facts_of, weights, acc, heads, tails, live):
    rows = live.shape[0]
    block_len = rows // 2
    others = len(weights)
    slots = facts_of(None).slots

    def body(facts_ref, acc_ref, live_ref, *refs):
        w_refs, h_refs, t_refs = refs[:others], refs[others : 2 * others], refs[2 * others : 3 * others]
        out_ref, mark_ref, v_scr = refs[3 * others :]
        mark_ref[...] = jnp.zeros_like(mark_ref)
        for turn in range(others):
            first, rest = h_refs[turn].shape[0] // 2, t_refs[turn].shape[0] // 2
            for half in range(2):
                v_scr[turn, columns(half, block_len)] = jnp.concatenate(
                    [h_refs[turn][columns(half, first)], t_refs[turn][columns(half, rest)]], axis=0
                )
        facts = facts_of(facts_ref)
        slot = slot_and_head_group()[0]
        low, high = facts.halves(slot)
        low_rows, high_rows = rows_at(low, block_len), rows_at(high, block_len)
        for head in range(Q_DEV):
            key_head = columns(head * KV_DEV // Q_DEV)
            both = columns(head, 2 * HEAD_SIZE)
            low_sum, high_sum = acc_ref[low_rows, both], acc_ref[high_rows, both]
            for turn in range(1, slots):
                outer, *tiles = tiles_of(facts, slot, (slot - turn + slots) % slots)
                either, upper = [
                    dot(
                        w_refs[turn - 1][index, head],
                        beside_ones(v_scr[turn - 1, rows_at(other, block_len), key_head]),
                    )
                    for index, (_, other) in enumerate(tiles)
                ]
                low_sum = low_sum + jnp.where(outer, 0.0, either)
                high_sum = high_sum + upper + jnp.where(outer, either, 0.0)
            for part, total in ((low_rows, low_sum), (high_rows, high_sum)):
                scale = live_ref[part] / total[:, HEAD_SIZE:]
                out_ref[part, columns(head)] = (total[:, :HEAD_SIZE] * scale).astype(bf16)

    shape = [
        jax.ShapeDtypeStruct((rows, Q_DEV * HEAD_SIZE), bf16),
        jax.ShapeDtypeStruct((8, HEAD_SIZE), f32),
    ]
    specs = [SMEM] + [VMEM] * (2 + 3 * others)
    scratch = [pltpu.VMEM((others, rows, KV_WIDTH), bf16)]
    return call(body, shape, specs, "attend", scratch)(
        facts_row, acc, live, *weights, *heads, *tails
    )


def cache_part(early, late, kept, mark):
    cache_rows = kept.shape[0]
    piece = early[0].shape[0] // 2
    width = early[0].shape[1]

    def body(kept_ref, *refs):
        f_refs, s_refs, out_ref = refs[:4], refs[4:8], refs[9]
        head_group = slot_and_head_group()[1]
        later = cache_rows - piece
        for index, m in enumerate(HAND_ORDER):
            for kind in range(2):
                lines = jnp.concatenate(
                    [f_refs[index][columns(kind, piece)], s_refs[index][columns(kind, later)]], axis=0
                )
                column = ((head_group ^ m) + kind * HEAD_DIVISIONS) * width
                out_ref[:, pl.ds(pl.multiple_of(column, HEAD_SIZE), width)] = dot(
                    kept_ref[...], lines
                ).astype(bf16)

    shape = jax.ShapeDtypeStruct((cache_rows, 2 * HEAD_DIVISIONS * width), bf16)
    return call(body, shape, [VMEM] * 10, "cache_part")(kept, *early, *late, mark)


def on_device(queries, keys, values, block_map, lengths, group_of_prompt, decode_rank):
    block_len = queries.shape[2] // 2
    slots = block_map.shape[1]
    q, k, v = queries[0, 0], keys[0, 0], values[0, 0]
    tables = rotary_tables(block_len, 2 * slots)

    def to_slots(parts):
        return [shifted(parts[t - 1], "blk", HEAD_DIVISIONS * t) for t in range(1, slots)]

    def hand_on(pieces):
        return [pieces[0]] + [crossed(pieces[m], "blk", m) for m in HAND_ORDER[1:]]

    key_in = to_slots([k] * (slots - 1))
    facts_row, facts_of, block, operands, tables, (select, order), early, sent = prepare(
        q,
        k,
        v,
        block_map,
        decode_rank,
        group_of_prompt,
        tables,
        lengths,
        crossed(lengths, "req", 1),
    )
    heads = to_slots(sent[0::2])
    tails, key_in = lax.optimization_barrier((sent[1::2], key_in))
    tails = to_slots(tails)
    early = hand_on(early)
    span, groups = 2, lax.axis_size("req")
    while 2 * span < groups:
        other = crossed(block, "req", span)
        upper = (lax.axis_index("req") & span) > 0
        block = jnp.where(
            upper, jnp.concatenate([other, block]), jnp.concatenate([block, other])
        )
        span = 2 * span
    lens = (block, crossed(block, "req", span))
    query_rot, acc, kept, live, angles = own_part(facts_row, facts_of, operands, tables, lens)
    key_rot, chosen = receive_keys(key_in, select, order, angles)
    late = hand_on(late_pieces(heads, chosen, early[1:]))
    weights = weigh(facts_row, facts_of, query_rot, key_rot)
    attended, mark = attend(facts_row, facts_of, weights, acc, heads, tails, live)
    cache = cache_part(early, late, kept, mark)
    return (attended[None, None], cache[None])


def solution(mesh):
    placed = (
        P("req", "blk", None, None),
        P("req", "blk", None, None),
        P("req", "blk", None, None),
        P("req", None, None),
        P("req"),
        P(),
        P("req", None),
    )
    return jax.shard_map(
        on_device,
        mesh=mesh,
        in_specs=placed,
        out_specs=(P("req", "blk", None, None), P("req", "blk", None)),
        check_vma=False,
    )
```

```python
import math

import jax
import jax.numpy as jnp
import numpy as np
from jax import lax
from jax.experimental import pallas as pl
from jax.experimental.pallas import tpu as pltpu
from jax.sharding import PartitionSpec as P

QUERY_HEADS = 16
KEY_VALUE_HEADS = 8
HEAD_SIZE = 128
HEAD_DIVISIONS = 4
Q_DEV = 4
KV_DEV = 2
KV_WIDTH = KV_DEV * HEAD_SIZE

cap_value = 50.0
query_scale = 1.0 / 12.0
HAND_ORDER = (0, 2, 3, 1)
rope_base = 10000.0
VMEM_BYTES = 48 * 1024 * 1024

f32 = jnp.float32
bf16 = jnp.bfloat16
SMEM = pl.BlockSpec(memory_space=pltpu.SMEM)
VMEM = pl.BlockSpec(memory_space=pltpu.VMEM)
HBM = pl.BlockSpec(memory_space=pltpu.HBM)


def shifted(shard, axis, by):
    peers = lax.axis_size(axis)
    return lax.ppermute(shard, axis, [(i, (i + by) % peers) for i in range(peers)])


def crossed(shard, axis, by):
    peers = lax.axis_size(axis)
    return lax.ppermute(shard, axis, [(i, i ^ by) for i in range(peers)])


def rotary_tables(block_len, block_count):
    half = HEAD_SIZE // 2
    frequency = np.exp(
        np.float32(-math.log(rope_base)) * (2.0 * np.arange(half, dtype=np.float32)) / HEAD_SIZE
    ).astype(np.float64)

    def table(positions):
        angles = positions.astype(np.float64)[:, None] * frequency[None, :]
        cosine, sine = np.cos(angles), np.sin(angles)
        return np.stack(
            [np.concatenate([cosine, cosine], 1), np.concatenate([-sine, sine], 1)]
        ).astype(np.float32)

    return table(np.arange(block_len)), table(np.arange(block_count) * block_len)


def block_angles(row_table, block_table, block):
    row_cos, row_sin = row_table[0], row_table[1]
    blk_cos, blk_sin = block_table[0, pl.ds(block, 1)], block_table[1, pl.ds(block, 1)]
    return row_cos * blk_cos - row_sin * blk_sin, row_sin * blk_cos + row_cos * blk_sin


def turned(head, angles):
    x = head.astype(f32)
    return x * angles[0] + pltpu.roll(x, HEAD_SIZE // 2, 1) * angles[1]


def order_matrix(rank_of, slot, head_group, out_rows, rows, residues):
    row_ids = lax.broadcasted_iota(jnp.int32, (1, rows), 1)
    residue = row_ids % residues
    rank = jnp.zeros_like(row_ids)
    for r in range(residues):
        rank = jnp.where(residue == r, rank_of(r), rank)
    ahead = (rank - HEAD_DIVISIONS * slot + residues) % residues
    ahead = jnp.where(ahead < HEAD_DIVISIONS, ahead ^ head_group, ahead)
    index = ahead * (rows // residues) + row_ids // residues
    out_ids = lax.broadcasted_iota(jnp.int32, (out_rows, rows), 0)
    return jnp.where(out_ids == index, 1.0, 0.0).astype(bf16)


def dot(a, b):
    return jnp.dot(a, b, preferred_element_type=f32)


def dot_t(a, b):
    return lax.dot_general(a, b, (((1,), (1,)), ((), ())), preferred_element_type=f32)


def expo_of(scores):
    return jnp.exp2(cap_value * math.log2(math.e) * jnp.tanh(scores * (1.0 / cap_value)))


def columns(index, width=HEAD_SIZE):
    return slice(index * width, (index + 1) * width)


def call(body, out_shape, in_specs, name, scratch=(), out_specs=None, cost=1000):
    return pl.pallas_call(
        body,
        out_shape=out_shape,
        in_specs=in_specs,
        out_specs=jax.tree.map(lambda _: VMEM, out_shape) if out_specs is None else out_specs,
        scratch_shapes=scratch,
        compiler_params=pltpu.CompilerParams(vmem_limit_bytes=VMEM_BYTES),
        cost_estimate=pl.CostEstimate(flops=cost, bytes_accessed=1000, transcendentals=0),
        name=name,
    )


def in_hbm(arrays):
    return [pltpu.with_memory_space_constraint(x, pltpu.HBM) for x in arrays]


def rows_at(index, size):
    return pl.ds(pl.multiple_of(index * size, size), size)


def beside_ones(values):
    return jnp.concatenate([values, jnp.ones(values.shape, bf16)], axis=1)


class Facts:
    def __init__(self, ref, slots, residues, groups):
        self.ref, self.slots, self.residues, self.groups = ref, slots, residues, groups
        self.size = 2 * slots + residues + groups

    def block(self, slot, half):
        return self.ref[0, 2 * slot + half]

    def rank(self, residue):
        return self.ref[0, 2 * self.slots + residue]

    def owner(self, prompt):
        return self.ref[0, 2 * self.slots + self.residues + prompt]

    def store(self, map_ref, rank_ref, owner_ref):
        for slot in range(self.slots):
            for half in range(2):
                self.ref[0, 2 * slot + half] = map_ref[0, slot, half]
        for residue in range(self.residues):
            self.ref[0, 2 * self.slots + residue] = rank_ref[0, residue]
        for prompt in range(self.groups):
            self.ref[0, 2 * self.slots + self.residues + prompt] = owner_ref[prompt]

    def halves(self, slot):
        high = jnp.where(self.block(slot, 1) > self.block(slot, 0), 1, 0)
        return 1 - high, high


def slot_and_head_group():
    member = lax.axis_index("blk")
    return member // HEAD_DIVISIONS, member % HEAD_DIVISIONS


def prepare(queries, keys, values, table, decode_rank, owner, tables, own_length, near_length):
    rows, width = keys.shape
    block_len = rows // 2
    slots = table.shape[1]
    residues = decode_rank.shape[1]
    piece = rows // residues
    first = block_len // slots
    arrays = (keys, values, queries, *tables, table, decode_rank, owner)
    count = len(arrays)
    facts_of = lambda ref: Facts(ref, slots, residues, owner.shape[0])

    def body(own_ref, near_ref, *refs):
        inputs, refs = refs[:count], refs[count:]
        facts_ref, pair_ref, q_ref, kr_ref, v_ref, row_ref, blk_ref, select_ref, order_ref = refs[:9]
        e_refs, refs = refs[9:13], refs[13:]
        sent_refs, refs = refs[: 2 * slots - 2], refs[2 * slots - 2 :]
        k_ref, map_ref, rank_ref, owner_ref, sems = refs
        targets = (k_ref, v_ref, q_ref, row_ref, blk_ref, map_ref, rank_ref, owner_ref)
        copies = []
        for index in range(count):
            copies.append(pltpu.make_async_copy(inputs[index], targets[index], sems.at[index]))
            copies[-1].start()
        slot, head_group = slot_and_head_group()
        odd = lax.axis_index("req") % 2 == 1
        pair_ref[0] = jnp.where(odd, near_ref[0], own_ref[0])
        pair_ref[1] = jnp.where(odd, own_ref[0], near_ref[0])
        for index in (0, 3, 4, 5, 6, 7):
            copies[index].wait()
        facts_of(facts_ref).store(map_ref, rank_ref, owner_ref)
        for half in range(2):
            part = columns(half, block_len)
            angles = block_angles(row_ref, blk_ref, map_ref[0, slot, half])
            for head in range(KV_DEV):
                kr_ref[part, columns(head)] = turned(k_ref[part, columns(head)], angles).astype(bf16)
        select = order_matrix(
            lambda r: rank_ref[0, r], slot, head_group, rows // slots, rows, residues
        )
        select_ref[...] = select
        copies[1].wait()
        for turn in range(1, slots):
            order = order_matrix(
                lambda r: rank_ref[0, r],
                (slot + turn) % slots,
                head_group,
                block_len,
                block_len,
                residues,
            )
            for half in range(2):
                moved = dot(order, v_ref[columns(half, block_len)]).astype(bf16)
                sent_refs[2 * turn - 2][columns(half, first)] = moved[:first]
                sent_refs[2 * turn - 1][columns(half, block_len - first)] = moved[first:]
        order_ref[...] = order_matrix(
            lambda r: rank_ref[0, r], slot, head_group, block_len, block_len, residues
        )
        for kind, source in enumerate((kr_ref, v_ref)):
            chosen = dot(select, source[...]).astype(bf16)
            for m in range(HEAD_DIVISIONS):
                e_refs[m][columns(kind, piece)] = chosen[columns(m, piece)]
        copies[2].wait()

    shapes = [
        jax.ShapeDtypeStruct((1, facts_of(None).size), jnp.int32),
        jax.ShapeDtypeStruct((2,), jnp.int32),
        jax.ShapeDtypeStruct(queries.shape, bf16),
        jax.ShapeDtypeStruct(keys.shape, bf16),
        jax.ShapeDtypeStruct(values.shape, bf16),
        jax.ShapeDtypeStruct(tables[0].shape, f32),
        jax.ShapeDtypeStruct(tables[1].shape, f32),
        jax.ShapeDtypeStruct((rows // slots, rows), bf16),
        jax.ShapeDtypeStruct((block_len, block_len), bf16),
    ]
    shapes += [jax.ShapeDtypeStruct((2 * piece, width), bf16) for _ in range(HEAD_DIVISIONS)]
    for _ in range(1, slots):
        shapes.append(jax.ShapeDtypeStruct((2 * first, width), bf16))
        shapes.append(jax.ShapeDtypeStruct((2 * (block_len - first), width), bf16))
    scratch = [pltpu.VMEM(keys.shape, keys.dtype)]
    scratch += [pltpu.SMEM(x.shape, x.dtype) for x in (table, decode_rank, owner)]
    scratch.append(pltpu.SemaphoreType.DMA((count,)))
    outs = call(
        body,
        shapes,
        [SMEM] * 2 + [HBM] * count,
        "prepare",
        scratch,
        out_specs=[SMEM] * 2 + [VMEM] * (len(shapes) - 2),
    )(own_length, near_length, *in_hbm(arrays))
    return outs[0], facts_of, outs[1], outs[2:5], outs[5:7], outs[7:9], outs[9:13], outs[13:]


def own_part(facts_row, facts_of, operands, tables, lens):
    queries = operands[0]
    rows = queries.shape[0]
    block_len = rows // 2
    sizes = facts_of(None)
    slots, residues, groups = sizes.slots, sizes.residues, sizes.groups
    run = block_len // residues
    cache_rows = 2 * slots * run

    def body(facts_ref, here_ref, there_ref, q_ref, kr_ref, v_ref, row_ref, blk_ref, *refs):
        qr_ref, acc_ref, kept_ref, live_ref, angle_ref = refs
        facts = facts_of(facts_ref)
        slot = slot_and_head_group()[0]
        group = lax.axis_index("req")
        for half in range(2):
            part = columns(half, block_len)
            angles = block_angles(row_ref, blk_ref, facts.block(slot, half))
            for head in range(Q_DEV):
                qr_ref[part, columns(head)] = (
                    turned(q_ref[part, columns(head)], angles) * query_scale
                ).astype(bf16)
            for turn in range(1, slots):
                block = facts.block((slot - turn + slots) % slots, half)
                other = block_angles(row_ref, blk_ref, block)
                angle_ref[turn - 1, half, 0] = other[0]
                angle_ref[turn - 1, half, 1] = other[1]
        low, high = facts.halves(slot)
        low, high = rows_at(low, block_len), rows_at(high, block_len)
        row = lax.broadcasted_iota(jnp.int32, (block_len, block_len), 0)
        col = lax.broadcasted_iota(jnp.int32, (block_len, block_len), 1)
        for head in range(Q_DEV):
            key_head = columns(head * KV_DEV // Q_DEV)
            both = columns(head, 2 * HEAD_SIZE)

            def tile(q_part, k_part, diagonal):
                expo = expo_of(dot_t(qr_ref[q_part, columns(head)], kr_ref[k_part, key_head]))
                if diagonal:
                    expo = jnp.where(col <= row, expo, 0.0)
                return dot(expo.astype(bf16), beside_ones(v_ref[k_part, key_head]))

            acc_ref[low, both] = tile(low, low, True)
            acc_ref[high, both] = tile(high, high, True) + tile(high, low, False)

        col = lax.broadcasted_iota(jnp.int32, (1, cache_rows), 1)
        part, offset = col // run, col % run
        target = jnp.zeros_like(col)
        for turn in range(slots):
            for half in range(2):
                block = facts.block((slot - turn + slots) % slots, half)
                target = jnp.where(part == 2 * turn + half, block * run + offset, target)
        length = 0
        half_count = groups // 2
        for index in range(half_count):
            same = (group & half_count) | index
            length = length + jnp.where(facts.owner(same) == group, here_ref[index], 0)
            other = same ^ half_count
            length = length + jnp.where(facts.owner(other) == group, there_ref[index], 0)
        residue = 0
        for r in range(1, residues):
            residue = jnp.where(facts.rank(r) == lax.axis_index("blk"), r, residue)
        target = jnp.where(target * residues + residue < length, target, -1)
        row = lax.broadcasted_iota(jnp.int32, (cache_rows, cache_rows), 0)
        kept_ref[...] = jnp.where(row == target, 1.0, 0.0).astype(bf16)
        for half in range(2):
            offset = lax.broadcasted_iota(jnp.int32, (block_len, HEAD_SIZE), 0)
            at = facts.block(slot, half) * block_len + offset
            live_ref[columns(half, block_len)] = jnp.where(at < length, 1.0, 0.0)

    shapes = [
        jax.ShapeDtypeStruct(queries.shape, bf16),
        jax.ShapeDtypeStruct((rows, 2 * Q_DEV * HEAD_SIZE), f32),
        jax.ShapeDtypeStruct((cache_rows, cache_rows), bf16),
        jax.ShapeDtypeStruct((rows, HEAD_SIZE), f32),
        jax.ShapeDtypeStruct((slots - 1, 2, 2, block_len, HEAD_SIZE), f32),
    ]
    return call(body, shapes, [SMEM] * 3 + [VMEM] * 5, "own_part")(
        facts_row, *lens, *operands, *tables
    )


def tiles_of(facts, slot, source):
    low, high = facts.halves(slot)
    source_low, source_high = facts.halves(source)
    outer = facts.block(slot, low) < facts.block(source, source_low)
    first = (jnp.where(outer, high, low), source_low)
    second = (high, jnp.where(outer, source_high, source_low))
    return outer, first, second


def receive_keys(key_in, select, order, angles):
    others = len(key_in)
    rows, width = key_in[0].shape
    block_len = rows // 2

    def body(select_ref, order_ref, angle_ref, *refs):
        k_refs, refs = refs[:others], refs[others:]
        p_refs, chosen_ref, kr_ref = refs[:others], refs[others], refs[others + 1]
        for turn in range(others):
            for half in range(2):
                part = columns(half, block_len)
                there = angle_ref[turn, half, 0], angle_ref[turn, half, 1]
                for head in range(KV_DEV):
                    kr_ref[part, columns(head)] = turned(
                        k_refs[turn][part, columns(head)], there
                    ).astype(bf16)
                p_refs[turn][part] = dot(order_ref[...], kr_ref[part]).astype(bf16)
            chosen_ref[turn] = dot(select_ref[...], kr_ref[...]).astype(bf16)

    shapes = [jax.ShapeDtypeStruct((rows, width), bf16) for _ in range(others)]
    shapes.append(jax.ShapeDtypeStruct((others, select.shape[0], width), bf16))
    scratch = [pltpu.VMEM((rows, width), bf16)]
    outs = call(body, shapes, [VMEM] * (3 + others), "receive_keys", scratch, cost=10**10)(
        select, order, angles, *key_in
    )
    return outs[:others], outs[others]


def weigh(facts_row, facts_of, query_rot, key_rot, payload):
    others = len(key_rot)
    rows = query_rot.shape[0]
    block_len = rows // 2
    slots = facts_of(None).slots

    def body(facts_ref, q_ref, *refs):
        k_refs, pay_refs, refs = refs[:others], refs[others : 2 * others], refs[2 * others :]
        w_refs, out_refs = refs[:others], refs[others:]
        for pay_ref, out_ref in zip(pay_refs, out_refs):
            out_ref[...] = pay_ref[...]
        facts = facts_of(facts_ref)
        slot = slot_and_head_group()[0]
        for turn in range(1, slots):
            _, *tiles = tiles_of(facts, slot, (slot - turn + slots) % slots)
            for index, (half, other) in enumerate(tiles):
                for head in range(Q_DEV):
                    key_head = columns(head * KV_DEV // Q_DEV)
                    queries = q_ref[rows_at(half, block_len), columns(head)]
                    keys = k_refs[turn - 1][rows_at(other, block_len), key_head]
                    w_refs[turn - 1][index, head] = expo_of(dot_t(queries, keys)).astype(bf16)

    shapes = [
        jax.ShapeDtypeStruct((2, Q_DEV, block_len, block_len), bf16) for _ in range(others)
    ]
    shapes += [jax.ShapeDtypeStruct(x.shape, bf16) for x in payload]
    outs = call(body, shapes, [SMEM] + [VMEM] * (1 + 2 * others), "weigh")(
        facts_row, query_rot, *key_rot, *payload
    )
    return outs[:others], outs[others:]


def late_pieces(heads, key_chosen, after):
    others, rows, width = key_chosen.shape
    piece = rows // HEAD_DIVISIONS
    run = piece // 2
    first = heads[0].shape[0] // 2

    def body(key_ref, *refs):
        v_refs, e_refs = refs[:others], refs[others + len(after) :]
        for m in range(HEAD_DIVISIONS):
            for turn in range(others):
                e_refs[m][columns(turn, piece)] = key_ref[turn, columns(m, piece)]
                place = 2 * (others + turn)
                if run % 16 == 0:
                    for half in range(2):
                        start = half * first + m * run
                        e_refs[m][columns(place + half, run)] = v_refs[turn][start : start + run]
                    continue
                lines = [
                    v_refs[turn][columns(half, first)].astype(f32)[columns(m, run)]
                    for half in range(2)
                ]
                e_refs[m][place * run : (place + 2) * run] = jnp.concatenate(lines, 0).astype(bf16)

    shapes = [
        jax.ShapeDtypeStruct((2 * others * piece, width), bf16) for _ in range(HEAD_DIVISIONS)
    ]
    return call(body, shapes, [VMEM] * (1 + others + len(after)), "late_pieces")(
        key_chosen, *heads, *after
    )


def attend(facts_row, facts_of, weights, acc, heads, tails, live):
    rows = live.shape[0]
    block_len = rows // 2
    others = len(weights)
    slots = facts_of(None).slots

    def body(facts_ref, acc_ref, live_ref, *refs):
        w_refs, h_refs, t_refs = refs[:others], refs[others : 2 * others], refs[2 * others : 3 * others]
        out_ref, mark_ref, v_scr = refs[3 * others :]
        mark_ref[...] = jnp.zeros_like(mark_ref)
        for turn in range(others):
            first, rest = h_refs[turn].shape[0] // 2, t_refs[turn].shape[0] // 2
            for half in range(2):
                v_scr[turn, columns(half, block_len)] = jnp.concatenate(
                    [h_refs[turn][columns(half, first)], t_refs[turn][columns(half, rest)]], axis=0
                )
        facts = facts_of(facts_ref)
        slot = slot_and_head_group()[0]
        low, high = facts.halves(slot)
        low_rows, high_rows = rows_at(low, block_len), rows_at(high, block_len)
        for head in range(Q_DEV):
            key_head = columns(head * KV_DEV // Q_DEV)
            both = columns(head, 2 * HEAD_SIZE)
            low_sum, high_sum = acc_ref[low_rows, both], acc_ref[high_rows, both]
            for turn in range(1, slots):
                outer, *tiles = tiles_of(facts, slot, (slot - turn + slots) % slots)
                either, upper = [
                    dot(
                        w_refs[turn - 1][index, head],
                        beside_ones(v_scr[turn - 1, rows_at(other, block_len), key_head]),
                    )
                    for index, (_, other) in enumerate(tiles)
                ]
                low_sum = low_sum + jnp.where(outer, 0.0, either)
                high_sum = high_sum + upper + jnp.where(outer, either, 0.0)
            for part, total in ((low_rows, low_sum), (high_rows, high_sum)):
                scale = live_ref[part] / total[:, HEAD_SIZE:]
                out_ref[part, columns(head)] = (total[:, :HEAD_SIZE] * scale).astype(bf16)

    shape = [
        jax.ShapeDtypeStruct((rows, Q_DEV * HEAD_SIZE), bf16),
        jax.ShapeDtypeStruct((8, HEAD_SIZE), f32),
    ]
    specs = [SMEM] + [VMEM] * (2 + 3 * others)
    scratch = [pltpu.VMEM((others, rows, KV_WIDTH), bf16)]
    return call(body, shape, specs, "attend", scratch)(
        facts_row, acc, live, *weights, *heads, *tails
    )


def cache_part(early, late, kept, mark):
    cache_rows = kept.shape[0]
    piece = early[0].shape[0] // 2
    width = early[0].shape[1]

    def body(kept_ref, *refs):
        f_refs, s_refs, out_ref = refs[:4], refs[4:8], refs[9]
        head_group = slot_and_head_group()[1]
        later = cache_rows - piece
        for index, m in enumerate(HAND_ORDER):
            for kind in range(2):
                lines = jnp.concatenate(
                    [f_refs[index][columns(kind, piece)], s_refs[index][columns(kind, later)]], axis=0
                )
                column = ((head_group ^ m) + kind * HEAD_DIVISIONS) * width
                out_ref[:, pl.ds(pl.multiple_of(column, HEAD_SIZE), width)] = dot(
                    kept_ref[...], lines
                ).astype(bf16)

    shape = jax.ShapeDtypeStruct((cache_rows, 2 * HEAD_DIVISIONS * width), bf16)
    return call(body, shape, [VMEM] * 10, "cache_part")(kept, *early, *late, mark)


def on_device(queries, keys, values, block_map, lengths, group_of_prompt, decode_rank):
    block_len = queries.shape[2] // 2
    slots = block_map.shape[1]
    q, k, v = queries[0, 0], keys[0, 0], values[0, 0]
    tables = rotary_tables(block_len, 2 * slots)

    def to_slots(parts):
        return [shifted(parts[t - 1], "blk", HEAD_DIVISIONS * t) for t in range(1, slots)]

    def hand_on(pieces):
        return [pieces[0]] + [crossed(pieces[m], "blk", m) for m in HAND_ORDER[1:]]

    key_in = to_slots([k] * (slots - 1))
    facts_row, facts_of, block, operands, tables, (select, order), early, sent = prepare(
        q,
        k,
        v,
        block_map,
        decode_rank,
        group_of_prompt,
        tables,
        lengths,
        crossed(lengths, "req", 1),
    )
    heads = to_slots(sent[0::2])
    early = hand_on(early)
    span, groups = 2, lax.axis_size("req")
    while 2 * span < groups:
        other = crossed(block, "req", span)
        upper = (lax.axis_index("req") & span) > 0
        block = jnp.where(
            upper, jnp.concatenate([other, block]), jnp.concatenate([block, other])
        )
        span = 2 * span
    lens = (block, crossed(block, "req", span))
    query_rot, acc, kept, live, angles = own_part(facts_row, facts_of, operands, tables, lens)
    key_rot, chosen = receive_keys(key_in, select, order, angles)
    weights, tails = weigh(facts_row, facts_of, query_rot, key_rot, sent[1::2])
    tails = to_slots(tails)
    late = hand_on(late_pieces(heads, chosen, early[1:]))
    attended, mark = attend(facts_row, facts_of, weights, acc, heads, tails, live)
    cache = cache_part(early, late, kept, mark)
    return (attended[None, None], cache[None])


def solution(mesh):
    placed = (
        P("req", "blk", None, None),
        P("req", "blk", None, None),
        P("req", "blk", None, None),
        P("req", None, None),
        P("req"),
        P(),
        P("req", None),
    )
    return jax.shard_map(
        on_device,
        mesh=mesh,
        in_specs=placed,
        out_specs=(P("req", "blk", None, None), P("req", "blk", None)),
        check_vma=False,
    )
```

```python
import math

import jax
import jax.numpy as jnp
import numpy as np
from jax import lax
from jax.experimental import pallas as pl
from jax.experimental.pallas import tpu as pltpu
from jax.sharding import PartitionSpec as P

QUERY_HEADS = 16
KEY_VALUE_HEADS = 8
HEAD_SIZE = 128
HEAD_DIVISIONS = 4
Q_DEV = 4
KV_DEV = 2
KV_WIDTH = KV_DEV * HEAD_SIZE

cap_value = 50.0
query_scale = 1.0 / 12.0
HAND_ORDER = (0, 2, 3, 1)
rope_base = 10000.0
VMEM_BYTES = 48 * 1024 * 1024

f32 = jnp.float32
bf16 = jnp.bfloat16
SMEM = pl.BlockSpec(memory_space=pltpu.SMEM)
VMEM = pl.BlockSpec(memory_space=pltpu.VMEM)
HBM = pl.BlockSpec(memory_space=pltpu.HBM)


def shifted(shard, axis, by):
    peers = lax.axis_size(axis)
    return lax.ppermute(shard, axis, [(i, (i + by) % peers) for i in range(peers)])


def crossed(shard, axis, by):
    peers = lax.axis_size(axis)
    return lax.ppermute(shard, axis, [(i, i ^ by) for i in range(peers)])


def rotary_tables(block_len, block_count):
    half = HEAD_SIZE // 2
    frequency = np.exp(
        np.float32(-math.log(rope_base)) * (2.0 * np.arange(half, dtype=np.float32)) / HEAD_SIZE
    ).astype(np.float64)

    def table(positions):
        angles = positions.astype(np.float64)[:, None] * frequency[None, :]
        cosine, sine = np.cos(angles), np.sin(angles)
        return np.stack(
            [np.concatenate([cosine, cosine], 1), np.concatenate([-sine, sine], 1)]
        ).astype(np.float32)

    return table(np.arange(block_len)), table(np.arange(block_count) * block_len)


def block_angles(row_table, block_table, block):
    row_cos, row_sin = row_table[0], row_table[1]
    blk_cos, blk_sin = block_table[0, pl.ds(block, 1)], block_table[1, pl.ds(block, 1)]
    return row_cos * blk_cos - row_sin * blk_sin, row_sin * blk_cos + row_cos * blk_sin


def turned(head, angles):
    x = head.astype(f32)
    return x * angles[0] + pltpu.roll(x, HEAD_SIZE // 2, 1) * angles[1]


def order_matrix(rank_of, slot, head_group, out_rows, rows, residues):
    row_ids = lax.broadcasted_iota(jnp.int32, (1, rows), 1)
    residue = row_ids % residues
    rank = jnp.zeros_like(row_ids)
    for r in range(residues):
        rank = jnp.where(residue == r, rank_of(r), rank)
    ahead = (rank - HEAD_DIVISIONS * slot + residues) % residues
    ahead = jnp.where(ahead < HEAD_DIVISIONS, ahead ^ head_group, ahead)
    index = ahead * (rows // residues) + row_ids // residues
    out_ids = lax.broadcasted_iota(jnp.int32, (out_rows, rows), 0)
    return jnp.where(out_ids == index, 1.0, 0.0).astype(bf16)


def dot(a, b):
    return jnp.dot(a, b, preferred_element_type=f32)


def dot_t(a, b):
    return lax.dot_general(a, b, (((1,), (1,)), ((), ())), preferred_element_type=f32)


def expo_of(scores):
    return jnp.exp2(cap_value * math.log2(math.e) * jnp.tanh(scores * (1.0 / cap_value)))


def columns(index, width=HEAD_SIZE):
    return slice(index * width, (index + 1) * width)


def call(body, out_shape, in_specs, name, scratch=(), out_specs=None, cost=1000):
    return pl.pallas_call(
        body,
        out_shape=out_shape,
        in_specs=in_specs,
        out_specs=jax.tree.map(lambda _: VMEM, out_shape) if out_specs is None else out_specs,
        scratch_shapes=scratch,
        compiler_params=pltpu.CompilerParams(vmem_limit_bytes=VMEM_BYTES),
        cost_estimate=pl.CostEstimate(flops=cost, bytes_accessed=1000, transcendentals=0),
        name=name,
    )


def in_hbm(arrays):
    return [pltpu.with_memory_space_constraint(x, pltpu.HBM) for x in arrays]


def rows_at(index, size):
    return pl.ds(pl.multiple_of(index * size, size), size)


def beside_ones(values):
    return jnp.concatenate([values, jnp.ones(values.shape, bf16)], axis=1)


class Facts:
    def __init__(self, ref, slots, residues, groups):
        self.ref, self.slots, self.residues, self.groups = ref, slots, residues, groups
        self.size = 2 * slots + residues + groups

    def block(self, slot, half):
        return self.ref[0, 2 * slot + half]

    def rank(self, residue):
        return self.ref[0, 2 * self.slots + residue]

    def owner(self, prompt):
        return self.ref[0, 2 * self.slots + self.residues + prompt]

    def store(self, map_ref, rank_ref, owner_ref):
        for slot in range(self.slots):
            for half in range(2):
                self.ref[0, 2 * slot + half] = map_ref[0, slot, half]
        for residue in range(self.residues):
            self.ref[0, 2 * self.slots + residue] = rank_ref[0, residue]
        for prompt in range(self.groups):
            self.ref[0, 2 * self.slots + self.residues + prompt] = owner_ref[prompt]

    def halves(self, slot):
        high = jnp.where(self.block(slot, 1) > self.block(slot, 0), 1, 0)
        return 1 - high, high


def slot_and_head_group():
    member = lax.axis_index("blk")
    return member // HEAD_DIVISIONS, member % HEAD_DIVISIONS


def prepare(keys, values, table, decode_rank, owner, tables):
    rows, width = keys.shape
    block_len = rows // 2
    slots = table.shape[1]
    residues = decode_rank.shape[1]
    piece = rows // residues
    first = block_len // slots
    arrays = (keys, values, *tables, table, decode_rank, owner)
    count = len(arrays)
    facts_of = lambda ref: Facts(ref, slots, residues, owner.shape[0])

    def body(*refs):
        inputs, refs = refs[:count], refs[count:]
        facts_ref, kr_ref, v_ref, row_ref, blk_ref, select_ref, order_ref = refs[:7]
        e_refs, refs = refs[7:11], refs[11:]
        sent_refs, refs = refs[: 2 * slots - 2], refs[2 * slots - 2 :]
        k_ref, map_ref, rank_ref, owner_ref, sems = refs
        targets = (k_ref, v_ref, row_ref, blk_ref, map_ref, rank_ref, owner_ref)
        copies = []
        for index in range(count):
            copies.append(pltpu.make_async_copy(inputs[index], targets[index], sems.at[index]))
            copies[-1].start()
        slot, head_group = slot_and_head_group()
        for index in (0, 2, 3, 4, 5, 6):
            copies[index].wait()
        facts_of(facts_ref).store(map_ref, rank_ref, owner_ref)
        for half in range(2):
            part = columns(half, block_len)
            angles = block_angles(row_ref, blk_ref, map_ref[0, slot, half])
            for head in range(KV_DEV):
                kr_ref[part, columns(head)] = turned(k_ref[part, columns(head)], angles).astype(bf16)
        select = order_matrix(
            lambda r: rank_ref[0, r], slot, head_group, rows // slots, rows, residues
        )
        select_ref[...] = select
        copies[1].wait()
        for turn in range(1, slots):
            order = order_matrix(
                lambda r: rank_ref[0, r],
                (slot + turn) % slots,
                head_group,
                block_len,
                block_len,
                residues,
            )
            for half in range(2):
                moved = dot(order, v_ref[columns(half, block_len)]).astype(bf16)
                sent_refs[2 * turn - 2][columns(half, first)] = moved[:first]
                sent_refs[2 * turn - 1][columns(half, block_len - first)] = moved[first:]
        order_ref[...] = order_matrix(
            lambda r: rank_ref[0, r], slot, head_group, block_len, block_len, residues
        )
        for kind, source in enumerate((kr_ref, v_ref)):
            chosen = dot(select, source[...]).astype(bf16)
            for m in range(HEAD_DIVISIONS):
                e_refs[m][columns(kind, piece)] = chosen[columns(m, piece)]

    shapes = [
        jax.ShapeDtypeStruct((1, facts_of(None).size), jnp.int32),
        jax.ShapeDtypeStruct(keys.shape, bf16),
        jax.ShapeDtypeStruct(values.shape, bf16),
        jax.ShapeDtypeStruct(tables[0].shape, f32),
        jax.ShapeDtypeStruct(tables[1].shape, f32),
        jax.ShapeDtypeStruct((rows // slots, rows), bf16),
        jax.ShapeDtypeStruct((block_len, block_len), bf16),
    ]
    shapes += [jax.ShapeDtypeStruct((2 * piece, width), bf16) for _ in range(HEAD_DIVISIONS)]
    for _ in range(1, slots):
        shapes.append(jax.ShapeDtypeStruct((2 * first, width), bf16))
        shapes.append(jax.ShapeDtypeStruct((2 * (block_len - first), width), bf16))
    scratch = [pltpu.VMEM(keys.shape, keys.dtype)]
    scratch += [pltpu.SMEM(x.shape, x.dtype) for x in (table, decode_rank, owner)]
    scratch.append(pltpu.SemaphoreType.DMA((count,)))
    outs = call(
        body,
        shapes,
        [HBM] * count,
        "prepare",
        scratch,
        out_specs=[SMEM] + [VMEM] * (len(shapes) - 1),
    )(*in_hbm(arrays))
    return outs[0], facts_of, outs[1:3], outs[3:5], outs[5:7], outs[7:11], outs[11:]


def pair_up(own_length, near_length):
    def body(own_ref, near_ref, pair_ref):
        odd = lax.axis_index("req") % 2 == 1
        pair_ref[0] = jnp.where(odd, near_ref[0], own_ref[0])
        pair_ref[1] = jnp.where(odd, own_ref[0], near_ref[0])

    shape = jax.ShapeDtypeStruct((2,), jnp.int32)
    return call(body, shape, [SMEM] * 2, "pair_up", out_specs=SMEM)(own_length, near_length)


def own_part(facts_row, facts_of, queries, operands, tables, lens):
    rows = queries.shape[0]
    block_len = rows // 2
    sizes = facts_of(None)
    slots, residues, groups = sizes.slots, sizes.residues, sizes.groups
    run = block_len // residues
    cache_rows = 2 * slots * run

    def body(facts_ref, here_ref, there_ref, q_hbm, kr_ref, v_ref, row_ref, blk_ref, *refs):
        qr_ref, acc_ref, kept_ref, live_ref, angle_ref, q_ref, sem = refs
        copy = pltpu.make_async_copy(q_hbm, q_ref, sem.at[0])
        copy.start()
        facts = facts_of(facts_ref)
        slot = slot_and_head_group()[0]
        group = lax.axis_index("req")
        copy.wait()
        for half in range(2):
            part = columns(half, block_len)
            angles = block_angles(row_ref, blk_ref, facts.block(slot, half))
            for head in range(Q_DEV):
                qr_ref[part, columns(head)] = (
                    turned(q_ref[part, columns(head)], angles) * query_scale
                ).astype(bf16)
            for turn in range(1, slots):
                block = facts.block((slot - turn + slots) % slots, half)
                other = block_angles(row_ref, blk_ref, block)
                angle_ref[turn - 1, half, 0] = other[0]
                angle_ref[turn - 1, half, 1] = other[1]
        low, high = facts.halves(slot)
        low, high = rows_at(low, block_len), rows_at(high, block_len)
        row = lax.broadcasted_iota(jnp.int32, (block_len, block_len), 0)
        col = lax.broadcasted_iota(jnp.int32, (block_len, block_len), 1)
        for head in range(Q_DEV):
            key_head = columns(head * KV_DEV // Q_DEV)
            both = columns(head, 2 * HEAD_SIZE)

            def tile(q_part, k_part, diagonal):
                expo = expo_of(dot_t(qr_ref[q_part, columns(head)], kr_ref[k_part, key_head]))
                if diagonal:
                    expo = jnp.where(col <= row, expo, 0.0)
                return dot(expo.astype(bf16), beside_ones(v_ref[k_part, key_head]))

            acc_ref[low, both] = tile(low, low, True)
            acc_ref[high, both] = tile(high, high, True) + tile(high, low, False)

        col = lax.broadcasted_iota(jnp.int32, (1, cache_rows), 1)
        part, offset = col // run, col % run
        target = jnp.zeros_like(col)
        for turn in range(slots):
            for half in range(2):
                block = facts.block((slot - turn + slots) % slots, half)
                target = jnp.where(part == 2 * turn + half, block * run + offset, target)
        length = 0
        half_count = groups // 2
        for index in range(half_count):
            same = (group & half_count) | index
            length = length + jnp.where(facts.owner(same) == group, here_ref[index], 0)
            other = same ^ half_count
            length = length + jnp.where(facts.owner(other) == group, there_ref[index], 0)
        residue = 0
        for r in range(1, residues):
            residue = jnp.where(facts.rank(r) == lax.axis_index("blk"), r, residue)
        target = jnp.where(target * residues + residue < length, target, -1)
        row = lax.broadcasted_iota(jnp.int32, (cache_rows, cache_rows), 0)
        kept_ref[...] = jnp.where(row == target, 1.0, 0.0).astype(bf16)
        for half in range(2):
            offset = lax.broadcasted_iota(jnp.int32, (block_len, HEAD_SIZE), 0)
            at = facts.block(slot, half) * block_len + offset
            live_ref[columns(half, block_len)] = jnp.where(at < length, 1.0, 0.0)

    shapes = [
        jax.ShapeDtypeStruct(queries.shape, bf16),
        jax.ShapeDtypeStruct((rows, 2 * Q_DEV * HEAD_SIZE), f32),
        jax.ShapeDtypeStruct((cache_rows, cache_rows), bf16),
        jax.ShapeDtypeStruct((rows, HEAD_SIZE), f32),
        jax.ShapeDtypeStruct((slots - 1, 2, 2, block_len, HEAD_SIZE), f32),
    ]
    scratch = [pltpu.VMEM(queries.shape, bf16), pltpu.SemaphoreType.DMA((1,))]
    specs = [SMEM] * 3 + [HBM] + [VMEM] * 4
    return call(body, shapes, specs, "own_part", scratch)(
        facts_row, *lens, *in_hbm([queries]), *operands, *tables
    )


def tiles_of(facts, slot, source):
    low, high = facts.halves(slot)
    source_low, source_high = facts.halves(source)
    outer = facts.block(slot, low) < facts.block(source, source_low)
    first = (jnp.where(outer, high, low), source_low)
    second = (high, jnp.where(outer, source_high, source_low))
    return outer, first, second


def receive_keys(key_in, select, order, angles):
    others = len(key_in)
    rows, width = key_in[0].shape
    block_len = rows // 2

    def body(select_ref, order_ref, angle_ref, *refs):
        k_refs, refs = refs[:others], refs[others:]
        p_refs, chosen_ref, kr_ref = refs[:others], refs[others], refs[others + 1]
        for turn in range(others):
            for half in range(2):
                part = columns(half, block_len)
                there = angle_ref[turn, half, 0], angle_ref[turn, half, 1]
                for head in range(KV_DEV):
                    kr_ref[part, columns(head)] = turned(
                        k_refs[turn][part, columns(head)], there
                    ).astype(bf16)
                p_refs[turn][part] = dot(order_ref[...], kr_ref[part]).astype(bf16)
            chosen_ref[turn] = dot(select_ref[...], kr_ref[...]).astype(bf16)

    shapes = [jax.ShapeDtypeStruct((rows, width), bf16) for _ in range(others)]
    shapes.append(jax.ShapeDtypeStruct((others, select.shape[0], width), bf16))
    scratch = [pltpu.VMEM((rows, width), bf16)]
    outs = call(body, shapes, [VMEM] * (3 + others), "receive_keys", scratch, cost=10**10)(
        select, order, angles, *key_in
    )
    return outs[:others], outs[others]


def weigh(facts_row, facts_of, query_rot, key_rot, payload):
    others = len(key_rot)
    rows = query_rot.shape[0]
    block_len = rows // 2
    slots = facts_of(None).slots

    def body(facts_ref, q_ref, *refs):
        k_refs, pay_refs, refs = refs[:others], refs[others : 2 * others], refs[2 * others :]
        w_refs, out_refs = refs[:others], refs[others:]
        for pay_ref, out_ref in zip(pay_refs, out_refs):
            out_ref[...] = pay_ref[...]
        facts = facts_of(facts_ref)
        slot = slot_and_head_group()[0]
        for turn in range(1, slots):
            _, *tiles = tiles_of(facts, slot, (slot - turn + slots) % slots)
            for index, (half, other) in enumerate(tiles):
                for head in range(Q_DEV):
                    key_head = columns(head * KV_DEV // Q_DEV)
                    queries = q_ref[rows_at(half, block_len), columns(head)]
                    keys = k_refs[turn - 1][rows_at(other, block_len), key_head]
                    w_refs[turn - 1][index, head] = expo_of(dot_t(queries, keys)).astype(bf16)

    shapes = [
        jax.ShapeDtypeStruct((2, Q_DEV, block_len, block_len), bf16) for _ in range(others)
    ]
    shapes += [jax.ShapeDtypeStruct(x.shape, bf16) for x in payload]
    outs = call(body, shapes, [SMEM] + [VMEM] * (1 + 2 * others), "weigh")(
        facts_row, query_rot, *key_rot, *payload
    )
    return outs[:others], outs[others:]


def late_pieces(heads, key_chosen, after):
    others, rows, width = key_chosen.shape
    piece = rows // HEAD_DIVISIONS
    run = piece // 2
    first = heads[0].shape[0] // 2

    def body(key_ref, *refs):
        v_refs, e_refs = refs[:others], refs[others + len(after) :]
        for m in range(HEAD_DIVISIONS):
            for turn in range(others):
                e_refs[m][columns(turn, piece)] = key_ref[turn, columns(m, piece)]
                place = 2 * (others + turn)
                if run % 16 == 0:
                    for half in range(2):
                        start = half * first + m * run
                        e_refs[m][columns(place + half, run)] = v_refs[turn][start : start + run]
                    continue
                lines = [
                    v_refs[turn][columns(half, first)].astype(f32)[columns(m, run)]
                    for half in range(2)
                ]
                e_refs[m][place * run : (place + 2) * run] = jnp.concatenate(lines, 0).astype(bf16)

    shapes = [
        jax.ShapeDtypeStruct((2 * others * piece, width), bf16) for _ in range(HEAD_DIVISIONS)
    ]
    return call(body, shapes, [VMEM] * (1 + others + len(after)), "late_pieces")(
        key_chosen, *heads, *after
    )


def attend(facts_row, facts_of, weights, acc, heads, tails, live):
    rows = live.shape[0]
    block_len = rows // 2
    others = len(weights)
    slots = facts_of(None).slots

    def body(facts_ref, acc_ref, live_ref, *refs):
        w_refs, h_refs, t_refs = refs[:others], refs[others : 2 * others], refs[2 * others : 3 * others]
        out_ref, mark_ref, v_scr = refs[3 * others :]
        mark_ref[...] = jnp.zeros_like(mark_ref)
        for turn in range(others):
            first, rest = h_refs[turn].shape[0] // 2, t_refs[turn].shape[0] // 2
            for half in range(2):
                v_scr[turn, columns(half, block_len)] = jnp.concatenate(
                    [h_refs[turn][columns(half, first)], t_refs[turn][columns(half, rest)]], axis=0
                )
        facts = facts_of(facts_ref)
        slot = slot_and_head_group()[0]
        low, high = facts.halves(slot)
        low_rows, high_rows = rows_at(low, block_len), rows_at(high, block_len)
        for head in range(Q_DEV):
            key_head = columns(head * KV_DEV // Q_DEV)
            both = columns(head, 2 * HEAD_SIZE)
            low_sum, high_sum = acc_ref[low_rows, both], acc_ref[high_rows, both]
            for turn in range(1, slots):
                outer, *tiles = tiles_of(facts, slot, (slot - turn + slots) % slots)
                either, upper = [
                    dot(
                        w_refs[turn - 1][index, head],
                        beside_ones(v_scr[turn - 1, rows_at(other, block_len), key_head]),
                    )
                    for index, (_, other) in enumerate(tiles)
                ]
                low_sum = low_sum + jnp.where(outer, 0.0, either)
                high_sum = high_sum + upper + jnp.where(outer, either, 0.0)
            for part, total in ((low_rows, low_sum), (high_rows, high_sum)):
                scale = live_ref[part] / total[:, HEAD_SIZE:]
                out_ref[part, columns(head)] = (total[:, :HEAD_SIZE] * scale).astype(bf16)

    shape = [
        jax.ShapeDtypeStruct((rows, Q_DEV * HEAD_SIZE), bf16),
        jax.ShapeDtypeStruct((8, HEAD_SIZE), f32),
    ]
    specs = [SMEM] + [VMEM] * (2 + 3 * others)
    scratch = [pltpu.VMEM((others, rows, KV_WIDTH), bf16)]
    return call(body, shape, specs, "attend", scratch)(
        facts_row, acc, live, *weights, *heads, *tails
    )


def cache_part(early, late, kept, mark):
    cache_rows = kept.shape[0]
    piece = early[0].shape[0] // 2
    width = early[0].shape[1]

    def body(kept_ref, *refs):
        f_refs, s_refs, out_ref = refs[:4], refs[4:8], refs[9]
        head_group = slot_and_head_group()[1]
        later = cache_rows - piece
        for index, m in enumerate(HAND_ORDER):
            for kind in range(2):
                lines = jnp.concatenate(
                    [f_refs[index][columns(kind, piece)], s_refs[index][columns(kind, later)]], axis=0
                )
                column = ((head_group ^ m) + kind * HEAD_DIVISIONS) * width
                out_ref[:, pl.ds(pl.multiple_of(column, HEAD_SIZE), width)] = dot(
                    kept_ref[...], lines
                ).astype(bf16)

    shape = jax.ShapeDtypeStruct((cache_rows, 2 * HEAD_DIVISIONS * width), bf16)
    return call(body, shape, [VMEM] * 10, "cache_part")(kept, *early, *late, mark)


def on_device(queries, keys, values, block_map, lengths, group_of_prompt, decode_rank):
    block_len = queries.shape[2] // 2
    slots = block_map.shape[1]
    q, k, v = queries[0, 0], keys[0, 0], values[0, 0]
    tables = rotary_tables(block_len, 2 * slots)

    def to_slots(parts):
        return [shifted(parts[t - 1], "blk", HEAD_DIVISIONS * t) for t in range(1, slots)]

    def hand_on(pieces):
        return [pieces[0]] + [crossed(pieces[m], "blk", m) for m in HAND_ORDER[1:]]

    key_in = to_slots([k] * (slots - 1))
    facts_row, facts_of, operands, tables, (select, order), early, sent = prepare(
        k, v, block_map, decode_rank, group_of_prompt, tables
    )
    heads = to_slots(sent[0::2])
    early = hand_on(early)
    block = pair_up(lengths, crossed(lengths, "req", 1))
    span, groups = 2, lax.axis_size("req")
    while 2 * span < groups:
        other = crossed(block, "req", span)
        upper = (lax.axis_index("req") & span) > 0
        block = jnp.where(
            upper, jnp.concatenate([other, block]), jnp.concatenate([block, other])
        )
        span = 2 * span
    lens = (block, crossed(block, "req", span))
    query_rot, acc, kept, live, angles = own_part(facts_row, facts_of, q, operands, tables, lens)
    key_rot, chosen = receive_keys(key_in, select, order, angles)
    weights, tails = weigh(facts_row, facts_of, query_rot, key_rot, sent[1::2])
    tails = to_slots(tails)
    late = hand_on(late_pieces(heads, chosen, early[1:]))
    attended, mark = attend(facts_row, facts_of, weights, acc, heads, tails, live)
    cache = cache_part(early, late, kept, mark)
    return (attended[None, None], cache[None])


def solution(mesh):
    placed = (
        P("req", "blk", None, None),
        P("req", "blk", None, None),
        P("req", "blk", None, None),
        P("req", None, None),
        P("req"),
        P(),
        P("req", None),
    )
    return jax.shard_map(
        on_device,
        mesh=mesh,
        in_specs=placed,
        out_specs=(P("req", "blk", None, None), P("req", "blk", None)),
        check_vma=False,
    )
```

```python
import math

import jax
import jax.numpy as jnp
import numpy as np
from jax import lax
from jax.experimental import pallas as pl
from jax.experimental.pallas import tpu as pltpu
from jax.sharding import PartitionSpec as P

QUERY_HEADS = 16
KEY_VALUE_HEADS = 8
HEAD_SIZE = 128
HEAD_DIVISIONS = 4
Q_DEV = 4
KV_DEV = 2
KV_WIDTH = KV_DEV * HEAD_SIZE

cap_value = 50.0
query_scale = 1.0 / 12.0
HAND_ORDER = (0, 2, 3, 1)
rope_base = 10000.0
VMEM_BYTES = 48 * 1024 * 1024

f32 = jnp.float32
bf16 = jnp.bfloat16
SMEM = pl.BlockSpec(memory_space=pltpu.SMEM)
VMEM = pl.BlockSpec(memory_space=pltpu.VMEM)
HBM = pl.BlockSpec(memory_space=pltpu.HBM)


def shifted(shard, axis, by):
    peers = lax.axis_size(axis)
    return lax.ppermute(shard, axis, [(i, (i + by) % peers) for i in range(peers)])


def crossed(shard, axis, by):
    peers = lax.axis_size(axis)
    return lax.ppermute(shard, axis, [(i, i ^ by) for i in range(peers)])


def rotary_tables(block_len, block_count):
    half = HEAD_SIZE // 2
    frequency = np.exp(
        np.float32(-math.log(rope_base)) * (2.0 * np.arange(half, dtype=np.float32)) / HEAD_SIZE
    ).astype(np.float64)

    def table(positions):
        angles = positions.astype(np.float64)[:, None] * frequency[None, :]
        cosine, sine = np.cos(angles), np.sin(angles)
        return np.stack(
            [np.concatenate([cosine, cosine], 1), np.concatenate([-sine, sine], 1)]
        ).astype(np.float32)

    return table(np.arange(block_len)), table(np.arange(block_count) * block_len)


def block_angles(row_table, block_table, block):
    row_cos, row_sin = row_table[0], row_table[1]
    blk_cos, blk_sin = block_table[0, pl.ds(block, 1)], block_table[1, pl.ds(block, 1)]
    return row_cos * blk_cos - row_sin * blk_sin, row_sin * blk_cos + row_cos * blk_sin


def turned(head, angles):
    x = head.astype(f32)
    return x * angles[0] + pltpu.roll(x, HEAD_SIZE // 2, 1) * angles[1]


def order_matrix(rank_of, slot, head_group, out_rows, rows, residues):
    row_ids = lax.broadcasted_iota(jnp.int32, (1, rows), 1)
    residue = row_ids % residues
    rank = jnp.zeros_like(row_ids)
    for r in range(residues):
        rank = jnp.where(residue == r, rank_of(r), rank)
    ahead = (rank - HEAD_DIVISIONS * slot + residues) % residues
    ahead = jnp.where(ahead < HEAD_DIVISIONS, ahead ^ head_group, ahead)
    index = ahead * (rows // residues) + row_ids // residues
    out_ids = lax.broadcasted_iota(jnp.int32, (out_rows, rows), 0)
    return jnp.where(out_ids == index, 1.0, 0.0).astype(bf16)


def dot(a, b):
    return jnp.dot(a, b, preferred_element_type=f32)


def dot_t(a, b):
    return lax.dot_general(a, b, (((1,), (1,)), ((), ())), preferred_element_type=f32)


def expo_of(scores):
    return jnp.exp2(cap_value * math.log2(math.e) * jnp.tanh(scores * (1.0 / cap_value)))


def columns(index, width=HEAD_SIZE):
    return slice(index * width, (index + 1) * width)


def call(body, out_shape, in_specs, name, scratch=(), out_specs=None, cost=1000):
    return pl.pallas_call(
        body,
        out_shape=out_shape,
        in_specs=in_specs,
        out_specs=jax.tree.map(lambda _: VMEM, out_shape) if out_specs is None else out_specs,
        scratch_shapes=scratch,
        compiler_params=pltpu.CompilerParams(vmem_limit_bytes=VMEM_BYTES),
        cost_estimate=pl.CostEstimate(flops=cost, bytes_accessed=1000, transcendentals=0),
        name=name,
    )


def in_hbm(arrays):
    return [pltpu.with_memory_space_constraint(x, pltpu.HBM) for x in arrays]


def rows_at(index, size):
    return pl.ds(pl.multiple_of(index * size, size), size)


def beside_ones(values):
    return jnp.concatenate([values, jnp.ones(values.shape, bf16)], axis=1)


class Facts:
    def __init__(self, ref, slots, residues, groups):
        self.ref, self.slots, self.residues, self.groups = ref, slots, residues, groups
        self.size = 2 * slots + residues + groups

    def block(self, slot, half):
        return self.ref[0, 2 * slot + half]

    def rank(self, residue):
        return self.ref[0, 2 * self.slots + residue]

    def owner(self, prompt):
        return self.ref[0, 2 * self.slots + self.residues + prompt]

    def store(self, map_ref, rank_ref, owner_ref):
        for slot in range(self.slots):
            for half in range(2):
                self.ref[0, 2 * slot + half] = map_ref[0, slot, half]
        for residue in range(self.residues):
            self.ref[0, 2 * self.slots + residue] = rank_ref[0, residue]
        for prompt in range(self.groups):
            self.ref[0, 2 * self.slots + self.residues + prompt] = owner_ref[prompt]

    def halves(self, slot):
        high = jnp.where(self.block(slot, 1) > self.block(slot, 0), 1, 0)
        return 1 - high, high


def slot_and_head_group():
    member = lax.axis_index("blk")
    return member // HEAD_DIVISIONS, member % HEAD_DIVISIONS


def prepare(keys, values, table, decode_rank, owner, tables):
    rows, width = keys.shape
    block_len = rows // 2
    slots = table.shape[1]
    residues = decode_rank.shape[1]
    piece = rows // residues
    first = block_len // slots
    arrays = (keys, values, *tables, table, decode_rank, owner)
    count = len(arrays)
    facts_of = lambda ref: Facts(ref, slots, residues, owner.shape[0])

    def body(*refs):
        inputs, refs = refs[:count], refs[count:]
        facts_ref, kr_ref, v_ref, row_ref, blk_ref, select_ref, order_ref = refs[:7]
        e_refs, refs = refs[7:11], refs[11:]
        sent_refs, refs = refs[: 2 * slots - 2], refs[2 * slots - 2 :]
        k_ref, map_ref, rank_ref, owner_ref, sems = refs
        targets = (k_ref, v_ref, row_ref, blk_ref, map_ref, rank_ref, owner_ref)
        copies = []
        for index in range(count):
            copies.append(pltpu.make_async_copy(inputs[index], targets[index], sems.at[index]))
            copies[-1].start()
        slot, head_group = slot_and_head_group()
        for index in (0, 2, 3, 4, 5, 6):
            copies[index].wait()
        facts_of(facts_ref).store(map_ref, rank_ref, owner_ref)
        for half in range(2):
            part = columns(half, block_len)
            angles = block_angles(row_ref, blk_ref, map_ref[0, slot, half])
            for head in range(KV_DEV):
                kr_ref[part, columns(head)] = turned(k_ref[part, columns(head)], angles).astype(bf16)
        select = order_matrix(
            lambda r: rank_ref[0, r], slot, head_group, rows // slots, rows, residues
        )
        select_ref[...] = select
        copies[1].wait()
        for turn in range(1, slots):
            order = order_matrix(
                lambda r: rank_ref[0, r],
                (slot + turn) % slots,
                head_group,
                block_len,
                block_len,
                residues,
            )
            for half in range(2):
                moved = dot(order, v_ref[columns(half, block_len)]).astype(bf16)
                sent_refs[2 * turn - 2][columns(half, first)] = moved[:first]
                sent_refs[2 * turn - 1][columns(half, block_len - first)] = moved[first:]
        order_ref[...] = order_matrix(
            lambda r: rank_ref[0, r], slot, head_group, block_len, block_len, residues
        )
        for kind, source in enumerate((kr_ref, v_ref)):
            chosen = dot(select, source[...]).astype(bf16)
            for m in range(HEAD_DIVISIONS):
                e_refs[m][columns(kind, piece)] = chosen[columns(m, piece)]

    shapes = [
        jax.ShapeDtypeStruct((1, facts_of(None).size), jnp.int32),
        jax.ShapeDtypeStruct(keys.shape, bf16),
        jax.ShapeDtypeStruct(values.shape, bf16),
        jax.ShapeDtypeStruct(tables[0].shape, f32),
        jax.ShapeDtypeStruct(tables[1].shape, f32),
        jax.ShapeDtypeStruct((rows // slots, rows), bf16),
        jax.ShapeDtypeStruct((block_len, block_len), bf16),
    ]
    shapes += [jax.ShapeDtypeStruct((2 * piece, width), bf16) for _ in range(HEAD_DIVISIONS)]
    for _ in range(1, slots):
        shapes.append(jax.ShapeDtypeStruct((2 * first, width), bf16))
        shapes.append(jax.ShapeDtypeStruct((2 * (block_len - first), width), bf16))
    scratch = [pltpu.VMEM(keys.shape, keys.dtype)]
    scratch += [pltpu.SMEM(x.shape, x.dtype) for x in (table, decode_rank, owner)]
    scratch.append(pltpu.SemaphoreType.DMA((count,)))
    outs = call(
        body,
        shapes,
        [HBM] * count,
        "prepare",
        scratch,
        out_specs=[SMEM] + [VMEM] * (len(shapes) - 1),
    )(*in_hbm(arrays))
    return outs[0], facts_of, outs[1:3], outs[3:5], outs[5:7], outs[7:11], outs[11:]


def pair_up(own_length, near_length):
    def body(own_ref, near_ref, pair_ref):
        odd = lax.axis_index("req") % 2 == 1
        pair_ref[0] = jnp.where(odd, near_ref[0], own_ref[0])
        pair_ref[1] = jnp.where(odd, own_ref[0], near_ref[0])

    shape = jax.ShapeDtypeStruct((2,), jnp.int32)
    return call(body, shape, [SMEM] * 2, "pair_up", out_specs=SMEM)(own_length, near_length)


def own_part(facts_row, facts_of, queries, operands, tables):
    rows = queries.shape[0]
    block_len = rows // 2
    slots = facts_of(None).slots

    def body(facts_ref, q_hbm, kr_ref, v_ref, row_ref, blk_ref, *refs):
        qr_ref, acc_ref, angle_ref, q_ref, sem = refs
        copy = pltpu.make_async_copy(q_hbm, q_ref, sem.at[0])
        copy.start()
        facts = facts_of(facts_ref)
        slot = slot_and_head_group()[0]
        copy.wait()
        for half in range(2):
            part = columns(half, block_len)
            angles = block_angles(row_ref, blk_ref, facts.block(slot, half))
            for head in range(Q_DEV):
                qr_ref[part, columns(head)] = (
                    turned(q_ref[part, columns(head)], angles) * query_scale
                ).astype(bf16)
            for turn in range(1, slots):
                block = facts.block((slot - turn + slots) % slots, half)
                other = block_angles(row_ref, blk_ref, block)
                angle_ref[turn - 1, half, 0] = other[0]
                angle_ref[turn - 1, half, 1] = other[1]
        low, high = facts.halves(slot)
        low, high = rows_at(low, block_len), rows_at(high, block_len)
        row = lax.broadcasted_iota(jnp.int32, (block_len, block_len), 0)
        col = lax.broadcasted_iota(jnp.int32, (block_len, block_len), 1)
        for head in range(Q_DEV):
            key_head = columns(head * KV_DEV // Q_DEV)
            both = columns(head, 2 * HEAD_SIZE)

            def tile(q_part, k_part, diagonal):
                expo = expo_of(dot_t(qr_ref[q_part, columns(head)], kr_ref[k_part, key_head]))
                if diagonal:
                    expo = jnp.where(col <= row, expo, 0.0)
                return dot(expo.astype(bf16), beside_ones(v_ref[k_part, key_head]))

            acc_ref[low, both] = tile(low, low, True)
            acc_ref[high, both] = tile(high, high, True) + tile(high, low, False)

    shapes = [
        jax.ShapeDtypeStruct(queries.shape, bf16),
        jax.ShapeDtypeStruct((rows, 2 * Q_DEV * HEAD_SIZE), f32),
        jax.ShapeDtypeStruct((slots - 1, 2, 2, block_len, HEAD_SIZE), f32),
    ]
    scratch = [pltpu.VMEM(queries.shape, bf16), pltpu.SemaphoreType.DMA((1,))]
    specs = [SMEM] + [HBM] + [VMEM] * 4
    return call(body, shapes, specs, "own_part", scratch)(
        facts_row, *in_hbm([queries]), *operands, *tables
    )


def masks_of(facts_row, facts_of, rows, lens):
    block_len = rows // 2
    sizes = facts_of(None)
    slots, residues, groups = sizes.slots, sizes.residues, sizes.groups
    run = block_len // residues
    cache_rows = 2 * slots * run

    def body(facts_ref, here_ref, there_ref, kept_ref, live_ref):
        facts = facts_of(facts_ref)
        slot = slot_and_head_group()[0]
        group = lax.axis_index("req")
        col = lax.broadcasted_iota(jnp.int32, (1, cache_rows), 1)
        part, offset = col // run, col % run
        target = jnp.zeros_like(col)
        for turn in range(slots):
            for half in range(2):
                block = facts.block((slot - turn + slots) % slots, half)
                target = jnp.where(part == 2 * turn + half, block * run + offset, target)
        length = 0
        half_count = groups // 2
        for index in range(half_count):
            same = (group & half_count) | index
            length = length + jnp.where(facts.owner(same) == group, here_ref[index], 0)
            other = same ^ half_count
            length = length + jnp.where(facts.owner(other) == group, there_ref[index], 0)
        residue = 0
        for r in range(1, residues):
            residue = jnp.where(facts.rank(r) == lax.axis_index("blk"), r, residue)
        target = jnp.where(target * residues + residue < length, target, -1)
        row = lax.broadcasted_iota(jnp.int32, (cache_rows, cache_rows), 0)
        kept_ref[...] = jnp.where(row == target, 1.0, 0.0).astype(bf16)
        for half in range(2):
            offset = lax.broadcasted_iota(jnp.int32, (block_len, HEAD_SIZE), 0)
            at = facts.block(slot, half) * block_len + offset
            live_ref[columns(half, block_len)] = jnp.where(at < length, 1.0, 0.0)

    shapes = [
        jax.ShapeDtypeStruct((cache_rows, cache_rows), bf16),
        jax.ShapeDtypeStruct((rows, HEAD_SIZE), f32),
    ]
    return call(body, shapes, [SMEM] * 3, "masks")(facts_row, *lens)


def tiles_of(facts, slot, source):
    low, high = facts.halves(slot)
    source_low, source_high = facts.halves(source)
    outer = facts.block(slot, low) < facts.block(source, source_low)
    first = (jnp.where(outer, high, low), source_low)
    second = (high, jnp.where(outer, source_high, source_low))
    return outer, first, second


def receive_keys(key_in, select, order, angles):
    others = len(key_in)
    rows, width = key_in[0].shape
    block_len = rows // 2

    def body(select_ref, order_ref, angle_ref, *refs):
        k_refs, refs = refs[:others], refs[others:]
        p_refs, chosen_ref, kr_ref = refs[:others], refs[others], refs[others + 1]
        for turn in range(others):
            for half in range(2):
                part = columns(half, block_len)
                there = angle_ref[turn, half, 0], angle_ref[turn, half, 1]
                for head in range(KV_DEV):
                    kr_ref[part, columns(head)] = turned(
                        k_refs[turn][part, columns(head)], there
                    ).astype(bf16)
                p_refs[turn][part] = dot(order_ref[...], kr_ref[part]).astype(bf16)
            chosen_ref[turn] = dot(select_ref[...], kr_ref[...]).astype(bf16)

    shapes = [jax.ShapeDtypeStruct((rows, width), bf16) for _ in range(others)]
    shapes.append(jax.ShapeDtypeStruct((others, select.shape[0], width), bf16))
    scratch = [pltpu.VMEM((rows, width), bf16)]
    outs = call(body, shapes, [VMEM] * (3 + others), "receive_keys", scratch, cost=10**10)(
        select, order, angles, *key_in
    )
    return outs[:others], outs[others]


def weigh(facts_row, facts_of, query_rot, key_rot, payload):
    others = len(key_rot)
    rows = query_rot.shape[0]
    block_len = rows // 2
    slots = facts_of(None).slots

    def body(facts_ref, q_ref, *refs):
        k_refs, pay_refs, refs = refs[:others], refs[others : 2 * others], refs[2 * others :]
        w_refs, out_refs = refs[:others], refs[others:]
        for pay_ref, out_ref in zip(pay_refs, out_refs):
            out_ref[...] = pay_ref[...]
        facts = facts_of(facts_ref)
        slot = slot_and_head_group()[0]
        for turn in range(1, slots):
            _, *tiles = tiles_of(facts, slot, (slot - turn + slots) % slots)
            for index, (half, other) in enumerate(tiles):
                for head in range(Q_DEV):
                    key_head = columns(head * KV_DEV // Q_DEV)
                    queries = q_ref[rows_at(half, block_len), columns(head)]
                    keys = k_refs[turn - 1][rows_at(other, block_len), key_head]
                    w_refs[turn - 1][index, head] = expo_of(dot_t(queries, keys)).astype(bf16)

    shapes = [
        jax.ShapeDtypeStruct((2, Q_DEV, block_len, block_len), bf16) for _ in range(others)
    ]
    shapes += [jax.ShapeDtypeStruct(x.shape, bf16) for x in payload]
    outs = call(body, shapes, [SMEM] + [VMEM] * (1 + 2 * others), "weigh")(
        facts_row, query_rot, *key_rot, *payload
    )
    return outs[:others], outs[others:]


def late_pieces(heads, key_chosen, after):
    others, rows, width = key_chosen.shape
    piece = rows // HEAD_DIVISIONS
    run = piece // 2
    first = heads[0].shape[0] // 2

    def body(key_ref, *refs):
        v_refs, e_refs = refs[:others], refs[others + len(after) :]
        for m in range(HEAD_DIVISIONS):
            for turn in range(others):
                e_refs[m][columns(turn, piece)] = key_ref[turn, columns(m, piece)]
                place = 2 * (others + turn)
                if run % 16 == 0:
                    for half in range(2):
                        start = half * first + m * run
                        e_refs[m][columns(place + half, run)] = v_refs[turn][start : start + run]
                    continue
                lines = [
                    v_refs[turn][columns(half, first)].astype(f32)[columns(m, run)]
                    for half in range(2)
                ]
                e_refs[m][place * run : (place + 2) * run] = jnp.concatenate(lines, 0).astype(bf16)

    shapes = [
        jax.ShapeDtypeStruct((2 * others * piece, width), bf16) for _ in range(HEAD_DIVISIONS)
    ]
    return call(body, shapes, [VMEM] * (1 + others + len(after)), "late_pieces")(
        key_chosen, *heads, *after
    )


def attend(facts_row, facts_of, weights, acc, heads, tails, live):
    rows = live.shape[0]
    block_len = rows // 2
    others = len(weights)
    slots = facts_of(None).slots

    def body(facts_ref, acc_ref, live_ref, *refs):
        w_refs, h_refs, t_refs = refs[:others], refs[others : 2 * others], refs[2 * others : 3 * others]
        out_ref, mark_ref, v_scr = refs[3 * others :]
        mark_ref[...] = jnp.zeros_like(mark_ref)
        for turn in range(others):
            first, rest = h_refs[turn].shape[0] // 2, t_refs[turn].shape[0] // 2
            for half in range(2):
                v_scr[turn, columns(half, block_len)] = jnp.concatenate(
                    [h_refs[turn][columns(half, first)], t_refs[turn][columns(half, rest)]], axis=0
                )
        facts = facts_of(facts_ref)
        slot = slot_and_head_group()[0]
        low, high = facts.halves(slot)
        low_rows, high_rows = rows_at(low, block_len), rows_at(high, block_len)
        for head in range(Q_DEV):
            key_head = columns(head * KV_DEV // Q_DEV)
            both = columns(head, 2 * HEAD_SIZE)
            low_sum, high_sum = acc_ref[low_rows, both], acc_ref[high_rows, both]
            for turn in range(1, slots):
                outer, *tiles = tiles_of(facts, slot, (slot - turn + slots) % slots)
                either, upper = [
                    dot(
                        w_refs[turn - 1][index, head],
                        beside_ones(v_scr[turn - 1, rows_at(other, block_len), key_head]),
                    )
                    for index, (_, other) in enumerate(tiles)
                ]
                low_sum = low_sum + jnp.where(outer, 0.0, either)
                high_sum = high_sum + upper + jnp.where(outer, either, 0.0)
            for part, total in ((low_rows, low_sum), (high_rows, high_sum)):
                scale = live_ref[part] / total[:, HEAD_SIZE:]
                out_ref[part, columns(head)] = (total[:, :HEAD_SIZE] * scale).astype(bf16)

    shape = [
        jax.ShapeDtypeStruct((rows, Q_DEV * HEAD_SIZE), bf16),
        jax.ShapeDtypeStruct((8, HEAD_SIZE), f32),
    ]
    specs = [SMEM] + [VMEM] * (2 + 3 * others)
    scratch = [pltpu.VMEM((others, rows, KV_WIDTH), bf16)]
    return call(body, shape, specs, "attend", scratch)(
        facts_row, acc, live, *weights, *heads, *tails
    )


def cache_part(early, late, kept, mark):
    cache_rows = kept.shape[0]
    piece = early[0].shape[0] // 2
    width = early[0].shape[1]

    def body(kept_ref, *refs):
        f_refs, s_refs, out_ref = refs[:4], refs[4:8], refs[9]
        head_group = slot_and_head_group()[1]
        later = cache_rows - piece
        for index, m in enumerate(HAND_ORDER):
            for kind in range(2):
                lines = jnp.concatenate(
                    [f_refs[index][columns(kind, piece)], s_refs[index][columns(kind, later)]], axis=0
                )
                column = ((head_group ^ m) + kind * HEAD_DIVISIONS) * width
                out_ref[:, pl.ds(pl.multiple_of(column, HEAD_SIZE), width)] = dot(
                    kept_ref[...], lines
                ).astype(bf16)

    shape = jax.ShapeDtypeStruct((cache_rows, 2 * HEAD_DIVISIONS * width), bf16)
    return call(body, shape, [VMEM] * 10, "cache_part")(kept, *early, *late, mark)


def on_device(queries, keys, values, block_map, lengths, group_of_prompt, decode_rank):
    block_len = queries.shape[2] // 2
    slots = block_map.shape[1]
    q, k, v = queries[0, 0], keys[0, 0], values[0, 0]
    tables = rotary_tables(block_len, 2 * slots)

    def to_slots(parts):
        return [shifted(parts[t - 1], "blk", HEAD_DIVISIONS * t) for t in range(1, slots)]

    def hand_on(pieces):
        return [pieces[0]] + [crossed(pieces[m], "blk", m) for m in HAND_ORDER[1:]]

    key_in = to_slots([k] * (slots - 1))
    facts_row, facts_of, operands, tables, (select, order), early, sent = prepare(
        k, v, block_map, decode_rank, group_of_prompt, tables
    )
    heads = to_slots(sent[0::2])
    early = hand_on(early)
    block = pair_up(lengths, crossed(lengths, "req", 1))
    span, groups = 2, lax.axis_size("req")
    while 2 * span < groups:
        other = crossed(block, "req", span)
        upper = (lax.axis_index("req") & span) > 0
        block = jnp.where(
            upper, jnp.concatenate([other, block]), jnp.concatenate([block, other])
        )
        span = 2 * span
    lens = (block, crossed(block, "req", span))
    query_rot, acc, angles = own_part(facts_row, facts_of, q, operands, tables)
    kept, live = masks_of(facts_row, facts_of, q.shape[0], lens)
    key_rot, chosen = receive_keys(key_in, select, order, angles)
    weights, tails = weigh(facts_row, facts_of, query_rot, key_rot, sent[1::2])
    tails = to_slots(tails)
    late = hand_on(late_pieces(heads, chosen, early[1:] + [live]))
    attended, mark = attend(facts_row, facts_of, weights, acc, heads, tails, live)
    cache = cache_part(early, late, kept, mark)
    return (attended[None, None], cache[None])


def solution(mesh):
    placed = (
        P("req", "blk", None, None),
        P("req", "blk", None, None),
        P("req", "blk", None, None),
        P("req", None, None),
        P("req"),
        P(),
        P("req", None),
    )
    return jax.shard_map(
        on_device,
        mesh=mesh,
        in_specs=placed,
        out_specs=(P("req", "blk", None, None), P("req", "blk", None)),
        check_vma=False,
    )
```

```python
import math

import jax
import jax.numpy as jnp
import numpy as np
from jax import lax
from jax.experimental import pallas as pl
from jax.experimental.pallas import tpu as pltpu
from jax.sharding import PartitionSpec as P

QUERY_HEADS = 16
KEY_VALUE_HEADS = 8
HEAD_SIZE = 128
HEAD_DIVISIONS = 4
Q_DEV = 4
KV_DEV = 2
KV_WIDTH = KV_DEV * HEAD_SIZE

cap_value = 50.0
query_scale = 1.0 / 12.0
HAND_ORDER = (0, 2, 3, 1)
rope_base = 10000.0
VMEM_BYTES = 48 * 1024 * 1024

f32 = jnp.float32
bf16 = jnp.bfloat16
SMEM = pl.BlockSpec(memory_space=pltpu.SMEM)
VMEM = pl.BlockSpec(memory_space=pltpu.VMEM)
HBM = pl.BlockSpec(memory_space=pltpu.HBM)


def shifted(shard, axis, by):
    peers = lax.axis_size(axis)
    return lax.ppermute(shard, axis, [(i, (i + by) % peers) for i in range(peers)])


def crossed(shard, axis, by):
    peers = lax.axis_size(axis)
    return lax.ppermute(shard, axis, [(i, i ^ by) for i in range(peers)])


def rotary_tables(block_len, block_count):
    half = HEAD_SIZE // 2
    frequency = np.exp(
        np.float32(-math.log(rope_base)) * (2.0 * np.arange(half, dtype=np.float32)) / HEAD_SIZE
    ).astype(np.float64)

    def table(positions):
        angles = positions.astype(np.float64)[:, None] * frequency[None, :]
        cosine, sine = np.cos(angles), np.sin(angles)
        return np.stack(
            [np.concatenate([cosine, cosine], 1), np.concatenate([-sine, sine], 1)]
        ).astype(np.float32)

    return table(np.arange(block_len)), table(np.arange(block_count) * block_len)


def block_angles(row_table, block_table, block):
    row_cos, row_sin = row_table[0], row_table[1]
    blk_cos, blk_sin = block_table[0, pl.ds(block, 1)], block_table[1, pl.ds(block, 1)]
    return row_cos * blk_cos - row_sin * blk_sin, row_sin * blk_cos + row_cos * blk_sin


def turned(head, angles):
    x = head.astype(f32)
    return x * angles[0] + pltpu.roll(x, HEAD_SIZE // 2, 1) * angles[1]


def order_matrix(rank_of, slot, head_group, out_rows, rows, residues):
    row_ids = lax.broadcasted_iota(jnp.int32, (1, rows), 1)
    residue = row_ids % residues
    rank = jnp.zeros_like(row_ids)
    for r in range(residues):
        rank = jnp.where(residue == r, rank_of(r), rank)
    ahead = (rank - HEAD_DIVISIONS * slot + residues) % residues
    ahead = jnp.where(ahead < HEAD_DIVISIONS, ahead ^ head_group, ahead)
    index = ahead * (rows // residues) + row_ids // residues
    out_ids = lax.broadcasted_iota(jnp.int32, (out_rows, rows), 0)
    return jnp.where(out_ids == index, 1.0, 0.0).astype(bf16)


def dot(a, b):
    return jnp.dot(a, b, preferred_element_type=f32)


def dot_t(a, b):
    return lax.dot_general(a, b, (((1,), (1,)), ((), ())), preferred_element_type=f32)


def expo_of(scores):
    return jnp.exp2(cap_value * math.log2(math.e) * jnp.tanh(scores * (1.0 / cap_value)))


def columns(index, width=HEAD_SIZE):
    return slice(index * width, (index + 1) * width)


def call(body, out_shape, in_specs, name, scratch=(), out_specs=None, cost=1000):
    return pl.pallas_call(
        body,
        out_shape=out_shape,
        in_specs=in_specs,
        out_specs=jax.tree.map(lambda _: VMEM, out_shape) if out_specs is None else out_specs,
        scratch_shapes=scratch,
        compiler_params=pltpu.CompilerParams(vmem_limit_bytes=VMEM_BYTES),
        cost_estimate=pl.CostEstimate(flops=cost, bytes_accessed=1000, transcendentals=0),
        name=name,
    )


def in_hbm(arrays):
    return [pltpu.with_memory_space_constraint(x, pltpu.HBM) for x in arrays]


def rows_at(index, size):
    return pl.ds(pl.multiple_of(index * size, size), size)


def beside_ones(values):
    return jnp.concatenate([values, jnp.ones(values.shape, bf16)], axis=1)


class Facts:
    def __init__(self, ref, slots, residues, groups):
        self.ref, self.slots, self.residues, self.groups = ref, slots, residues, groups
        self.size = 2 * slots + residues + groups

    def block(self, slot, half):
        return self.ref[0, 2 * slot + half]

    def rank(self, residue):
        return self.ref[0, 2 * self.slots + residue]

    def owner(self, prompt):
        return self.ref[0, 2 * self.slots + self.residues + prompt]

    def store(self, map_ref, rank_ref, owner_ref):
        for slot in range(self.slots):
            for half in range(2):
                self.ref[0, 2 * slot + half] = map_ref[0, slot, half]
        for residue in range(self.residues):
            self.ref[0, 2 * self.slots + residue] = rank_ref[0, residue]
        for prompt in range(self.groups):
            self.ref[0, 2 * self.slots + self.residues + prompt] = owner_ref[prompt]

    def halves(self, slot):
        high = jnp.where(self.block(slot, 1) > self.block(slot, 0), 1, 0)
        return 1 - high, high


def slot_and_head_group():
    member = lax.axis_index("blk")
    return member // HEAD_DIVISIONS, member % HEAD_DIVISIONS


def prepare(keys, values, table, decode_rank, owner, tables):
    rows, width = keys.shape
    block_len = rows // 2
    slots = table.shape[1]
    residues = decode_rank.shape[1]
    piece = rows // residues
    first = block_len // slots
    arrays = (keys, values, *tables, table, decode_rank, owner)
    count = len(arrays)
    facts_of = lambda ref: Facts(ref, slots, residues, owner.shape[0])

    def body(*refs):
        inputs, refs = refs[:count], refs[count:]
        facts_ref, kr_ref, v_ref, row_ref, blk_ref, select_ref, order_ref = refs[:7]
        e_refs, refs = refs[7:11], refs[11:]
        sent_refs, refs = refs[: 2 * slots - 2], refs[2 * slots - 2 :]
        k_ref, map_ref, rank_ref, owner_ref, sems = refs
        targets = (k_ref, v_ref, row_ref, blk_ref, map_ref, rank_ref, owner_ref)
        copies = []
        for index in range(count):
            copies.append(pltpu.make_async_copy(inputs[index], targets[index], sems.at[index]))
            copies[-1].start()
        slot, head_group = slot_and_head_group()
        for index in (0, 2, 3, 4, 5, 6):
            copies[index].wait()
        facts_of(facts_ref).store(map_ref, rank_ref, owner_ref)
        for half in range(2):
            part = columns(half, block_len)
            angles = block_angles(row_ref, blk_ref, map_ref[0, slot, half])
            for head in range(KV_DEV):
                kr_ref[part, columns(head)] = turned(k_ref[part, columns(head)], angles).astype(bf16)
        select = order_matrix(
            lambda r: rank_ref[0, r], slot, head_group, rows // slots, rows, residues
        )
        select_ref[...] = select
        copies[1].wait()
        for turn in range(1, slots):
            order = order_matrix(
                lambda r: rank_ref[0, r],
                (slot + turn) % slots,
                head_group,
                block_len,
                block_len,
                residues,
            )
            for half in range(2):
                moved = dot(order, v_ref[columns(half, block_len)]).astype(bf16)
                sent_refs[2 * turn - 2][columns(half, first)] = moved[:first]
                sent_refs[2 * turn - 1][columns(half, block_len - first)] = moved[first:]
        order_ref[...] = order_matrix(
            lambda r: rank_ref[0, r], slot, head_group, block_len, block_len, residues
        )
        for kind, source in enumerate((kr_ref, v_ref)):
            chosen = dot(select, source[...]).astype(bf16)
            for m in range(HEAD_DIVISIONS):
                e_refs[m][columns(kind, piece)] = chosen[columns(m, piece)]

    shapes = [
        jax.ShapeDtypeStruct((1, facts_of(None).size), jnp.int32),
        jax.ShapeDtypeStruct(keys.shape, bf16),
        jax.ShapeDtypeStruct(values.shape, bf16),
        jax.ShapeDtypeStruct(tables[0].shape, f32),
        jax.ShapeDtypeStruct(tables[1].shape, f32),
        jax.ShapeDtypeStruct((rows // slots, rows), bf16),
        jax.ShapeDtypeStruct((block_len, block_len), bf16),
    ]
    shapes += [jax.ShapeDtypeStruct((2 * piece, width), bf16) for _ in range(HEAD_DIVISIONS)]
    for _ in range(1, slots):
        shapes.append(jax.ShapeDtypeStruct((2 * first, width), bf16))
        shapes.append(jax.ShapeDtypeStruct((2 * (block_len - first), width), bf16))
    scratch = [pltpu.VMEM(keys.shape, keys.dtype)]
    scratch += [pltpu.SMEM(x.shape, x.dtype) for x in (table, decode_rank, owner)]
    scratch.append(pltpu.SemaphoreType.DMA((count,)))
    outs = call(
        body,
        shapes,
        [HBM] * count,
        "prepare",
        scratch,
        out_specs=[SMEM] + [VMEM] * (len(shapes) - 1),
    )(*in_hbm(arrays))
    return outs[0], facts_of, outs[1:3], outs[3:5], outs[5:7], outs[7:11], outs[11:]


def pair_up(own_length, near_length):
    def body(own_ref, near_ref, pair_ref):
        odd = lax.axis_index("req") % 2 == 1
        pair_ref[0] = jnp.where(odd, near_ref[0], own_ref[0])
        pair_ref[1] = jnp.where(odd, own_ref[0], near_ref[0])

    shape = jax.ShapeDtypeStruct((2,), jnp.int32)
    return call(body, shape, [SMEM] * 2, "pair_up", out_specs=SMEM)(own_length, near_length)


def own_part(facts_row, facts_of, queries, operands, tables):
    rows = queries.shape[0]
    block_len = rows // 2
    slots = facts_of(None).slots

    def body(facts_ref, q_hbm, kr_ref, v_ref, row_ref, blk_ref, *refs):
        qr_ref, acc_ref, angle_ref, q_ref, sem = refs
        copy = pltpu.make_async_copy(q_hbm, q_ref, sem.at[0])
        copy.start()
        facts = facts_of(facts_ref)
        slot = slot_and_head_group()[0]
        copy.wait()
        for half in range(2):
            part = columns(half, block_len)
            angles = block_angles(row_ref, blk_ref, facts.block(slot, half))
            for head in range(Q_DEV):
                qr_ref[part, columns(head)] = (
                    turned(q_ref[part, columns(head)], angles) * query_scale
                ).astype(bf16)
            for turn in range(1, slots):
                block = facts.block((slot - turn + slots) % slots, half)
                other = block_angles(row_ref, blk_ref, block)
                angle_ref[turn - 1, half, 0] = other[0]
                angle_ref[turn - 1, half, 1] = other[1]
        low, high = facts.halves(slot)
        low, high = rows_at(low, block_len), rows_at(high, block_len)
        row = lax.broadcasted_iota(jnp.int32, (block_len, block_len), 0)
        col = lax.broadcasted_iota(jnp.int32, (block_len, block_len), 1)
        for head in range(Q_DEV):
            key_head = columns(head * KV_DEV // Q_DEV)
            both = columns(head, 2 * HEAD_SIZE)

            def tile(q_part, k_part, diagonal):
                expo = expo_of(dot_t(qr_ref[q_part, columns(head)], kr_ref[k_part, key_head]))
                if diagonal:
                    expo = jnp.where(col <= row, expo, 0.0)
                return dot(expo.astype(bf16), beside_ones(v_ref[k_part, key_head]))

            acc_ref[low, both] = tile(low, low, True)
            acc_ref[high, both] = tile(high, high, True) + tile(high, low, False)

    shapes = [
        jax.ShapeDtypeStruct(queries.shape, bf16),
        jax.ShapeDtypeStruct((rows, 2 * Q_DEV * HEAD_SIZE), f32),
        jax.ShapeDtypeStruct((slots - 1, 2, 2, block_len, HEAD_SIZE), f32),
    ]
    scratch = [pltpu.VMEM(queries.shape, bf16), pltpu.SemaphoreType.DMA((1,))]
    specs = [SMEM] + [HBM] + [VMEM] * 4
    return call(body, shapes, specs, "own_part", scratch)(
        facts_row, *in_hbm([queries]), *operands, *tables
    )


def masks_of(facts_row, facts_of, rows, lens):
    block_len = rows // 2
    sizes = facts_of(None)
    slots, residues, groups = sizes.slots, sizes.residues, sizes.groups
    run = block_len // residues
    cache_rows = 2 * slots * run

    def body(facts_ref, here_ref, there_ref, kept_ref, live_ref):
        facts = facts_of(facts_ref)
        slot = slot_and_head_group()[0]
        group = lax.axis_index("req")
        col = lax.broadcasted_iota(jnp.int32, (1, cache_rows), 1)
        part, offset = col // run, col % run
        target = jnp.zeros_like(col)
        for turn in range(slots):
            for half in range(2):
                block = facts.block((slot - turn + slots) % slots, half)
                target = jnp.where(part == 2 * turn + half, block * run + offset, target)
        length = 0
        half_count = groups // 2
        for index in range(half_count):
            same = (group & half_count) | index
            length = length + jnp.where(facts.owner(same) == group, here_ref[index], 0)
            other = same ^ half_count
            length = length + jnp.where(facts.owner(other) == group, there_ref[index], 0)
        residue = 0
        for r in range(1, residues):
            residue = jnp.where(facts.rank(r) == lax.axis_index("blk"), r, residue)
        target = jnp.where(target * residues + residue < length, target, -1)
        row = lax.broadcasted_iota(jnp.int32, (cache_rows, cache_rows), 0)
        kept_ref[...] = jnp.where(row == target, 1.0, 0.0).astype(bf16)
        for half in range(2):
            offset = lax.broadcasted_iota(jnp.int32, (block_len, HEAD_SIZE), 0)
            at = facts.block(slot, half) * block_len + offset
            live_ref[columns(half, block_len)] = jnp.where(at < length, 1.0, 0.0)

    shapes = [
        jax.ShapeDtypeStruct((cache_rows, cache_rows), bf16),
        jax.ShapeDtypeStruct((rows, HEAD_SIZE), f32),
    ]
    return call(body, shapes, [SMEM] * 3, "masks")(facts_row, *lens)


def tiles_of(facts, slot, source):
    low, high = facts.halves(slot)
    source_low, source_high = facts.halves(source)
    outer = facts.block(slot, low) < facts.block(source, source_low)
    first = (jnp.where(outer, high, low), source_low)
    second = (high, jnp.where(outer, source_high, source_low))
    return outer, first, second


def receive_keys(key_in, select, order, angles):
    others = len(key_in)
    rows, width = key_in[0].shape
    block_len = rows // 2

    def body(select_ref, order_ref, angle_ref, *refs):
        k_refs, refs = refs[:others], refs[others:]
        p_refs, chosen_ref, kr_ref = refs[:others], refs[others], refs[others + 1]
        for turn in range(others):
            for half in range(2):
                part = columns(half, block_len)
                there = angle_ref[turn, half, 0], angle_ref[turn, half, 1]
                for head in range(KV_DEV):
                    kr_ref[part, columns(head)] = turned(
                        k_refs[turn][part, columns(head)], there
                    ).astype(bf16)
                p_refs[turn][part] = dot(order_ref[...], kr_ref[part]).astype(bf16)
            chosen_ref[turn] = dot(select_ref[...], kr_ref[...]).astype(bf16)

    shapes = [jax.ShapeDtypeStruct((rows, width), bf16) for _ in range(others)]
    shapes.append(jax.ShapeDtypeStruct((others, select.shape[0], width), bf16))
    scratch = [pltpu.VMEM((rows, width), bf16)]
    outs = call(body, shapes, [VMEM] * (3 + others), "receive_keys", scratch, cost=10**10)(
        select, order, angles, *key_in
    )
    return outs[:others], outs[others]


def weigh(facts_row, facts_of, query_rot, key_rot, payload, after):
    others = len(key_rot)
    rows = query_rot.shape[0]
    block_len = rows // 2
    slots = facts_of(None).slots

    def body(facts_ref, _, q_ref, *refs):
        k_refs, pay_refs, refs = refs[:others], refs[others : 2 * others], refs[2 * others :]
        w_refs, out_refs = refs[:others], refs[others:]
        for pay_ref, out_ref in zip(pay_refs, out_refs):
            out_ref[...] = pay_ref[...]
        facts = facts_of(facts_ref)
        slot = slot_and_head_group()[0]
        for turn in range(1, slots):
            _, *tiles = tiles_of(facts, slot, (slot - turn + slots) % slots)
            for index, (half, other) in enumerate(tiles):
                for head in range(Q_DEV):
                    key_head = columns(head * KV_DEV // Q_DEV)
                    queries = q_ref[rows_at(half, block_len), columns(head)]
                    keys = k_refs[turn - 1][rows_at(other, block_len), key_head]
                    w_refs[turn - 1][index, head] = expo_of(dot_t(queries, keys)).astype(bf16)

    shapes = [
        jax.ShapeDtypeStruct((2, Q_DEV, block_len, block_len), bf16) for _ in range(others)
    ]
    shapes += [jax.ShapeDtypeStruct(x.shape, bf16) for x in payload]
    outs = call(body, shapes, [SMEM] + [VMEM] * (2 + 2 * others), "weigh")(
        facts_row, after, query_rot, *key_rot, *payload
    )
    return outs[:others], outs[others:]


def late_pieces(heads, key_chosen, after):
    others, rows, width = key_chosen.shape
    piece = rows // HEAD_DIVISIONS
    run = piece // 2
    first = heads[0].shape[0] // 2

    def body(key_ref, *refs):
        v_refs, e_refs = refs[:others], refs[others + len(after) :]
        for m in range(HEAD_DIVISIONS):
            for turn in range(others):
                e_refs[m][columns(turn, piece)] = key_ref[turn, columns(m, piece)]
                place = 2 * (others + turn)
                if run % 16 == 0:
                    for half in range(2):
                        start = half * first + m * run
                        e_refs[m][columns(place + half, run)] = v_refs[turn][start : start + run]
                    continue
                lines = [
                    v_refs[turn][columns(half, first)].astype(f32)[columns(m, run)]
                    for half in range(2)
                ]
                e_refs[m][place * run : (place + 2) * run] = jnp.concatenate(lines, 0).astype(bf16)

    shapes = [
        jax.ShapeDtypeStruct((2 * others * piece, width), bf16) for _ in range(HEAD_DIVISIONS)
    ]
    return call(body, shapes, [VMEM] * (1 + others + len(after)), "late_pieces")(
        key_chosen, *heads, *after
    )


def attend(facts_row, facts_of, weights, acc, heads, tails, live):
    rows = live.shape[0]
    block_len = rows // 2
    others = len(weights)
    slots = facts_of(None).slots

    def body(facts_ref, acc_ref, live_ref, *refs):
        w_refs, h_refs, t_refs = refs[:others], refs[others : 2 * others], refs[2 * others : 3 * others]
        out_ref, mark_ref, v_scr = refs[3 * others :]
        mark_ref[...] = jnp.zeros_like(mark_ref)
        for turn in range(others):
            first, rest = h_refs[turn].shape[0] // 2, t_refs[turn].shape[0] // 2
            for half in range(2):
                v_scr[turn, columns(half, block_len)] = jnp.concatenate(
                    [h_refs[turn][columns(half, first)], t_refs[turn][columns(half, rest)]], axis=0
                )
        facts = facts_of(facts_ref)
        slot = slot_and_head_group()[0]
        low, high = facts.halves(slot)
        low_rows, high_rows = rows_at(low, block_len), rows_at(high, block_len)
        for head in range(Q_DEV):
            key_head = columns(head * KV_DEV // Q_DEV)
            both = columns(head, 2 * HEAD_SIZE)
            low_sum, high_sum = acc_ref[low_rows, both], acc_ref[high_rows, both]
            for turn in range(1, slots):
                outer, *tiles = tiles_of(facts, slot, (slot - turn + slots) % slots)
                either, upper = [
                    dot(
                        w_refs[turn - 1][index, head],
                        beside_ones(v_scr[turn - 1, rows_at(other, block_len), key_head]),
                    )
                    for index, (_, other) in enumerate(tiles)
                ]
                low_sum = low_sum + jnp.where(outer, 0.0, either)
                high_sum = high_sum + upper + jnp.where(outer, either, 0.0)
            for part, total in ((low_rows, low_sum), (high_rows, high_sum)):
                scale = live_ref[part] / total[:, HEAD_SIZE:]
                out_ref[part, columns(head)] = (total[:, :HEAD_SIZE] * scale).astype(bf16)

    shape = [
        jax.ShapeDtypeStruct((rows, Q_DEV * HEAD_SIZE), bf16),
        jax.ShapeDtypeStruct((8, HEAD_SIZE), f32),
    ]
    specs = [SMEM] + [VMEM] * (2 + 3 * others)
    scratch = [pltpu.VMEM((others, rows, KV_WIDTH), bf16)]
    return call(body, shape, specs, "attend", scratch)(
        facts_row, acc, live, *weights, *heads, *tails
    )


def cache_part(early, late, kept, mark):
    cache_rows = kept.shape[0]
    piece = early[0].shape[0] // 2
    width = early[0].shape[1]

    def body(kept_ref, *refs):
        f_refs, s_refs, out_ref = refs[:4], refs[4:8], refs[9]
        head_group = slot_and_head_group()[1]
        later = cache_rows - piece
        for index, m in enumerate(HAND_ORDER):
            for kind in range(2):
                lines = jnp.concatenate(
                    [f_refs[index][columns(kind, piece)], s_refs[index][columns(kind, later)]], axis=0
                )
                column = ((head_group ^ m) + kind * HEAD_DIVISIONS) * width
                out_ref[:, pl.ds(pl.multiple_of(column, HEAD_SIZE), width)] = dot(
                    kept_ref[...], lines
                ).astype(bf16)

    shape = jax.ShapeDtypeStruct((cache_rows, 2 * HEAD_DIVISIONS * width), bf16)
    return call(body, shape, [VMEM] * 10, "cache_part")(kept, *early, *late, mark)


def on_device(queries, keys, values, block_map, lengths, group_of_prompt, decode_rank):
    block_len = queries.shape[2] // 2
    slots = block_map.shape[1]
    q, k, v = queries[0, 0], keys[0, 0], values[0, 0]
    tables = rotary_tables(block_len, 2 * slots)

    def to_slots(parts):
        return [shifted(parts[t - 1], "blk", HEAD_DIVISIONS * t) for t in range(1, slots)]

    def hand_on(pieces):
        return [pieces[0]] + [crossed(pieces[m], "blk", m) for m in HAND_ORDER[1:]]

    key_in = to_slots([k] * (slots - 1))
    facts_row, facts_of, operands, tables, (select, order), early, sent = prepare(
        k, v, block_map, decode_rank, group_of_prompt, tables
    )
    heads = to_slots(sent[0::2])
    early = hand_on(early)
    block = pair_up(lengths, crossed(lengths, "req", 1))
    span, groups = 2, lax.axis_size("req")
    while 2 * span < groups:
        other = crossed(block, "req", span)
        upper = (lax.axis_index("req") & span) > 0
        block = jnp.where(
            upper, jnp.concatenate([other, block]), jnp.concatenate([block, other])
        )
        span = 2 * span
    lens = (block, crossed(block, "req", span))
    query_rot, acc, angles = own_part(facts_row, facts_of, q, operands, tables)
    kept, live = masks_of(facts_row, facts_of, q.shape[0], lens)
    key_rot, chosen = receive_keys(key_in, select, order, angles)
    weights, tails = weigh(facts_row, facts_of, query_rot, key_rot, sent[1::2], live)
    tails = to_slots(tails)
    late = hand_on(late_pieces(heads, chosen, early[1:]))
    attended, mark = attend(facts_row, facts_of, weights, acc, heads, tails, live)
    cache = cache_part(early, late, kept, mark)
    return (attended[None, None], cache[None])


def solution(mesh):
    placed = (
        P("req", "blk", None, None),
        P("req", "blk", None, None),
        P("req", "blk", None, None),
        P("req", None, None),
        P("req"),
        P(),
        P("req", None),
    )
    return jax.shard_map(
        on_device,
        mesh=mesh,
        in_specs=placed,
        out_specs=(P("req", "blk", None, None), P("req", "blk", None)),
        check_vma=False,
    )
```

```python
import math

import jax
import jax.numpy as jnp
import numpy as np
from jax import lax
from jax.experimental import pallas as pl
from jax.experimental.pallas import tpu as pltpu
from jax.sharding import PartitionSpec as P

QUERY_HEADS = 16
KEY_VALUE_HEADS = 8
HEAD_SIZE = 128
HEAD_DIVISIONS = 4
Q_DEV = 4
KV_DEV = 2
KV_WIDTH = KV_DEV * HEAD_SIZE

cap_value = 50.0
query_scale = 1.0 / 12.0
HAND_ORDER = (0, 2, 3, 1)
rope_base = 10000.0
VMEM_BYTES = 48 * 1024 * 1024

f32 = jnp.float32
bf16 = jnp.bfloat16
SMEM = pl.BlockSpec(memory_space=pltpu.SMEM)
VMEM = pl.BlockSpec(memory_space=pltpu.VMEM)
HBM = pl.BlockSpec(memory_space=pltpu.HBM)


def shifted(shard, axis, by):
    peers = lax.axis_size(axis)
    return lax.ppermute(shard, axis, [(i, (i + by) % peers) for i in range(peers)])


def crossed(shard, axis, by):
    peers = lax.axis_size(axis)
    return lax.ppermute(shard, axis, [(i, i ^ by) for i in range(peers)])


def rotary_tables(block_len, block_count):
    half = HEAD_SIZE // 2
    frequency = np.exp(
        np.float32(-math.log(rope_base)) * (2.0 * np.arange(half, dtype=np.float32)) / HEAD_SIZE
    ).astype(np.float64)

    def table(positions):
        angles = positions.astype(np.float64)[:, None] * frequency[None, :]
        cosine, sine = np.cos(angles), np.sin(angles)
        return np.stack(
            [np.concatenate([cosine, cosine], 1), np.concatenate([-sine, sine], 1)]
        ).astype(np.float32)

    return table(np.arange(block_len)), table(np.arange(block_count) * block_len)


def block_angles(row_table, block_table, block):
    row_cos, row_sin = row_table[0], row_table[1]
    blk_cos, blk_sin = block_table[0, pl.ds(block, 1)], block_table[1, pl.ds(block, 1)]
    return row_cos * blk_cos - row_sin * blk_sin, row_sin * blk_cos + row_cos * blk_sin


def turned(head, angles):
    x = head.astype(f32)
    return x * angles[0] + pltpu.roll(x, HEAD_SIZE // 2, 1) * angles[1]


def order_matrix(rank_of, slot, head_group, out_rows, rows, residues):
    row_ids = lax.broadcasted_iota(jnp.int32, (1, rows), 1)
    residue = row_ids % residues
    rank = jnp.zeros_like(row_ids)
    for r in range(residues):
        rank = jnp.where(residue == r, rank_of(r), rank)
    ahead = (rank - HEAD_DIVISIONS * slot + residues) % residues
    ahead = jnp.where(ahead < HEAD_DIVISIONS, ahead ^ head_group, ahead)
    index = ahead * (rows // residues) + row_ids // residues
    out_ids = lax.broadcasted_iota(jnp.int32, (out_rows, rows), 0)
    return jnp.where(out_ids == index, 1.0, 0.0).astype(bf16)


def dot(a, b):
    return jnp.dot(a, b, preferred_element_type=f32)


def dot_t(a, b):
    return lax.dot_general(a, b, (((1,), (1,)), ((), ())), preferred_element_type=f32)


def expo_of(scores):
    return jnp.exp2(cap_value * math.log2(math.e) * jnp.tanh(scores * (1.0 / cap_value)))


def columns(index, width=HEAD_SIZE):
    return slice(index * width, (index + 1) * width)


def call(body, out_shape, in_specs, name, scratch=(), out_specs=None, cost=1000):
    return pl.pallas_call(
        body,
        out_shape=out_shape,
        in_specs=in_specs,
        out_specs=jax.tree.map(lambda _: VMEM, out_shape) if out_specs is None else out_specs,
        scratch_shapes=scratch,
        compiler_params=pltpu.CompilerParams(vmem_limit_bytes=VMEM_BYTES),
        cost_estimate=pl.CostEstimate(flops=cost, bytes_accessed=1000, transcendentals=0),
        name=name,
    )


def in_hbm(arrays):
    return [pltpu.with_memory_space_constraint(x, pltpu.HBM) for x in arrays]


def rows_at(index, size):
    return pl.ds(pl.multiple_of(index * size, size), size)


def beside_ones(values):
    return jnp.concatenate([values, jnp.ones(values.shape, bf16)], axis=1)


class Facts:
    def __init__(self, ref, slots, residues, groups):
        self.ref, self.slots, self.residues, self.groups = ref, slots, residues, groups
        self.size = 2 * slots + residues + groups

    def block(self, slot, half):
        return self.ref[0, 2 * slot + half]

    def rank(self, residue):
        return self.ref[0, 2 * self.slots + residue]

    def owner(self, prompt):
        return self.ref[0, 2 * self.slots + self.residues + prompt]

    def store(self, map_ref, rank_ref, owner_ref):
        for slot in range(self.slots):
            for half in range(2):
                self.ref[0, 2 * slot + half] = map_ref[0, slot, half]
        for residue in range(self.residues):
            self.ref[0, 2 * self.slots + residue] = rank_ref[0, residue]
        for prompt in range(self.groups):
            self.ref[0, 2 * self.slots + self.residues + prompt] = owner_ref[prompt]

    def halves(self, slot):
        high = jnp.where(self.block(slot, 1) > self.block(slot, 0), 1, 0)
        return 1 - high, high


def slot_and_head_group():
    member = lax.axis_index("blk")
    return member // HEAD_DIVISIONS, member % HEAD_DIVISIONS


def prepare(keys, values, table, decode_rank, owner, tables):
    rows, width = keys.shape
    block_len = rows // 2
    slots = table.shape[1]
    residues = decode_rank.shape[1]
    piece = rows // residues
    first = block_len // slots
    arrays = (keys, values, *tables, table, decode_rank, owner)
    count = len(arrays)
    facts_of = lambda ref: Facts(ref, slots, residues, owner.shape[0])

    def body(*refs):
        inputs, refs = refs[:count], refs[count:]
        facts_ref, kr_ref, v_ref, row_ref, blk_ref, select_ref, order_ref = refs[:7]
        e_refs, refs = refs[7:11], refs[11:]
        sent_refs, refs = refs[: 2 * slots - 2], refs[2 * slots - 2 :]
        k_ref, map_ref, rank_ref, owner_ref, sems = refs
        targets = (k_ref, v_ref, row_ref, blk_ref, map_ref, rank_ref, owner_ref)
        copies = []
        for index in range(count):
            copies.append(pltpu.make_async_copy(inputs[index], targets[index], sems.at[index]))
            copies[-1].start()
        slot, head_group = slot_and_head_group()
        for index in (0, 2, 3, 4, 5, 6):
            copies[index].wait()
        facts_of(facts_ref).store(map_ref, rank_ref, owner_ref)
        for half in range(2):
            part = columns(half, block_len)
            angles = block_angles(row_ref, blk_ref, map_ref[0, slot, half])
            for head in range(KV_DEV):
                kr_ref[part, columns(head)] = turned(k_ref[part, columns(head)], angles).astype(bf16)
        select = order_matrix(
            lambda r: rank_ref[0, r], slot, head_group, rows // slots, rows, residues
        )
        select_ref[...] = select
        copies[1].wait()
        for turn in range(1, slots):
            order = order_matrix(
                lambda r: rank_ref[0, r],
                (slot + turn) % slots,
                head_group,
                block_len,
                block_len,
                residues,
            )
            for half in range(2):
                moved = dot(order, v_ref[columns(half, block_len)]).astype(bf16)
                sent_refs[2 * turn - 2][columns(half, first)] = moved[:first]
                sent_refs[2 * turn - 1][columns(half, block_len - first)] = moved[first:]
        order_ref[...] = order_matrix(
            lambda r: rank_ref[0, r], slot, head_group, block_len, block_len, residues
        )
        for kind, source in enumerate((kr_ref, v_ref)):
            chosen = dot(select, source[...]).astype(bf16)
            for m in range(HEAD_DIVISIONS):
                e_refs[m][columns(kind, piece)] = chosen[columns(m, piece)]

    shapes = [
        jax.ShapeDtypeStruct((1, facts_of(None).size), jnp.int32),
        jax.ShapeDtypeStruct(keys.shape, bf16),
        jax.ShapeDtypeStruct(values.shape, bf16),
        jax.ShapeDtypeStruct(tables[0].shape, f32),
        jax.ShapeDtypeStruct(tables[1].shape, f32),
        jax.ShapeDtypeStruct((rows // slots, rows), bf16),
        jax.ShapeDtypeStruct((block_len, block_len), bf16),
    ]
    shapes += [jax.ShapeDtypeStruct((2 * piece, width), bf16) for _ in range(HEAD_DIVISIONS)]
    for _ in range(1, slots):
        shapes.append(jax.ShapeDtypeStruct((2 * first, width), bf16))
        shapes.append(jax.ShapeDtypeStruct((2 * (block_len - first), width), bf16))
    scratch = [pltpu.VMEM(keys.shape, keys.dtype)]
    scratch += [pltpu.SMEM(x.shape, x.dtype) for x in (table, decode_rank, owner)]
    scratch.append(pltpu.SemaphoreType.DMA((count,)))
    outs = call(
        body,
        shapes,
        [HBM] * count,
        "prepare",
        scratch,
        out_specs=[SMEM] + [VMEM] * (len(shapes) - 1),
    )(*in_hbm(arrays))
    return outs[0], facts_of, outs[1:3], outs[3:5], outs[5:7], outs[7:11], outs[11:]


def own_part(facts_row, facts_of, queries, operands, tables):
    rows = queries.shape[0]
    block_len = rows // 2
    slots = facts_of(None).slots

    def body(facts_ref, q_hbm, kr_ref, v_ref, row_ref, blk_ref, *refs):
        qr_ref, acc_ref, angle_ref, q_ref, sem = refs
        copy = pltpu.make_async_copy(q_hbm, q_ref, sem.at[0])
        copy.start()
        facts = facts_of(facts_ref)
        slot = slot_and_head_group()[0]
        copy.wait()
        for half in range(2):
            part = columns(half, block_len)
            angles = block_angles(row_ref, blk_ref, facts.block(slot, half))
            for head in range(Q_DEV):
                qr_ref[part, columns(head)] = (
                    turned(q_ref[part, columns(head)], angles) * query_scale
                ).astype(bf16)
            for turn in range(1, slots):
                block = facts.block((slot - turn + slots) % slots, half)
                other = block_angles(row_ref, blk_ref, block)
                angle_ref[turn - 1, half, 0] = other[0]
                angle_ref[turn - 1, half, 1] = other[1]
        low, high = facts.halves(slot)
        low, high = rows_at(low, block_len), rows_at(high, block_len)
        row = lax.broadcasted_iota(jnp.int32, (block_len, block_len), 0)
        col = lax.broadcasted_iota(jnp.int32, (block_len, block_len), 1)
        for head in range(Q_DEV):
            key_head = columns(head * KV_DEV // Q_DEV)
            both = columns(head, 2 * HEAD_SIZE)

            def tile(q_part, k_part, diagonal):
                expo = expo_of(dot_t(qr_ref[q_part, columns(head)], kr_ref[k_part, key_head]))
                if diagonal:
                    expo = jnp.where(col <= row, expo, 0.0)
                return dot(expo.astype(bf16), beside_ones(v_ref[k_part, key_head]))

            acc_ref[low, both] = tile(low, low, True)
            acc_ref[high, both] = tile(high, high, True) + tile(high, low, False)

    shapes = [
        jax.ShapeDtypeStruct(queries.shape, bf16),
        jax.ShapeDtypeStruct((rows, 2 * Q_DEV * HEAD_SIZE), f32),
        jax.ShapeDtypeStruct((slots - 1, 2, 2, block_len, HEAD_SIZE), f32),
    ]
    scratch = [pltpu.VMEM(queries.shape, bf16), pltpu.SemaphoreType.DMA((1,))]
    specs = [SMEM] + [HBM] + [VMEM] * 4
    return call(body, shapes, specs, "own_part", scratch)(
        facts_row, *in_hbm([queries]), *operands, *tables
    )


def masks_of(facts_row, facts_of, rows, lens):
    block_len = rows // 2
    sizes = facts_of(None)
    slots, residues, groups = sizes.slots, sizes.residues, sizes.groups
    run = block_len // residues
    cache_rows = 2 * slots * run

    def body(facts_ref, *refs):
        len_refs, kept_ref, live_ref = refs[:groups], refs[groups], refs[groups + 1]
        facts = facts_of(facts_ref)
        slot = slot_and_head_group()[0]
        group = lax.axis_index("req")
        col = lax.broadcasted_iota(jnp.int32, (1, cache_rows), 1)
        part, offset = col // run, col % run
        target = jnp.zeros_like(col)
        for turn in range(slots):
            for half in range(2):
                block = facts.block((slot - turn + slots) % slots, half)
                target = jnp.where(part == 2 * turn + half, block * run + offset, target)
        length = 0
        for turn in range(groups):
            mine = facts.owner(lax.rem(group - turn + groups, groups)) == group
            length = length + jnp.where(mine, len_refs[turn][0], 0)
        residue = 0
        for r in range(1, residues):
            residue = jnp.where(facts.rank(r) == lax.axis_index("blk"), r, residue)
        target = jnp.where(target * residues + residue < length, target, -1)
        row = lax.broadcasted_iota(jnp.int32, (cache_rows, cache_rows), 0)
        kept_ref[...] = jnp.where(row == target, 1.0, 0.0).astype(bf16)
        for half in range(2):
            offset = lax.broadcasted_iota(jnp.int32, (block_len, HEAD_SIZE), 0)
            at = facts.block(slot, half) * block_len + offset
            live_ref[columns(half, block_len)] = jnp.where(at < length, 1.0, 0.0)

    shapes = [
        jax.ShapeDtypeStruct((cache_rows, cache_rows), bf16),
        jax.ShapeDtypeStruct((rows, HEAD_SIZE), f32),
    ]
    return call(body, shapes, [SMEM] * (1 + groups), "masks")(facts_row, *lens)


def tiles_of(facts, slot, source):
    low, high = facts.halves(slot)
    source_low, source_high = facts.halves(source)
    outer = facts.block(slot, low) < facts.block(source, source_low)
    first = (jnp.where(outer, high, low), source_low)
    second = (high, jnp.where(outer, source_high, source_low))
    return outer, first, second


def receive_keys(key_in, select, order, angles):
    others = len(key_in)
    rows, width = key_in[0].shape
    block_len = rows // 2

    def body(select_ref, order_ref, angle_ref, *refs):
        k_refs, refs = refs[:others], refs[others:]
        p_refs, chosen_ref, kr_ref = refs[:others], refs[others], refs[others + 1]
        for turn in range(others):
            for half in range(2):
                part = columns(half, block_len)
                there = angle_ref[turn, half, 0], angle_ref[turn, half, 1]
                for head in range(KV_DEV):
                    kr_ref[part, columns(head)] = turned(
                        k_refs[turn][part, columns(head)], there
                    ).astype(bf16)
                p_refs[turn][part] = dot(order_ref[...], kr_ref[part]).astype(bf16)
            chosen_ref[turn] = dot(select_ref[...], kr_ref[...]).astype(bf16)

    shapes = [jax.ShapeDtypeStruct((rows, width), bf16) for _ in range(others)]
    shapes.append(jax.ShapeDtypeStruct((others, select.shape[0], width), bf16))
    scratch = [pltpu.VMEM((rows, width), bf16)]
    outs = call(body, shapes, [VMEM] * (3 + others), "receive_keys", scratch, cost=10**10)(
        select, order, angles, *key_in
    )
    return outs[:others], outs[others]


def weigh(facts_row, facts_of, query_rot, key_rot, payload, after):
    others = len(key_rot)
    rows = query_rot.shape[0]
    block_len = rows // 2
    slots = facts_of(None).slots

    def body(facts_ref, _, q_ref, *refs):
        k_refs, pay_refs, refs = refs[:others], refs[others : 2 * others], refs[2 * others :]
        w_refs, out_refs = refs[:others], refs[others:]
        for pay_ref, out_ref in zip(pay_refs, out_refs):
            out_ref[...] = pay_ref[...]
        facts = facts_of(facts_ref)
        slot = slot_and_head_group()[0]
        for turn in range(1, slots):
            _, *tiles = tiles_of(facts, slot, (slot - turn + slots) % slots)
            for index, (half, other) in enumerate(tiles):
                for head in range(Q_DEV):
                    key_head = columns(head * KV_DEV // Q_DEV)
                    queries = q_ref[rows_at(half, block_len), columns(head)]
                    keys = k_refs[turn - 1][rows_at(other, block_len), key_head]
                    w_refs[turn - 1][index, head] = expo_of(dot_t(queries, keys)).astype(bf16)

    shapes = [
        jax.ShapeDtypeStruct((2, Q_DEV, block_len, block_len), bf16) for _ in range(others)
    ]
    shapes += [jax.ShapeDtypeStruct(x.shape, bf16) for x in payload]
    outs = call(body, shapes, [SMEM] + [VMEM] * (2 + 2 * others), "weigh")(
        facts_row, after, query_rot, *key_rot, *payload
    )
    return outs[:others], outs[others:]


def late_pieces(heads, key_chosen, after):
    others, rows, width = key_chosen.shape
    piece = rows // HEAD_DIVISIONS
    run = piece // 2
    first = heads[0].shape[0] // 2

    def body(key_ref, *refs):
        v_refs, e_refs = refs[:others], refs[others + len(after) :]
        for m in range(HEAD_DIVISIONS):
            for turn in range(others):
                e_refs[m][columns(turn, piece)] = key_ref[turn, columns(m, piece)]
                place = 2 * (others + turn)
                if run % 16 == 0:
                    for half in range(2):
                        start = half * first + m * run
                        e_refs[m][columns(place + half, run)] = v_refs[turn][start : start + run]
                    continue
                lines = [
                    v_refs[turn][columns(half, first)].astype(f32)[columns(m, run)]
                    for half in range(2)
                ]
                e_refs[m][place * run : (place + 2) * run] = jnp.concatenate(lines, 0).astype(bf16)

    shapes = [
        jax.ShapeDtypeStruct((2 * others * piece, width), bf16) for _ in range(HEAD_DIVISIONS)
    ]
    return call(body, shapes, [VMEM] * (1 + others + len(after)), "late_pieces")(
        key_chosen, *heads, *after
    )


def attend(facts_row, facts_of, weights, acc, heads, tails, live):
    rows = live.shape[0]
    block_len = rows // 2
    others = len(weights)
    slots = facts_of(None).slots

    def body(facts_ref, acc_ref, live_ref, *refs):
        w_refs, h_refs, t_refs = refs[:others], refs[others : 2 * others], refs[2 * others : 3 * others]
        out_ref, mark_ref, v_scr = refs[3 * others :]
        mark_ref[...] = jnp.zeros_like(mark_ref)
        for turn in range(others):
            first, rest = h_refs[turn].shape[0] // 2, t_refs[turn].shape[0] // 2
            for half in range(2):
                v_scr[turn, columns(half, block_len)] = jnp.concatenate(
                    [h_refs[turn][columns(half, first)], t_refs[turn][columns(half, rest)]], axis=0
                )
        facts = facts_of(facts_ref)
        slot = slot_and_head_group()[0]
        low, high = facts.halves(slot)
        low_rows, high_rows = rows_at(low, block_len), rows_at(high, block_len)
        for head in range(Q_DEV):
            key_head = columns(head * KV_DEV // Q_DEV)
            both = columns(head, 2 * HEAD_SIZE)
            low_sum, high_sum = acc_ref[low_rows, both], acc_ref[high_rows, both]
            for turn in range(1, slots):
                outer, *tiles = tiles_of(facts, slot, (slot - turn + slots) % slots)
                either, upper = [
                    dot(
                        w_refs[turn - 1][index, head],
                        beside_ones(v_scr[turn - 1, rows_at(other, block_len), key_head]),
                    )
                    for index, (_, other) in enumerate(tiles)
                ]
                low_sum = low_sum + jnp.where(outer, 0.0, either)
                high_sum = high_sum + upper + jnp.where(outer, either, 0.0)
            for part, total in ((low_rows, low_sum), (high_rows, high_sum)):
                scale = live_ref[part] / total[:, HEAD_SIZE:]
                out_ref[part, columns(head)] = (total[:, :HEAD_SIZE] * scale).astype(bf16)

    shape = [
        jax.ShapeDtypeStruct((rows, Q_DEV * HEAD_SIZE), bf16),
        jax.ShapeDtypeStruct((8, HEAD_SIZE), f32),
    ]
    specs = [SMEM] + [VMEM] * (2 + 3 * others)
    scratch = [pltpu.VMEM((others, rows, KV_WIDTH), bf16)]
    return call(body, shape, specs, "attend", scratch)(
        facts_row, acc, live, *weights, *heads, *tails
    )


def cache_part(early, late, kept, mark):
    cache_rows = kept.shape[0]
    piece = early[0].shape[0] // 2
    width = early[0].shape[1]

    def body(kept_ref, *refs):
        f_refs, s_refs, out_ref = refs[:4], refs[4:8], refs[9]
        head_group = slot_and_head_group()[1]
        later = cache_rows - piece
        for index, m in enumerate(HAND_ORDER):
            for kind in range(2):
                lines = jnp.concatenate(
                    [f_refs[index][columns(kind, piece)], s_refs[index][columns(kind, later)]], axis=0
                )
                column = ((head_group ^ m) + kind * HEAD_DIVISIONS) * width
                out_ref[:, pl.ds(pl.multiple_of(column, HEAD_SIZE), width)] = dot(
                    kept_ref[...], lines
                ).astype(bf16)

    shape = jax.ShapeDtypeStruct((cache_rows, 2 * HEAD_DIVISIONS * width), bf16)
    return call(body, shape, [VMEM] * 10, "cache_part")(kept, *early, *late, mark)


def on_device(queries, keys, values, block_map, lengths, group_of_prompt, decode_rank):
    block_len = queries.shape[2] // 2
    slots = block_map.shape[1]
    q, k, v = queries[0, 0], keys[0, 0], values[0, 0]
    tables = rotary_tables(block_len, 2 * slots)

    def to_slots(parts):
        return [shifted(parts[t - 1], "blk", HEAD_DIVISIONS * t) for t in range(1, slots)]

    def hand_on(pieces):
        return [pieces[0]] + [crossed(pieces[m], "blk", m) for m in HAND_ORDER[1:]]

    key_in = to_slots([k] * (slots - 1))
    facts_row, facts_of, operands, tables, (select, order), early, sent = prepare(
        k, v, block_map, decode_rank, group_of_prompt, tables
    )
    heads = to_slots(sent[0::2])
    early = hand_on(early)
    groups = lax.axis_size("req")
    lens = [lengths] + [shifted(lengths, "req", t) for t in range(1, groups)]
    query_rot, acc, angles = own_part(facts_row, facts_of, q, operands, tables)
    kept, live = masks_of(facts_row, facts_of, q.shape[0], lens)
    key_rot, chosen = receive_keys(key_in, select, order, angles)
    weights, tails = weigh(facts_row, facts_of, query_rot, key_rot, sent[1::2], live)
    tails = to_slots(tails)
    late = hand_on(late_pieces(heads, chosen, early[1:]))
    attended, mark = attend(facts_row, facts_of, weights, acc, heads, tails, live)
    cache = cache_part(early, late, kept, mark)
    return (attended[None, None], cache[None])


def solution(mesh):
    placed = (
        P("req", "blk", None, None),
        P("req", "blk", None, None),
        P("req", "blk", None, None),
        P("req", None, None),
        P("req"),
        P(),
        P("req", None),
    )
    return jax.shard_map(
        on_device,
        mesh=mesh,
        in_specs=placed,
        out_specs=(P("req", "blk", None, None), P("req", "blk", None)),
        check_vma=False,
    )
```
